32 devices in a mesh: row: 8 (over y, x, core), head: 4 (over z).
Axes of the slice: x: 2, y: 2, z: 4, core: 2. Of those that a mesh axis runs over, the one named last changes fastest.
Arguments:
- alignment: float32 [128, 512, 256], P('row'), may hold values from -6 to 6
- pairs: float32 [512, 512, 128], P('row', 'head'), may hold values from -6 to 6
- residue_mask: int32 [512], replicated, may hold values 0 or 1
- row_mask: int32 [128], P('row'), may hold values 0 or 1
- alignment_back: float32 [128, 512, 256], P('row'), may hold values from -6 to 6
- pairs_back: float32 [512, 512, 128], P('row', 'head'), may hold values from -6 to 6
- norm_scales: float32 [2, 640], replicated, may hold values from -0.8 to 1.2
- heads_in: float32 [4, 256, 256], P(None, None, 'head'), may hold values from -0.375 to 0.375
- heads_out: float32 [256, 256], P('head'), may hold values from -6 to 6
- bias_weight: float32 [128, 8], replicated, may hold values from -0.5 to 0.5
- outer_in: float32 [2, 256, 32], replicated, may hold values from -0.375 to 0.375
- outer_out: float32 [1024, 128], replicated, may hold values from -2 to 2
- first_norms: float32 [2, 640], replicated, may hold values from -160 to 160
- second_norms: float32 [2, 640], replicated, may hold values from 65.536 to 262.144
- first_heads_in: float32 [4, 256, 256], P(None, None, 'head'), may hold values from -160 to 160
- second_heads_in: float32 [4, 256, 256], P(None, None, 'head'), may hold values from 65.536 to 262.144
- first_heads_out: float32 [256, 256], P('head'), may hold values from -4 to 4
- second_heads_out: float32 [256, 256], P('head'), may hold values from 0.256 to 1.024
- first_bias_weight: float32 [128, 8], replicated, may hold values from -2560 to 2560
- second_bias_weight: float32 [128, 8], replicated, may hold values from 16777.217 to 67108.87
- first_outer_in: float32 [2, 256, 32], replicated, may hold values from -640 to 640
- second_outer_in: float32 [2, 256, 32], replicated, may hold values from 1048.576 to 4194.304
- first_outer_out: float32 [1024, 128], replicated, may hold values from -28 to 28
- second_outer_out: float32 [1024, 128], replicated, may hold values from 2.048 to 8.192
Outputs:
- alignment_out: float32 [128, 512, 256], P('row')
- pairs_out: float32 [512, 512, 128], P('row', 'head')
- alignment_grad: float32 [128, 512, 256], P('row')
- pairs_grad: float32 [512, 512, 128], P('row', 'head')
- norms_first_new: float32 [2, 640], replicated
- norms_second_new: float32 [2, 640], replicated
- norm_scales_new: float32 [2, 640], replicated
- heads_in_first: float32 [4, 256, 256], P(None, None, 'head')
- heads_in_second: float32 [4, 256, 256], P(None, None, 'head')
- heads_in_new: float32 [4, 256, 256], P(None, None, 'head')
- heads_out_first: float32 [256, 256], P('head')
- heads_out_second: float32 [256, 256], P('head')
- heads_out_new: float32 [256, 256], P('head')
- bias_weight_first: float32 [128, 8], replicated
- bias_weight_second: float32 [128, 8], replicated
- bias_weight_new: float32 [128, 8], replicated
- outer_in_first: float32 [2, 256, 32], replicated
- outer_in_second: float32 [2, 256, 32], replicated
- outer_in_new: float32 [2, 256, 32], replicated
- outer_out_first: float32 [1024, 128], replicated
- outer_out_second: float32 [1024, 128], replicated
- outer_out_new: float32 [1024, 128], replicated
The draws below stay inside these ranges and needn't reach their ends.
All inputs are finite; a program needn't handle non-finite values. No bound on the sum of `row_mask` on one device may be relied on, other than what follows from the above.
Results may differ from the reference program's by a relative error of at most 0.012.
Values may be sent and summed in bfloat16 or wider, within the bound.
A program may use at most 320 MiB of HBM per device.

```python
import math
import jax
import jax.numpy as jnp
from jax import lax

C_M = 256
C_Z = 128
HEADS = 8
D_HEAD = 32
C_O = 32
RESIDUES = 512
ROWS = 128
NORMS = 640
STEP = 10


def draw_norm_scales(key, part):
    key = jax.random.fold_in(key, 5)
    gain_key, shift_key = jax.random.split(key)
    gain_values = 1.0 + 0.2 * jax.random.uniform(gain_key, (NORMS,), jnp.float32, -1.0, 1.0)
    shift_values = jnp.clip(0.2 * jax.random.normal(shift_key, (NORMS,), jnp.float32), -0.8, 0.8)
    return jnp.stack([gain_values, shift_values])


def with_ends(values, stream_key, least, top_value):
    spot = [jax.random.randint(jax.random.fold_in(stream_key, axis), (), 0, length) for axis, length in enumerate(values.shape)]
    widest = values.shape.index(max(values.shape))
    beside = spot[:widest] + [(spot[widest] + 1) % values.shape[widest]] + spot[widest + 1:]
    return values.at[tuple(spot)].set(least).at[tuple(beside)].set(top_value)


def levels(rng, dims, cuts, smallest, largest):
    factor_of, own = 1.0, jax.random.fold_in(rng, 6)
    for position, blocks in cuts:
        heights = jnp.exp(jax.random.uniform(jax.random.fold_in(own, position), (blocks,), jnp.float32, smallest / len(cuts), largest / len(cuts)))
        factor_of = factor_of * jnp.repeat(heights, dims[position] // blocks).reshape([-1 if axis == position else 1 for axis in range(len(dims))])
    return factor_of


def centred(own_key, dims, deviation, most, cuts=(), held_as=jnp.bfloat16):
    loudness = levels(own_key, dims, cuts, -0.22, 0.18) if cuts else 1.0
    values = jax.random.normal(own_key, dims, jnp.float32) * deviation * loudness
    return jnp.minimum(jnp.maximum(values, -most), most).astype(held_as)


def setup_inputs(seed: int = 0) -> dict:
    key_list = jax.random.split(jax.random.key(seed), 25)
    return {
        "alignment": centred(key_list[0], (ROWS, RESIDUES, C_M), 1.0, 6.0, ((0, 8),), jnp.float32),
        "pairs": centred(key_list[1], (RESIDUES, RESIDUES, C_Z), 1.0, 6.0, ((0, 8), (1, 4)), jnp.float32),
        "residue_mask": with_ends((jax.random.randint(key_list[2], (RESIDUES,), 0, 8) < 7).astype(jnp.int32), jax.random.fold_in(key_list[2], 1), 0, 1),
        "row_mask": with_ends((jax.random.randint(key_list[3], (ROWS,), 0, 4) < 3).astype(jnp.int32), jax.random.fold_in(key_list[3], 1), 0, 1),
        "alignment_back": centred(key_list[4], (ROWS, RESIDUES, C_M), 1.0, 6.0, ((0, 8),), jnp.float32),
        "pairs_back": centred(key_list[5], (RESIDUES, RESIDUES, C_Z), 1.0, 6.0, ((0, 8), (1, 4)), jnp.float32),
        "norm_scales": draw_norm_scales(jax.random.fold_in(key_list[24], 71), 0),
        "heads_in": centred(key_list[7], (4, C_M, HEADS * D_HEAD), C_M ** -0.5, 0.375, ((2, 4),), jnp.float32),
        "heads_out": centred(key_list[8], (HEADS * D_HEAD, C_M), (max(2 * HEADS * D_HEAD // RESIDUES, 1)) ** -0.5, 6.0, ((0, 4),), jnp.float32),
        "bias_weight": centred(key_list[9], (C_Z, HEADS), C_Z ** -0.5, 0.5, (), jnp.float32),
        "outer_in": centred(key_list[10], (2, C_M, C_O), C_M ** -0.5, 0.375, (), jnp.float32),
        "outer_out": centred(key_list[11], (C_O * C_O, C_Z), (max(C_O * C_O // ROWS, 1)) ** -0.5, 2.0, (), jnp.float32),
        "first_norms": centred(key_list[12], (2, NORMS), (0.1 * (ROWS * RESIDUES) ** 0.5), 160.0, (), jnp.float32),
        "second_norms": jnp.clip(jnp.exp(jax.random.uniform(key_list[13], (2, NORMS), jnp.float32, math.log(65.536), math.log(262.144))), 65.536, 262.144),
        "first_heads_in": centred(key_list[14], (4, C_M, HEADS * D_HEAD), (0.1 * (ROWS * RESIDUES) ** 0.5), 160.0, ((2, 4),), jnp.float32),
        "second_heads_in": jnp.clip(jnp.exp(math.log(262.144) - 1.3862944 * jax.random.uniform(key_list[15], (4, C_M, HEADS * D_HEAD), jnp.float32) ** levels(key_list[15], (4, C_M, HEADS * D_HEAD), ((2, 4),), -0.2, 0.2)), 65.536, 262.144),
        "first_heads_out": centred(key_list[16], (HEADS * D_HEAD, C_M), (0.1 * (2 * ROWS) ** 0.5), 4.0, ((0, 4),), jnp.float32),
        "second_heads_out": jnp.clip(jnp.exp(math.log(1.024) - 1.3862944 * jax.random.uniform(key_list[17], (HEADS * D_HEAD, C_M), jnp.float32) ** levels(key_list[17], (HEADS * D_HEAD, C_M), ((0, 4),), -0.2, 0.2)), 0.256, 1.024),
        "first_bias_weight": centred(key_list[18], (C_Z, HEADS), (0.07 * RESIDUES * ROWS ** 0.5), 2560.0, (), jnp.float32),
        "second_bias_weight": jnp.clip(jnp.exp(jax.random.uniform(key_list[19], (C_Z, HEADS), jnp.float32, math.log(16777.217), math.log(67108.87))), 16777.217, 67108.87),
        "first_outer_in": centred(key_list[20], (2, C_M, C_O), (0.2 * RESIDUES), 640.0, (), jnp.float32),
        "second_outer_in": jnp.clip(jnp.exp(jax.random.uniform(key_list[21], (2, C_M, C_O), jnp.float32, math.log(1048.576), math.log(4194.304))), 1048.576, 4194.304),
        "first_outer_out": centred(key_list[22], (C_O * C_O, C_Z), (0.1 * RESIDUES / ROWS ** 0.5), 28.0, (), jnp.float32),
        "second_outer_out": jnp.clip(jnp.exp(jax.random.uniform(key_list[23], (C_O * C_O, C_Z), jnp.float32, math.log(2.048), math.log(8.192))), 2.048, 8.192),
    }


@jax.custom_vjp
def low(v):
    return lax.optimization_barrier(v.astype(jnp.bfloat16)).astype(jnp.float32)

@jax.custom_vjp
def low_back(v):
    return v

def low_keep(v):
    return (low(v), None)

def low_pass(kept, grad):
    return (grad,)

def back_keep(v):
    return (v, None)

def back_low(kept, grad):
    return (low(grad),)
low.defvjp(low_keep, low_pass)
low_back.defvjp(back_keep, back_low)
precise = lax.Precision.HIGHEST

def layer_norm(values, norm_gain, norm_shift):
    center = values - lax.optimization_barrier(jnp.mean(values, axis=-1, keepdims=True))
    spread = lax.optimization_barrier(jnp.mean(center * center, axis=-1, keepdims=True))
    return center * lax.rsqrt(spread + 1e-05) * norm_gain + norm_shift

def adam_update(weight, gradient, moment_one, moment_two, step_rate):
    first_new = 0.9 * moment_one + 0.1 * gradient
    second_new = 0.999 * moment_two + 0.001 * gradient * gradient
    first_hat = first_new / (1.0 - 0.9 ** STEP)
    second_hat = second_new / (1.0 - 0.999 ** STEP)
    updated = weight - step_rate * (first_hat / (jnp.sqrt(second_hat) + 1e-08) + 0.01 * weight)
    return (first_new, second_new, updated)

def forward_apply(alignment, pairs, norm_scales, heads_in, heads_out, bias_weight, outer_in, outer_out, key_start_position, row_valid_mask, residue_valid_mask):
    gain_rows = norm_scales[0]
    shift_rows = norm_scales[1]
    normed = low(layer_norm(alignment, gain_rows[:C_M], shift_rows[:C_M]))
    pair_normed = low(layer_norm(pairs, gain_rows[2 * C_M:], shift_rows[2 * C_M:]))
    pair_bias = low_back(low(jnp.einsum('ijc,ch->hij', pair_normed, low(bias_weight), precision=precise)))
    projected = jnp.einsum('snc,kcd->ksnd', normed, low(heads_in), precision=precise)
    head_shape = (ROWS, RESIDUES, HEADS, D_HEAD)
    query_heads = low_back(low(projected[0])).reshape(head_shape)
    key_heads = low_back(low(projected[1])).reshape(head_shape)
    value_heads = low_back(low(projected[2])).reshape(head_shape)
    gate_heads = low_back(projected[3]).reshape(head_shape)
    score_scale = D_HEAD ** (-0.5)

    def attend(pieces):
        query_row, key_row, value_row, gate_row = pieces
        scores = jnp.einsum('ihd,jhd->hij', query_row, key_row, precision=precise) * score_scale + pair_bias + key_start_position
        scores = low_back(scores)
        highest = lax.optimization_barrier(jnp.max(scores, axis=-1, keepdims=True))
        powers = jnp.exp(scores - highest)
        soft_weights = powers / lax.optimization_barrier(jnp.sum(powers, axis=-1, keepdims=True))
        mixed_values = low_back(jnp.einsum('hij,jhd->ihd', low(soft_weights), value_row, precision=precise))
        return low(jax.nn.sigmoid(gate_row) * mixed_values).reshape(RESIDUES, HEADS * D_HEAD)
    attended = lax.map(jax.checkpoint(attend), (query_heads, key_heads, value_heads, gate_heads))
    alignment_new = alignment + low_back(jnp.einsum('snd,dc->snc', attended, low(heads_out), precision=precise))
    normed_second = low(layer_norm(alignment_new, gain_rows[C_M:2 * C_M], shift_rows[C_M:2 * C_M]))
    live = row_valid_mask[:, None, None] * residue_valid_mask[None, :, None]
    outer_sides = jnp.einsum('snc,kco->ksno', normed_second, low(outer_in), precision=precise) * live[None]
    left_side = low_back(low(outer_sides[0])).reshape(ROWS // 8, 8, RESIDUES, C_O)
    right_side = low_back(low(outer_sides[1])).reshape(ROWS // 8, 8, RESIDUES, C_O)
    out_table = low(outer_out).reshape(C_O, C_O, C_Z)

    def accumulate(running, pieces):
        left_block, right_block = pieces
        mapped = low_back(low(jnp.einsum('sjf,efz->sjez', right_block, out_table, precision=precise)))
        return (running + jnp.einsum('sie,sjez->ijz', left_block, mapped, precision=precise), None)
    running, unused = lax.scan(jax.checkpoint(accumulate), jnp.zeros((RESIDUES, RESIDUES, C_Z), jnp.float32), (left_side, right_side))
    pairs_new = pairs + low_back(running / ROWS)
    return (alignment_new, pairs_new)

def reference(alignment, pairs, residue_mask, row_mask, alignment_back, pairs_back, norm_scales, heads_in, heads_out, bias_weight, outer_in, outer_out, first_norms, second_norms, first_heads_in, second_heads_in, first_heads_out, second_heads_out, first_bias_weight, second_bias_weight, first_outer_in, second_outer_in, first_outer_out, second_outer_out):
    residue_valid_mask = residue_mask.astype(jnp.float32)
    row_valid_mask = row_mask.astype(jnp.float32)
    key_start_position = (residue_valid_mask - 1.0) * 1000000000.0

    def wrapped_function(alignment_tensor, pair_tensor, norm_tensor, input_tensor, output_tensor, pair_bias_tensor, outer_product_tensor, lookup_table_tensor):
        return forward_apply(alignment_tensor, pair_tensor, norm_tensor, input_tensor, output_tensor, pair_bias_tensor, outer_product_tensor, lookup_table_tensor, key_start_position, row_valid_mask, residue_valid_mask)
    outputs, pullback = jax.vjp(wrapped_function, alignment, pairs, norm_scales, heads_in, heads_out, bias_weight, outer_in, outer_out)
    gradients = pullback((alignment_back, pairs_back))
    norms_new = adam_update(norm_scales, gradients[2], first_norms, second_norms, 0.5)
    heads_in_upd = adam_update(heads_in, gradients[3], first_heads_in, second_heads_in, C_M ** (-0.5))
    heads_out_upd = adam_update(heads_out, gradients[4], first_heads_out, second_heads_out, max(2 * HEADS * D_HEAD // RESIDUES, 1) ** (-0.5))
    bias_upd = adam_update(bias_weight, gradients[5], first_bias_weight, second_bias_weight, C_Z ** (-0.5))
    outer_in_upd = adam_update(outer_in, gradients[6], first_outer_in, second_outer_in, C_M ** (-0.5))
    outer_out_upd = adam_update(outer_out, gradients[7], first_outer_out, second_outer_out, max(C_O * C_O // ROWS, 1) ** (-0.5))
    return (outputs[0], outputs[1], gradients[0], gradients[1], norms_new[0], norms_new[1], norms_new[2], heads_in_upd[0], heads_in_upd[1], heads_in_upd[2], heads_out_upd[0], heads_out_upd[1], heads_out_upd[2], bias_upd[0], bias_upd[1], bias_upd[2], outer_in_upd[0], outer_in_upd[1], outer_in_upd[2], outer_out_upd[0], outer_out_upd[1], outer_out_upd[2])
```

```python
import jax
import jax.numpy as jnp
from jax import lax
from jax.sharding import PartitionSpec as P

HEADS = 8
STEP = 10
F32 = jnp.float32
BF16 = jnp.bfloat16
LOG2E = 1.4426950408889634
EVERY = ("row", "head")


def adam_update(weight, gradient, moment_one, moment_two, step_rate):
    first_new = 0.9 * moment_one + 0.1 * gradient
    second_new = 0.999 * moment_two + 0.001 * gradient * gradient
    first_hat = first_new / (1.0 - 0.9**STEP)
    second_hat = second_new / (1.0 - 0.999**STEP)
    updated = weight - step_rate * (first_hat / (jnp.sqrt(second_hat) + 1e-08) + 0.01 * weight)
    return (first_new, second_new, updated)


def normalize(values):
    center = values - jnp.mean(values, axis=-1, keepdims=True)
    rstd = lax.rsqrt(jnp.mean(center * center, axis=-1, keepdims=True) + 1e-05)
    return center * rstd, rstd


def norm_backward(hat, rstd, gain, grad):
    scaled = grad * gain
    return rstd * (
        scaled
        - jnp.mean(scaled, axis=-1, keepdims=True)
        - hat * jnp.mean(scaled * hat, axis=-1, keepdims=True)
    )


def mm(spec, a, b):
    return jnp.einsum(spec, a, b, preferred_element_type=F32)


def pair_forward(pairs, gain, shift, bias_low):
    hat, _ = normalize(pairs)
    low = (hat * gain + shift).astype(BF16)
    return (mm("ijc,ch->hij", low, bias_low) * LOG2E).astype(BF16)


def pair_backward(pairs, pairs_back, gain, shift, bias_low, bias_grad):
    hat, rstd = normalize(pairs)
    low = (hat * gain + shift).astype(BF16)
    weight_grad = mm("ijc,hij->ch", low, bias_grad)
    in_grad = mm("hij,ch->ijc", bias_grad, bias_low)
    gain_grad = jnp.sum(in_grad * hat, axis=(0, 1))
    shift_grad = jnp.sum(in_grad, axis=(0, 1))
    return pairs_back + norm_backward(hat, rstd, gain, in_grad), weight_grad, gain_grad, shift_grad


def attention_forward(rows, gains, shifts, in_t, out_low, outer_t, bias, key_mask, live):
    own, residues, width = rows.shape
    size = width // HEADS
    hat, _ = normalize(rows)
    normed = (hat * gains[0] + shifts[0]).astype(BF16)
    projected = mm("oc,snc->son", in_t, normed)
    query = (projected[:, :width] * (size**-0.5 * LOG2E)).astype(BF16)
    keys = projected[:, width : 2 * width].astype(BF16)
    values = projected[:, 2 * width : 3 * width].astype(BF16)
    gate = jax.nn.sigmoid(projected[:, 3 * width :])
    split = (own, HEADS, size, residues)
    scores = mm("shdj,shdi->shji", keys.reshape(split), query.reshape(split))
    scores = scores + (bias.astype(F32).swapaxes(1, 2) + key_mask[None, :, None])[None]
    powers = jnp.exp2(scores - jnp.max(scores, axis=2, keepdims=True))
    inverse = 1.0 / jnp.sum(powers, axis=2)
    powers = powers.astype(BF16)
    mixed = mm("shdj,shji->shdi", values.reshape(split), powers) * inverse[:, :, None, :]
    mixed = mixed.reshape(own, width, residues)
    attended = (gate * mixed).astype(BF16)
    update = mm("sdn,dc->snc", attended, out_low)
    hat_two, _ = normalize(rows + update)
    second = (hat_two * gains[1] + shifts[1]).astype(BF16)
    sides = (mm("oc,snc->son", outer_t, second) * live[:, None, :]).astype(BF16)
    return update, sides, (query, keys, values, gate, powers, inverse, mixed, attended)


def outer_product(left, right, pairs_back, table, all_rows):
    low = pairs_back.astype(BF16)
    product = mm("sei,sfj->eifj", left, right).astype(BF16)
    total = mm("eifj,efz->ijz", product, table) / all_rows
    table_grad = mm("eifj,ijz->efz", product, low) / all_rows
    back = mm("ijz,efz->eifj", low, table).astype(BF16)
    left_grad = mm("eifj,sfj->sei", back, right) / all_rows
    right_grad = mm("eifj,sei->sfj", back, left) / all_rows
    return total, table_grad, left_grad.astype(BF16), right_grad.astype(BF16)


def attention_backward(rows, update, rows_back, gains, shifts, in_t, out_low, outer_t, sides_grad, kept):
    query, keys, values, gate, powers, inverse, mixed, attended = kept
    own, residues, width = rows.shape
    size = width // HEADS
    hat, rstd = normalize(rows)
    normed = (hat * gains[0] + shifts[0]).astype(BF16)
    hat_two, rstd_two = normalize(rows + update)
    second = (hat_two * gains[1] + shifts[1]).astype(BF16)
    outer_in_grad = mm("son,snc->oc", sides_grad, second)
    second_grad = mm("son,oc->snc", sides_grad, outer_t)
    gain_two = jnp.sum(second_grad * hat_two, axis=(0, 1))
    shift_two = jnp.sum(second_grad, axis=(0, 1))
    new_part = norm_backward(hat_two, rstd_two, gains[1], second_grad)
    out_grad_low = (rows_back + new_part).astype(BF16)
    heads_out_grad = mm("sdn,snc->dc", attended, out_grad_low)
    attended_grad = mm("dc,snc->sdn", out_low, out_grad_low)
    gate_grad = (attended_grad * mixed * gate * (1.0 - gate)).astype(BF16)
    split = (own, HEADS, size, residues)
    mixed_grad = (attended_grad * gate).reshape(split) * inverse[:, :, None, :]
    delta = jnp.sum(mixed_grad * mixed.reshape(split), axis=2, keepdims=True)
    mixed_grad = mixed_grad.astype(BF16)
    value_grad = mm("shdi,shji->shdj", mixed_grad, powers).astype(BF16)
    prob_grad = mm("shdj,shdi->shji", values.reshape(split), mixed_grad)
    score_grad = (powers.astype(F32) * (prob_grad - delta)).astype(BF16)
    query_grad = (mm("shdj,shji->shdi", keys.reshape(split), score_grad) * size**-0.5).astype(BF16)
    key_grad = (mm("shdi,shji->shdj", query.reshape(split), score_grad) / LOG2E).astype(BF16)
    bias_grad = jnp.sum(score_grad.astype(F32), axis=0).swapaxes(1, 2).astype(BF16)
    flat = (own, width, residues)
    proj_grad = jnp.concatenate(
        [query_grad.reshape(flat), key_grad.reshape(flat), value_grad.reshape(flat), gate_grad], axis=1
    )
    heads_in_grad = mm("son,snc->oc", proj_grad, normed)
    normed_grad = mm("son,oc->snc", proj_grad, in_t)
    gain_one = jnp.sum(normed_grad * hat, axis=(0, 1))
    shift_one = jnp.sum(normed_grad, axis=(0, 1))
    part = new_part + norm_backward(hat, rstd, gains[0], normed_grad)
    norms = jnp.stack([jnp.concatenate([gain_one, gain_two]), jnp.concatenate([shift_one, shift_two])])
    return part, bias_grad, heads_in_grad, heads_out_grad, outer_in_grad, norms


def per_device(
    alignment,
    pairs,
    residue_mask,
    row_mask,
    alignment_back,
    pairs_back,
    norm_scales,
    heads_in,
    heads_out,
    bias_weight,
    outer_in,
    outer_out,
    first_norms,
    second_norms,
    first_heads_in,
    second_heads_in,
    first_heads_out,
    second_heads_out,
    first_bias_weight,
    second_bias_weight,
    first_outer_in,
    second_outer_in,
    first_outer_out,
    second_outer_out,
):
    row_count = lax.axis_size("row")
    head_count = lax.axis_size("head")
    head_index = lax.axis_index("head")
    devices = row_count * head_count
    rows_here, residues, width = alignment.shape
    pair_rows, pair_cols, pair_width = pairs.shape
    size = width // HEADS
    outer_width = outer_in.shape[2]
    all_rows = rows_here * row_count
    own = rows_here // head_count
    start = head_index * own
    gains = (norm_scales[0:1, :width], norm_scales[0:1, width : 2 * width])
    shifts = (norm_scales[1:2, :width], norm_scales[1:2, width : 2 * width])
    pair_gain = norm_scales[0:1, 2 * width :]
    pair_shift = norm_scales[1:2, 2 * width :]
    residue_live = residue_mask.astype(F32)
    key_mask = (residue_live - 1.0) * (1e9 * LOG2E)
    live = lax.dynamic_slice_in_dim(row_mask, start, own, 0).astype(F32)[:, None] * residue_live[None]
    bias_low = bias_weight.astype(BF16)

    local = heads_in.shape[2]
    in_local = heads_in.astype(BF16).swapaxes(1, 2).reshape(4 * local, width)
    weights = lax.all_gather(
        jnp.concatenate([in_local, heads_out.astype(BF16)]), "head", axis=0
    ).reshape(head_count, 5, local, width)
    weights = weights.swapaxes(0, 1).reshape(5, head_count * local, width)
    in_t = weights[:4].reshape(4 * width, width)
    out_low = weights[4]
    outer_t = outer_in.astype(BF16).swapaxes(1, 2).reshape(2 * outer_width, width)
    table = outer_out.astype(BF16).reshape(outer_width, outer_width, pair_width)

    bias_block = pair_forward(pairs, pair_gain, pair_shift, bias_low)
    bias = lax.all_gather(bias_block, "head", axis=2, tiled=True)
    bias = lax.all_gather(bias, "row", axis=1, tiled=True)

    rows = lax.dynamic_slice_in_dim(alignment, start, own, 0)
    rows_back = lax.dynamic_slice_in_dim(alignment_back, start, own, 0)
    update, sides, kept = attention_forward(
        rows, gains, shifts, in_t, out_low, outer_t, bias, key_mask, live
    )
    update_all = lax.all_gather(update.astype(BF16), "head", axis=0, tiled=True)
    alignment_new = alignment + update_all.astype(F32)

    left_send = sides[:, :outer_width].reshape(own, outer_width, row_count, pair_rows)
    left_send = jnp.broadcast_to(
        left_send.transpose(2, 0, 1, 3)[:, None], (row_count, head_count, own, outer_width, pair_rows)
    )
    right_send = sides[:, outer_width:].reshape(own, outer_width, head_count, pair_cols)
    right_send = jnp.broadcast_to(
        right_send.transpose(2, 0, 1, 3)[None], (row_count, head_count, own, outer_width, pair_cols)
    )
    send = jnp.concatenate([left_send, right_send], axis=4).reshape(
        devices, own, outer_width, pair_rows + pair_cols
    )
    got = lax.all_to_all(send, EVERY, split_axis=0, concat_axis=0, tiled=True)
    got = got.reshape(all_rows, outer_width, pair_rows + pair_cols)
    total, table_grad, left_grad, right_grad = outer_product(
        got[:, :, :pair_rows], got[:, :, pair_rows:], pairs_back, table, all_rows
    )
    pairs_new = pairs + total

    send = jnp.concatenate([left_grad, right_grad], axis=2).reshape(
        devices, own, outer_width, pair_rows + pair_cols
    )
    got = lax.all_to_all(send, EVERY, split_axis=0, concat_axis=0, tiled=True)
    got = got.reshape(row_count, head_count, own, outer_width, pair_rows + pair_cols).astype(F32)
    left_total = jnp.sum(got[..., :pair_rows], axis=1).transpose(1, 2, 0, 3)
    right_total = jnp.sum(got[..., pair_rows:], axis=0).transpose(1, 2, 0, 3)
    sides_grad = jnp.concatenate(
        [
            left_total.reshape(own, outer_width, residues),
            right_total.reshape(own, outer_width, residues),
        ],
        axis=1,
    )
    sides_grad = (sides_grad * live[:, None, :]).astype(BF16)

    part, bias_grad, heads_in_grad, heads_out_grad, outer_in_grad, norms = attention_backward(
        rows, update, rows_back, gains, shifts, in_t, out_low, outer_t, sides_grad, kept
    )
    part_all = lax.all_gather(part.astype(BF16), "head", axis=0, tiled=True)
    alignment_grad = alignment_back + part_all.astype(F32)

    bias_grad = lax.psum_scatter(bias_grad, "row", scatter_dimension=1, tiled=True)
    bias_grad = lax.psum_scatter(bias_grad, "head", scatter_dimension=2, tiled=True)
    pairs_grad, bias_weight_grad, pair_gain_grad, pair_shift_grad = pair_backward(
        pairs, pairs_back, pair_gain, pair_shift, bias_low, bias_grad
    )

    sums = lax.psum(
        (
            heads_in_grad,
            heads_out_grad,
            outer_in_grad,
            table_grad,
            norms,
            bias_weight_grad,
            jnp.stack([pair_gain_grad, pair_shift_grad]),
        ),
        EVERY,
    )
    heads_in_total = lax.dynamic_slice_in_dim(
        sums[0].reshape(4, width, width), head_index * local, local, 1
    ).swapaxes(1, 2)
    heads_out_total = lax.dynamic_slice_in_dim(sums[1], head_index * local, local, 0)
    outer_in_total = sums[2].reshape(2, outer_width, width).swapaxes(1, 2)
    table_total = sums[3].reshape(outer_width * outer_width, pair_width)
    norms_total = jnp.concatenate([sums[4], sums[6]], axis=1)
    norms_new = adam_update(norm_scales, norms_total, first_norms, second_norms, 0.5)
    heads_in_upd = adam_update(
        heads_in, heads_in_total, first_heads_in, second_heads_in, width ** (-0.5)
    )
    heads_out_upd = adam_update(
        heads_out,
        heads_out_total,
        first_heads_out,
        second_heads_out,
        max(2 * HEADS * size // residues, 1) ** (-0.5),
    )
    bias_upd = adam_update(
        bias_weight, sums[5], first_bias_weight, second_bias_weight, pair_width ** (-0.5)
    )
    outer_in_upd = adam_update(
        outer_in, outer_in_total, first_outer_in, second_outer_in, width ** (-0.5)
    )
    outer_out_upd = adam_update(
        outer_out,
        table_total,
        first_outer_out,
        second_outer_out,
        max(outer_width * outer_width // all_rows, 1) ** (-0.5),
    )
    return (
        alignment_new,
        pairs_new,
        alignment_grad,
        pairs_grad,
        *norms_new,
        *heads_in_upd,
        *heads_out_upd,
        *bias_upd,
        *outer_in_upd,
        *outer_out_upd,
    )


def solution(mesh):
    row_msa = P("row", None, None)
    pair = P("row", "head", None)
    columns = P(None, None, "head")
    lines = P("head", None)
    in_specs = (
        (row_msa, pair, P(), P("row"), row_msa, pair, P(), columns, lines)
        + (P(),) * 5
        + (columns,) * 2
        + (lines,) * 2
        + (P(),) * 6
    )
    out_specs = (row_msa, pair, row_msa, pair) + (P(),) * 3 + (columns,) * 3 + (lines,) * 3 + (P(),) * 9
    return jax.shard_map(
        per_device, mesh=mesh, in_specs=in_specs, out_specs=out_specs, check_vma=False
    )
```

```python
import functools

import jax
import jax.numpy as jnp
from jax import lax
from jax.experimental import pallas as pl
from jax.experimental.pallas import tpu as pltpu
from jax.sharding import PartitionSpec as P

HEADS = 8
STEP = 10
F32 = jnp.float32
BF16 = jnp.bfloat16
LOG2E = 1.4426950408889634
EVERY = ("row", "head")


def adam_update(weight, gradient, moment_one, moment_two, step_rate):
    first_new = 0.9 * moment_one + 0.1 * gradient
    second_new = 0.999 * moment_two + 0.001 * gradient * gradient
    first_hat = first_new / (1.0 - 0.9**STEP)
    second_hat = second_new / (1.0 - 0.999**STEP)
    updated = weight - step_rate * (first_hat / (jnp.sqrt(second_hat) + 1e-08) + 0.01 * weight)
    return (first_new, second_new, updated)


def dot(a, b, along):
    return lax.dot_general(a, b, (((along[0],), (along[1],)), ((), ())), preferred_element_type=F32)


def normalize(values):
    center = values - jnp.mean(values, axis=-1, keepdims=True)
    rstd = lax.rsqrt(jnp.mean(center * center, axis=-1, keepdims=True) + 1e-05)
    return center * rstd, rstd


def norm_backward(hat, rstd, gain, grad):
    scaled = grad * gain
    return rstd * (
        scaled
        - jnp.mean(scaled, axis=-1, keepdims=True)
        - hat * jnp.mean(scaled * hat, axis=-1, keepdims=True)
    )


def forward_kernel(
    rows, scales, in_t, out_low, outer_t, bias, key_mask, live,
    update, sides, qkv, gate, powers, inverse, mixed, attended,
    bias_t, *, chunk,
):
    row, head = pl.program_id(0), pl.program_id(1)
    width = rows.shape[2]
    residues = rows.shape[1]
    size = width // HEADS

    @pl.when(row == 0)
    def _():
        bias_t[head] = bias[0].astype(F32).T + key_mask[...]

    @pl.when(head == 0)
    def _():
        hat, _ = normalize(rows[0])
        normed = (hat * scales[0:1] + scales[1:2]).astype(BF16)
        qkv[0, :width] = (
            dot(in_t[:width], normed, (1, 1)) * (size**-0.5 * LOG2E)
        ).astype(BF16)
        qkv[0, width:] = dot(in_t[width : 3 * width], normed, (1, 1)).astype(BF16)
        gate[0] = jax.nn.sigmoid(dot(in_t[3 * width :], normed, (1, 1)))

    at = pl.multiple_of(head * size, size)
    keys = qkv[0, pl.ds(width + at, size), :]
    values = qkv[0, pl.ds(2 * width + at, size), :]
    for first in range(0, residues, chunk):
        span = slice(first, first + chunk)
        query = qkv[0, pl.ds(at, size), span]
        scores = dot(keys, query, (0, 0)) + bias_t[head, :, span]
        exps = jnp.exp2(scores - jnp.max(scores, axis=0, keepdims=True))
        over = 1.0 / jnp.sum(exps, axis=0, keepdims=True)
        low = exps.astype(BF16)
        powers[0, 0, :, span] = low
        inverse[0, 0, :, span] = over
        mixed[0, pl.ds(at, size), span] = dot(values, low, (1, 0)) * over

    @pl.when(head == HEADS - 1)
    def _():
        att = (gate[0] * mixed[0]).astype(BF16)
        attended[0] = att
        change = dot(att, out_low[...], (0, 0)).astype(BF16)
        update[0] = change
        hat, _ = normalize(rows[0] + change.astype(F32))
        second = (hat * scales[2:3] + scales[3:4]).astype(BF16)
        sides[0] = (dot(outer_t[...], second, (1, 1)) * live[0]).astype(BF16)


def attention_forward(rows, scales, in_t, out_low, outer_t, bias, key_mask, live, chunk=256):
    own, residues, width = rows.shape
    sides = outer_t.shape[0]
    by_row = lambda s, h: (s, 0, 0)
    whole = lambda s, h: (0, 0)
    last = lambda s, h: (jnp.where(s == 0, h, HEADS - 1), 0, 0)
    out = pl.pallas_call(
        functools.partial(forward_kernel, chunk=chunk),
        grid=(own, HEADS),
        in_specs=[
            pl.BlockSpec((1, residues, width), by_row),
            pl.BlockSpec(scales.shape, whole),
            pl.BlockSpec(in_t.shape, whole),
            pl.BlockSpec(out_low.shape, whole),
            pl.BlockSpec(outer_t.shape, whole),
            pl.BlockSpec((1, residues, residues), last),
            pl.BlockSpec((residues, 1), whole),
            pl.BlockSpec((1, 1, residues), by_row),
        ],
        out_specs=[
            pl.BlockSpec((1, residues, width), by_row),
            pl.BlockSpec((1, sides, residues), by_row),
            pl.BlockSpec((1, 3 * width, residues), by_row),
            pl.BlockSpec((1, width, residues), by_row),
            pl.BlockSpec((1, 1, residues, residues), lambda s, h: (s, h, 0, 0)),
            pl.BlockSpec((1, 1, 1, residues), lambda s, h: (s, h, 0, 0)),
            pl.BlockSpec((1, width, residues), by_row),
            pl.BlockSpec((1, width, residues), by_row),
        ],
        out_shape=[
            jax.ShapeDtypeStruct((own, residues, width), BF16),
            jax.ShapeDtypeStruct((own, sides, residues), BF16),
            jax.ShapeDtypeStruct((own, 3 * width, residues), BF16),
            jax.ShapeDtypeStruct((own, width, residues), F32),
            jax.ShapeDtypeStruct((own, HEADS, residues, residues), BF16),
            jax.ShapeDtypeStruct((own, HEADS, 1, residues), F32),
            jax.ShapeDtypeStruct((own, width, residues), F32),
            jax.ShapeDtypeStruct((own, width, residues), BF16),
        ],
        scratch_shapes=[pltpu.VMEM((HEADS, residues, residues), F32)],
        compiler_params=pltpu.CompilerParams(vmem_limit_bytes=50 << 20),
    )(rows, scales, in_t, out_low, outer_t, bias, key_mask, live)
    return out[0], out[1], tuple(out[2:])


def backward_kernel(
    rows, update, back, scales, in_t, out_low, outer_t, sides_grad,
    qkv, gate, powers, inverse, mixed, attended,
    part, bias_grad, heads_in_grad, heads_out_grad, outer_in_grad, norms,
    bias_sum, mixed_grad, delta, proj_grad, new_part, *, chunk,
):
    row, head = pl.program_id(0), pl.program_id(1)
    width = rows.shape[2]
    residues = rows.shape[1]
    size = width // HEADS
    last_row = row == pl.num_programs(0) - 1

    @pl.when((row == 0) & (head == 0))
    def _():
        heads_in_grad[...] = jnp.zeros_like(heads_in_grad)
        heads_out_grad[...] = jnp.zeros_like(heads_out_grad)
        outer_in_grad[...] = jnp.zeros_like(outer_in_grad)
        norms[...] = jnp.zeros_like(norms)
        bias_sum[...] = jnp.zeros_like(bias_sum)

    @pl.when(head == 0)
    def _():
        hat, rstd = normalize(rows[0] + update[0].astype(F32))
        second = (hat * scales[2:3] + scales[3:4]).astype(BF16)
        grads = sides_grad[0]
        outer_in_grad[...] += dot(grads, second, (1, 0))
        second_grad = dot(grads, outer_t[...], (0, 0))
        norms[2:3] += jnp.sum(second_grad * hat, axis=0, keepdims=True)
        norms[3:4] += jnp.sum(second_grad, axis=0, keepdims=True)
        new = norm_backward(hat, rstd, scales[2:3], second_grad)
        new_part[...] = new
        out_grad = (back[0] + new).astype(BF16)
        heads_out_grad[...] += dot(attended[0], out_grad, (1, 0))
        attended_grad = dot(out_low[...], out_grad, (1, 1))
        sig = gate[0]
        gated = attended_grad * sig
        proj_grad[3 * width :] = (gated * mixed[0] * (1.0 - sig)).astype(BF16)
        for h in range(HEADS):
            span = slice(h * size, (h + 1) * size)
            grad = gated[span] * inverse[0, h]
            mixed_grad[span] = grad.astype(BF16)
            delta[h] = jnp.sum(grad * mixed[0, span], axis=0, keepdims=True)

    at = pl.multiple_of(head * size, size)
    keys = qkv[0, pl.ds(width + at, size), :]
    values = qkv[0, pl.ds(2 * width + at, size), :]
    key_grad = jnp.zeros((size, residues), F32)
    value_grad = jnp.zeros((size, residues), F32)
    for first in range(0, residues, chunk):
        span = slice(first, first + chunk)
        grad = mixed_grad[pl.ds(at, size), span]
        query = qkv[0, pl.ds(at, size), span]
        low = powers[0, 0, :, span]
        prob_grad = dot(values, grad, (0, 0))
        score_grad = low.astype(F32) * (prob_grad - delta[head, :, span])
        bias_sum[head, :, span] += score_grad
        score_low = score_grad.astype(BF16)
        value_grad += dot(grad, low, (1, 1))
        key_grad += dot(query, score_low, (1, 1))
        proj_grad[pl.ds(at, size), span] = (dot(keys, score_low, (1, 0)) * size**-0.5).astype(BF16)
    proj_grad[pl.ds(width + at, size), :] = (key_grad / LOG2E).astype(BF16)
    proj_grad[pl.ds(2 * width + at, size), :] = value_grad.astype(BF16)

    @pl.when(last_row)
    def _():
        bias_grad[0] = bias_sum[head].T.astype(BF16)

    @pl.when(head == HEADS - 1)
    def _():
        hat, rstd = normalize(rows[0])
        normed = (hat * scales[0:1] + scales[1:2]).astype(BF16)
        grads = proj_grad[...]
        heads_in_grad[...] += dot(grads, normed, (1, 0))
        normed_grad = dot(grads, in_t[...], (0, 0))
        norms[0:1] += jnp.sum(normed_grad * hat, axis=0, keepdims=True)
        norms[1:2] += jnp.sum(normed_grad, axis=0, keepdims=True)
        part[0] = (new_part[...] + norm_backward(hat, rstd, scales[0:1], normed_grad)).astype(BF16)


def attention_backward(rows, update, back, scales, in_t, out_low, outer_t, sides_grad, kept, chunk=256):
    own, residues, width = rows.shape
    qkv, gate, powers, inverse, mixed, attended = kept
    sides = outer_t.shape[0]
    by_row = lambda s, h: (s, 0, 0)
    whole = lambda s, h: (0, 0)
    out = pl.pallas_call(
        functools.partial(backward_kernel, chunk=chunk),
        grid=(own, HEADS),
        in_specs=[
            pl.BlockSpec((1, residues, width), by_row),
            pl.BlockSpec((1, residues, width), by_row),
            pl.BlockSpec((1, residues, width), by_row),
            pl.BlockSpec(scales.shape, whole),
            pl.BlockSpec(in_t.shape, whole),
            pl.BlockSpec(out_low.shape, whole),
            pl.BlockSpec(outer_t.shape, whole),
            pl.BlockSpec((1, sides, residues), by_row),
            pl.BlockSpec((1, 3 * width, residues), by_row),
            pl.BlockSpec((1, width, residues), by_row),
            pl.BlockSpec((1, 1, residues, residues), lambda s, h: (s, h, 0, 0)),
            pl.BlockSpec((1, HEADS, 1, residues), lambda s, h: (s, 0, 0, 0)),
            pl.BlockSpec((1, width, residues), by_row),
            pl.BlockSpec((1, width, residues), by_row),
        ],
        out_specs=[
            pl.BlockSpec((1, residues, width), by_row),
            pl.BlockSpec((1, residues, residues), lambda s, h: (jnp.where(s == own - 1, h, 0), 0, 0)),
            pl.BlockSpec(in_t.shape, whole),
            pl.BlockSpec(out_low.shape, whole),
            pl.BlockSpec(outer_t.shape, whole),
            pl.BlockSpec((4, width), whole),
        ],
        out_shape=[
            jax.ShapeDtypeStruct((own, residues, width), BF16),
            jax.ShapeDtypeStruct((HEADS, residues, residues), BF16),
            jax.ShapeDtypeStruct(in_t.shape, F32),
            jax.ShapeDtypeStruct(out_low.shape, F32),
            jax.ShapeDtypeStruct(outer_t.shape, F32),
            jax.ShapeDtypeStruct((4, width), F32),
        ],
        scratch_shapes=[
            pltpu.VMEM((HEADS, residues, residues), F32),
            pltpu.VMEM((width, residues), BF16),
            pltpu.VMEM((HEADS, 1, residues), F32),
            pltpu.VMEM((4 * width, residues), BF16),
            pltpu.VMEM((residues, width), F32),
        ],
        compiler_params=pltpu.CompilerParams(vmem_limit_bytes=50 << 20),
    )(rows, update, back, scales, in_t, out_low, outer_t, sides_grad, qkv, gate, powers, inverse, mixed, attended)
    return out


def outer_kernel(
    left, right, pairs, back, table, table_t,
    total, left_grad, right_grad, table_grad,
    product, backed, *, scale, group,
):
    step = pl.program_id(0)
    rows = pairs.shape[0]
    cols = pairs.shape[1]
    channels = pairs.shape[2]
    width = left.shape[0] // rows
    wide = right.shape[1] // cols

    @pl.when(step == 0)
    def _():
        right_grad[...] = jnp.zeros_like(right_grad)
        table_grad[...] = jnp.zeros_like(table_grad)

    product[...] = dot(left[...], right[...], (1, 0)).astype(BF16)
    for first in range(0, rows, group):
        low = back[first : first + group].astype(BF16).reshape(group * cols, channels)
        both = jnp.concatenate(
            [
                jnp.concatenate(
                    [
                        product[(first + g) * width : (first + g + 1) * width, f * cols : (f + 1) * cols]
                        for f in range(wide)
                    ],
                    axis=0,
                )
                for g in range(group)
            ],
            axis=1,
        )
        out = dot(table_t[...], both, (1, 0)) * scale
        for g in range(group):
            total[first + g] = pairs[first + g] + out[:, g * cols : (g + 1) * cols].T
        table_grad[...] += dot(both, low, (1, 0)) * scale
        spread = dot(table[...], low, (1, 1)).astype(BF16)
        for g in range(group):
            for f in range(wide):
                backed[(first + g) * width : (first + g + 1) * width, f * cols : (f + 1) * cols] = spread[
                    f * width : (f + 1) * width, g * cols : (g + 1) * cols
                ]
    left_grad[...] = (dot(backed[...], right[...], (1, 1)) * scale).astype(BF16)
    right_grad[...] += dot(left[...], backed[...], (0, 0)) * scale


def outer_product(left, right, pairs, back, table, all_rows, block=8, group=2):
    rows, cols, channels = pairs.shape
    width = left.shape[0] // rows
    table_t = table.T
    by_row = lambda n: (n, 0, 0)
    whole = lambda n: (0, 0)
    return pl.pallas_call(
        functools.partial(outer_kernel, scale=1.0 / all_rows, group=group),
        grid=(rows // block,),
        in_specs=[
            pl.BlockSpec((block * width, left.shape[1]), lambda n: (n, 0)),
            pl.BlockSpec(right.shape, whole),
            pl.BlockSpec((block, cols, channels), by_row),
            pl.BlockSpec((block, cols, channels), by_row),
            pl.BlockSpec(table.shape, whole),
            pl.BlockSpec(table_t.shape, whole),
        ],
        out_specs=[
            pl.BlockSpec((block, cols, channels), by_row),
            pl.BlockSpec((block * width, left.shape[1]), lambda n: (n, 0)),
            pl.BlockSpec(right.shape, whole),
            pl.BlockSpec(table.shape, whole),
        ],
        out_shape=[
            jax.ShapeDtypeStruct(pairs.shape, F32),
            jax.ShapeDtypeStruct(left.shape, BF16),
            jax.ShapeDtypeStruct(right.shape, F32),
            jax.ShapeDtypeStruct(table.shape, F32),
        ],
        scratch_shapes=[
            pltpu.VMEM((block * width, right.shape[1]), BF16),
            pltpu.VMEM((block * width, right.shape[1]), BF16),
        ],
        compiler_params=pltpu.CompilerParams(vmem_limit_bytes=50 << 20),
    )(left, right, pairs, back, table, table_t)


def outer_product_plain(left, right, pairs_back, table, all_rows):
    low = pairs_back.astype(BF16)
    product = mm("sei,sfj->eifj", left, right).astype(BF16)
    total = mm("eifj,efz->ijz", product, table) / all_rows
    table_grad = mm("eifj,ijz->efz", product, low) / all_rows
    back = mm("ijz,efz->eifj", low, table).astype(BF16)
    left_grad = mm("eifj,sfj->sei", back, right) / all_rows
    right_grad = mm("eifj,sei->sfj", back, left) / all_rows
    return total, table_grad, left_grad.astype(BF16), right_grad.astype(BF16)


def mm(spec, a, b):
    return jnp.einsum(spec, a, b, preferred_element_type=F32)


def pair_forward(pairs, gain, shift, bias_low):
    hat, _ = normalize(pairs)
    low = (hat * gain + shift).astype(BF16)
    return (mm("ijc,ch->hij", low, bias_low) * LOG2E).astype(BF16)


def pair_backward(pairs, pairs_back, gain, shift, bias_low, bias_grad):
    hat, rstd = normalize(pairs)
    low = (hat * gain + shift).astype(BF16)
    weight_grad = mm("ijc,hij->ch", low, bias_grad)
    in_grad = mm("hij,ch->ijc", bias_grad, bias_low)
    gain_grad = jnp.sum(in_grad * hat, axis=(0, 1))
    shift_grad = jnp.sum(in_grad, axis=(0, 1))
    return pairs_back + norm_backward(hat, rstd, gain, in_grad), weight_grad, gain_grad, shift_grad


def per_device(
    alignment,
    pairs,
    residue_mask,
    row_mask,
    alignment_back,
    pairs_back,
    norm_scales,
    heads_in,
    heads_out,
    bias_weight,
    outer_in,
    outer_out,
    first_norms,
    second_norms,
    first_heads_in,
    second_heads_in,
    first_heads_out,
    second_heads_out,
    first_bias_weight,
    second_bias_weight,
    first_outer_in,
    second_outer_in,
    first_outer_out,
    second_outer_out,
):
    row_count = lax.axis_size("row")
    head_count = lax.axis_size("head")
    head_index = lax.axis_index("head")
    devices = row_count * head_count
    rows_here, residues, width = alignment.shape
    pair_rows, pair_cols, pair_width = pairs.shape
    size = width // HEADS
    outer_width = outer_in.shape[2]
    all_rows = rows_here * row_count
    own = rows_here // head_count
    start = head_index * own
    scales = norm_scales[:, : 2 * width].reshape(2, 2, width).swapaxes(0, 1).reshape(4, width)
    pair_gain = norm_scales[0:1, 2 * width :]
    pair_shift = norm_scales[1:2, 2 * width :]
    residue_live = residue_mask.astype(F32)
    key_mask = ((residue_live - 1.0) * (1e9 * LOG2E))[:, None]
    live = lax.dynamic_slice_in_dim(row_mask, start, own, 0).astype(F32)[:, None] * residue_live[None]
    bias_low = bias_weight.astype(BF16)

    local = heads_in.shape[2]
    in_local = heads_in.astype(BF16).swapaxes(1, 2).reshape(4 * local, width)
    weights = lax.all_gather(
        jnp.concatenate([in_local, heads_out.astype(BF16)]), "head", axis=0
    ).reshape(head_count, 5, local, width)
    weights = weights.swapaxes(0, 1).reshape(5, head_count * local, width)
    in_t = weights[:4].reshape(4 * width, width)
    out_low = weights[4]
    outer_t = outer_in.astype(BF16).swapaxes(1, 2).reshape(2 * outer_width, width)
    table = outer_out.astype(BF16).reshape(outer_width, outer_width, pair_width)

    bias_block = pair_forward(pairs, pair_gain, pair_shift, bias_low)
    bias = lax.all_gather(bias_block, "head", axis=2, tiled=True)
    bias = lax.all_gather(bias, "row", axis=1, tiled=True)

    rows = lax.dynamic_slice_in_dim(alignment, start, own, 0)
    rows_back = lax.dynamic_slice_in_dim(alignment_back, start, own, 0)
    update, sides, kept = attention_forward(
        rows, scales, in_t, out_low, outer_t, bias, key_mask, live[:, None]
    )
    update_all = lax.all_gather(update, "head", axis=0, tiled=True)
    alignment_new = alignment + update_all.astype(F32)

    left_send = sides[:, :outer_width].reshape(own, outer_width, row_count, pair_rows)
    left_send = jnp.broadcast_to(
        left_send.transpose(2, 0, 1, 3)[:, None], (row_count, head_count, own, outer_width, pair_rows)
    )
    right_send = sides[:, outer_width:].reshape(own, outer_width, head_count, pair_cols)
    right_send = jnp.broadcast_to(
        right_send.transpose(2, 0, 1, 3)[None], (row_count, head_count, own, outer_width, pair_cols)
    )
    send = jnp.concatenate([left_send, right_send], axis=4).reshape(
        devices, own, outer_width, pair_rows + pair_cols
    )
    got = lax.all_to_all(send, EVERY, split_axis=0, concat_axis=0, tiled=True)
    got = got.reshape(all_rows, outer_width, pair_rows + pair_cols)
    left, right = got[:, :, :pair_rows], got[:, :, pair_rows:]
    if pair_cols % 128 == 0:
        pairs_new, left_grad, right_grad, table_grad = outer_product(
            left.transpose(2, 1, 0).reshape(pair_rows * outer_width, all_rows),
            right.reshape(all_rows, outer_width * pair_cols),
            pairs,
            pairs_back,
            table.swapaxes(0, 1).reshape(outer_width * outer_width, pair_width),
            all_rows,
        )
        left_grad = left_grad.reshape(pair_rows, outer_width, all_rows).transpose(2, 1, 0)
        right_grad = right_grad.astype(BF16).reshape(all_rows, outer_width, pair_cols)
        table_grad = table_grad.reshape(outer_width, outer_width, pair_width).swapaxes(0, 1)
    else:
        total, table_grad, left_grad, right_grad = outer_product_plain(
            left, right, pairs_back, table, all_rows
        )
        pairs_new = pairs + total

    send = jnp.concatenate([left_grad, right_grad], axis=2).reshape(
        devices, own, outer_width, pair_rows + pair_cols
    )
    got = lax.all_to_all(send, EVERY, split_axis=0, concat_axis=0, tiled=True)
    got = got.reshape(row_count, head_count, own, outer_width, pair_rows + pair_cols).astype(F32)
    left_total = jnp.sum(got[..., :pair_rows], axis=1).transpose(1, 2, 0, 3)
    right_total = jnp.sum(got[..., pair_rows:], axis=0).transpose(1, 2, 0, 3)
    sides_grad = jnp.concatenate(
        [
            left_total.reshape(own, outer_width, residues),
            right_total.reshape(own, outer_width, residues),
        ],
        axis=1,
    )
    sides_grad = (sides_grad * live[:, None, :]).astype(BF16)

    part, bias_grad, heads_in_grad, heads_out_grad, outer_in_grad, norms = attention_backward(
        rows, update, rows_back, scales, in_t, out_low, outer_t, sides_grad, kept
    )
    part_all = lax.all_gather(part, "head", axis=0, tiled=True)
    alignment_grad = alignment_back + part_all.astype(F32)

    bias_grad = lax.psum_scatter(bias_grad, "row", scatter_dimension=1, tiled=True)
    bias_grad = lax.psum_scatter(bias_grad, "head", scatter_dimension=2, tiled=True)
    pairs_grad, bias_weight_grad, pair_gain_grad, pair_shift_grad = pair_backward(
        pairs, pairs_back, pair_gain, pair_shift, bias_low, bias_grad
    )

    sums = lax.psum(
        (
            heads_in_grad,
            heads_out_grad,
            outer_in_grad,
            table_grad,
            norms,
            bias_weight_grad,
            jnp.stack([pair_gain_grad, pair_shift_grad]),
        ),
        EVERY,
    )
    heads_in_total = lax.dynamic_slice_in_dim(
        sums[0].reshape(4, width, width), head_index * local, local, 1
    ).swapaxes(1, 2)
    heads_out_total = lax.dynamic_slice_in_dim(sums[1], head_index * local, local, 0)
    outer_in_total = sums[2].reshape(2, outer_width, width).swapaxes(1, 2)
    table_total = sums[3].reshape(outer_width * outer_width, pair_width)
    norms_total = jnp.concatenate(
        [sums[4].reshape(2, 2, width).swapaxes(0, 1).reshape(2, 2 * width), sums[6]], axis=1
    )
    norms_new = adam_update(norm_scales, norms_total, first_norms, second_norms, 0.5)
    heads_in_upd = adam_update(
        heads_in, heads_in_total, first_heads_in, second_heads_in, width ** (-0.5)
    )
    heads_out_upd = adam_update(
        heads_out,
        heads_out_total,
        first_heads_out,
        second_heads_out,
        max(2 * HEADS * size // residues, 1) ** (-0.5),
    )
    bias_upd = adam_update(
        bias_weight, sums[5], first_bias_weight, second_bias_weight, pair_width ** (-0.5)
    )
    outer_in_upd = adam_update(
        outer_in, outer_in_total, first_outer_in, second_outer_in, width ** (-0.5)
    )
    outer_out_upd = adam_update(
        outer_out,
        table_total,
        first_outer_out,
        second_outer_out,
        max(outer_width * outer_width // all_rows, 1) ** (-0.5),
    )
    return (
        alignment_new,
        pairs_new,
        alignment_grad,
        pairs_grad,
        *norms_new,
        *heads_in_upd,
        *heads_out_upd,
        *bias_upd,
        *outer_in_upd,
        *outer_out_upd,
    )


def solution(mesh):
    row_msa = P("row", None, None)
    pair = P("row", "head", None)
    columns = P(None, None, "head")
    lines = P("head", None)
    in_specs = (
        (row_msa, pair, P(), P("row"), row_msa, pair, P(), columns, lines)
        + (P(),) * 5
        + (columns,) * 2
        + (lines,) * 2
        + (P(),) * 6
    )
    out_specs = (row_msa, pair, row_msa, pair) + (P(),) * 3 + (columns,) * 3 + (lines,) * 3 + (P(),) * 9
    return jax.shard_map(
        per_device, mesh=mesh, in_specs=in_specs, out_specs=out_specs, check_vma=False
    )
```

```python
import functools

import jax
import jax.numpy as jnp
from jax import lax
from jax.experimental import pallas as pl
from jax.experimental.pallas import tpu as pltpu
from jax.sharding import PartitionSpec as P

HEADS = 8
STEP = 10
F32 = jnp.float32
BF16 = jnp.bfloat16
LOG2E = 1.4426950408889634
EVERY = ("row", "head")


def adam_update(weight, gradient, moment_one, moment_two, step_rate):
    first_new = 0.9 * moment_one + 0.1 * gradient
    second_new = 0.999 * moment_two + 0.001 * gradient * gradient
    first_hat = first_new / (1.0 - 0.9**STEP)
    second_hat = second_new / (1.0 - 0.999**STEP)
    updated = weight - step_rate * (first_hat / (jnp.sqrt(second_hat) + 1e-08) + 0.01 * weight)
    return (first_new, second_new, updated)


def dot(a, b, along):
    return lax.dot_general(a, b, (((along[0],), (along[1],)), ((), ())), preferred_element_type=F32)


def normalize(values):
    center = values - jnp.mean(values, axis=-1, keepdims=True)
    rstd = lax.rsqrt(jnp.mean(center * center, axis=-1, keepdims=True) + 1e-05)
    return center * rstd, rstd


def norm_backward(hat, rstd, gain, grad):
    scaled = grad * gain
    return rstd * (
        scaled
        - jnp.mean(scaled, axis=-1, keepdims=True)
        - hat * jnp.mean(scaled * hat, axis=-1, keepdims=True)
    )


def forward_kernel(
    rows, scales, in_t, out_low, outer_t, bias, key_mask, live,
    update, sides, qkv, gate, powers, inverse, mixed, attended,
    bias_t, *, chunk,
):
    row, head = pl.program_id(0), pl.program_id(1)
    width = rows.shape[2]
    residues = rows.shape[1]
    size = width // HEADS

    @pl.when(row == 0)
    def _():
        across, down, _, lines, cols = bias.shape
        group = max(1, 128 // lines)
        for r in range(0, across, group):
            for c in range(down):
                tile = jnp.concatenate([bias[r + g, c, 0] for g in range(group)], axis=0)
                bias_t[head, c * cols : (c + 1) * cols, r * lines : (r + group) * lines] = (
                    tile.astype(F32).T + key_mask[c * cols : (c + 1) * cols]
                )

    @pl.when(head == 0)
    def _():
        hat, _ = normalize(rows[0])
        normed = (hat * scales[0:1] + scales[1:2]).astype(BF16)
        qkv[0, :width] = (
            dot(in_t[:width], normed, (1, 1)) * (size**-0.5 * LOG2E)
        ).astype(BF16)
        qkv[0, width:] = dot(in_t[width : 3 * width], normed, (1, 1)).astype(BF16)
        gate[0] = jax.nn.sigmoid(dot(in_t[3 * width :], normed, (1, 1)))

    at = pl.multiple_of(head * size, size)
    keys = qkv[0, pl.ds(width + at, size), :]
    values = qkv[0, pl.ds(2 * width + at, size), :]
    for first in range(0, residues, chunk):
        span = slice(first, first + chunk)
        query = qkv[0, pl.ds(at, size), span]
        scores = dot(keys, query, (0, 0)) + bias_t[head, :, span]
        exps = jnp.exp2(scores - jnp.max(scores, axis=0, keepdims=True))
        over = 1.0 / jnp.sum(exps, axis=0, keepdims=True)
        low = exps.astype(BF16)
        powers[0, 0, :, span] = low
        inverse[0, 0, :, span] = over
        mixed[0, pl.ds(at, size), span] = dot(values, low, (1, 0)) * over

    @pl.when(head == HEADS - 1)
    def _():
        att = (gate[0] * mixed[0]).astype(BF16)
        attended[0] = att
        change = dot(att, out_low[...], (0, 0)).astype(BF16)
        update[0] = change
        hat, _ = normalize(rows[0] + change.astype(F32))
        second = (hat * scales[2:3] + scales[3:4]).astype(BF16)
        sides[0] = (dot(outer_t[...], second, (1, 1)) * live[0]).astype(BF16)


def attention_forward(rows, scales, in_t, out_low, outer_t, bias, key_mask, live, chunk=512):
    own, residues, width = rows.shape
    sides = outer_t.shape[0]
    by_row = lambda s, h: (s, 0, 0)
    whole = lambda s, h: (0, 0)
    last = lambda s, h: (0, 0, jnp.where(s == 0, h, HEADS - 1), 0, 0)
    out = pl.pallas_call(
        functools.partial(forward_kernel, chunk=chunk),
        grid=(own, HEADS),
        in_specs=[
            pl.BlockSpec((1, residues, width), by_row),
            pl.BlockSpec(scales.shape, whole),
            pl.BlockSpec(in_t.shape, whole),
            pl.BlockSpec(out_low.shape, whole),
            pl.BlockSpec(outer_t.shape, whole),
            pl.BlockSpec(bias.shape[:2] + (1,) + bias.shape[3:], last),
            pl.BlockSpec((residues, 1), whole),
            pl.BlockSpec((1, 1, residues), by_row),
        ],
        out_specs=[
            pl.BlockSpec((1, residues, width), by_row),
            pl.BlockSpec((1, sides, residues), by_row),
            pl.BlockSpec((1, 3 * width, residues), by_row),
            pl.BlockSpec((1, width, residues), by_row),
            pl.BlockSpec((1, 1, residues, residues), lambda s, h: (s, h, 0, 0)),
            pl.BlockSpec((1, 1, 1, residues), lambda s, h: (s, h, 0, 0)),
            pl.BlockSpec((1, width, residues), by_row),
            pl.BlockSpec((1, width, residues), by_row),
        ],
        out_shape=[
            jax.ShapeDtypeStruct((own, residues, width), BF16),
            jax.ShapeDtypeStruct((own, sides, residues), BF16),
            jax.ShapeDtypeStruct((own, 3 * width, residues), BF16),
            jax.ShapeDtypeStruct((own, width, residues), F32),
            jax.ShapeDtypeStruct((own, HEADS, residues, residues), BF16),
            jax.ShapeDtypeStruct((own, HEADS, 1, residues), F32),
            jax.ShapeDtypeStruct((own, width, residues), F32),
            jax.ShapeDtypeStruct((own, width, residues), BF16),
        ],
        scratch_shapes=[pltpu.VMEM((HEADS, residues, residues), F32)],
        compiler_params=pltpu.CompilerParams(vmem_limit_bytes=50 << 20),
    )(rows, scales, in_t, out_low, outer_t, bias, key_mask, live)
    return out[0], out[1], tuple(out[2:])


def backward_kernel(
    rows, update, back, scales, in_t, out_low, outer_t, sides_grad,
    qkv, gate, powers, inverse, mixed, attended,
    part, bias_grad, heads_in_grad, heads_out_grad, outer_in_grad, norms,
    bias_total, mixed_grad, delta, proj_grad, new_part, *, chunk,
):
    row, head = pl.program_id(0), pl.program_id(1)
    width = rows.shape[2]
    residues = rows.shape[1]
    size = width // HEADS
    last_row = row == pl.num_programs(0) - 1

    @pl.when((row == 0) & (head == 0))
    def _():
        heads_in_grad[...] = jnp.zeros_like(heads_in_grad)
        heads_out_grad[...] = jnp.zeros_like(heads_out_grad)
        outer_in_grad[...] = jnp.zeros_like(outer_in_grad)
        norms[...] = jnp.zeros_like(norms)
        bias_total[...] = jnp.zeros_like(bias_total)

    @pl.when(head == 0)
    def _():
        hat, rstd = normalize(rows[0] + update[0].astype(F32))
        second = (hat * scales[2:3] + scales[3:4]).astype(BF16)
        grads = sides_grad[0]
        outer_in_grad[...] += dot(grads, second, (1, 0))
        second_grad = dot(grads, outer_t[...], (0, 0))
        norms[2:3] += jnp.sum(second_grad * hat, axis=0, keepdims=True)
        norms[3:4] += jnp.sum(second_grad, axis=0, keepdims=True)
        new = norm_backward(hat, rstd, scales[2:3], second_grad)
        new_part[...] = new
        out_grad = (back[0] + new).astype(BF16)
        heads_out_grad[...] += dot(attended[0], out_grad, (1, 0))
        attended_grad = dot(out_low[...], out_grad, (1, 1))
        sig = gate[0]
        gated = attended_grad * sig
        proj_grad[3 * width :] = (gated * mixed[0] * (1.0 - sig)).astype(BF16)
        for h in range(HEADS):
            span = slice(h * size, (h + 1) * size)
            grad = gated[span] * inverse[0, h]
            mixed_grad[span] = grad.astype(BF16)
            delta[h] = jnp.sum(grad * mixed[0, span], axis=0, keepdims=True)

    at = pl.multiple_of(head * size, size)
    keys = qkv[0, pl.ds(width + at, size), :]
    values = qkv[0, pl.ds(2 * width + at, size), :]
    key_grad = jnp.zeros((size, residues), F32)
    value_grad = jnp.zeros((size, residues), F32)
    for first in range(0, residues, chunk):
        span = slice(first, first + chunk)
        grad = mixed_grad[pl.ds(at, size), span]
        query = qkv[0, pl.ds(at, size), span]
        low = powers[0, 0, :, span]
        prob_grad = dot(values, grad, (0, 0))
        score_grad = low.astype(F32) * (prob_grad - delta[head, :, span])
        bias_total[head, :, span] += score_grad
        score_low = score_grad.astype(BF16)
        value_grad += dot(grad, low, (1, 1))
        key_grad += dot(query, score_low, (1, 1))
        proj_grad[pl.ds(at, size), span] = (dot(keys, score_low, (1, 0)) * size**-0.5).astype(BF16)
    proj_grad[pl.ds(width + at, size), :] = (key_grad / LOG2E).astype(BF16)
    proj_grad[pl.ds(2 * width + at, size), :] = value_grad.astype(BF16)

    @pl.when(last_row)
    def _():
        across, down, _, lines, cols = bias_grad.shape
        group = max(1, 128 // lines)
        for r in range(0, across, group):
            for c in range(down):
                tile = bias_total[head, c * cols : (c + 1) * cols, r * lines : (r + group) * lines]
                tile = tile.T.astype(BF16)
                for g in range(group):
                    bias_grad[r + g, c, 0] = tile[g * lines : (g + 1) * lines]

    @pl.when(head == HEADS - 1)
    def _():
        hat, rstd = normalize(rows[0])
        normed = (hat * scales[0:1] + scales[1:2]).astype(BF16)
        grads = proj_grad[...]
        heads_in_grad[...] += dot(grads, normed, (1, 0))
        normed_grad = dot(grads, in_t[...], (0, 0))
        norms[0:1] += jnp.sum(normed_grad * hat, axis=0, keepdims=True)
        norms[1:2] += jnp.sum(normed_grad, axis=0, keepdims=True)
        part[0] = (new_part[...] + norm_backward(hat, rstd, scales[0:1], normed_grad)).astype(BF16)


def attention_backward(rows, update, back, scales, in_t, out_low, outer_t, sides_grad, kept, blocks, chunk=512):
    own, residues, width = rows.shape
    qkv, gate, powers, inverse, mixed, attended = kept
    sides = outer_t.shape[0]
    by_row = lambda s, h: (s, 0, 0)
    whole = lambda s, h: (0, 0)
    out = pl.pallas_call(
        functools.partial(backward_kernel, chunk=chunk),
        grid=(own, HEADS),
        in_specs=[
            pl.BlockSpec((1, residues, width), by_row),
            pl.BlockSpec((1, residues, width), by_row),
            pl.BlockSpec((1, residues, width), by_row),
            pl.BlockSpec(scales.shape, whole),
            pl.BlockSpec(in_t.shape, whole),
            pl.BlockSpec(out_low.shape, whole),
            pl.BlockSpec(outer_t.shape, whole),
            pl.BlockSpec((1, sides, residues), by_row),
            pl.BlockSpec((1, 3 * width, residues), by_row),
            pl.BlockSpec((1, width, residues), by_row),
            pl.BlockSpec((1, 1, residues, residues), lambda s, h: (s, h, 0, 0)),
            pl.BlockSpec((1, HEADS, 1, residues), lambda s, h: (s, 0, 0, 0)),
            pl.BlockSpec((1, width, residues), by_row),
            pl.BlockSpec((1, width, residues), by_row),
        ],
        out_specs=[
            pl.BlockSpec((1, residues, width), by_row),
            pl.BlockSpec(
                blocks[:2] + (1,) + blocks[3:], lambda s, h: (0, 0, jnp.where(s == own - 1, h, 0), 0, 0)
            ),
            pl.BlockSpec(in_t.shape, whole),
            pl.BlockSpec(out_low.shape, whole),
            pl.BlockSpec(outer_t.shape, whole),
            pl.BlockSpec((4, width), whole),
        ],
        out_shape=[
            jax.ShapeDtypeStruct((own, residues, width), BF16),
            jax.ShapeDtypeStruct(blocks, BF16),
            jax.ShapeDtypeStruct(in_t.shape, F32),
            jax.ShapeDtypeStruct(out_low.shape, F32),
            jax.ShapeDtypeStruct(outer_t.shape, F32),
            jax.ShapeDtypeStruct((4, width), F32),
        ],
        scratch_shapes=[
            pltpu.VMEM((HEADS, residues, residues), F32),
            pltpu.VMEM((width, residues), BF16),
            pltpu.VMEM((HEADS, 1, residues), F32),
            pltpu.VMEM((4 * width, residues), BF16),
            pltpu.VMEM((residues, width), F32),
        ],
        compiler_params=pltpu.CompilerParams(vmem_limit_bytes=50 << 20),
    )(rows, update, back, scales, in_t, out_low, outer_t, sides_grad, qkv, gate, powers, inverse, mixed, attended)
    return out


def outer_kernel(
    left, right, pairs, back, table, table_t,
    total, left_grad, right_grad, table_grad,
    product, backed, *, scale, group,
):
    step = pl.program_id(0)
    rows = pairs.shape[0]
    cols = pairs.shape[1]
    channels = pairs.shape[2]
    width = left.shape[0] // rows
    wide = right.shape[1] // cols

    @pl.when(step == 0)
    def _():
        right_grad[...] = jnp.zeros_like(right_grad)
        table_grad[...] = jnp.zeros_like(table_grad)

    product[...] = dot(left[...], right[...], (1, 0)).astype(BF16)
    for first in range(0, rows, group):
        low = back[first : first + group].astype(BF16).reshape(group * cols, channels)
        both = jnp.concatenate(
            [
                jnp.concatenate(
                    [
                        product[(first + g) * width : (first + g + 1) * width, f * cols : (f + 1) * cols]
                        for f in range(wide)
                    ],
                    axis=0,
                )
                for g in range(group)
            ],
            axis=1,
        )
        out = dot(table_t[...], both, (1, 0)) * scale
        for g in range(group):
            total[first + g] = pairs[first + g] + out[:, g * cols : (g + 1) * cols].T
        table_grad[...] += dot(both, low, (1, 0)) * scale
        spread = dot(table[...], low, (1, 1)).astype(BF16)
        for g in range(group):
            for f in range(wide):
                backed[(first + g) * width : (first + g + 1) * width, f * cols : (f + 1) * cols] = spread[
                    f * width : (f + 1) * width, g * cols : (g + 1) * cols
                ]
    left_grad[...] = (dot(backed[...], right[...], (1, 1)) * scale).astype(BF16)
    right_grad[...] += dot(left[...], backed[...], (0, 0)) * scale


def outer_product(left, right, pairs, back, table, all_rows, block=8, group=2):
    rows, cols, channels = pairs.shape
    width = left.shape[0] // rows
    table_t = table.T
    by_row = lambda n: (n, 0, 0)
    whole = lambda n: (0, 0)
    return pl.pallas_call(
        functools.partial(outer_kernel, scale=1.0 / all_rows, group=group),
        grid=(rows // block,),
        in_specs=[
            pl.BlockSpec((block * width, left.shape[1]), lambda n: (n, 0)),
            pl.BlockSpec(right.shape, whole),
            pl.BlockSpec((block, cols, channels), by_row),
            pl.BlockSpec((block, cols, channels), by_row),
            pl.BlockSpec(table.shape, whole),
            pl.BlockSpec(table_t.shape, whole),
        ],
        out_specs=[
            pl.BlockSpec((block, cols, channels), by_row),
            pl.BlockSpec((block * width, left.shape[1]), lambda n: (n, 0)),
            pl.BlockSpec(right.shape, whole),
            pl.BlockSpec(table.shape, whole),
        ],
        out_shape=[
            jax.ShapeDtypeStruct(pairs.shape, F32),
            jax.ShapeDtypeStruct(left.shape, BF16),
            jax.ShapeDtypeStruct(right.shape, F32),
            jax.ShapeDtypeStruct(table.shape, F32),
        ],
        scratch_shapes=[
            pltpu.VMEM((block * width, right.shape[1]), BF16),
            pltpu.VMEM((block * width, right.shape[1]), BF16),
        ],
        compiler_params=pltpu.CompilerParams(vmem_limit_bytes=50 << 20),
    )(left, right, pairs, back, table, table_t)


def outer_product_plain(left, right, pairs_back, table, all_rows):
    low = pairs_back.astype(BF16)
    product = mm("sei,sfj->eifj", left, right).astype(BF16)
    total = mm("eifj,efz->ijz", product, table) / all_rows
    table_grad = mm("eifj,ijz->efz", product, low) / all_rows
    back = mm("ijz,efz->eifj", low, table).astype(BF16)
    left_grad = mm("eifj,sfj->sei", back, right) / all_rows
    right_grad = mm("eifj,sei->sfj", back, left) / all_rows
    return total, table_grad, left_grad.astype(BF16), right_grad.astype(BF16)


def mm(spec, a, b):
    return jnp.einsum(spec, a, b, preferred_element_type=F32)


def pair_forward(pairs, gain, shift, bias_low):
    hat, _ = normalize(pairs)
    low = (hat * gain + shift).astype(BF16)
    return (mm("ijc,ch->hij", low, bias_low) * LOG2E).astype(BF16)


def pair_backward(pairs, pairs_back, gain, shift, bias_low, bias_grad):
    hat, rstd = normalize(pairs)
    low = (hat * gain + shift).astype(BF16)
    weight_grad = mm("ijc,hij->ch", low, bias_grad)
    in_grad = mm("hij,ch->ijc", bias_grad, bias_low)
    gain_grad = jnp.sum(in_grad * hat, axis=(0, 1))
    shift_grad = jnp.sum(in_grad, axis=(0, 1))
    return pairs_back + norm_backward(hat, rstd, gain, in_grad), weight_grad, gain_grad, shift_grad


MESH = pl.DeviceIdType.MESH
CORE, ACROSS, DOWN, CORNER = 1, 2, 4, 6


def place():
    return lax.axis_index("row"), lax.axis_index("head")


def flip(row, way):
    out = row
    for bit in (1, 2, 4):
        if way & bit:
            out = out + bit - 2 * bit * ((row // bit) % 2)
    return out


def greet(devices):
    barrier = pltpu.get_barrier_semaphore()
    for device in devices:
        pl.semaphore_signal(barrier, inc=1, device_id=device, device_id_type=MESH)
    pl.semaphore_wait(barrier, len(devices))


class Sends:
    def __init__(self, send_sem, recv_sem):
        self.send_sem, self.recv_sem, self.count, self.open = send_sem, recv_sem, 0, []

    def start(self, source, target, device):
        copy = pltpu.make_async_remote_copy(
            src_ref=source,
            dst_ref=target,
            send_sem=self.send_sem.at[self.count],
            recv_sem=self.recv_sem.at[self.count],
            device_id=device,
            device_id_type=MESH,
        )
        copy.start()
        self.count += 1
        self.open.append(copy)
        return copy

    def finish(self):
        for copy in self.open:
            copy.wait_send()


GATHER_SENDS = 6 + 3 + 31 + 3


def pair_bias_kernel(pairs, norm, weight, shard, bias, weights, block, low, local_sem, send_sem, recv_sem):
    row, head = place()
    rows, cols, channels = pairs.shape
    part = shard.shape[1] // 2
    core = row % 2
    beyond = [(head + k) % 4 for k in range(4)]
    behind = [(head + 4 - k) % 4 for k in range(4)]
    across, down, other = (flip(row, ACROSS), head), (flip(row, DOWN), head), (flip(row, CORE), head)
    greet([across, down, other] + [(row, beyond[k]) for k in (1, 2, 3)])
    sends = Sends(send_sem, recv_sem)

    def own_part(at, side):
        return weights.at[:, pl.ds(pl.multiple_of(at * 2 * part + side * part, part), part), :]

    half = shard.at[:, pl.ds(pl.multiple_of(core * part, part), part), :]
    keep = pltpu.make_async_copy(
        shard, weights.at[:, pl.ds(pl.multiple_of(head * 2 * part, 2 * part), 2 * part), :], local_sem.at[0]
    )
    keep.start()
    shards = [None] + [sends.start(half, own_part(head, core), (row, beyond[k])) for k in (1, 2, 3)]

    step = 8

    def norm_block(n, carry):
        first = pl.multiple_of(n * step, step)
        values = pairs[pl.ds(first, step)].reshape(step * cols, channels)
        center = values - jnp.mean(values, axis=-1, keepdims=True)
        rstd = lax.rsqrt(jnp.mean(center * center, axis=-1, keepdims=True) + 1e-05)
        normed = (center * rstd * norm[0:1] + norm[1:2]).astype(BF16)
        out = lax.dot_general(weight[...], normed, (((1,), (1,)), ((), ())), preferred_element_type=F32)
        for i in range(step):
            block[:, pl.ds(first + i, 1), :] = (out[:, i * cols : (i + 1) * cols] * LOG2E).reshape(
                HEADS, 1, cols
            )
        return carry

    lax.fori_loop(0, rows // step, norm_block, 0)
    low[...] = block[...].astype(BF16)

    mine = pltpu.make_async_copy(low, bias.at[row, head], local_sem.at[1])
    mine.start()
    stage = [None] * 4
    stage[0] = low
    along = [None] + [sends.start(low, bias.at[row, head], (row, beyond[k])) for k in (1, 2, 3)]
    from_across, from_down, from_corner, from_core = [None] * 4, [None] * 4, [None] * 4, []

    def spread(k, source):
        here = bias.at[row, behind[k]]
        from_across[k] = sends.start(source, here, across)
        from_down[k] = sends.start(source, here, down)
        from_core.append(sends.start(source, here, other))

    def relay(k):
        from_across[k].wait_recv()
        block_across = bias.at[flip(row, ACROSS), behind[k]]
        if k < 2:
            from_corner[k] = sends.start(block_across, block_across, down)
        from_core.append(sends.start(block_across, block_across, other))
        from_down[k].wait_recv()
        block_down = bias.at[flip(row, DOWN), behind[k]]
        if k >= 2:
            from_corner[k] = sends.start(block_down, block_down, across)
        from_core.append(sends.start(block_down, block_down, other))

    spread(0, low)
    for k in (1, 2, 3):
        along[k].wait_recv()
        spread(k, bias.at[row, behind[k]])
        relay(k - 1)
    relay(3)
    for k in range(4):
        from_corner[k].wait_recv()
        block_corner = bias.at[flip(row, CORNER), behind[k]]
        from_core.append(sends.start(block_corner, block_corner, other))
    for k in (1, 2, 3):
        shards[k].wait_recv()
        piece = own_part(behind[k], core)
        from_core.append(sends.start(piece, piece, other))
    for copy in from_core:
        copy.wait_recv()
    sends.finish()
    keep.wait()
    mine.wait()


def pair_bias(pairs, norm, weight, shard):
    rows, cols, channels = pairs.shape
    vmem = pl.BlockSpec(memory_space=pltpu.VMEM)
    hbm = pl.BlockSpec(memory_space=pl.ANY)
    return pl.pallas_call(
        pair_bias_kernel,
        out_shape=[
            jax.ShapeDtypeStruct((8, 4, HEADS, rows, cols), BF16),
            jax.ShapeDtypeStruct((shard.shape[0], 4 * shard.shape[1], shard.shape[2]), BF16),
        ],
        in_specs=[vmem, vmem, vmem, hbm],
        out_specs=[hbm, hbm],
        scratch_shapes=[
            pltpu.VMEM((HEADS, rows, cols), F32),
            pltpu.VMEM((HEADS, rows, cols), BF16),
            pltpu.SemaphoreType.DMA((2,)),
            pltpu.SemaphoreType.DMA((GATHER_SENDS,)),
            pltpu.SemaphoreType.DMA((GATHER_SENDS,)),
        ],
        compiler_params=pltpu.CompilerParams(
            collective_id=0, has_side_effects=True, vmem_limit_bytes=32 << 20
        ),
    )(pairs, norm, weight, shard)


SIDES_SENDS = 6 + 28 + 16 + 12


def sides_kernel(left, right, left_all, right_all, left_on, right_on, local_sem, send_sem, recv_sem):
    row, head = place()
    beyond = [(head + k) % 4 for k in range(4)]
    behind = [(head + 4 - k) % 4 for k in range(4)]
    plane = [(flip(row, way), head) for way in range(8)]
    greet(plane[1:] + [(row, beyond[k]) for k in (1, 2, 3)])
    sends = Sends(send_sem, recv_sem)
    from_left, from_right = [None] * 4, [None] * 4
    for k in (1, 2, 3):
        from_right[k] = sends.start(right.at[beyond[k]], right_on.at[k], (row, beyond[k]))
        from_left[k] = sends.start(left, left_on.at[k], (row, beyond[k]))
    locals_ = []
    arrive, onward = [], []
    for k in range(4):
        if k:
            from_right[k].wait_recv()
        ours = right_on.at[k] if k else right.at[head]
        for way in (ACROSS, DOWN, CORNER):
            onward.append((way, k, sends.start(ours, right_all.at[row, behind[k]], plane[way])))
        arrive.append(sends.start(ours, right_all.at[row, behind[k]], plane[CORE]))
        copy = pltpu.make_async_copy(ours, right_all.at[row, behind[k]], local_sem.at[2 * k])
        copy.start()
        locals_.append(copy)
        if k:
            from_left[k].wait_recv()
        ours = left_on.at[k] if k else left
        for way in (2, 4, 6, 3, 5, 7, 1):
            arrive.append(sends.start(ours.at[plane[way][0]], left_all.at[row, behind[k]], plane[way]))
        copy = pltpu.make_async_copy(ours.at[row], left_all.at[row, behind[k]], local_sem.at[2 * k + 1])
        copy.start()
        locals_.append(copy)
    for way, k, copy in onward:
        copy.wait_recv()
        block = right_all.at[plane[way][0], behind[k]]
        arrive.append(sends.start(block, block, plane[CORE]))
    for copy in arrive:
        copy.wait_recv()
    sends.finish()
    for copy in locals_:
        copy.wait()


def share_sides(left, right):
    hbm = pl.BlockSpec(memory_space=pl.ANY)
    return pl.pallas_call(
        sides_kernel,
        out_shape=[
            jax.ShapeDtypeStruct((8, 4) + left.shape[1:], BF16),
            jax.ShapeDtypeStruct((8, 4) + right.shape[1:], BF16),
        ],
        in_specs=[hbm, hbm],
        out_specs=[hbm, hbm],
        scratch_shapes=[
            pltpu.VMEM((4,) + left.shape, BF16),
            pltpu.VMEM((4,) + right.shape[1:], BF16),
            pltpu.SemaphoreType.DMA((8,)),
            pltpu.SemaphoreType.DMA((SIDES_SENDS,)),
            pltpu.SemaphoreType.DMA((SIDES_SENDS,)),
        ],
        compiler_params=pltpu.CompilerParams(
            collective_id=1, has_side_effects=True, vmem_limit_bytes=32 << 20
        ),
    )(left, right)


RETURN_SENDS = 1 + 7 + 3 + 6


def return_kernel(
    left, right, left_out, right_out, right_core, left_in, right_in, left_on, right_sum, local_sem, send_sem, recv_sem
):
    row, head = place()
    beyond = [(head + k) % 4 for k in range(4)]
    behind = [(head + 4 - k) % 4 for k in range(4)]
    plane = [(flip(row, way), head) for way in range(8)]
    greet(plane[1:] + [(row, beyond[k]) for k in (1, 2, 3)])
    sends = Sends(send_sem, recv_sem)
    core = row % 2
    swap = sends.start(right.at[:, 1 - core], right_core, plane[CORE])
    lefts = [sends.start(left.at[plane[way][0]], left_in.at[row], plane[way]) for way in (2, 4, 6, 3, 5, 7, 1)]
    copy = pltpu.make_async_copy(left.at[row], left_in.at[row], local_sem.at[0])
    copy.start()
    swap.wait_recv()
    chip = row // 2
    blocks = right.shape[2]
    for n in range(right.shape[0]):
        for b in range(blocks):
            right_sum[n, b] = (
                right[n, core, b].astype(F32) + right_core[n, b].astype(F32)
            ).astype(BF16)
    rights = []
    for slot, way in enumerate((ACROSS, DOWN, CORNER)):
        rights.append(sends.start(right_sum.at[plane[way][0] // 2], right_in.at[slot], plane[way]))
    for arrival in lefts:
        arrival.wait_recv()
    copy.wait()
    on = []
    for k in (1, 2, 3):
        on.append(sends.start(left_in.at[:, beyond[k]], left_on.at[k - 1], (row, beyond[k])))
    for arrival in rights:
        arrival.wait_recv()
    for b in range(blocks):
        total = right_sum[chip, b].astype(F32)
        for slot in range(3):
            total = total + right_in[slot, b].astype(F32)
        right_core[0, b] = total.astype(BF16)
    last = []
    for k in (1, 2, 3):
        last.append(sends.start(right_core.at[0, beyond[k]], right_out.at[head], (row, beyond[k])))
    mine = pltpu.make_async_copy(right_core.at[0, head], right_out.at[head], local_sem.at[1])
    mine.start()
    for arrival in on:
        arrival.wait_recv()
    for n in range(left_in.shape[0]):
        total = left_in[n, head].astype(F32)
        for k in range(3):
            total = total + left_on[k, n].astype(F32)
        left_out[n] = total.astype(BF16)
    for arrival in last:
        arrival.wait_recv()
    mine.wait()
    sends.finish()


def return_sides(left, right):
    vmem = pl.BlockSpec(memory_space=pltpu.VMEM)
    piece_left, piece_right = left.shape[2:], right.shape[2:]
    return pl.pallas_call(
        return_kernel,
        out_shape=[
            jax.ShapeDtypeStruct((8,) + piece_left, BF16),
            jax.ShapeDtypeStruct((4,) + piece_right, BF16),
        ],
        in_specs=[vmem, vmem],
        out_specs=[vmem, vmem],
        scratch_shapes=[
            pltpu.VMEM((4, 4) + piece_right, BF16),
            pltpu.VMEM((8, 4) + piece_left, BF16),
            pltpu.VMEM((3, 4) + piece_right, BF16),
            pltpu.VMEM((3, 8) + piece_left, BF16),
            pltpu.VMEM((4, 4) + piece_right, BF16),
            pltpu.SemaphoreType.DMA((2,)),
            pltpu.SemaphoreType.DMA((RETURN_SENDS,)),
            pltpu.SemaphoreType.DMA((RETURN_SENDS,)),
        ],
        compiler_params=pltpu.CompilerParams(
            collective_id=2, has_side_effects=True, vmem_limit_bytes=32 << 20
        ),
    )(left, right.reshape((4, 2) + right.shape[1:]))


BIAS_SENDS = 4 + 12 + 3


def bias_sum_kernel(grads, out, swapped, chip_sum, plane_in, down_sum, line_in, send_sem, recv_sem):
    row, head = place()
    beyond = [(head + k) % 4 for k in range(4)]
    core, chip = row % 2, row // 2
    ways = (CORNER, ACROSS, DOWN)
    plane = [(flip(row, way), head) for way in range(8)]
    other = plane[CORE]
    greet([plane[way] for way in (CORE,) + ways] + [(row, beyond[k]) for k in (1, 2, 3)])
    sends = Sends(send_sem, recv_sem)
    chips = [plane[way][0] // 2 for way in ways] + [chip]
    swaps = [sends.start(grads.at[n, 1 - core], swapped.at[slot], other) for slot, n in enumerate(chips)]
    order = (2, 1, 3, 0)
    arrive = [[None] * 3 for _ in range(4)]
    for slot, n in enumerate(chips):
        swaps[slot].wait_recv()
        for k in order:
            z = beyond[k]
            chip_sum[slot, z] = (
                grads[n, core, z].astype(F32) + swapped[slot, z].astype(F32)
            ).astype(BF16)
            if slot < 3:
                arrive[k][slot] = sends.start(
                    chip_sum.at[slot, z], plane_in.at[slot, k], plane[ways[slot]]
                )
    line = []
    for k in order:
        for slot in range(3):
            arrive[k][slot].wait_recv()
        total = chip_sum[3, beyond[k]].astype(F32)
        for slot in range(3):
            total = total + plane_in[slot, k].astype(F32)
        if k:
            down_sum[k - 1] = total.astype(BF16)
            line.append(sends.start(down_sum.at[k - 1], line_in.at[k - 1], (row, beyond[k])))
        else:
            out[...] = total
    for slot, copy in zip((1, 0, 2), line):
        copy.wait_recv()
        out[...] += line_in[slot].astype(F32)
    sends.finish()


def bias_sum(grads):
    block = grads.shape[2:]
    lines = block[0] * block[1]
    vmem = pl.BlockSpec(memory_space=pltpu.VMEM)
    out = pl.pallas_call(
        bias_sum_kernel,
        out_shape=jax.ShapeDtypeStruct((lines, block[2]), F32),
        in_specs=[vmem],
        out_specs=vmem,
        scratch_shapes=[
            pltpu.VMEM((4, 4, lines, block[2]), BF16),
            pltpu.VMEM((4, 4, lines, block[2]), BF16),
            pltpu.VMEM((3, 4, lines, block[2]), BF16),
            pltpu.VMEM((3, lines, block[2]), BF16),
            pltpu.VMEM((3, lines, block[2]), BF16),
            pltpu.SemaphoreType.DMA((BIAS_SENDS,)),
            pltpu.SemaphoreType.DMA((BIAS_SENDS,)),
        ],
        compiler_params=pltpu.CompilerParams(
            collective_id=3, has_side_effects=True, vmem_limit_bytes=32 << 20
        ),
    )(grads.reshape(4, 2, 4, lines, block[2]))
    return out.reshape(block)


SUM_SENDS = 1 + 3 + 3 + 3 + 12 + 16


def weight_sum_kernel(parts, out, swapped, chip_sum, plane_in, down_sum, line_in, final, local_sem, send_sem, recv_sem):
    row, head = place()
    beyond = [(head + k) % 4 for k in range(4)]
    behind = [(head + 4 - k) % 4 for k in range(4)]
    core, chip = row % 2, row // 2
    ways = (CORNER, ACROSS, DOWN)
    plane = [(flip(row, way), head) for way in range(8)]
    other = plane[CORE]
    greet([plane[way] for way in (CORE,) + ways] + [(row, beyond[k]) for k in (1, 2, 3)])
    sends = Sends(send_sem, recv_sem)
    swap = sends.start(parts.at[1 - core], swapped, other)
    swap.wait_recv()
    arrive = []
    for slot, way in enumerate(ways + (0,)):
        n = plane[way][0] // 2
        for z in range(4):
            chip_sum[slot, z] = (parts[core, n, z].astype(F32) + swapped[n, z].astype(F32)).astype(BF16)
        if way:
            arrive.append(sends.start(chip_sum.at[slot], plane_in.at[slot], plane[way]))
    for copy in arrive:
        copy.wait_recv()
    for z in range(4):
        total = chip_sum[3, z].astype(F32)
        for slot in range(3):
            total = total + plane_in[slot, z].astype(F32)
        down_sum[z] = total.astype(BF16)
    arrive = [sends.start(down_sum.at[beyond[k]], line_in.at[k - 1], (row, beyond[k])) for k in (1, 2, 3)]
    total = down_sum[head].astype(F32)
    for k, copy in enumerate(arrive):
        copy.wait_recv()
        total = total + line_in[k].astype(F32)
    final[...] = total.astype(BF16)
    mine = pltpu.make_async_copy(final, out.at[core, chip, head], local_sem)
    mine.start()
    line = [None] + [sends.start(final, out.at[core, chip, head], (row, beyond[k])) for k in (1, 2, 3)]
    across, end = [], []
    for k in range(4):
        if k:
            line[k].wait_recv()
        here = out.at[core, chip, behind[k]]
        source = here if k else final
        for way in ways:
            across.append((plane[way][0] // 2, k, sends.start(source, here, plane[way])))
        end.append(sends.start(source, here, other))
    for n, k, copy in across:
        copy.wait_recv()
        block = out.at[core, n, behind[k]]
        end.append(sends.start(block, block, other))
    for copy in end:
        copy.wait_recv()
    mine.wait()
    sends.finish()


def weight_sum(parts):
    rows, cols = parts.shape
    lines = rows // 32
    vmem = pl.BlockSpec(memory_space=pltpu.VMEM)
    shape = (2, 4, 4, lines, cols)
    out = pl.pallas_call(
        weight_sum_kernel,
        out_shape=jax.ShapeDtypeStruct(shape, BF16),
        in_specs=[vmem],
        out_specs=vmem,
        scratch_shapes=[
            pltpu.VMEM((4, 4, lines, cols), BF16),
            pltpu.VMEM((4, 4, lines, cols), BF16),
            pltpu.VMEM((3, 4, lines, cols), BF16),
            pltpu.VMEM((4, lines, cols), BF16),
            pltpu.VMEM((3, lines, cols), BF16),
            pltpu.VMEM((lines, cols), BF16),
            pltpu.SemaphoreType.DMA,
            pltpu.SemaphoreType.DMA((SUM_SENDS,)),
            pltpu.SemaphoreType.DMA((SUM_SENDS,)),
        ],
        compiler_params=pltpu.CompilerParams(
            collective_id=4, has_side_effects=True, vmem_limit_bytes=32 << 20
        ),
    )(parts.reshape(shape))
    return out.reshape(rows, cols)


def per_device(
    alignment,
    pairs,
    residue_mask,
    row_mask,
    alignment_back,
    pairs_back,
    norm_scales,
    heads_in,
    heads_out,
    bias_weight,
    outer_in,
    outer_out,
    first_norms,
    second_norms,
    first_heads_in,
    second_heads_in,
    first_heads_out,
    second_heads_out,
    first_bias_weight,
    second_bias_weight,
    first_outer_in,
    second_outer_in,
    first_outer_out,
    second_outer_out,
):
    row_count = lax.axis_size("row")
    head_count = lax.axis_size("head")
    head_index = lax.axis_index("head")
    devices = row_count * head_count
    rows_here, residues, width = alignment.shape
    pair_rows, pair_cols, pair_width = pairs.shape
    size = width // HEADS
    outer_width = outer_in.shape[2]
    all_rows = rows_here * row_count
    own = rows_here // head_count
    start = head_index * own
    scales = norm_scales[:, : 2 * width].reshape(2, 2, width).swapaxes(0, 1).reshape(4, width)
    pair_gain = norm_scales[0:1, 2 * width :]
    pair_shift = norm_scales[1:2, 2 * width :]
    residue_live = residue_mask.astype(F32)
    key_mask = ((residue_live - 1.0) * (1e9 * LOG2E))[:, None]
    live = lax.dynamic_slice_in_dim(row_mask, start, own, 0).astype(F32)[:, None] * residue_live[None]
    bias_low = bias_weight.astype(BF16)

    fast = (row_count, head_count, pair_cols, own * outer_width) == (8, 4, 128, 128)

    local = heads_in.shape[2]
    shard = jnp.concatenate([heads_in.astype(BF16).swapaxes(1, 2), heads_out.astype(BF16)[None]])
    outer_t = outer_in.astype(BF16).swapaxes(1, 2).reshape(2 * outer_width, width)
    table = outer_out.astype(BF16).reshape(outer_width, outer_width, pair_width)
    if fast:
        bias, weights = pair_bias(pairs, norm_scales[:, 2 * width :], bias_low.T, shard)
    else:
        weights = lax.all_gather(shard, "head", axis=1, tiled=True)
        bias = pair_forward(pairs, pair_gain, pair_shift, bias_low)
        bias = lax.all_gather(bias, "head", axis=2, tiled=True)
        bias = lax.all_gather(bias, "row", axis=1, tiled=True)[None, None]
    in_t = weights[:4].reshape(4 * width, width)
    out_low = weights[4]

    rows = lax.dynamic_slice_in_dim(alignment, start, own, 0)
    rows_back = lax.dynamic_slice_in_dim(alignment_back, start, own, 0)
    update, sides, kept = attention_forward(
        rows, scales, in_t, out_low, outer_t, bias, key_mask, live[:, None]
    )
    update_all = lax.all_gather(update, "head", axis=0, tiled=True)
    alignment_new = alignment + update_all.astype(F32)

    left, right = sides[:, :outer_width], sides[:, outer_width:]
    if fast:
        left_all, right_all = share_sides(
            left.reshape(own * outer_width, residues).T.reshape(row_count, pair_rows, own * outer_width),
            right.reshape(own * outer_width, head_count, pair_cols).swapaxes(0, 1),
        )
        left_all = left_all.reshape(devices, pair_rows, own, outer_width).transpose(1, 3, 0, 2)
        pairs_new, left_grad, right_grad, table_grad = outer_product(
            left_all.reshape(pair_rows * outer_width, all_rows),
            right_all.reshape(all_rows, outer_width * pair_cols),
            pairs,
            pairs_back,
            table.swapaxes(0, 1).reshape(outer_width * outer_width, pair_width),
            all_rows,
        )
        left_grad = left_grad.reshape(pair_rows, outer_width, devices, own).transpose(2, 0, 3, 1)
        left_total, right_total = return_sides(
            left_grad.reshape(row_count, head_count, pair_rows, own * outer_width),
            right_grad.astype(BF16).reshape(row_count, head_count, own * outer_width, pair_cols),
        )
        left_total = left_total.reshape(residues, own * outer_width).T
        right_total = right_total.swapaxes(0, 1)
        table_grad = table_grad.reshape(outer_width, outer_width, pair_width).swapaxes(0, 1)
    else:
        left = left.reshape(own, outer_width, row_count, pair_rows).transpose(2, 0, 1, 3)
        right = right.reshape(own, outer_width, head_count, pair_cols).transpose(2, 0, 1, 3)
        both = (row_count, head_count, own, outer_width)
        send = jnp.concatenate(
            [
                jnp.broadcast_to(left[:, None], both + (pair_rows,)),
                jnp.broadcast_to(right[None], both + (pair_cols,)),
            ],
            axis=4,
        )
        flat = (devices, own, outer_width, pair_rows + pair_cols)
        got = lax.all_to_all(send.reshape(flat), EVERY, split_axis=0, concat_axis=0, tiled=True)
        got = got.reshape(all_rows, outer_width, pair_rows + pair_cols)
        total, table_grad, left_grad, right_grad = outer_product_plain(
            got[:, :, :pair_rows], got[:, :, pair_rows:], pairs_back, table, all_rows
        )
        pairs_new = pairs + total
        send = jnp.concatenate([left_grad, right_grad], axis=2).reshape(flat)
        got = lax.all_to_all(send, EVERY, split_axis=0, concat_axis=0, tiled=True)
        got = got.reshape(both + (pair_rows + pair_cols,)).astype(F32)
        left_total = jnp.sum(got[..., :pair_rows], axis=1).transpose(1, 2, 0, 3)
        right_total = jnp.sum(got[..., pair_rows:], axis=0).transpose(1, 2, 0, 3)
    sides_grad = jnp.concatenate(
        [
            left_total.reshape(own, outer_width, residues),
            right_total.reshape(own, outer_width, residues),
        ],
        axis=1,
    )
    sides_grad = (sides_grad * live[:, None, :]).astype(BF16)

    part, bias_grad, heads_in_grad, heads_out_grad, outer_in_grad, norms = attention_backward(
        rows, update, rows_back, scales, in_t, out_low, outer_t, sides_grad, kept, bias.shape
    )
    part_all = lax.all_gather(part, "head", axis=0, tiled=True)
    alignment_grad = alignment_back + part_all.astype(F32)

    if fast:
        bias_grad = bias_sum(bias_grad).astype(BF16)
    else:
        bias_grad = lax.psum_scatter(bias_grad[0, 0], "row", scatter_dimension=1, tiled=True)
        bias_grad = lax.psum_scatter(bias_grad, "head", scatter_dimension=2, tiled=True)
    pairs_grad, bias_weight_grad, pair_gain_grad, pair_shift_grad = pair_backward(
        pairs, pairs_back, pair_gain, pair_shift, bias_low, bias_grad
    )

    sums = (
        heads_in_grad,
        heads_out_grad,
        outer_in_grad,
        table_grad,
        norms,
        bias_weight_grad,
        jnp.stack([pair_gain_grad, pair_shift_grad]),
    )
    if fast:
        sizes = [part.size for part in sums]
        rest = -sum(sizes) % (512 * 128)
        packed = jnp.concatenate(
            [part.astype(BF16).reshape(-1, 128) for part in sums] + [jnp.zeros((rest // 128, 128), BF16)]
        )
        packed = weight_sum(packed).astype(F32)
        summed, first = [], 0
        for part in sums:
            lines = part.size // 128
            summed.append(packed[first : first + lines].reshape(part.shape))
            first += lines
        sums = summed
    else:
        sums = lax.psum(sums, EVERY)
    heads_in_total = lax.dynamic_slice_in_dim(
        sums[0].reshape(4, width, width), head_index * local, local, 1
    ).swapaxes(1, 2)
    heads_out_total = lax.dynamic_slice_in_dim(sums[1], head_index * local, local, 0)
    outer_in_total = sums[2].reshape(2, outer_width, width).swapaxes(1, 2)
    table_total = sums[3].reshape(outer_width * outer_width, pair_width)
    norms_total = jnp.concatenate(
        [sums[4].reshape(2, 2, width).swapaxes(0, 1).reshape(2, 2 * width), sums[6]], axis=1
    )
    norms_new = adam_update(norm_scales, norms_total, first_norms, second_norms, 0.5)
    heads_in_upd = adam_update(
        heads_in, heads_in_total, first_heads_in, second_heads_in, width ** (-0.5)
    )
    heads_out_upd = adam_update(
        heads_out,
        heads_out_total,
        first_heads_out,
        second_heads_out,
        max(2 * HEADS * size // residues, 1) ** (-0.5),
    )
    bias_upd = adam_update(
        bias_weight, sums[5], first_bias_weight, second_bias_weight, pair_width ** (-0.5)
    )
    outer_in_upd = adam_update(
        outer_in, outer_in_total, first_outer_in, second_outer_in, width ** (-0.5)
    )
    outer_out_upd = adam_update(
        outer_out,
        table_total,
        first_outer_out,
        second_outer_out,
        max(outer_width * outer_width // all_rows, 1) ** (-0.5),
    )
    return (
        alignment_new,
        pairs_new,
        alignment_grad,
        pairs_grad,
        *norms_new,
        *heads_in_upd,
        *heads_out_upd,
        *bias_upd,
        *outer_in_upd,
        *outer_out_upd,
    )


def solution(mesh):
    row_msa = P("row", None, None)
    pair = P("row", "head", None)
    columns = P(None, None, "head")
    lines = P("head", None)
    in_specs = (
        (row_msa, pair, P(), P("row"), row_msa, pair, P(), columns, lines)
        + (P(),) * 5
        + (columns,) * 2
        + (lines,) * 2
        + (P(),) * 6
    )
    out_specs = (row_msa, pair, row_msa, pair) + (P(),) * 3 + (columns,) * 3 + (lines,) * 3 + (P(),) * 9
    return jax.shard_map(
        per_device, mesh=mesh, in_specs=in_specs, out_specs=out_specs, check_vma=False
    )
```

```python
import functools

import jax
import jax.numpy as jnp
from jax import lax
from jax.experimental import pallas as pl
from jax.experimental.pallas import tpu as pltpu
from jax.sharding import PartitionSpec as P

HEADS = 8
STEP = 10
F32 = jnp.float32
BF16 = jnp.bfloat16
LOG2E = 1.4426950408889634
EVERY = ("row", "head")


def adam_update(weight, gradient, moment_one, moment_two, step_rate):
    first_new = 0.9 * moment_one + 0.1 * gradient
    second_new = 0.999 * moment_two + 0.001 * gradient * gradient
    first_hat = first_new / (1.0 - 0.9**STEP)
    second_hat = second_new / (1.0 - 0.999**STEP)
    updated = weight - step_rate * (first_hat / (jnp.sqrt(second_hat) + 1e-08) + 0.01 * weight)
    return (first_new, second_new, updated)


def cost(micros):
    return pl.CostEstimate(flops=0, bytes_accessed=int(micros * 3.5e6), transcendentals=0)


def dot(a, b, along):
    return lax.dot_general(a, b, (((along[0],), (along[1],)), ((), ())), preferred_element_type=F32)


def normalize(values):
    center = values - jnp.mean(values, axis=-1, keepdims=True)
    rstd = lax.rsqrt(jnp.mean(center * center, axis=-1, keepdims=True) + 1e-05)
    return center * rstd, rstd


def norm_backward(hat, rstd, gain, grad):
    scaled = grad * gain
    return rstd * (
        scaled
        - jnp.mean(scaled, axis=-1, keepdims=True)
        - hat * jnp.mean(scaled * hat, axis=-1, keepdims=True)
    )


def forward_kernel(
    rows, scales, in_t, out_low, outer_t, bias, key_mask, live,
    update, sides, qkv, gate, powers, inverse, mixed, attended,
    bias_t, *, chunk,
):
    row, head = pl.program_id(0), pl.program_id(1)
    width = rows.shape[2]
    residues = rows.shape[1]
    size = width // HEADS

    @pl.when(row == 0)
    def _():
        across, down, _, lines, cols = bias.shape
        group = max(1, 128 // lines)
        for r in range(0, across, group):
            for c in range(down):
                tile = jnp.concatenate([bias[r + g, c, 0] for g in range(group)], axis=0)
                bias_t[head, c * cols : (c + 1) * cols, r * lines : (r + group) * lines] = (
                    tile.astype(F32).T + key_mask[c * cols : (c + 1) * cols]
                )

    @pl.when(head == 0)
    def _():
        hat, _ = normalize(rows[0])
        normed = (hat * scales[0:1] + scales[1:2]).astype(BF16)
        qkv[0, :width] = (
            dot(in_t[:width], normed, (1, 1)) * (size**-0.5 * LOG2E)
        ).astype(BF16)
        qkv[0, width:] = dot(in_t[width : 3 * width], normed, (1, 1)).astype(BF16)
        gate[0] = jax.nn.sigmoid(dot(in_t[3 * width :], normed, (1, 1)))

    at = pl.multiple_of(head * size, size)
    keys = qkv[0, pl.ds(width + at, size), :]
    values = qkv[0, pl.ds(2 * width + at, size), :]
    for first in range(0, residues, chunk):
        span = slice(first, first + chunk)
        query = qkv[0, pl.ds(at, size), span]
        scores = dot(keys, query, (0, 0)) + bias_t[head, :, span]
        exps = jnp.exp2(scores - jnp.max(scores, axis=0, keepdims=True))
        over = 1.0 / jnp.sum(exps, axis=0, keepdims=True)
        low = exps.astype(BF16)
        powers[0, 0, :, span] = low
        inverse[0, 0, :, span] = over
        mixed[0, pl.ds(at, size), span] = dot(values, low, (1, 0)) * over

    @pl.when(head == HEADS - 1)
    def _():
        att = (gate[0] * mixed[0]).astype(BF16)
        attended[0] = att
        change = dot(att, out_low[...], (0, 0)).astype(BF16)
        update[0] = change
        hat, _ = normalize(rows[0] + change.astype(F32))
        second = (hat * scales[2:3] + scales[3:4]).astype(BF16)
        sides[0] = (dot(outer_t[...], second, (1, 1)) * live[0]).astype(BF16)


def attention_forward(rows, scales, in_t, out_low, outer_t, bias, key_mask, live, chunk=512):
    own, residues, width = rows.shape
    sides = outer_t.shape[0]
    by_row = lambda s, h: (s, 0, 0)
    whole = lambda s, h: (0, 0)
    last = lambda s, h: (0, 0, jnp.where(s == 0, h, HEADS - 1), 0, 0)
    out = pl.pallas_call(
        functools.partial(forward_kernel, chunk=chunk),
        grid=(own, HEADS),
        in_specs=[
            pl.BlockSpec((1, residues, width), by_row),
            pl.BlockSpec(scales.shape, whole),
            pl.BlockSpec(in_t.shape, whole),
            pl.BlockSpec(out_low.shape, whole),
            pl.BlockSpec(outer_t.shape, whole),
            pl.BlockSpec(bias.shape[:2] + (1,) + bias.shape[3:], last),
            pl.BlockSpec((residues, 1), whole),
            pl.BlockSpec((1, 1, residues), by_row),
        ],
        out_specs=[
            pl.BlockSpec((1, residues, width), by_row),
            pl.BlockSpec((1, sides, residues), by_row),
            pl.BlockSpec((1, 3 * width, residues), by_row),
            pl.BlockSpec((1, width, residues), by_row),
            pl.BlockSpec((1, 1, residues, residues), lambda s, h: (s, h, 0, 0)),
            pl.BlockSpec((1, 1, 1, residues), lambda s, h: (s, h, 0, 0)),
            pl.BlockSpec((1, width, residues), by_row),
            pl.BlockSpec((1, width, residues), by_row),
        ],
        out_shape=[
            jax.ShapeDtypeStruct((own, residues, width), BF16),
            jax.ShapeDtypeStruct((own, sides, residues), BF16),
            jax.ShapeDtypeStruct((own, 3 * width, residues), BF16),
            jax.ShapeDtypeStruct((own, width, residues), F32),
            jax.ShapeDtypeStruct((own, HEADS, residues, residues), BF16),
            jax.ShapeDtypeStruct((own, HEADS, 1, residues), F32),
            jax.ShapeDtypeStruct((own, width, residues), F32),
            jax.ShapeDtypeStruct((own, width, residues), BF16),
        ],
        scratch_shapes=[pltpu.VMEM((HEADS, residues, residues), F32)],
        cost_estimate=cost(36),
        compiler_params=pltpu.CompilerParams(vmem_limit_bytes=50 << 20),
    )(rows, scales, in_t, out_low, outer_t, bias, key_mask, live)
    return out[0], out[1], tuple(out[2:])


def backward_kernel(
    rows, update, back, scales, in_t, out_low, outer_t, sides_grad,
    qkv, gate, powers, inverse, mixed, attended,
    part, bias_grad, heads_in_grad, heads_out_grad, outer_in_grad, norms,
    bias_total, mixed_grad, delta, proj_grad, new_part, *, chunk,
):
    row, head = pl.program_id(0), pl.program_id(1)
    width = rows.shape[2]
    residues = rows.shape[1]
    size = width // HEADS
    last_row = row == pl.num_programs(0) - 1

    @pl.when((row == 0) & (head == 0))
    def _():
        heads_in_grad[...] = jnp.zeros_like(heads_in_grad)
        heads_out_grad[...] = jnp.zeros_like(heads_out_grad)
        outer_in_grad[...] = jnp.zeros_like(outer_in_grad)
        norms[...] = jnp.zeros_like(norms)
        bias_total[...] = jnp.zeros_like(bias_total)

    @pl.when(head == 0)
    def _():
        hat, rstd = normalize(rows[0] + update[0].astype(F32))
        second = (hat * scales[2:3] + scales[3:4]).astype(BF16)
        grads = sides_grad[0]
        outer_in_grad[...] += dot(grads, second, (1, 0))
        second_grad = dot(grads, outer_t[...], (0, 0))
        norms[2:3] += jnp.sum(second_grad * hat, axis=0, keepdims=True)
        norms[3:4] += jnp.sum(second_grad, axis=0, keepdims=True)
        new = norm_backward(hat, rstd, scales[2:3], second_grad)
        new_part[...] = new
        out_grad = (back[0] + new).astype(BF16)
        heads_out_grad[...] += dot(attended[0], out_grad, (1, 0))
        attended_grad = dot(out_low[...], out_grad, (1, 1))
        sig = gate[0]
        gated = attended_grad * sig
        proj_grad[3 * width :] = (gated * mixed[0] * (1.0 - sig)).astype(BF16)
        for h in range(HEADS):
            span = slice(h * size, (h + 1) * size)
            grad = gated[span] * inverse[0, h]
            mixed_grad[span] = grad.astype(BF16)
            delta[h] = jnp.sum(grad * mixed[0, span], axis=0, keepdims=True)

    at = pl.multiple_of(head * size, size)
    keys = qkv[0, pl.ds(width + at, size), :]
    values = qkv[0, pl.ds(2 * width + at, size), :]
    key_grad = jnp.zeros((size, residues), F32)
    value_grad = jnp.zeros((size, residues), F32)
    for first in range(0, residues, chunk):
        span = slice(first, first + chunk)
        grad = mixed_grad[pl.ds(at, size), span]
        query = qkv[0, pl.ds(at, size), span]
        low = powers[0, 0, :, span]
        prob_grad = dot(values, grad, (0, 0))
        score_grad = low.astype(F32) * (prob_grad - delta[head, :, span])
        bias_total[head, :, span] += score_grad
        score_low = score_grad.astype(BF16)
        value_grad += dot(grad, low, (1, 1))
        key_grad += dot(query, score_low, (1, 1))
        proj_grad[pl.ds(at, size), span] = (dot(keys, score_low, (1, 0)) * size**-0.5).astype(BF16)
    proj_grad[pl.ds(width + at, size), :] = (key_grad / LOG2E).astype(BF16)
    proj_grad[pl.ds(2 * width + at, size), :] = value_grad.astype(BF16)

    @pl.when(last_row)
    def _():
        across, down, _, lines, cols = bias_grad.shape
        group = max(1, 128 // lines)
        for r in range(0, across, group):
            for c in range(down):
                tile = bias_total[head, c * cols : (c + 1) * cols, r * lines : (r + group) * lines]
                tile = tile.T.astype(BF16)
                for g in range(group):
                    bias_grad[r + g, c, 0] = tile[g * lines : (g + 1) * lines]

    @pl.when(head == HEADS - 1)
    def _():
        hat, rstd = normalize(rows[0])
        normed = (hat * scales[0:1] + scales[1:2]).astype(BF16)
        grads = proj_grad[...]
        heads_in_grad[...] += dot(grads, normed, (1, 0))
        normed_grad = dot(grads, in_t[...], (0, 0))
        norms[0:1] += jnp.sum(normed_grad * hat, axis=0, keepdims=True)
        norms[1:2] += jnp.sum(normed_grad, axis=0, keepdims=True)
        part[0] = (new_part[...] + norm_backward(hat, rstd, scales[0:1], normed_grad)).astype(BF16)


def attention_backward(rows, update, back, scales, in_t, out_low, outer_t, sides_grad, kept, blocks, chunk=512):
    own, residues, width = rows.shape
    qkv, gate, powers, inverse, mixed, attended = kept
    sides = outer_t.shape[0]
    by_row = lambda s, h: (s, 0, 0)
    whole = lambda s, h: (0, 0)
    out = pl.pallas_call(
        functools.partial(backward_kernel, chunk=chunk),
        grid=(own, HEADS),
        in_specs=[
            pl.BlockSpec((1, residues, width), by_row),
            pl.BlockSpec((1, residues, width), by_row),
            pl.BlockSpec((1, residues, width), by_row),
            pl.BlockSpec(scales.shape, whole),
            pl.BlockSpec(in_t.shape, whole),
            pl.BlockSpec(out_low.shape, whole),
            pl.BlockSpec(outer_t.shape, whole),
            pl.BlockSpec((1, sides, residues), by_row),
            pl.BlockSpec((1, 3 * width, residues), by_row),
            pl.BlockSpec((1, width, residues), by_row),
            pl.BlockSpec((1, 1, residues, residues), lambda s, h: (s, h, 0, 0)),
            pl.BlockSpec((1, HEADS, 1, residues), lambda s, h: (s, 0, 0, 0)),
            pl.BlockSpec((1, width, residues), by_row),
            pl.BlockSpec((1, width, residues), by_row),
        ],
        out_specs=[
            pl.BlockSpec((1, residues, width), by_row),
            pl.BlockSpec(
                blocks[:2] + (1,) + blocks[3:], lambda s, h: (0, 0, jnp.where(s == own - 1, h, 0), 0, 0)
            ),
            pl.BlockSpec(in_t.shape, whole),
            pl.BlockSpec(out_low.shape, whole),
            pl.BlockSpec(outer_t.shape, whole),
            pl.BlockSpec((4, width), whole),
        ],
        out_shape=[
            jax.ShapeDtypeStruct((own, residues, width), BF16),
            jax.ShapeDtypeStruct(blocks, BF16),
            jax.ShapeDtypeStruct(in_t.shape, F32),
            jax.ShapeDtypeStruct(out_low.shape, F32),
            jax.ShapeDtypeStruct(outer_t.shape, F32),
            jax.ShapeDtypeStruct((4, width), F32),
        ],
        scratch_shapes=[
            pltpu.VMEM((HEADS, residues, residues), F32),
            pltpu.VMEM((width, residues), BF16),
            pltpu.VMEM((HEADS, 1, residues), F32),
            pltpu.VMEM((4 * width, residues), BF16),
            pltpu.VMEM((residues, width), F32),
        ],
        cost_estimate=cost(41),
        compiler_params=pltpu.CompilerParams(vmem_limit_bytes=50 << 20),
    )(rows, update, back, scales, in_t, out_low, outer_t, sides_grad, qkv, gate, powers, inverse, mixed, attended)
    return out


def outer_kernel(
    left, right, pairs, back, table, table_t,
    total, left_grad, right_grad, table_grad,
    product, backed, *, scale, group,
):
    step = pl.program_id(0)
    rows = pairs.shape[0]
    cols = pairs.shape[1]
    channels = pairs.shape[2]
    width = left.shape[0] // rows
    wide = right.shape[1] // cols

    @pl.when(step == 0)
    def _():
        right_grad[...] = jnp.zeros_like(right_grad)
        table_grad[...] = jnp.zeros_like(table_grad)

    product[...] = dot(left[...], right[...], (1, 0)).astype(BF16)
    for first in range(0, rows, group):
        low = back[first : first + group].astype(BF16).reshape(group * cols, channels)
        both = jnp.concatenate(
            [
                jnp.concatenate(
                    [
                        product[(first + g) * width : (first + g + 1) * width, f * cols : (f + 1) * cols]
                        for f in range(wide)
                    ],
                    axis=0,
                )
                for g in range(group)
            ],
            axis=1,
        )
        out = dot(table_t[...], both, (1, 0)) * scale
        for g in range(group):
            total[first + g] = pairs[first + g] + out[:, g * cols : (g + 1) * cols].T
        table_grad[...] += dot(both, low, (1, 0)) * scale
        spread = dot(table[...], low, (1, 1)).astype(BF16)
        for g in range(group):
            for f in range(wide):
                backed[(first + g) * width : (first + g + 1) * width, f * cols : (f + 1) * cols] = spread[
                    f * width : (f + 1) * width, g * cols : (g + 1) * cols
                ]
    left_grad[...] = (dot(backed[...], right[...], (1, 1)) * scale).astype(BF16)
    right_grad[...] += dot(left[...], backed[...], (0, 0)) * scale


def outer_product(left, right, pairs, back, table, all_rows, block=8, group=2):
    rows, cols, channels = pairs.shape
    width = left.shape[0] // rows
    table_t = table.T
    by_row = lambda n: (n, 0, 0)
    whole = lambda n: (0, 0)
    return pl.pallas_call(
        functools.partial(outer_kernel, scale=1.0 / all_rows, group=group),
        grid=(rows // block,),
        in_specs=[
            pl.BlockSpec((block * width, left.shape[1]), lambda n: (n, 0)),
            pl.BlockSpec(right.shape, whole),
            pl.BlockSpec((block, cols, channels), by_row),
            pl.BlockSpec((block, cols, channels), by_row),
            pl.BlockSpec(table.shape, whole),
            pl.BlockSpec(table_t.shape, whole),
        ],
        out_specs=[
            pl.BlockSpec((block, cols, channels), by_row),
            pl.BlockSpec((block * width, left.shape[1]), lambda n: (n, 0)),
            pl.BlockSpec(right.shape, whole),
            pl.BlockSpec(table.shape, whole),
        ],
        out_shape=[
            jax.ShapeDtypeStruct(pairs.shape, F32),
            jax.ShapeDtypeStruct(left.shape, BF16),
            jax.ShapeDtypeStruct(right.shape, F32),
            jax.ShapeDtypeStruct(table.shape, F32),
        ],
        scratch_shapes=[
            pltpu.VMEM((block * width, right.shape[1]), BF16),
            pltpu.VMEM((block * width, right.shape[1]), BF16),
        ],
        cost_estimate=cost(29),
        compiler_params=pltpu.CompilerParams(vmem_limit_bytes=50 << 20),
    )(left, right, pairs, back, table, table_t)


def outer_product_plain(left, right, pairs_back, table, all_rows):
    low = pairs_back.astype(BF16)
    product = mm("sei,sfj->eifj", left, right).astype(BF16)
    total = mm("eifj,efz->ijz", product, table) / all_rows
    table_grad = mm("eifj,ijz->efz", product, low) / all_rows
    back = mm("ijz,efz->eifj", low, table).astype(BF16)
    left_grad = mm("eifj,sfj->sei", back, right) / all_rows
    right_grad = mm("eifj,sei->sfj", back, left) / all_rows
    return total, table_grad, left_grad.astype(BF16), right_grad.astype(BF16)


def mm(spec, a, b):
    return jnp.einsum(spec, a, b, preferred_element_type=F32)


def pair_forward(pairs, gain, shift, bias_low):
    hat, _ = normalize(pairs)
    low = (hat * gain + shift).astype(BF16)
    return (mm("ijc,ch->hij", low, bias_low) * LOG2E).astype(BF16)


def pair_backward(pairs, pairs_back, gain, shift, bias_low, bias_grad):
    hat, rstd = normalize(pairs)
    low = (hat * gain + shift).astype(BF16)
    weight_grad = mm("ijc,hij->ch", low, bias_grad)
    in_grad = mm("hij,ch->ijc", bias_grad, bias_low)
    gain_grad = jnp.sum(in_grad * hat, axis=(0, 1))
    shift_grad = jnp.sum(in_grad, axis=(0, 1))
    return pairs_back + norm_backward(hat, rstd, gain, in_grad), weight_grad, gain_grad, shift_grad


MESH = pl.DeviceIdType.MESH
CORE, ACROSS, DOWN, CORNER = 1, 2, 4, 6


def place():
    return lax.axis_index("row"), lax.axis_index("head")


def flip(row, way):
    out = row
    for bit in (1, 2, 4):
        if way & bit:
            out = out + bit - 2 * bit * ((row // bit) % 2)
    return out


def greet(devices):
    barrier = pltpu.get_barrier_semaphore()
    for device in devices:
        pl.semaphore_signal(barrier, inc=1, device_id=device, device_id_type=MESH)
    pl.semaphore_wait(barrier, len(devices))


class Sends:
    def __init__(self, send_sem, recv_sem):
        self.send_sem, self.recv_sem, self.count, self.open = send_sem, recv_sem, 0, []

    def start(self, source, target, device):
        copy = pltpu.make_async_remote_copy(
            src_ref=source,
            dst_ref=target,
            send_sem=self.send_sem.at[self.count],
            recv_sem=self.recv_sem.at[self.count],
            device_id=device,
            device_id_type=MESH,
        )
        copy.start()
        self.count += 1
        self.open.append(copy)
        return copy

    def finish(self):
        for copy in self.open:
            copy.wait_send()


GATHER_SENDS = 6 + 3 + 31 + 3


def pair_bias_kernel(pairs, norm, weight, shard, bias, weights, block, low, local_sem, send_sem, recv_sem):
    row, head = place()
    rows, cols, channels = pairs.shape
    part = shard.shape[1] // 2
    core = row % 2
    beyond = [(head + k) % 4 for k in range(4)]
    behind = [(head + 4 - k) % 4 for k in range(4)]
    across, down, other = (flip(row, ACROSS), head), (flip(row, DOWN), head), (flip(row, CORE), head)
    greet([across, down, other] + [(row, beyond[k]) for k in (1, 2, 3)])
    sends = Sends(send_sem, recv_sem)

    def own_part(at, side):
        return weights.at[:, pl.ds(pl.multiple_of(at * 2 * part + side * part, part), part), :]

    half = shard.at[:, pl.ds(pl.multiple_of(core * part, part), part), :]
    keep = pltpu.make_async_copy(
        shard, weights.at[:, pl.ds(pl.multiple_of(head * 2 * part, 2 * part), 2 * part), :], local_sem.at[0]
    )
    keep.start()
    shards = [None] + [sends.start(half, own_part(head, core), (row, beyond[k])) for k in (1, 2, 3)]

    step = 8

    def norm_block(n, carry):
        first = pl.multiple_of(n * step, step)
        values = pairs[pl.ds(first, step)].reshape(step * cols, channels)
        center = values - jnp.mean(values, axis=-1, keepdims=True)
        rstd = lax.rsqrt(jnp.mean(center * center, axis=-1, keepdims=True) + 1e-05)
        normed = (center * rstd * norm[0:1] + norm[1:2]).astype(BF16)
        out = lax.dot_general(weight[...], normed, (((1,), (1,)), ((), ())), preferred_element_type=F32)
        for i in range(step):
            block[:, pl.ds(first + i, 1), :] = (out[:, i * cols : (i + 1) * cols] * LOG2E).reshape(
                HEADS, 1, cols
            )
        return carry

    lax.fori_loop(0, rows // step, norm_block, 0)
    low[...] = block[...].astype(BF16)

    mine = pltpu.make_async_copy(low, bias.at[row, head], local_sem.at[1])
    mine.start()
    stage = [None] * 4
    stage[0] = low
    along = [None] + [sends.start(low, bias.at[row, head], (row, beyond[k])) for k in (1, 2, 3)]
    from_across, from_down, from_corner, from_core = [None] * 4, [None] * 4, [None] * 4, []

    def spread(k, source):
        here = bias.at[row, behind[k]]
        from_across[k] = sends.start(source, here, across)
        from_down[k] = sends.start(source, here, down)
        from_core.append(sends.start(source, here, other))

    def relay(k):
        from_across[k].wait_recv()
        block_across = bias.at[flip(row, ACROSS), behind[k]]
        if k < 2:
            from_corner[k] = sends.start(block_across, block_across, down)
        from_core.append(sends.start(block_across, block_across, other))
        from_down[k].wait_recv()
        block_down = bias.at[flip(row, DOWN), behind[k]]
        if k >= 2:
            from_corner[k] = sends.start(block_down, block_down, across)
        from_core.append(sends.start(block_down, block_down, other))

    spread(0, low)
    for k in (1, 2, 3):
        along[k].wait_recv()
        spread(k, bias.at[row, behind[k]])
        relay(k - 1)
    relay(3)
    for k in range(4):
        from_corner[k].wait_recv()
        block_corner = bias.at[flip(row, CORNER), behind[k]]
        from_core.append(sends.start(block_corner, block_corner, other))
    for k in (1, 2, 3):
        shards[k].wait_recv()
        piece = own_part(behind[k], core)
        from_core.append(sends.start(piece, piece, other))
    for copy in from_core:
        copy.wait_recv()
    sends.finish()
    keep.wait()
    mine.wait()


def pair_bias(pairs, norm, weight, shard):
    rows, cols, channels = pairs.shape
    vmem = pl.BlockSpec(memory_space=pltpu.VMEM)
    hbm = pl.BlockSpec(memory_space=pl.ANY)
    return pl.pallas_call(
        pair_bias_kernel,
        out_shape=[
            jax.ShapeDtypeStruct((8, 4, HEADS, rows, cols), BF16),
            jax.ShapeDtypeStruct((shard.shape[0], 4 * shard.shape[1], shard.shape[2]), BF16),
        ],
        in_specs=[vmem, vmem, vmem, hbm],
        out_specs=[hbm, hbm],
        scratch_shapes=[
            pltpu.VMEM((HEADS, rows, cols), F32),
            pltpu.VMEM((HEADS, rows, cols), BF16),
            pltpu.SemaphoreType.DMA((2,)),
            pltpu.SemaphoreType.DMA((GATHER_SENDS,)),
            pltpu.SemaphoreType.DMA((GATHER_SENDS,)),
        ],
        cost_estimate=cost(34),
        compiler_params=pltpu.CompilerParams(
            collective_id=0, has_side_effects=True, vmem_limit_bytes=32 << 20
        ),
    )(pairs, norm, weight, shard)


SIDES_SENDS = 6 + 28 + 16 + 12


def sides_kernel(left, right, left_all, right_all, left_on, right_on, local_sem, send_sem, recv_sem):
    row, head = place()
    beyond = [(head + k) % 4 for k in range(4)]
    behind = [(head + 4 - k) % 4 for k in range(4)]
    plane = [(flip(row, way), head) for way in range(8)]
    greet(plane[1:] + [(row, beyond[k]) for k in (1, 2, 3)])
    sends = Sends(send_sem, recv_sem)
    from_left, from_right = [None] * 4, [None] * 4
    for k in (1, 2, 3):
        from_right[k] = sends.start(right.at[beyond[k]], right_on.at[k], (row, beyond[k]))
        from_left[k] = sends.start(left, left_on.at[k], (row, beyond[k]))
    locals_ = []
    arrive, onward = [], []
    for k in range(4):
        if k:
            from_right[k].wait_recv()
        ours = right_on.at[k] if k else right.at[head]
        for way in (ACROSS, DOWN, CORNER):
            onward.append((way, k, sends.start(ours, right_all.at[row, behind[k]], plane[way])))
        arrive.append(sends.start(ours, right_all.at[row, behind[k]], plane[CORE]))
        copy = pltpu.make_async_copy(ours, right_all.at[row, behind[k]], local_sem.at[2 * k])
        copy.start()
        locals_.append(copy)
        if k:
            from_left[k].wait_recv()
        ours = left_on.at[k] if k else left
        for way in (2, 4, 6, 3, 5, 7, 1):
            arrive.append(sends.start(ours.at[plane[way][0]], left_all.at[row, behind[k]], plane[way]))
        copy = pltpu.make_async_copy(ours.at[row], left_all.at[row, behind[k]], local_sem.at[2 * k + 1])
        copy.start()
        locals_.append(copy)
    for way, k, copy in onward:
        copy.wait_recv()
        block = right_all.at[plane[way][0], behind[k]]
        arrive.append(sends.start(block, block, plane[CORE]))
    for copy in arrive:
        copy.wait_recv()
    sends.finish()
    for copy in locals_:
        copy.wait()


def share_sides(left, right):
    hbm = pl.BlockSpec(memory_space=pl.ANY)
    return pl.pallas_call(
        sides_kernel,
        out_shape=[
            jax.ShapeDtypeStruct((8, 4) + left.shape[1:], BF16),
            jax.ShapeDtypeStruct((8, 4) + right.shape[1:], BF16),
        ],
        in_specs=[hbm, hbm],
        out_specs=[hbm, hbm],
        scratch_shapes=[
            pltpu.VMEM((4,) + left.shape, BF16),
            pltpu.VMEM((4,) + right.shape[1:], BF16),
            pltpu.SemaphoreType.DMA((8,)),
            pltpu.SemaphoreType.DMA((SIDES_SENDS,)),
            pltpu.SemaphoreType.DMA((SIDES_SENDS,)),
        ],
        cost_estimate=cost(24),
        compiler_params=pltpu.CompilerParams(
            collective_id=1, has_side_effects=True, vmem_limit_bytes=32 << 20
        ),
    )(left, right)


RETURN_SENDS = 1 + 7 + 3 + 6


def return_kernel(
    left, right, left_out, right_out, right_core, left_in, right_in, left_on, right_sum, local_sem, send_sem, recv_sem
):
    row, head = place()
    beyond = [(head + k) % 4 for k in range(4)]
    behind = [(head + 4 - k) % 4 for k in range(4)]
    plane = [(flip(row, way), head) for way in range(8)]
    greet(plane[1:] + [(row, beyond[k]) for k in (1, 2, 3)])
    sends = Sends(send_sem, recv_sem)
    core = row % 2
    swap = sends.start(right.at[:, 1 - core], right_core, plane[CORE])
    lefts = [sends.start(left.at[plane[way][0]], left_in.at[row], plane[way]) for way in (2, 4, 6, 3, 5, 7, 1)]
    copy = pltpu.make_async_copy(left.at[row], left_in.at[row], local_sem.at[0])
    copy.start()
    swap.wait_recv()
    chip = row // 2
    blocks = right.shape[2]
    for n in range(right.shape[0]):
        for b in range(blocks):
            right_sum[n, b] = (
                right[n, core, b].astype(F32) + right_core[n, b].astype(F32)
            ).astype(BF16)
    rights = []
    for slot, way in enumerate((ACROSS, DOWN, CORNER)):
        rights.append(sends.start(right_sum.at[plane[way][0] // 2], right_in.at[slot], plane[way]))
    for arrival in lefts:
        arrival.wait_recv()
    copy.wait()
    on = []
    for k in (1, 2, 3):
        on.append(sends.start(left_in.at[:, beyond[k]], left_on.at[k - 1], (row, beyond[k])))
    for arrival in rights:
        arrival.wait_recv()
    for b in range(blocks):
        total = right_sum[chip, b].astype(F32)
        for slot in range(3):
            total = total + right_in[slot, b].astype(F32)
        right_core[0, b] = total.astype(BF16)
    last = []
    for k in (1, 2, 3):
        last.append(sends.start(right_core.at[0, beyond[k]], right_out.at[head], (row, beyond[k])))
    mine = pltpu.make_async_copy(right_core.at[0, head], right_out.at[head], local_sem.at[1])
    mine.start()
    for arrival in on:
        arrival.wait_recv()
    for n in range(left_in.shape[0]):
        total = left_in[n, head].astype(F32)
        for k in range(3):
            total = total + left_on[k, n].astype(F32)
        left_out[n] = total.astype(BF16)
    for arrival in last:
        arrival.wait_recv()
    mine.wait()
    sends.finish()


def return_sides(left, right):
    vmem = pl.BlockSpec(memory_space=pltpu.VMEM)
    piece_left, piece_right = left.shape[2:], right.shape[2:]
    return pl.pallas_call(
        return_kernel,
        out_shape=[
            jax.ShapeDtypeStruct((8,) + piece_left, BF16),
            jax.ShapeDtypeStruct((4,) + piece_right, BF16),
        ],
        in_specs=[vmem, vmem],
        out_specs=[vmem, vmem],
        scratch_shapes=[
            pltpu.VMEM((4, 4) + piece_right, BF16),
            pltpu.VMEM((8, 4) + piece_left, BF16),
            pltpu.VMEM((3, 4) + piece_right, BF16),
            pltpu.VMEM((3, 8) + piece_left, BF16),
            pltpu.VMEM((4, 4) + piece_right, BF16),
            pltpu.SemaphoreType.DMA((2,)),
            pltpu.SemaphoreType.DMA((RETURN_SENDS,)),
            pltpu.SemaphoreType.DMA((RETURN_SENDS,)),
        ],
        cost_estimate=cost(27),
        compiler_params=pltpu.CompilerParams(
            collective_id=2, has_side_effects=True, vmem_limit_bytes=32 << 20
        ),
    )(left, right.reshape((4, 2) + right.shape[1:]))


SUM_SENDS = 4 + 12 + 3 + 1 + 3 + 3


def sum_kernel(
    grads, parts, out, piece,
    swapped, chip_sum, plane_in, down_sum, line_in,
    part_swapped, part_sum, part_plane, part_down, part_line,
    send_sem, recv_sem,
):
    row, head = place()
    beyond = [(head + k) % 4 for k in range(4)]
    core, chip = row % 2, row // 2
    ways = (CORNER, ACROSS, DOWN)
    plane = [(flip(row, way), head) for way in range(8)]
    other = plane[CORE]
    greet([plane[way] for way in (CORE,) + ways] + [(row, beyond[k]) for k in (1, 2, 3)])
    sends = Sends(send_sem, recv_sem)
    chips = [plane[way][0] // 2 for way in ways] + [chip]
    swaps = [sends.start(grads.at[n, 1 - core], swapped.at[slot], other) for slot, n in enumerate(chips)]
    part_swap = sends.start(parts.at[1 - core], part_swapped, other)
    order = (2, 1, 3, 0)
    arrive = [[None] * 3 for _ in range(4)]
    for slot, n in enumerate(chips):
        swaps[slot].wait_recv()
        for k in order:
            z = beyond[k]
            chip_sum[slot, z] = (grads[n, core, z].astype(F32) + swapped[slot, z].astype(F32)).astype(BF16)
            if slot < 3:
                arrive[k][slot] = sends.start(chip_sum.at[slot, z], plane_in.at[slot, k], plane[ways[slot]])
    part_swap.wait_recv()
    part_arrive = []
    for slot, n in enumerate(chips):
        for z in range(4):
            part_sum[slot, z] = (parts[core, n, z].astype(F32) + part_swapped[n, z].astype(F32)).astype(BF16)
        if slot < 3:
            part_arrive.append(sends.start(part_sum.at[slot], part_plane.at[slot], plane[ways[slot]]))
    line = []
    for k in order:
        for slot in range(3):
            arrive[k][slot].wait_recv()
        total = chip_sum[3, beyond[k]].astype(F32)
        for slot in range(3):
            total = total + plane_in[slot, k].astype(F32)
        if k:
            down_sum[k - 1] = total.astype(BF16)
            line.append(sends.start(down_sum.at[k - 1], line_in.at[k - 1], (row, beyond[k])))
        else:
            out[...] = total
    for copy in part_arrive:
        copy.wait_recv()
    for z in range(4):
        total = part_sum[3, z].astype(F32)
        for slot in range(3):
            total = total + part_plane[slot, z].astype(F32)
        part_down[z] = total.astype(BF16)
    part_arrive = [
        sends.start(part_down.at[beyond[k]], part_line.at[k - 1], (row, beyond[k])) for k in (1, 2, 3)
    ]
    for slot, copy in zip((1, 0, 2), line):
        copy.wait_recv()
        out[...] += line_in[slot].astype(F32)
    total = part_down[head].astype(F32)
    for slot, copy in enumerate(part_arrive):
        copy.wait_recv()
        total = total + part_line[slot].astype(F32)
    piece[...] = total.astype(BF16)
    sends.finish()


def sum_gradients(grads, parts):
    block = grads.shape[2:]
    lines = block[0] * block[1]
    rows, cols = parts.shape
    share = rows // 32
    vmem = pl.BlockSpec(memory_space=pltpu.VMEM)
    wide = lambda *first: pltpu.VMEM(first + (lines, block[2]), BF16)
    thin = lambda *first: pltpu.VMEM(first + (share, cols), BF16)
    out, piece = pl.pallas_call(
        sum_kernel,
        out_shape=[
            jax.ShapeDtypeStruct((lines, block[2]), F32),
            jax.ShapeDtypeStruct((share, cols), BF16),
        ],
        in_specs=[vmem, vmem],
        out_specs=[vmem, vmem],
        scratch_shapes=[
            wide(4, 4), wide(4, 4), wide(3, 4), wide(3), wide(3),
            thin(4, 4), thin(4, 4), thin(3, 4), thin(4), thin(3),
            pltpu.SemaphoreType.DMA((SUM_SENDS,)),
            pltpu.SemaphoreType.DMA((SUM_SENDS,)),
        ],
        compiler_params=pltpu.CompilerParams(
            collective_id=3, has_side_effects=True, vmem_limit_bytes=40 << 20
        ),
        cost_estimate=cost(40),
    )(grads.reshape(4, 2, 4, lines, block[2]), parts.reshape(2, 4, 4, share, cols))
    return out.reshape(block), piece


SPREAD_SENDS = 3 + 12 + 16 + 3 + 7


def spread_kernel(
    piece, small, out, total, line_in, line_sum, plane_in, local_sem, send_sem, recv_sem
):
    row, head = place()
    beyond = [(head + k) % 4 for k in range(4)]
    behind = [(head + 4 - k) % 4 for k in range(4)]
    core, chip = row % 2, row // 2
    ways = (CORNER, ACROSS, DOWN)
    plane = [(flip(row, way), head) for way in range(8)]
    other = plane[CORE]
    greet(plane[1:] + [(row, beyond[k]) for k in (1, 2, 3)])
    sends = Sends(send_sem, recv_sem)
    small_line = [sends.start(small, line_in.at[head], (row, beyond[k])) for k in (1, 2, 3)]
    line = [None] + [sends.start(piece, out.at[core, chip, head], (row, beyond[k])) for k in (1, 2, 3)]
    mine = pltpu.make_async_copy(piece, out.at[core, chip, head], local_sem)
    mine.start()
    line_in[head] = small[...]
    across, end = [], []

    def forward(k):
        here = out.at[core, chip, behind[k]]
        source = here if k else piece
        for way in ways:
            across.append((plane[way][0] // 2, k, sends.start(source, here, plane[way])))
        end.append(sends.start(source, here, other))

    forward(0)
    for copy in small_line:
        copy.wait_recv()
    line_sum[...] = (line_in[0] + line_in[1]) + (line_in[2] + line_in[3])
    small_plane = [sends.start(line_sum, plane_in.at[row], plane[way]) for way in range(1, 8)]
    plane_in[row] = line_sum[...]
    for k in (1, 2, 3):
        line[k].wait_recv()
        forward(k)
    for n, k, copy in across:
        copy.wait_recv()
        block = out.at[core, n, behind[k]]
        end.append(sends.start(block, block, other))
    for copy in small_plane:
        copy.wait_recv()
    summed = plane_in[0]
    for n in range(1, 8):
        summed = summed + plane_in[n]
    total[...] = summed
    for copy in end:
        copy.wait_recv()
    mine.wait()
    sends.finish()


def spread_gradients(piece, small):
    lines, cols = piece.shape
    vmem = pl.BlockSpec(memory_space=pltpu.VMEM)
    out, total = pl.pallas_call(
        spread_kernel,
        out_shape=[
            jax.ShapeDtypeStruct((2, 4, 4, lines, cols), BF16),
            jax.ShapeDtypeStruct(small.shape, F32),
        ],
        in_specs=[vmem, vmem],
        out_specs=[vmem, vmem],
        scratch_shapes=[
            pltpu.VMEM((4,) + small.shape, F32),
            pltpu.VMEM(small.shape, F32),
            pltpu.VMEM((8,) + small.shape, F32),
            pltpu.SemaphoreType.DMA,
            pltpu.SemaphoreType.DMA((SPREAD_SENDS,)),
            pltpu.SemaphoreType.DMA((SPREAD_SENDS,)),
        ],
        compiler_params=pltpu.CompilerParams(
            collective_id=4, has_side_effects=True, vmem_limit_bytes=32 << 20
        ),
        cost_estimate=cost(15),
    )(piece, small)
    return out.reshape(32 * lines, cols), total


def pair_backward_kernel(pairs, back, grads, norm, weight, out, small):
    step = pl.program_id(0)
    rows, cols, channels = pairs.shape

    @pl.when(step == 0)
    def _():
        small[...] = jnp.zeros_like(small)

    values = pairs[...].reshape(rows * cols, channels)
    hat, rstd = normalize(values)
    low = (hat * norm[0:1] + norm[1:2]).astype(BF16)
    bias = jnp.concatenate([grads[:, i, :] for i in range(rows)], axis=1).astype(BF16)
    small[0:HEADS] += dot(bias, low, (1, 0))
    in_grad = dot(bias, weight[...], (0, 0))
    small[HEADS : HEADS + 1] += jnp.sum(in_grad * hat, axis=0, keepdims=True)
    small[HEADS + 1 : HEADS + 2] += jnp.sum(in_grad, axis=0, keepdims=True)
    change = norm_backward(hat, rstd, norm[0:1], in_grad)
    out[...] = back[...] + change.reshape(rows, cols, channels)


def pair_norm_backward(pairs, back, grads, norm, weight, block=8):
    rows, cols, channels = pairs.shape
    by_row = lambda n: (n, 0, 0)
    return pl.pallas_call(
        pair_backward_kernel,
        grid=(rows // block,),
        in_specs=[
            pl.BlockSpec((block, cols, channels), by_row),
            pl.BlockSpec((block, cols, channels), by_row),
            pl.BlockSpec((HEADS, block, cols), lambda n: (0, n, 0)),
            pl.BlockSpec(norm.shape, lambda n: (0, 0)),
            pl.BlockSpec(weight.shape, lambda n: (0, 0)),
        ],
        out_specs=[
            pl.BlockSpec((block, cols, channels), by_row),
            pl.BlockSpec((2 * HEADS, channels), lambda n: (0, 0)),
        ],
        out_shape=[
            jax.ShapeDtypeStruct(pairs.shape, F32),
            jax.ShapeDtypeStruct((2 * HEADS, channels), F32),
        ],
        compiler_params=pltpu.CompilerParams(vmem_limit_bytes=40 << 20),
        cost_estimate=cost(6),
    )(pairs, back, grads, norm, weight)


def add_kernel(place_ref, base, piece, *refs):
    refs[-1][...] = base[...] + piece[...].astype(F32)


def add_rows(at, base, piece, into=None):
    own = piece.shape[0]
    block = (1,) + piece.shape[1:]
    spread = lambda n, at: (at[0] * own + n, 0, 0)
    return pl.pallas_call(
        add_kernel,
        grid_spec=pltpu.PrefetchScalarGridSpec(
            num_scalar_prefetch=1,
            grid=(own,),
            in_specs=[pl.BlockSpec(block, spread), pl.BlockSpec(block, lambda n, at: (n, 0, 0))]
            + ([] if into is None else [pl.BlockSpec(memory_space=pl.ANY)]),
            out_specs=pl.BlockSpec(block, spread),
        ),
        out_shape=jax.ShapeDtypeStruct(base.shape, F32),
        input_output_aliases={} if into is None else {3: 0},
        cost_estimate=cost(2),
    )(*((at, base, piece) if into is None else (at, base, piece, into)))


def hop(piece):
    count = lax.axis_size("head")
    return lax.ppermute(piece, "head", [(i, (i + 1) % count) for i in range(count)])


def together(moved, *values):
    return lax.optimization_barrier((moved,) + values)


def add_all(base, pieces):
    count = len(pieces)
    head = lax.axis_index("head")
    out = None
    for step, piece in enumerate(pieces):
        out = add_rows(((head + count - step) % count).astype(jnp.int32)[None], base, piece, out)
    return out


def per_device(
    alignment,
    pairs,
    residue_mask,
    row_mask,
    alignment_back,
    pairs_back,
    norm_scales,
    heads_in,
    heads_out,
    bias_weight,
    outer_in,
    outer_out,
    first_norms,
    second_norms,
    first_heads_in,
    second_heads_in,
    first_heads_out,
    second_heads_out,
    first_bias_weight,
    second_bias_weight,
    first_outer_in,
    second_outer_in,
    first_outer_out,
    second_outer_out,
):
    row_count = lax.axis_size("row")
    head_count = lax.axis_size("head")
    head_index = lax.axis_index("head")
    devices = row_count * head_count
    rows_here, residues, width = alignment.shape
    pair_rows, pair_cols, pair_width = pairs.shape
    size = width // HEADS
    outer_width = outer_in.shape[2]
    all_rows = rows_here * row_count
    own = rows_here // head_count
    start = head_index * own
    scales = norm_scales[:, : 2 * width].reshape(2, 2, width).swapaxes(0, 1).reshape(4, width)
    pair_gain = norm_scales[0:1, 2 * width :]
    pair_shift = norm_scales[1:2, 2 * width :]
    residue_live = residue_mask.astype(F32)
    key_mask = ((residue_live - 1.0) * (1e9 * LOG2E))[:, None]
    live = lax.dynamic_slice_in_dim(row_mask, start, own, 0).astype(F32)[:, None] * residue_live[None]
    bias_low = bias_weight.astype(BF16)

    fast = (row_count, head_count, pair_cols, own * outer_width) == (8, 4, 128, 128)

    local = heads_in.shape[2]
    shard = jnp.concatenate([heads_in.astype(BF16).swapaxes(1, 2), heads_out.astype(BF16)[None]])
    outer_t = outer_in.astype(BF16).swapaxes(1, 2).reshape(2 * outer_width, width)
    table = outer_out.astype(BF16).reshape(outer_width, outer_width, pair_width)
    if fast:
        bias, weights = pair_bias(pairs, norm_scales[:, 2 * width :], bias_low.T, shard)
    else:
        weights = lax.all_gather(shard, "head", axis=1, tiled=True)
        bias = pair_forward(pairs, pair_gain, pair_shift, bias_low)
        bias = lax.all_gather(bias, "head", axis=2, tiled=True)
        bias = lax.all_gather(bias, "row", axis=1, tiled=True)[None, None]
    in_t = weights[:4].reshape(4 * width, width)
    out_low = weights[4]

    rows = lax.dynamic_slice_in_dim(alignment, start, own, 0)
    rows_back = lax.dynamic_slice_in_dim(alignment_back, start, own, 0)
    update, sides, kept = attention_forward(
        rows, scales, in_t, out_low, outer_t, bias, key_mask, live[:, None]
    )
    left, right = sides[:, :outer_width], sides[:, outer_width:]
    if fast:
        left_all, right_all = share_sides(
            left.reshape(own * outer_width, residues).T.reshape(row_count, pair_rows, own * outer_width),
            right.reshape(own * outer_width, head_count, pair_cols).swapaxes(0, 1),
        )
        update, left_all, right_all = together(update, left_all, right_all)
        updates = [update, hop(update)]
        left_all = left_all.reshape(devices, pair_rows, own, outer_width).transpose(1, 3, 0, 2)
        pairs_new, left_grad, right_grad, table_grad = outer_product(
            left_all.reshape(pair_rows * outer_width, all_rows),
            right_all.reshape(all_rows, outer_width * pair_cols),
            pairs,
            pairs_back,
            table.swapaxes(0, 1).reshape(outer_width * outer_width, pair_width),
            all_rows,
        )
        left_grad = left_grad.reshape(pair_rows, outer_width, devices, own).transpose(2, 0, 3, 1)
        updates[1], left_grad, right_grad = together(updates[1], left_grad, right_grad)
        updates.append(hop(updates[1]))
        left_total, right_total = return_sides(
            left_grad.reshape(row_count, head_count, pair_rows, own * outer_width),
            right_grad.astype(BF16).reshape(row_count, head_count, own * outer_width, pair_cols),
        )
        updates[2], left_total, right_total = together(updates[2], left_total, right_total)
        updates.append(hop(updates[2]))
        left_total = left_total.reshape(residues, own * outer_width).T
        right_total = right_total.swapaxes(0, 1)
        table_grad = table_grad.reshape(outer_width, outer_width, pair_width).swapaxes(0, 1)
    else:
        updates = [update]
        for _ in range(head_count - 1):
            updates.append(hop(updates[-1]))
        left = left.reshape(own, outer_width, row_count, pair_rows).transpose(2, 0, 1, 3)
        right = right.reshape(own, outer_width, head_count, pair_cols).transpose(2, 0, 1, 3)
        both = (row_count, head_count, own, outer_width)
        send = jnp.concatenate(
            [
                jnp.broadcast_to(left[:, None], both + (pair_rows,)),
                jnp.broadcast_to(right[None], both + (pair_cols,)),
            ],
            axis=4,
        )
        flat = (devices, own, outer_width, pair_rows + pair_cols)
        got = lax.all_to_all(send.reshape(flat), EVERY, split_axis=0, concat_axis=0, tiled=True)
        got = got.reshape(all_rows, outer_width, pair_rows + pair_cols)
        total, table_grad, left_grad, right_grad = outer_product_plain(
            got[:, :, :pair_rows], got[:, :, pair_rows:], pairs_back, table, all_rows
        )
        pairs_new = pairs + total
        send = jnp.concatenate([left_grad, right_grad], axis=2).reshape(flat)
        got = lax.all_to_all(send, EVERY, split_axis=0, concat_axis=0, tiled=True)
        got = got.reshape(both + (pair_rows + pair_cols,)).astype(F32)
        left_total = jnp.sum(got[..., :pair_rows], axis=1).transpose(1, 2, 0, 3)
        right_total = jnp.sum(got[..., pair_rows:], axis=0).transpose(1, 2, 0, 3)
    sides_grad = jnp.concatenate(
        [
            left_total.reshape(own, outer_width, residues),
            right_total.reshape(own, outer_width, residues),
        ],
        axis=1,
    )
    sides_grad = (sides_grad * live[:, None, :]).astype(BF16)

    part, bias_grad, heads_in_grad, heads_out_grad, outer_in_grad, norms = attention_backward(
        rows, update, rows_back, scales, in_t, out_low, outer_t, sides_grad, kept, bias.shape
    )
    sums = (heads_in_grad, heads_out_grad, outer_in_grad, table_grad, norms)
    changes = [part]
    if fast:
        updates[3], bias_grad, changes[0] = together(updates[3], bias_grad, changes[0])
        changes.append(hop(changes[0]))
        sizes = [part.size for part in sums]
        rest = -sum(sizes) % (512 * 128)
        packed = jnp.concatenate(
            [part.astype(BF16).reshape(-1, 128) for part in sums] + [jnp.zeros((rest // 128, 128), BF16)]
        )
        bias_grad, packed = sum_gradients(bias_grad, packed)
        changes[1], bias_grad = together(changes[1], bias_grad)
        changes.append(hop(changes[1]))
        pairs_grad, pair_side = pair_norm_backward(
            pairs, pairs_back, bias_grad, norm_scales[:, 2 * width :], bias_low.T
        )
        packed, pair_side = spread_gradients(packed, pair_side)
        changes[2], packed = together(changes[2], packed)
        changes.append(hop(changes[2]))
        packed = packed.astype(F32)
        summed, first = [], 0
        for part in sums:
            lines = part.size // 128
            summed.append(packed[first : first + lines].reshape(part.shape))
            first += lines
        bias_weight_total = pair_side[:HEADS].T
        pair_norms_total = pair_side[HEADS : HEADS + 2]
        sums = summed
    else:
        for _ in range(head_count - 1):
            changes.append(hop(changes[-1]))
        bias_grad = lax.psum_scatter(bias_grad[0, 0], "row", scatter_dimension=1, tiled=True)
        bias_grad = lax.psum_scatter(bias_grad, "head", scatter_dimension=2, tiled=True)
        pairs_grad, bias_weight_grad, pair_gain_grad, pair_shift_grad = pair_backward(
            pairs, pairs_back, pair_gain, pair_shift, bias_low, bias_grad
        )
        sums, bias_weight_total, pair_norms_total = lax.psum(
            (sums, bias_weight_grad, jnp.stack([pair_gain_grad, pair_shift_grad])), EVERY
        )
    alignment_new = add_all(alignment, updates)
    alignment_grad = add_all(alignment_back, changes)
    heads_in_total = lax.dynamic_slice_in_dim(
        sums[0].reshape(4, width, width), head_index * local, local, 1
    ).swapaxes(1, 2)
    heads_out_total = lax.dynamic_slice_in_dim(sums[1], head_index * local, local, 0)
    outer_in_total = sums[2].reshape(2, outer_width, width).swapaxes(1, 2)
    table_total = sums[3].reshape(outer_width * outer_width, pair_width)
    norms_total = jnp.concatenate(
        [sums[4].reshape(2, 2, width).swapaxes(0, 1).reshape(2, 2 * width), pair_norms_total], axis=1
    )
    norms_new = adam_update(norm_scales, norms_total, first_norms, second_norms, 0.5)
    heads_in_upd = adam_update(
        heads_in, heads_in_total, first_heads_in, second_heads_in, width ** (-0.5)
    )
    heads_out_upd = adam_update(
        heads_out,
        heads_out_total,
        first_heads_out,
        second_heads_out,
        max(2 * HEADS * size // residues, 1) ** (-0.5),
    )
    bias_upd = adam_update(
        bias_weight, bias_weight_total, first_bias_weight, second_bias_weight, pair_width ** (-0.5)
    )
    outer_in_upd = adam_update(
        outer_in, outer_in_total, first_outer_in, second_outer_in, width ** (-0.5)
    )
    outer_out_upd = adam_update(
        outer_out,
        table_total,
        first_outer_out,
        second_outer_out,
        max(outer_width * outer_width // all_rows, 1) ** (-0.5),
    )
    return (
        alignment_new,
        pairs_new,
        alignment_grad,
        pairs_grad,
        *norms_new,
        *heads_in_upd,
        *heads_out_upd,
        *bias_upd,
        *outer_in_upd,
        *outer_out_upd,
    )


def solution(mesh):
    row_msa = P("row", None, None)
    pair = P("row", "head", None)
    columns = P(None, None, "head")
    lines = P("head", None)
    in_specs = (
        (row_msa, pair, P(), P("row"), row_msa, pair, P(), columns, lines)
        + (P(),) * 5
        + (columns,) * 2
        + (lines,) * 2
        + (P(),) * 6
    )
    out_specs = (row_msa, pair, row_msa, pair) + (P(),) * 3 + (columns,) * 3 + (lines,) * 3 + (P(),) * 9
    return jax.shard_map(
        per_device, mesh=mesh, in_specs=in_specs, out_specs=out_specs, check_vma=False
    )
```

```python
import functools

import jax
import jax.numpy as jnp
from jax import lax
from jax.experimental import pallas as pl
from jax.experimental.pallas import tpu as pltpu
from jax.sharding import PartitionSpec as P

HEADS = 8
STEP = 10
F32 = jnp.float32
BF16 = jnp.bfloat16
LOG2E = 1.4426950408889634
EVERY = ("row", "head")


def adam_update(weight, gradient, moment_one, moment_two, step_rate):
    first_new = 0.9 * moment_one + 0.1 * gradient
    second_new = 0.999 * moment_two + 0.001 * gradient * gradient
    first_hat = first_new / (1.0 - 0.9**STEP)
    second_hat = second_new / (1.0 - 0.999**STEP)
    updated = weight - step_rate * (first_hat / (jnp.sqrt(second_hat) + 1e-08) + 0.01 * weight)
    return (first_new, second_new, updated)


def cost(micros):
    return pl.CostEstimate(flops=0, bytes_accessed=int(micros * 3.5e6), transcendentals=0)


def dot(a, b, along):
    return lax.dot_general(a, b, (((along[0],), (along[1],)), ((), ())), preferred_element_type=F32)


def normalize(values):
    center = values - jnp.mean(values, axis=-1, keepdims=True)
    rstd = lax.rsqrt(jnp.mean(center * center, axis=-1, keepdims=True) + 1e-05)
    return center * rstd, rstd


def norm_backward(hat, rstd, gain, grad):
    scaled = grad * gain
    return rstd * (
        scaled
        - jnp.mean(scaled, axis=-1, keepdims=True)
        - hat * jnp.mean(scaled * hat, axis=-1, keepdims=True)
    )


def forward_kernel(
    at_ref, rows, scales, in_t, out_low, outer_t, bias, key_mask, live,
    update, sides, qkv, gate, powers, inverse, mixed, attended,
    bias_t, *, chunk,
):
    row, head = pl.program_id(0), pl.program_id(1)
    width = rows.shape[2]
    residues = rows.shape[1]
    size = width // HEADS

    @pl.when(row == 0)
    def _():
        across, down, _, lines, cols = bias.shape
        group = max(1, 128 // lines)
        for r in range(0, across, group):
            for c in range(down):
                tile = jnp.concatenate([bias[r + g, c, 0] for g in range(group)], axis=0)
                bias_t[head, c * cols : (c + 1) * cols, r * lines : (r + group) * lines] = (
                    tile.astype(F32).T + key_mask[c * cols : (c + 1) * cols]
                )

    @pl.when(head == 0)
    def _():
        hat, _ = normalize(rows[0])
        normed = (hat * scales[0:1] + scales[1:2]).astype(BF16)
        qkv[0, :width] = (
            dot(in_t[:width], normed, (1, 1)) * (size**-0.5 * LOG2E)
        ).astype(BF16)
        qkv[0, width:] = dot(in_t[width : 3 * width], normed, (1, 1)).astype(BF16)
        gate[0] = jax.nn.sigmoid(dot(in_t[3 * width :], normed, (1, 1)))

    at = pl.multiple_of(head * size, size)
    keys = qkv[0, pl.ds(width + at, size), :]
    values = qkv[0, pl.ds(2 * width + at, size), :]
    for first in range(0, residues, chunk):
        span = slice(first, first + chunk)
        query = qkv[0, pl.ds(at, size), span]
        scores = dot(keys, query, (0, 0)) + bias_t[head, :, span]
        exps = jnp.exp2(scores - jnp.max(scores, axis=0, keepdims=True))
        over = 1.0 / jnp.sum(exps, axis=0, keepdims=True)
        low = exps.astype(BF16)
        powers[0, 0, :, span] = low
        inverse[0, 0, :, span] = over
        mixed[0, pl.ds(at, size), span] = dot(values, low, (1, 0)) * over

    @pl.when(head == HEADS - 1)
    def _():
        att = (gate[0] * mixed[0]).astype(BF16)
        attended[0] = att
        change = dot(att, out_low[...], (0, 0)).astype(BF16)
        update[0] = change
        hat, _ = normalize(rows[0] + change.astype(F32))
        second = (hat * scales[2:3] + scales[3:4]).astype(BF16)
        sides[0] = (dot(outer_t[...], second, (1, 1)) * live[0]).astype(BF16)


def attention_forward(start, rows, scales, in_t, out_low, outer_t, bias, key_mask, live, chunk=512):
    _, residues, width = rows.shape
    own = live.shape[0]
    sides = outer_t.shape[0]
    by_row = lambda s, h, at: (s, 0, 0)
    whole = lambda s, h, at: (0, 0)
    last = lambda s, h, at: (0, 0, jnp.where(s == 0, h, HEADS - 1), 0, 0)
    out = pl.pallas_call(
        functools.partial(forward_kernel, chunk=chunk),
        grid_spec=pltpu.PrefetchScalarGridSpec(
        num_scalar_prefetch=1,
        grid=(own, HEADS),
        in_specs=[
            pl.BlockSpec((1, residues, width), lambda s, h, at: (at[0] + s, 0, 0)),
            pl.BlockSpec(scales.shape, whole),
            pl.BlockSpec(in_t.shape, whole),
            pl.BlockSpec(out_low.shape, whole),
            pl.BlockSpec(outer_t.shape, whole),
            pl.BlockSpec(bias.shape[:2] + (1,) + bias.shape[3:], last),
            pl.BlockSpec((residues, 1), whole),
            pl.BlockSpec((1, 1, residues), by_row),
        ],
        out_specs=[
            pl.BlockSpec((1, residues, width), by_row),
            pl.BlockSpec((1, sides, residues), by_row),
            pl.BlockSpec((1, 3 * width, residues), by_row),
            pl.BlockSpec((1, width, residues), by_row),
            pl.BlockSpec((1, 1, residues, residues), lambda s, h, at: (s, h, 0, 0)),
            pl.BlockSpec((1, 1, 1, residues), lambda s, h, at: (s, h, 0, 0)),
            pl.BlockSpec((1, width, residues), by_row),
            pl.BlockSpec((1, width, residues), by_row),
        ],
        scratch_shapes=[pltpu.VMEM((HEADS, residues, residues), F32)],
        ),
        out_shape=[
            jax.ShapeDtypeStruct((own, residues, width), BF16),
            jax.ShapeDtypeStruct((own, sides, residues), BF16),
            jax.ShapeDtypeStruct((own, 3 * width, residues), BF16),
            jax.ShapeDtypeStruct((own, width, residues), F32),
            jax.ShapeDtypeStruct((own, HEADS, residues, residues), BF16),
            jax.ShapeDtypeStruct((own, HEADS, 1, residues), F32),
            jax.ShapeDtypeStruct((own, width, residues), F32),
            jax.ShapeDtypeStruct((own, width, residues), BF16),
        ],
        cost_estimate=cost(36),
        compiler_params=pltpu.CompilerParams(vmem_limit_bytes=50 << 20),
    )(start, rows, scales, in_t, out_low, outer_t, bias, key_mask, live)
    return out[0], out[1], tuple(out[2:])


def backward_kernel(
    *refs, chunk, earlier, adds, per,
):
    (order, rows, update, back, scales, in_t, out_low, outer_t, sides_grad,
     qkv, gate, powers, inverse, mixed, attended), refs = refs[:15], refs[15:]
    if earlier:
        (so_far, base), pieces, refs = refs[:2], refs[2 : 2 + adds], refs[2 + adds :]
        added, refs = refs[0], refs[1:]
    (part, bias_grad, heads_in_grad, heads_out_grad, outer_in_grad, norms,
     bias_total, mixed_grad, delta, proj_grad, new_part) = refs
    row, head = pl.program_id(0), pl.program_id(1)
    width = rows.shape[2]
    residues = rows.shape[1]
    size = width // HEADS
    last_row = row == pl.num_programs(0) - 1

    if earlier:
        step = row * HEADS + head
        for n in range(adds):
            @pl.when(step // per == n)
            def _():
                added[...] = base[...] + pieces[n][...].astype(F32)

    @pl.when((row == 0) & (head == 0))
    def _():
        heads_in_grad[...] = jnp.zeros_like(heads_in_grad)
        heads_out_grad[...] = jnp.zeros_like(heads_out_grad)
        outer_in_grad[...] = jnp.zeros_like(outer_in_grad)
        norms[...] = jnp.zeros_like(norms)

    @pl.when(row == 0)
    def _():
        bias_total[head] = so_far[0] if earlier else jnp.zeros((residues, residues), F32)

    @pl.when(head == 0)
    def _():
        hat, rstd = normalize(rows[0] + update[0].astype(F32))
        second = (hat * scales[2:3] + scales[3:4]).astype(BF16)
        grads = sides_grad[0]
        outer_in_grad[...] += dot(grads, second, (1, 0))
        second_grad = dot(grads, outer_t[...], (0, 0))
        norms[2:3] += jnp.sum(second_grad * hat, axis=0, keepdims=True)
        norms[3:4] += jnp.sum(second_grad, axis=0, keepdims=True)
        new = norm_backward(hat, rstd, scales[2:3], second_grad)
        new_part[...] = new
        out_grad = (back[0] + new).astype(BF16)
        heads_out_grad[...] += dot(attended[0], out_grad, (1, 0))
        attended_grad = dot(out_low[...], out_grad, (1, 1))
        sig = gate[0]
        gated = attended_grad * sig
        proj_grad[3 * width :] = (gated * mixed[0] * (1.0 - sig)).astype(BF16)
        for h in range(HEADS):
            span = slice(h * size, (h + 1) * size)
            grad = gated[span] * inverse[0, h]
            mixed_grad[span] = grad.astype(BF16)
            delta[h] = jnp.sum(grad * mixed[0, span], axis=0, keepdims=True)

    at = pl.multiple_of(head * size, size)
    keys = qkv[0, pl.ds(width + at, size), :]
    values = qkv[0, pl.ds(2 * width + at, size), :]
    key_grad = jnp.zeros((size, residues), F32)
    value_grad = jnp.zeros((size, residues), F32)
    for first in range(0, residues, chunk):
        span = slice(first, first + chunk)
        grad = mixed_grad[pl.ds(at, size), span]
        query = qkv[0, pl.ds(at, size), span]
        low = powers[0, 0, :, span]
        prob_grad = dot(values, grad, (0, 0))
        score_grad = low.astype(F32) * (prob_grad - delta[head, :, span])
        bias_total[head, :, span] += score_grad
        score_low = score_grad.astype(BF16)
        value_grad += dot(grad, low, (1, 1))
        key_grad += dot(query, score_low, (1, 1))
        proj_grad[pl.ds(at, size), span] = (dot(keys, score_low, (1, 0)) * size**-0.5).astype(BF16)
    proj_grad[pl.ds(width + at, size), :] = (key_grad / LOG2E).astype(BF16)
    proj_grad[pl.ds(2 * width + at, size), :] = value_grad.astype(BF16)

    @pl.when(last_row)
    def _():
        if not earlier:
            bias_grad[0] = bias_total[head]
        else:
            across, down, _, lines, cols = bias_grad.shape
            group = max(1, 128 // lines)
            for r in range(0, across, group):
                for c in range(down):
                    tile = bias_total[head, c * cols : (c + 1) * cols, r * lines : (r + group) * lines]
                    tile = tile.T.astype(BF16)
                    for g in range(group):
                        bias_grad[r + g, c, 0] = tile[g * lines : (g + 1) * lines]

    @pl.when(head == HEADS - 1)
    def _():
        hat, rstd = normalize(rows[0])
        normed = (hat * scales[0:1] + scales[1:2]).astype(BF16)
        grads = proj_grad[...]
        heads_in_grad[...] += dot(grads, normed, (1, 0))
        normed_grad = dot(grads, in_t[...], (0, 0))
        norms[0:1] += jnp.sum(normed_grad * hat, axis=0, keepdims=True)
        norms[1:2] += jnp.sum(normed_grad, axis=0, keepdims=True)
        part[0] = (new_part[...] + norm_backward(hat, rstd, scales[0:1], normed_grad)).astype(BF16)


def attention_backward(
    order, rows, update, back, scales, in_t, out_low, outer_t, sides_grad, kept, blocks,
    first, own, earlier=None, pieces=(), chunk=512,
):
    _, residues, width = rows.shape
    qkv, gate, powers, inverse, mixed, attended = kept
    sides = outer_t.shape[0]
    here = lambda s, h, order: (order[0] + first + s, 0, 0)
    by_row = lambda s, h, order: (first + s, 0, 0)
    whole = lambda s, h, order: (0, 0)
    one = pl.BlockSpec((1, residues, width), here)
    args = [rows, update, back, scales, in_t, out_low, outer_t, sides_grad]
    args += [qkv, gate, powers, inverse, mixed, attended]
    in_specs = [
        one,
        pl.BlockSpec((1, residues, width), by_row),
        one,
        pl.BlockSpec(scales.shape, whole),
        pl.BlockSpec(in_t.shape, whole),
        pl.BlockSpec(out_low.shape, whole),
        pl.BlockSpec(outer_t.shape, whole),
        pl.BlockSpec((1, sides, residues), by_row),
        pl.BlockSpec((1, 3 * width, residues), by_row),
        pl.BlockSpec((1, width, residues), by_row),
        pl.BlockSpec((1, 1, residues, residues), lambda s, h, order: (first + s, h, 0, 0)),
        pl.BlockSpec((1, HEADS, 1, residues), lambda s, h, order: (first + s, 0, 0, 0)),
        pl.BlockSpec((1, width, residues), by_row),
        pl.BlockSpec((1, width, residues), by_row),
    ]
    out_specs = [
        pl.BlockSpec((1, residues, width), lambda s, h, order: (s, 0, 0)),
        pl.BlockSpec((1, residues, residues), lambda s, h, order: (jnp.where(s == own - 1, h, 0), 0, 0)),
        pl.BlockSpec(in_t.shape, whole),
        pl.BlockSpec(out_low.shape, whole),
        pl.BlockSpec(outer_t.shape, whole),
        pl.BlockSpec((4, width), whole),
    ]
    out_shape = [
        jax.ShapeDtypeStruct((own, residues, width), BF16),
        jax.ShapeDtypeStruct((HEADS, residues, residues), F32),
        jax.ShapeDtypeStruct(in_t.shape, F32),
        jax.ShapeDtypeStruct(out_low.shape, F32),
        jax.ShapeDtypeStruct(outer_t.shape, F32),
        jax.ShapeDtypeStruct((4, width), F32),
    ]
    per = 1
    if earlier is not None:
        each = rows.shape[0] // (own * HEADS)
        per = pieces[0].shape[0] // each
        lines = pl.BlockSpec(
            (each, residues, width), lambda s, h, order: (order[(s * HEADS + h) * each] // each, 0, 0)
        )

        def changes(n):
            return pl.BlockSpec(
                (each, residues, width),
                lambda s, h, order: (jnp.clip(s * HEADS + h - n * per, 0, per - 1), 0, 0),
            )

        args += [earlier, rows] + list(pieces)
        in_specs += [
            pl.BlockSpec(
                (1, residues, residues), lambda s, h, order: (jnp.where(s == 0, h, HEADS - 1), 0, 0)
            ),
            lines,
        ] + [changes(n) for n in range(len(pieces))]
        out_specs[1] = pl.BlockSpec(
            blocks[:2] + (1,) + blocks[3:],
            lambda s, h, order: (0, 0, jnp.where(s == own - 1, h, 0), 0, 0),
        )
        out_shape[1] = jax.ShapeDtypeStruct(blocks, BF16)
        out_specs = [lines] + out_specs
        out_shape = [jax.ShapeDtypeStruct(rows.shape, F32)] + out_shape
    return pl.pallas_call(
        functools.partial(
            backward_kernel, chunk=chunk, earlier=earlier is not None, adds=len(pieces), per=per
        ),
        grid_spec=pltpu.PrefetchScalarGridSpec(
            num_scalar_prefetch=1,
            grid=(own, HEADS),
            in_specs=in_specs,
            out_specs=out_specs,
            scratch_shapes=[
                pltpu.VMEM((HEADS, residues, residues), F32),
                pltpu.VMEM((width, residues), BF16),
                pltpu.VMEM((HEADS, 1, residues), F32),
                pltpu.VMEM((4 * width, residues), BF16),
                pltpu.VMEM((residues, width), F32),
            ],
        ),
        out_shape=out_shape,
        compiler_params=pltpu.CompilerParams(vmem_limit_bytes=50 << 20),
        cost_estimate=cost(22),
    )(order, *args)


def outer_kernel(
    left, right, pairs, back, table, table_t,
    total, left_grad, right_grad, table_grad,
    product, backed, *, scale, group,
):
    step = pl.program_id(0)
    rows = pairs.shape[0]
    cols = pairs.shape[1]
    channels = pairs.shape[2]
    width = left.shape[0] // rows
    wide = right.shape[1] // cols

    @pl.when(step == 0)
    def _():
        right_grad[...] = jnp.zeros_like(right_grad)
        table_grad[...] = jnp.zeros_like(table_grad)

    product[...] = dot(left[...], right[...], (1, 0)).astype(BF16)
    for first in range(0, rows, group):
        low = back[first : first + group].astype(BF16).reshape(group * cols, channels)
        both = jnp.concatenate(
            [
                jnp.concatenate(
                    [
                        product[(first + g) * width : (first + g + 1) * width, f * cols : (f + 1) * cols]
                        for f in range(wide)
                    ],
                    axis=0,
                )
                for g in range(group)
            ],
            axis=1,
        )
        out = dot(table_t[...], both, (1, 0)) * scale
        for g in range(group):
            total[first + g] = pairs[first + g] + out[:, g * cols : (g + 1) * cols].T
        table_grad[...] += dot(both, low, (1, 0)) * scale
        spread = dot(table[...], low, (1, 1)).astype(BF16)
        for g in range(group):
            for f in range(wide):
                backed[(first + g) * width : (first + g + 1) * width, f * cols : (f + 1) * cols] = spread[
                    f * width : (f + 1) * width, g * cols : (g + 1) * cols
                ]
    left_grad[...] = (dot(backed[...], right[...], (1, 1)) * scale).astype(BF16)
    right_grad[...] += dot(left[...], backed[...], (0, 0)) * scale


def outer_product(left, right, pairs, back, table, all_rows, block=8, group=2):
    rows, cols, channels = pairs.shape
    width = left.shape[0] // rows
    table_t = table.T
    by_row = lambda n: (n, 0, 0)
    whole = lambda n: (0, 0)
    return pl.pallas_call(
        functools.partial(outer_kernel, scale=1.0 / all_rows, group=group),
        grid=(rows // block,),
        in_specs=[
            pl.BlockSpec((block * width, left.shape[1]), lambda n: (n, 0)),
            pl.BlockSpec(right.shape, whole),
            pl.BlockSpec((block, cols, channels), by_row),
            pl.BlockSpec((block, cols, channels), by_row),
            pl.BlockSpec(table.shape, whole),
            pl.BlockSpec(table_t.shape, whole),
        ],
        out_specs=[
            pl.BlockSpec((block, cols, channels), by_row),
            pl.BlockSpec((block * width, left.shape[1]), lambda n: (n, 0)),
            pl.BlockSpec(right.shape, whole),
            pl.BlockSpec(table.shape, whole),
        ],
        out_shape=[
            jax.ShapeDtypeStruct(pairs.shape, F32),
            jax.ShapeDtypeStruct(left.shape, BF16),
            jax.ShapeDtypeStruct(right.shape, F32),
            jax.ShapeDtypeStruct(table.shape, F32),
        ],
        scratch_shapes=[
            pltpu.VMEM((block * width, right.shape[1]), BF16),
            pltpu.VMEM((block * width, right.shape[1]), BF16),
        ],
        cost_estimate=cost(29),
        compiler_params=pltpu.CompilerParams(vmem_limit_bytes=50 << 20),
    )(left, right, pairs, back, table, table_t)


def outer_product_plain(left, right, pairs_back, table, all_rows):
    low = pairs_back.astype(BF16)
    product = mm("sei,sfj->eifj", left, right).astype(BF16)
    total = mm("eifj,efz->ijz", product, table) / all_rows
    table_grad = mm("eifj,ijz->efz", product, low) / all_rows
    back = mm("ijz,efz->eifj", low, table).astype(BF16)
    left_grad = mm("eifj,sfj->sei", back, right) / all_rows
    right_grad = mm("eifj,sei->sfj", back, left) / all_rows
    return total, table_grad, left_grad.astype(BF16), right_grad.astype(BF16)


def mm(spec, a, b):
    return jnp.einsum(spec, a, b, preferred_element_type=F32)


def pair_forward(pairs, gain, shift, bias_low):
    hat, _ = normalize(pairs)
    low = (hat * gain + shift).astype(BF16)
    return (mm("ijc,ch->hij", low, bias_low) * LOG2E).astype(BF16)


def pair_backward(pairs, pairs_back, gain, shift, bias_low, bias_grad):
    hat, rstd = normalize(pairs)
    low = (hat * gain + shift).astype(BF16)
    weight_grad = mm("ijc,hij->ch", low, bias_grad)
    in_grad = mm("hij,ch->ijc", bias_grad, bias_low)
    gain_grad = jnp.sum(in_grad * hat, axis=(0, 1))
    shift_grad = jnp.sum(in_grad, axis=(0, 1))
    return pairs_back + norm_backward(hat, rstd, gain, in_grad), weight_grad, gain_grad, shift_grad


MESH = pl.DeviceIdType.MESH
CORE, ACROSS, DOWN, CORNER = 1, 2, 4, 6


def place():
    return lax.axis_index("row"), lax.axis_index("head")


def flip(row, way):
    out = row
    for bit in (1, 2, 4):
        if way & bit:
            out = out + bit - 2 * bit * ((row // bit) % 2)
    return out


def greet(devices):
    barrier = pltpu.get_barrier_semaphore()
    for device in devices:
        pl.semaphore_signal(barrier, inc=1, device_id=device, device_id_type=MESH)
    pl.semaphore_wait(barrier, len(devices))


class Sends:
    def __init__(self, send_sem, recv_sem):
        self.send_sem, self.recv_sem, self.count, self.open = send_sem, recv_sem, 0, []

    def start(self, source, target, device):
        copy = pltpu.make_async_remote_copy(
            src_ref=source,
            dst_ref=target,
            send_sem=self.send_sem.at[self.count],
            recv_sem=self.recv_sem.at[self.count],
            device_id=device,
            device_id_type=MESH,
        )
        copy.start()
        self.count += 1
        self.open.append(copy)
        return copy

    def finish(self):
        for copy in self.open:
            copy.wait_send()


GATHER_SENDS = 6 + 3 + 31 + 3


def pair_bias_kernel(pairs, norm, weight, shard, bias, weights, block, low, local_sem, send_sem, recv_sem):
    row, head = place()
    rows, cols, channels = pairs.shape
    part = shard.shape[1] // 2
    core = row % 2
    beyond = [(head + k) % 4 for k in range(4)]
    behind = [(head + 4 - k) % 4 for k in range(4)]
    across, down, other = (flip(row, ACROSS), head), (flip(row, DOWN), head), (flip(row, CORE), head)
    greet([across, down, other] + [(row, beyond[k]) for k in (1, 2, 3)])
    sends = Sends(send_sem, recv_sem)

    def own_part(at, side):
        return weights.at[:, pl.ds(pl.multiple_of(at * 2 * part + side * part, part), part), :]

    half = shard.at[:, pl.ds(pl.multiple_of(core * part, part), part), :]
    keep = pltpu.make_async_copy(
        shard, weights.at[:, pl.ds(pl.multiple_of(head * 2 * part, 2 * part), 2 * part), :], local_sem.at[0]
    )
    keep.start()
    shards = [None] + [sends.start(half, own_part(head, core), (row, beyond[k])) for k in (1, 2, 3)]

    step = 8

    def norm_block(n, carry):
        first = pl.multiple_of(n * step, step)
        values = pairs[pl.ds(first, step)].reshape(step * cols, channels)
        center = values - jnp.mean(values, axis=-1, keepdims=True)
        rstd = lax.rsqrt(jnp.mean(center * center, axis=-1, keepdims=True) + 1e-05)
        normed = (center * rstd * norm[0:1] + norm[1:2]).astype(BF16)
        out = lax.dot_general(weight[...], normed, (((1,), (1,)), ((), ())), preferred_element_type=F32)
        for i in range(step):
            block[:, pl.ds(first + i, 1), :] = (out[:, i * cols : (i + 1) * cols] * LOG2E).reshape(
                HEADS, 1, cols
            )
        return carry

    lax.fori_loop(0, rows // step, norm_block, 0)
    low[...] = block[...].astype(BF16)

    mine = pltpu.make_async_copy(low, bias.at[row, head], local_sem.at[1])
    mine.start()
    stage = [None] * 4
    stage[0] = low
    along = [None] + [sends.start(low, bias.at[row, head], (row, beyond[k])) for k in (1, 2, 3)]
    from_across, from_down, from_corner, from_core = [None] * 4, [None] * 4, [None] * 4, []

    def spread(k, source):
        here = bias.at[row, behind[k]]
        from_across[k] = sends.start(source, here, across)
        from_down[k] = sends.start(source, here, down)
        from_core.append(sends.start(source, here, other))

    def relay(k):
        from_across[k].wait_recv()
        block_across = bias.at[flip(row, ACROSS), behind[k]]
        if k < 2:
            from_corner[k] = sends.start(block_across, block_across, down)
        from_core.append(sends.start(block_across, block_across, other))
        from_down[k].wait_recv()
        block_down = bias.at[flip(row, DOWN), behind[k]]
        if k >= 2:
            from_corner[k] = sends.start(block_down, block_down, across)
        from_core.append(sends.start(block_down, block_down, other))

    spread(0, low)
    for k in (1, 2, 3):
        along[k].wait_recv()
        spread(k, bias.at[row, behind[k]])
        relay(k - 1)
    relay(3)
    for k in range(4):
        from_corner[k].wait_recv()
        block_corner = bias.at[flip(row, CORNER), behind[k]]
        from_core.append(sends.start(block_corner, block_corner, other))
    for k in (1, 2, 3):
        shards[k].wait_recv()
        piece = own_part(behind[k], core)
        from_core.append(sends.start(piece, piece, other))
    for copy in from_core:
        copy.wait_recv()
    sends.finish()
    keep.wait()
    mine.wait()


def pair_bias(pairs, norm, weight, shard):
    rows, cols, channels = pairs.shape
    vmem = pl.BlockSpec(memory_space=pltpu.VMEM)
    hbm = pl.BlockSpec(memory_space=pl.ANY)
    return pl.pallas_call(
        pair_bias_kernel,
        out_shape=[
            jax.ShapeDtypeStruct((8, 4, HEADS, rows, cols), BF16),
            jax.ShapeDtypeStruct((shard.shape[0], 4 * shard.shape[1], shard.shape[2]), BF16),
        ],
        in_specs=[vmem, vmem, vmem, hbm],
        out_specs=[hbm, hbm],
        scratch_shapes=[
            pltpu.VMEM((HEADS, rows, cols), F32),
            pltpu.VMEM((HEADS, rows, cols), BF16),
            pltpu.SemaphoreType.DMA((2,)),
            pltpu.SemaphoreType.DMA((GATHER_SENDS,)),
            pltpu.SemaphoreType.DMA((GATHER_SENDS,)),
        ],
        cost_estimate=cost(34),
        compiler_params=pltpu.CompilerParams(
            collective_id=0, has_side_effects=True, vmem_limit_bytes=32 << 20
        ),
    )(pairs, norm, weight, shard)


SIDES_SENDS = 6 + 28 + 16 + 12


def sides_kernel(left, right, left_all, right_all, left_on, right_on, local_sem, send_sem, recv_sem):
    row, head = place()
    beyond = [(head + k) % 4 for k in range(4)]
    behind = [(head + 4 - k) % 4 for k in range(4)]
    plane = [(flip(row, way), head) for way in range(8)]
    greet(plane[1:] + [(row, beyond[k]) for k in (1, 2, 3)])
    sends = Sends(send_sem, recv_sem)
    from_left, from_right = [None] * 4, [None] * 4
    for k in (1, 2, 3):
        from_right[k] = sends.start(right.at[beyond[k]], right_on.at[k], (row, beyond[k]))
        from_left[k] = sends.start(left, left_on.at[k], (row, beyond[k]))
    locals_ = []
    arrive, onward = [], []
    for k in range(4):
        if k:
            from_right[k].wait_recv()
        ours = right_on.at[k] if k else right.at[head]
        for way in (ACROSS, DOWN, CORNER):
            onward.append((way, k, sends.start(ours, right_all.at[row, behind[k]], plane[way])))
        arrive.append(sends.start(ours, right_all.at[row, behind[k]], plane[CORE]))
        copy = pltpu.make_async_copy(ours, right_all.at[row, behind[k]], local_sem.at[2 * k])
        copy.start()
        locals_.append(copy)
        if k:
            from_left[k].wait_recv()
        ours = left_on.at[k] if k else left
        for way in (2, 4, 6, 3, 5, 7, 1):
            arrive.append(sends.start(ours.at[plane[way][0]], left_all.at[row, behind[k]], plane[way]))
        copy = pltpu.make_async_copy(ours.at[row], left_all.at[row, behind[k]], local_sem.at[2 * k + 1])
        copy.start()
        locals_.append(copy)
    for way, k, copy in onward:
        copy.wait_recv()
        block = right_all.at[plane[way][0], behind[k]]
        arrive.append(sends.start(block, block, plane[CORE]))
    for copy in arrive:
        copy.wait_recv()
    sends.finish()
    for copy in locals_:
        copy.wait()


def share_sides(left, right):
    hbm = pl.BlockSpec(memory_space=pl.ANY)
    return pl.pallas_call(
        sides_kernel,
        out_shape=[
            jax.ShapeDtypeStruct((8, 4) + left.shape[1:], BF16),
            jax.ShapeDtypeStruct((8, 4) + right.shape[1:], BF16),
        ],
        in_specs=[hbm, hbm],
        out_specs=[hbm, hbm],
        scratch_shapes=[
            pltpu.VMEM((4,) + left.shape, BF16),
            pltpu.VMEM((4,) + right.shape[1:], BF16),
            pltpu.SemaphoreType.DMA((8,)),
            pltpu.SemaphoreType.DMA((SIDES_SENDS,)),
            pltpu.SemaphoreType.DMA((SIDES_SENDS,)),
        ],
        cost_estimate=cost(24),
        compiler_params=pltpu.CompilerParams(
            collective_id=1, has_side_effects=True, vmem_limit_bytes=32 << 20
        ),
    )(left, right)


RETURN_SENDS = 1 + 7 + 3 + 6


def return_kernel(
    left, right, left_out, right_out, right_core, left_in, right_in, left_on, right_sum, local_sem, send_sem, recv_sem
):
    row, head = place()
    beyond = [(head + k) % 4 for k in range(4)]
    behind = [(head + 4 - k) % 4 for k in range(4)]
    plane = [(flip(row, way), head) for way in range(8)]
    greet(plane[1:] + [(row, beyond[k]) for k in (1, 2, 3)])
    sends = Sends(send_sem, recv_sem)
    core = row % 2
    swap = sends.start(right.at[:, 1 - core], right_core, plane[CORE])
    lefts = [sends.start(left.at[plane[way][0]], left_in.at[row], plane[way]) for way in (2, 4, 6, 3, 5, 7, 1)]
    copy = pltpu.make_async_copy(left.at[row], left_in.at[row], local_sem.at[0])
    copy.start()
    swap.wait_recv()
    chip = row // 2
    blocks = right.shape[2]
    for n in range(right.shape[0]):
        for b in range(blocks):
            right_sum[n, b] = (
                right[n, core, b].astype(F32) + right_core[n, b].astype(F32)
            ).astype(BF16)
    rights = []
    for slot, way in enumerate((ACROSS, DOWN, CORNER)):
        rights.append(sends.start(right_sum.at[plane[way][0] // 2], right_in.at[slot], plane[way]))
    for arrival in lefts:
        arrival.wait_recv()
    copy.wait()
    on = []
    for k in (1, 2, 3):
        on.append(sends.start(left_in.at[:, beyond[k]], left_on.at[k - 1], (row, beyond[k])))
    for arrival in rights:
        arrival.wait_recv()
    for b in range(blocks):
        total = right_sum[chip, b].astype(F32)
        for slot in range(3):
            total = total + right_in[slot, b].astype(F32)
        right_core[0, b] = total.astype(BF16)
    last = []
    for k in (1, 2, 3):
        last.append(sends.start(right_core.at[0, beyond[k]], right_out.at[head], (row, beyond[k])))
    mine = pltpu.make_async_copy(right_core.at[0, head], right_out.at[head], local_sem.at[1])
    mine.start()
    for arrival in on:
        arrival.wait_recv()
    for n in range(left_in.shape[0]):
        total = left_in[n, head].astype(F32)
        for k in range(3):
            total = total + left_on[k, n].astype(F32)
        left_out[n] = total.astype(BF16)
    for arrival in last:
        arrival.wait_recv()
    mine.wait()
    sends.finish()


def return_sides(left, right):
    vmem = pl.BlockSpec(memory_space=pltpu.VMEM)
    piece_left, piece_right = left.shape[2:], right.shape[2:]
    return pl.pallas_call(
        return_kernel,
        out_shape=[
            jax.ShapeDtypeStruct((8,) + piece_left, BF16),
            jax.ShapeDtypeStruct((4,) + piece_right, BF16),
        ],
        in_specs=[vmem, vmem],
        out_specs=[vmem, vmem],
        scratch_shapes=[
            pltpu.VMEM((4, 4) + piece_right, BF16),
            pltpu.VMEM((8, 4) + piece_left, BF16),
            pltpu.VMEM((3, 4) + piece_right, BF16),
            pltpu.VMEM((3, 8) + piece_left, BF16),
            pltpu.VMEM((4, 4) + piece_right, BF16),
            pltpu.SemaphoreType.DMA((2,)),
            pltpu.SemaphoreType.DMA((RETURN_SENDS,)),
            pltpu.SemaphoreType.DMA((RETURN_SENDS,)),
        ],
        cost_estimate=cost(27),
        compiler_params=pltpu.CompilerParams(
            collective_id=2, has_side_effects=True, vmem_limit_bytes=32 << 20
        ),
    )(left, right.reshape((4, 2) + right.shape[1:]))


SUM_SENDS = 4 + 12 + 3 + 1 + 3 + 3


def sum_kernel(
    grads, parts, out, piece,
    swapped, chip_sum, plane_in, down_sum, line_in,
    part_swapped, part_sum, part_plane, part_down, part_line,
    send_sem, recv_sem,
):
    row, head = place()
    beyond = [(head + k) % 4 for k in range(4)]
    core, chip = row % 2, row // 2
    ways = (CORNER, ACROSS, DOWN)
    plane = [(flip(row, way), head) for way in range(8)]
    other = plane[CORE]
    greet([plane[way] for way in (CORE,) + ways] + [(row, beyond[k]) for k in (1, 2, 3)])
    sends = Sends(send_sem, recv_sem)
    chips = [plane[way][0] // 2 for way in ways] + [chip]
    swaps = [sends.start(grads.at[n, 1 - core], swapped.at[slot], other) for slot, n in enumerate(chips)]
    part_swap = sends.start(parts.at[1 - core], part_swapped, other)
    order = (2, 1, 3, 0)
    arrive = [[None] * 3 for _ in range(4)]
    for slot, n in enumerate(chips):
        swaps[slot].wait_recv()
        for k in order:
            z = beyond[k]
            chip_sum[slot, z] = (grads[n, core, z].astype(F32) + swapped[slot, z].astype(F32)).astype(BF16)
            if slot < 3:
                arrive[k][slot] = sends.start(chip_sum.at[slot, z], plane_in.at[slot, k], plane[ways[slot]])
    part_swap.wait_recv()
    part_arrive = []
    for slot, n in enumerate(chips):
        for z in range(4):
            part_sum[slot, z] = (parts[core, n, z].astype(F32) + part_swapped[n, z].astype(F32)).astype(BF16)
        if slot < 3:
            part_arrive.append(sends.start(part_sum.at[slot], part_plane.at[slot], plane[ways[slot]]))
    line = []
    for k in order:
        for slot in range(3):
            arrive[k][slot].wait_recv()
        total = chip_sum[3, beyond[k]].astype(F32)
        for slot in range(3):
            total = total + plane_in[slot, k].astype(F32)
        if k:
            down_sum[k - 1] = total.astype(BF16)
            line.append(sends.start(down_sum.at[k - 1], line_in.at[k - 1], (row, beyond[k])))
        else:
            out[...] = total
    for copy in part_arrive:
        copy.wait_recv()
    for z in range(4):
        total = part_sum[3, z].astype(F32)
        for slot in range(3):
            total = total + part_plane[slot, z].astype(F32)
        part_down[z] = total.astype(BF16)
    part_arrive = [
        sends.start(part_down.at[beyond[k]], part_line.at[k - 1], (row, beyond[k])) for k in (1, 2, 3)
    ]
    for slot, copy in zip((1, 0, 2), line):
        copy.wait_recv()
        out[...] += line_in[slot].astype(F32)
    total = part_down[head].astype(F32)
    for slot, copy in enumerate(part_arrive):
        copy.wait_recv()
        total = total + part_line[slot].astype(F32)
    piece[...] = total.astype(BF16)
    sends.finish()


def sum_gradients(grads, parts):
    block = grads.shape[2:]
    lines = block[0] * block[1]
    rows, cols = parts.shape
    share = rows // 32
    vmem = pl.BlockSpec(memory_space=pltpu.VMEM)
    wide = lambda *first: pltpu.VMEM(first + (lines, block[2]), BF16)
    thin = lambda *first: pltpu.VMEM(first + (share, cols), BF16)
    out, piece = pl.pallas_call(
        sum_kernel,
        out_shape=[
            jax.ShapeDtypeStruct((lines, block[2]), F32),
            jax.ShapeDtypeStruct((share, cols), BF16),
        ],
        in_specs=[vmem, vmem],
        out_specs=[vmem, vmem],
        scratch_shapes=[
            wide(4, 4), wide(4, 4), wide(3, 4), wide(3), wide(3),
            thin(4, 4), thin(4, 4), thin(3, 4), thin(4), thin(3),
            pltpu.SemaphoreType.DMA((SUM_SENDS,)),
            pltpu.SemaphoreType.DMA((SUM_SENDS,)),
        ],
        compiler_params=pltpu.CompilerParams(
            collective_id=3, has_side_effects=True, vmem_limit_bytes=40 << 20
        ),
        cost_estimate=cost(40),
    )(grads.reshape(4, 2, 4, lines, block[2]), parts.reshape(2, 4, 4, share, cols))
    return out.reshape(block), piece


SPREAD_SENDS = 3 + 12 + 16 + 3 + 7


def spread_kernel(
    piece, small, out, total, line_in, line_sum, plane_in, local_sem, send_sem, recv_sem
):
    row, head = place()
    beyond = [(head + k) % 4 for k in range(4)]
    behind = [(head + 4 - k) % 4 for k in range(4)]
    core, chip = row % 2, row // 2
    ways = (CORNER, ACROSS, DOWN)
    plane = [(flip(row, way), head) for way in range(8)]
    other = plane[CORE]
    greet(plane[1:] + [(row, beyond[k]) for k in (1, 2, 3)])
    sends = Sends(send_sem, recv_sem)
    small_line = [sends.start(small, line_in.at[head], (row, beyond[k])) for k in (1, 2, 3)]
    line = [None] + [sends.start(piece, out.at[core, chip, head], (row, beyond[k])) for k in (1, 2, 3)]
    mine = pltpu.make_async_copy(piece, out.at[core, chip, head], local_sem)
    mine.start()
    line_in[head] = small[...]
    across, end = [], []

    def forward(k):
        here = out.at[core, chip, behind[k]]
        source = here if k else piece
        for way in ways:
            across.append((plane[way][0] // 2, k, sends.start(source, here, plane[way])))
        end.append(sends.start(source, here, other))

    forward(0)
    for copy in small_line:
        copy.wait_recv()
    line_sum[...] = (line_in[0] + line_in[1]) + (line_in[2] + line_in[3])
    small_plane = [sends.start(line_sum, plane_in.at[row], plane[way]) for way in range(1, 8)]
    plane_in[row] = line_sum[...]
    for k in (1, 2, 3):
        line[k].wait_recv()
        forward(k)
    for n, k, copy in across:
        copy.wait_recv()
        block = out.at[core, n, behind[k]]
        end.append(sends.start(block, block, other))
    for copy in small_plane:
        copy.wait_recv()
    summed = plane_in[0]
    for n in range(1, 8):
        summed = summed + plane_in[n]
    total[...] = summed
    for copy in end:
        copy.wait_recv()
    mine.wait()
    sends.finish()


def spread_gradients(piece, small):
    lines, cols = piece.shape
    vmem = pl.BlockSpec(memory_space=pltpu.VMEM)
    out, total = pl.pallas_call(
        spread_kernel,
        out_shape=[
            jax.ShapeDtypeStruct((2, 4, 4, lines, cols), BF16),
            jax.ShapeDtypeStruct(small.shape, F32),
        ],
        in_specs=[vmem, vmem],
        out_specs=[vmem, vmem],
        scratch_shapes=[
            pltpu.VMEM((4,) + small.shape, F32),
            pltpu.VMEM(small.shape, F32),
            pltpu.VMEM((8,) + small.shape, F32),
            pltpu.SemaphoreType.DMA,
            pltpu.SemaphoreType.DMA((SPREAD_SENDS,)),
            pltpu.SemaphoreType.DMA((SPREAD_SENDS,)),
        ],
        compiler_params=pltpu.CompilerParams(
            collective_id=4, has_side_effects=True, vmem_limit_bytes=32 << 20
        ),
        cost_estimate=cost(15),
    )(piece, small)
    return out.reshape(32 * lines, cols), total


def add_pieces(step, base, pieces, out):
    per = 2
    for n, piece in enumerate(pieces):
        @pl.when(step // per == n)
        def _():
            out[...] = base[...] + piece[...].astype(F32)


def added_specs(base, pieces):
    block = (1,) + base.shape[1:]
    per = pieces[0].shape[0]
    count = per * len(pieces)
    by_order = pl.BlockSpec(block, lambda n, order: (order[jnp.minimum(n, count - 1)], 0, 0))

    def turn(k):
        return pl.BlockSpec(block, lambda n, order: (jnp.clip(n - k * per, 0, per - 1), 0, 0))

    return by_order, [by_order] + [turn(k) for k in range(len(pieces))]


def pair_backward_kernel(order, pairs, back, grads, norm, weight, base, *refs):
    pieces, (out, small, changed) = refs[:-3], refs[-3:]
    step = pl.program_id(0)
    rows, cols, channels = pairs.shape
    add_pieces(step, base, pieces, changed)

    @pl.when(step == 0)
    def _():
        small[...] = jnp.zeros_like(small)

    values = pairs[...].reshape(rows * cols, channels)
    hat, rstd = normalize(values)
    low = (hat * norm[0:1] + norm[1:2]).astype(BF16)
    bias = jnp.concatenate([grads[:, i, :] for i in range(rows)], axis=1).astype(BF16)
    small[0:HEADS] += dot(bias, low, (1, 0))
    in_grad = dot(bias, weight[...], (0, 0))
    small[HEADS : HEADS + 1] += jnp.sum(in_grad * hat, axis=0, keepdims=True)
    small[HEADS + 1 : HEADS + 2] += jnp.sum(in_grad, axis=0, keepdims=True)
    change = norm_backward(hat, rstd, norm[0:1], in_grad)
    out[...] = back[...] + change.reshape(rows, cols, channels)


def pair_norm_backward(order, pairs, back, grads, norm, weight, base, pieces, steps=16):
    rows, cols, channels = pairs.shape
    block = rows // steps
    by_row = lambda n, order: (n, 0, 0)
    whole = lambda n, order: (0, 0)
    by_order, added = added_specs(base, pieces)
    grads = grads.reshape(HEADS, steps, block, cols)
    return pl.pallas_call(
        pair_backward_kernel,
        grid_spec=pltpu.PrefetchScalarGridSpec(
            num_scalar_prefetch=1,
            grid=(steps,),
            in_specs=[
                pl.BlockSpec((block, cols, channels), by_row),
                pl.BlockSpec((block, cols, channels), by_row),
                pl.BlockSpec((HEADS, None, block, cols), lambda n, order: (0, n, 0, 0)),
                pl.BlockSpec(norm.shape, whole),
                pl.BlockSpec(weight.shape, whole),
            ]
            + added,
            out_specs=[
                pl.BlockSpec((block, cols, channels), by_row),
                pl.BlockSpec((2 * HEADS, channels), whole),
                by_order,
            ],
        ),
        out_shape=[
            jax.ShapeDtypeStruct(pairs.shape, F32),
            jax.ShapeDtypeStruct((2 * HEADS, channels), F32),
            jax.ShapeDtypeStruct(base.shape, F32),
        ],
        compiler_params=pltpu.CompilerParams(vmem_limit_bytes=40 << 20),
        cost_estimate=cost(9),
    )(order, pairs, back, grads, norm, weight, base, *pieces)


def add_kernel(place_ref, base, piece, *refs):
    refs[-1][...] = base[...] + piece[...].astype(F32)


def add_rows(at, base, piece, into=None):
    own = piece.shape[0]
    block = (1,) + piece.shape[1:]
    spread = lambda n, at: (at[0] * own + n, 0, 0)
    return pl.pallas_call(
        add_kernel,
        grid_spec=pltpu.PrefetchScalarGridSpec(
            num_scalar_prefetch=1,
            grid=(own,),
            in_specs=[pl.BlockSpec(block, spread), pl.BlockSpec(block, lambda n, at: (n, 0, 0))]
            + ([] if into is None else [pl.BlockSpec(memory_space=pl.ANY)]),
            out_specs=pl.BlockSpec(block, spread),
        ),
        out_shape=jax.ShapeDtypeStruct(base.shape, F32),
        input_output_aliases={} if into is None else {3: 0},
        cost_estimate=cost(2),
    )(*((at, base, piece) if into is None else (at, base, piece, into)))


def hop(piece):
    count = lax.axis_size("head")
    return lax.ppermute(piece, "head", [(i, (i + 1) % count) for i in range(count)])


def together(moved, *values):
    return lax.optimization_barrier((moved,) + values)


def adam_kernel(at, packed, pair_side, *refs, rates, pieces):
    olds, base, adds, news = refs[:18], refs[18], refs[19 : 19 + pieces], refs[20 + pieces : 38 + pieces]
    changed, table = refs[38 + pieces :]
    step = pl.program_id(0)
    add_pieces(step, base, adds, changed)

    @pl.when(step == 0)
    def _():
        adam_step(at, packed, pair_side, olds, news, table, rates)


def adam_step(at, packed, pair_side, olds, news, table, rates):
    norms, heads_in, heads_out, bias_weight, outer_in, outer_out = [olds[3 * n : 3 * n + 3] for n in range(6)]
    wide = heads_in[0].shape[1]
    count, local = heads_in[0].shape[0], heads_in[0].shape[2]
    all_heads = wide
    sides, size = outer_in[0].shape[0], outer_in[0].shape[2]

    def rows(first, lines):
        return packed[pl.ds(first, lines), :].astype(F32)

    def pair_of(first, offset, lines, span):
        return jnp.concatenate([rows(first + offset, lines), rows(first + span + offset, lines)], axis=1)

    def update(n, index, grad):
        weight, moment_one, moment_two = [ref[index] for ref in olds[3 * n : 3 * n + 3]]
        for ref, new in zip(
            news[3 * n : 3 * n + 3], adam_update(weight, grad, moment_one, moment_two, rates[n])
        ):
            ref[index] = new

    mine = pl.multiple_of(at[4], local)
    span = count * all_heads
    for k in range(count):
        update(1, k, pair_of(0, k * all_heads + mine, local, span).T)
    first = 2 * span
    update(2, slice(None), pair_of(first, mine, local, all_heads))
    first += 2 * all_heads
    for k in range(sides):
        update(4, k, pair_of(first, k * size, size, sides * size).T)
    first += 2 * sides * size
    table[...] = rows(first, size * size)
    for e in range(size):
        update(5, slice(e * size, (e + 1) * size), table[pl.ds(e, size, stride=size), :])
    first += size * size
    low = rows(first, 8)
    pair = pair_side[...]
    lines = [
        jnp.concatenate([low[n : n + 1], low[n + 4 : n + 5], low[n + 2 : n + 3], low[n + 6 : n + 7], pair[HEADS + n : HEADS + n + 1]], axis=1)
        for n in range(2)
    ]
    update(0, slice(None), jnp.concatenate(lines, axis=0))
    update(3, slice(None), pair[:HEADS].T)


def adam_all(at, packed, pair_side, olds, rates, base, pieces, into):
    flat = [array for triple in olds for array in triple]
    size = olds[4][0].shape[2]
    by_order, added = added_specs(base, pieces)
    whole = lambda array: pl.BlockSpec(array.shape, lambda n, at: (0,) * array.ndim)
    return pl.pallas_call(
        functools.partial(adam_kernel, rates=rates, pieces=len(pieces)),
        grid_spec=pltpu.PrefetchScalarGridSpec(
            num_scalar_prefetch=1,
            grid=(4,),
            in_specs=[whole(array) for array in [packed, pair_side] + flat]
            + added
            + [pl.BlockSpec(memory_space=pl.ANY)],
            out_specs=[whole(array) for array in flat] + [by_order],
            scratch_shapes=[pltpu.VMEM((size * size, packed.shape[1]), F32)],
        ),
        out_shape=[jax.ShapeDtypeStruct(array.shape, F32) for array in flat + [base]],
        input_output_aliases={3 + len(flat) + 1 + len(pieces): len(flat)},
        compiler_params=pltpu.CompilerParams(vmem_limit_bytes=40 << 20),
        cost_estimate=cost(5),
    )(at, packed, pair_side, *flat, base, *pieces, into)


def halves(array):
    return jnp.concatenate([array[:, :128], array[:, 128:]])


def per_device(
    alignment,
    pairs,
    residue_mask,
    row_mask,
    alignment_back,
    pairs_back,
    norm_scales,
    heads_in,
    heads_out,
    bias_weight,
    outer_in,
    outer_out,
    first_norms,
    second_norms,
    first_heads_in,
    second_heads_in,
    first_heads_out,
    second_heads_out,
    first_bias_weight,
    second_bias_weight,
    first_outer_in,
    second_outer_in,
    first_outer_out,
    second_outer_out,
):
    row_count = lax.axis_size("row")
    head_count = lax.axis_size("head")
    head_index = lax.axis_index("head")
    devices = row_count * head_count
    rows_here, residues, width = alignment.shape
    pair_rows, pair_cols, pair_width = pairs.shape
    size = width // HEADS
    outer_width = outer_in.shape[2]
    all_rows = rows_here * row_count
    own = rows_here // head_count
    start = head_index * own
    scales = norm_scales[:, : 2 * width].reshape(2, 2, width).swapaxes(0, 1).reshape(4, width)
    pair_gain = norm_scales[0:1, 2 * width :]
    pair_shift = norm_scales[1:2, 2 * width :]
    residue_live = residue_mask.astype(F32)
    key_mask = ((residue_live - 1.0) * (1e9 * LOG2E))[:, None]
    live = lax.dynamic_slice_in_dim(row_mask, start, own, 0).astype(F32)[:, None] * residue_live[None]
    bias_low = bias_weight.astype(BF16)

    fast = (row_count, head_count, pair_cols, own * outer_width) == (8, 4, 128, 128)

    local = heads_in.shape[2]
    shard = jnp.concatenate([heads_in.astype(BF16).swapaxes(1, 2), heads_out.astype(BF16)[None]])
    outer_t = outer_in.astype(BF16).swapaxes(1, 2).reshape(2 * outer_width, width)
    table = outer_out.astype(BF16).reshape(outer_width, outer_width, pair_width)
    if fast:
        bias, weights = pair_bias(pairs, norm_scales[:, 2 * width :], bias_low.T, shard)
    else:
        weights = lax.all_gather(shard, "head", axis=1, tiled=True)
        bias = pair_forward(pairs, pair_gain, pair_shift, bias_low)
        bias = lax.all_gather(bias, "head", axis=2, tiled=True)
        bias = lax.all_gather(bias, "row", axis=1, tiled=True)[None, None]
    in_t = weights[:4].reshape(4 * width, width)
    out_low = weights[4]

    update, sides, kept = attention_forward(
        start.astype(jnp.int32)[None], alignment, scales, in_t, out_low, outer_t, bias, key_mask, live[:, None]
    )

    left, right = sides[:, :outer_width], sides[:, outer_width:]
    if fast:
        left_all, right_all = share_sides(
            left.reshape(own * outer_width, residues).T.reshape(row_count, pair_rows, own * outer_width),
            right.reshape(own * outer_width, head_count, pair_cols).swapaxes(0, 1),
        )
        update, left_all, right_all = together(update, left_all, right_all)
        updates = [update, hop(update)]
        left_all = left_all.reshape(devices, pair_rows, own, outer_width).transpose(1, 3, 0, 2)
        pairs_new, left_grad, right_grad, table_grad = outer_product(
            left_all.reshape(pair_rows * outer_width, all_rows),
            right_all.reshape(all_rows, outer_width * pair_cols),
            pairs,
            pairs_back,
            table.swapaxes(0, 1).reshape(outer_width * outer_width, pair_width),
            all_rows,
        )
        left_grad = left_grad.reshape(pair_rows, outer_width, devices, own).transpose(2, 0, 3, 1)
        updates[1], left_grad, right_grad = together(updates[1], left_grad, right_grad)
        updates.append(hop(updates[1]))
        left_total, right_total = return_sides(
            left_grad.reshape(row_count, head_count, pair_rows, own * outer_width),
            right_grad.astype(BF16).reshape(row_count, head_count, own * outer_width, pair_cols),
        )
        updates[2], left_total, right_total = together(updates[2], left_total, right_total)
        updates.append(hop(updates[2]))
        left_total = left_total.reshape(residues, own * outer_width).T
        right_total = right_total.swapaxes(0, 1)
    else:
        updates = [update]
        for _ in range(head_count - 1):
            updates.append(hop(updates[-1]))
        left = left.reshape(own, outer_width, row_count, pair_rows).transpose(2, 0, 1, 3)
        right = right.reshape(own, outer_width, head_count, pair_cols).transpose(2, 0, 1, 3)
        both = (row_count, head_count, own, outer_width)
        send = jnp.concatenate(
            [
                jnp.broadcast_to(left[:, None], both + (pair_rows,)),
                jnp.broadcast_to(right[None], both + (pair_cols,)),
            ],
            axis=4,
        )
        flat = (devices, own, outer_width, pair_rows + pair_cols)
        got = lax.all_to_all(send.reshape(flat), EVERY, split_axis=0, concat_axis=0, tiled=True)
        got = got.reshape(all_rows, outer_width, pair_rows + pair_cols)
        total, table_grad, left_grad, right_grad = outer_product_plain(
            got[:, :, :pair_rows], got[:, :, pair_rows:], pairs_back, table, all_rows
        )
        pairs_new = pairs + total
        send = jnp.concatenate([left_grad, right_grad], axis=2).reshape(flat)
        got = lax.all_to_all(send, EVERY, split_axis=0, concat_axis=0, tiled=True)
        got = got.reshape(both + (pair_rows + pair_cols,)).astype(F32)
        left_total = jnp.sum(got[..., :pair_rows], axis=1).transpose(1, 2, 0, 3)
        right_total = jnp.sum(got[..., pair_rows:], axis=0).transpose(1, 2, 0, 3)
    sides_grad = jnp.concatenate(
        [
            left_total.reshape(own, outer_width, residues),
            right_total.reshape(own, outer_width, residues),
        ],
        axis=1,
    )
    sides_grad = (sides_grad * live[:, None, :]).astype(BF16)

    turns = (head_index + head_count - jnp.arange(head_count, dtype=jnp.int32)) % head_count
    order = (turns[:, None] * own + jnp.arange(own, dtype=jnp.int32)[None]).reshape(-1)
    half = own // 2

    def mine(first, hops, second, more):
        parts = [(first, step) for step in hops] + [(second, step) for step in more]
        return jnp.concatenate([order[step * own + n * half : step * own + (n + 1) * half] for n, step in parts])

    backward = functools.partial(
        attention_backward,
        order, alignment, update, alignment_back, scales, in_t, out_low, outer_t, sides_grad, kept, bias.shape,
    )
    part, bias_grad, *early = backward(first=0, own=half)
    updates[3:], (bias_grad, part) = together(updates[3:], (bias_grad, part))
    changes = [[part, hop(part)]]
    alignment_new, part, bias_grad, *late = backward(first=half, own=half, earlier=bias_grad, pieces=updates)
    if fast:
        changes[0][1], bias_grad, part, early, late = together(changes[0][1], bias_grad, part, early, late)
        sums = [one + two for one, two in zip(early, late)]
        changes[0].append(hop(changes[0][1]))
        changes.append([part, hop(part)])
        packed = [halves(sums[0]), halves(sums[1]), halves(sums[2]), table_grad, halves(sums[3])]
        rest = -sum(array.shape[0] for array in packed) % 512
        packed = jnp.concatenate([array.astype(BF16) for array in packed] + [jnp.zeros((rest, 128), BF16)])
        bias_grad, packed = sum_gradients(bias_grad, packed)
        changes[0][2], changes[1][1], bias_grad = together(changes[0][2], changes[1][1], bias_grad)
        changes[0].append(hop(changes[0][2]))
        changes[1].append(hop(changes[1][1]))
        pairs_grad, pair_side, alignment_grad = pair_norm_backward(
            mine(0, (0, 1, 2), 1, (0, 1)),
            pairs,
            pairs_back,
            bias_grad,
            norm_scales[:, 2 * width :],
            bias_low.T,
            alignment_back,
            changes[0][:3] + changes[1][:2],
        )
        packed, pair_side = spread_gradients(packed, pair_side)
        changes[0][3], changes[1][2], packed = together(changes[0][3], changes[1][2], packed)
        changes[1].append(hop(changes[1][2]))
    else:
        sums = [one + two for one, two in zip(early, late)]
        sums = (sums[0], sums[1], sums[2], table_grad, sums[3])
        for _ in range(head_count - 2):
            changes[0].append(hop(changes[0][-1]))
        changes.append([part])
        for _ in range(head_count - 1):
            changes[1].append(hop(changes[1][-1]))
        bias_grad = lax.psum_scatter(bias_grad[0, 0], "row", scatter_dimension=1, tiled=True)
        bias_grad = lax.psum_scatter(bias_grad, "head", scatter_dimension=2, tiled=True)
        pairs_grad, bias_weight_grad, pair_gain_grad, pair_shift_grad = pair_backward(
            pairs, pairs_back, pair_gain, pair_shift, bias_low, bias_grad
        )
        sums, bias_weight_total, pair_norms_total = lax.psum(
            (sums, bias_weight_grad, jnp.stack([pair_gain_grad, pair_shift_grad])), EVERY
        )
    olds = (
        (norm_scales, first_norms, second_norms),
        (heads_in, first_heads_in, second_heads_in),
        (heads_out, first_heads_out, second_heads_out),
        (bias_weight, first_bias_weight, second_bias_weight),
        (outer_in, first_outer_in, second_outer_in),
        (outer_out, first_outer_out, second_outer_out),
    )
    rates = (
        0.5,
        width ** (-0.5),
        max(2 * HEADS * size // residues, 1) ** (-0.5),
        pair_width ** (-0.5),
        width ** (-0.5),
        max(outer_width * outer_width // all_rows, 1) ** (-0.5),
    )
    if fast:
        at = (head_index * local).astype(jnp.int32)[None]
        *news, alignment_grad = adam_all(
            jnp.concatenate([mine(0, (3,), 1, (2,)), at]),
            packed, pair_side, olds, rates, alignment_back, [changes[0][3], changes[1][2]], alignment_grad,
        )
        at = (turns[3] * 2 + 1)[None]
        alignment_grad = add_rows(at, alignment_back, changes[1][3], alignment_grad)
        return (alignment_new, pairs_new, alignment_grad, pairs_grad, *news)
    alignment_grad = None
    for step in range(head_count):
        for n in range(2):
            at = (turns[step] * 2 + n)[None]
            alignment_grad = add_rows(at, alignment_back, changes[n][step], alignment_grad)
    heads_in_total = lax.dynamic_slice_in_dim(
        sums[0].reshape(4, width, width), head_index * local, local, 1
    ).swapaxes(1, 2)
    heads_out_total = lax.dynamic_slice_in_dim(sums[1], head_index * local, local, 0)
    outer_in_total = sums[2].reshape(2, outer_width, width).swapaxes(1, 2)
    table_total = sums[3].reshape(outer_width * outer_width, pair_width)
    norms_total = jnp.concatenate(
        [sums[4].reshape(2, 2, width).swapaxes(0, 1).reshape(2, 2 * width), pair_norms_total], axis=1
    )
    totals = (norms_total, heads_in_total, heads_out_total, bias_weight_total, outer_in_total, table_total)
    news = []
    for (weight, moment_one, moment_two), total, rate in zip(olds, totals, rates):
        news += adam_update(weight, total, moment_one, moment_two, rate)
    return (alignment_new, pairs_new, alignment_grad, pairs_grad, *news)


def solution(mesh):
    row_msa = P("row", None, None)
    pair = P("row", "head", None)
    columns = P(None, None, "head")
    lines = P("head", None)
    in_specs = (
        (row_msa, pair, P(), P("row"), row_msa, pair, P(), columns, lines)
        + (P(),) * 5
        + (columns,) * 2
        + (lines,) * 2
        + (P(),) * 6
    )
    out_specs = (row_msa, pair, row_msa, pair) + (P(),) * 3 + (columns,) * 3 + (lines,) * 3 + (P(),) * 9
    return jax.shard_map(
        per_device, mesh=mesh, in_specs=in_specs, out_specs=out_specs, check_vma=False
    )
```

```python
import functools

import jax
import jax.numpy as jnp
from jax import lax
from jax.experimental import pallas as pl
from jax.experimental.pallas import tpu as pltpu
from jax.sharding import PartitionSpec as P

HEADS = 8
STEP = 10
F32 = jnp.float32
BF16 = jnp.bfloat16
LOG2E = 1.4426950408889634
VMEM = 56 << 20
EVERY = ("row", "head")


def adam_update(weight, gradient, moment_one, moment_two, step_rate):
    first_new = 0.9 * moment_one + 0.1 * gradient
    second_new = 0.999 * moment_two + 0.001 * gradient * gradient
    first_hat = first_new / (1.0 - 0.9**STEP)
    second_hat = second_new / (1.0 - 0.999**STEP)
    updated = weight - step_rate * (first_hat / (jnp.sqrt(second_hat) + 1e-08) + 0.01 * weight)
    return (first_new, second_new, updated)


def cost(micros):
    return pl.CostEstimate(flops=0, bytes_accessed=int(micros * 3.5e6), transcendentals=0)


def dot(a, b, along):
    return lax.dot_general(a, b, (((along[0],), (along[1],)), ((), ())), preferred_element_type=F32)


def normalize(values):
    center = values - jnp.mean(values, axis=-1, keepdims=True)
    rstd = lax.rsqrt(jnp.mean(center * center, axis=-1, keepdims=True) + 1e-05)
    return center * rstd, rstd


def norm_backward(hat, rstd, gain, grad):
    scaled = grad * gain
    return rstd * (
        scaled
        - jnp.mean(scaled, axis=-1, keepdims=True)
        - hat * jnp.mean(scaled * hat, axis=-1, keepdims=True)
    )


def forward_kernel(
    at_ref, rows, scales, in_t, out_low, outer_t, bias, key_mask, live,
    update, sides, qkv, gate, powers, inverse, mixed, attended,
    bias_t, *, chunk,
):
    row, head = pl.program_id(0), pl.program_id(1)
    width = rows.shape[2]
    residues = rows.shape[1]
    size = width // HEADS

    @pl.when(row == 0)
    def _():
        across, down, _, lines, cols = bias.shape
        group = max(1, 128 // lines)
        for r in range(0, across, group):
            for c in range(down):
                tile = jnp.concatenate([bias[r + g, c, 0] for g in range(group)], axis=0)
                bias_t[head, c * cols : (c + 1) * cols, r * lines : (r + group) * lines] = (
                    tile.astype(F32).T + key_mask[c * cols : (c + 1) * cols]
                )

    @pl.when(head == 0)
    def _():
        hat, _ = normalize(rows[0])
        normed = (hat * scales[0:1] + scales[1:2]).astype(BF16)
        qkv[0, :width] = (
            dot(in_t[:width], normed, (1, 1)) * (size**-0.5 * LOG2E)
        ).astype(BF16)
        qkv[0, width:] = dot(in_t[width : 3 * width], normed, (1, 1)).astype(BF16)
        gate[0] = jax.nn.sigmoid(dot(in_t[3 * width :], normed, (1, 1)))

    at = pl.multiple_of(head * size, size)
    keys = qkv[0, pl.ds(width + at, size), :]
    values = qkv[0, pl.ds(2 * width + at, size), :]
    for first in range(0, residues, chunk):
        span = slice(first, first + chunk)
        query = qkv[0, pl.ds(at, size), span]
        scores = dot(keys, query, (0, 0)) + bias_t[head, :, span]
        exps = jnp.exp2(scores - jnp.max(scores, axis=0, keepdims=True))
        over = 1.0 / jnp.sum(exps, axis=0, keepdims=True)
        low = exps.astype(BF16)
        powers[0, 0, :, span] = low
        inverse[0, 0, :, span] = over
        mixed[0, pl.ds(at, size), span] = dot(values, low, (1, 0)) * over

    @pl.when(head == HEADS - 1)
    def _():
        att = (gate[0] * mixed[0]).astype(BF16)
        attended[0] = att
        change = dot(att, out_low[...], (0, 0)).astype(BF16)
        update[0] = change
        hat, _ = normalize(rows[0] + change.astype(F32))
        second = (hat * scales[2:3] + scales[3:4]).astype(BF16)
        sides[0] = (dot(outer_t[...], second, (1, 1)) * live[0]).astype(BF16)


def attention_forward(start, rows, scales, in_t, out_low, outer_t, bias, key_mask, live, chunk=512):
    _, residues, width = rows.shape
    own = live.shape[0]
    sides = outer_t.shape[0]
    by_row = lambda s, h, at: (s, 0, 0)
    whole = lambda s, h, at: (0, 0)
    last = lambda s, h, at: (0, 0, jnp.where(s == 0, h, HEADS - 1), 0, 0)
    out = pl.pallas_call(
        functools.partial(forward_kernel, chunk=chunk),
        grid_spec=pltpu.PrefetchScalarGridSpec(
        num_scalar_prefetch=1,
        grid=(own, HEADS),
        in_specs=[
            pl.BlockSpec((1, residues, width), lambda s, h, at: (at[0] + s, 0, 0)),
            pl.BlockSpec(scales.shape, whole),
            pl.BlockSpec(in_t.shape, whole),
            pl.BlockSpec(out_low.shape, whole),
            pl.BlockSpec(outer_t.shape, whole),
            pl.BlockSpec(bias.shape[:2] + (1,) + bias.shape[3:], last),
            pl.BlockSpec((residues, 1), whole),
            pl.BlockSpec((1, 1, residues), by_row),
        ],
        out_specs=[
            pl.BlockSpec((1, residues, width), by_row),
            pl.BlockSpec((1, sides, residues), by_row),
            pl.BlockSpec((1, 3 * width, residues), by_row),
            pl.BlockSpec((1, width, residues), by_row),
            pl.BlockSpec((1, 1, residues, residues), lambda s, h, at: (s, h, 0, 0)),
            pl.BlockSpec((1, 1, 1, residues), lambda s, h, at: (s, h, 0, 0)),
            pl.BlockSpec((1, width, residues), by_row),
            pl.BlockSpec((1, width, residues), by_row),
        ],
        scratch_shapes=[pltpu.VMEM((HEADS, residues, residues), F32)],
        ),
        out_shape=[
            jax.ShapeDtypeStruct((own, residues, width), BF16),
            jax.ShapeDtypeStruct((own, sides, residues), BF16),
            jax.ShapeDtypeStruct((own, 3 * width, residues), BF16),
            jax.ShapeDtypeStruct((own, width, residues), F32),
            jax.ShapeDtypeStruct((own, HEADS, residues, residues), BF16),
            jax.ShapeDtypeStruct((own, HEADS, 1, residues), F32),
            jax.ShapeDtypeStruct((own, width, residues), F32),
            jax.ShapeDtypeStruct((own, width, residues), BF16),
        ],
        cost_estimate=cost(36),
        compiler_params=pltpu.CompilerParams(vmem_limit_bytes=VMEM),
    )(start, rows, scales, in_t, out_low, outer_t, bias, key_mask, live)
    return out[0], out[1], tuple(out[2:])


def backward_kernel(
    *refs, chunk, earlier, adds, per,
):
    (order, rows, update, back, scales, in_t, out_low, outer_t, sides_grad,
     qkv, gate, powers, inverse, mixed, attended), refs = refs[:15], refs[15:]
    if earlier:
        (so_far, base), pieces, refs = refs[:2], refs[2 : 2 + adds], refs[2 + adds :]
        added, refs = refs[0], refs[1:]
    (part, bias_grad, heads_in_grad, heads_out_grad, outer_in_grad, norms,
     bias_total, mixed_grad, delta, proj_grad, new_part) = refs
    row, head = pl.program_id(0), pl.program_id(1)
    width = rows.shape[2]
    residues = rows.shape[1]
    size = width // HEADS
    last_row = row == pl.num_programs(0) - 1

    if earlier:
        step = row * HEADS + head
        for n in range(adds):
            @pl.when(step // per == n)
            def _():
                added[...] = base[...] + pieces[n][...].astype(F32)

    @pl.when((row == 0) & (head == 0))
    def _():
        heads_in_grad[...] = jnp.zeros_like(heads_in_grad)
        heads_out_grad[...] = jnp.zeros_like(heads_out_grad)
        outer_in_grad[...] = jnp.zeros_like(outer_in_grad)
        norms[...] = jnp.zeros_like(norms)

    @pl.when(row == 0)
    def _():
        bias_total[head] = so_far[0] if earlier else jnp.zeros((residues, residues), F32)

    @pl.when(head == 0)
    def _():
        hat, rstd = normalize(rows[0] + update[0].astype(F32))
        second = (hat * scales[2:3] + scales[3:4]).astype(BF16)
        grads = sides_grad[0]
        outer_in_grad[...] += dot(grads, second, (1, 0))
        second_grad = dot(grads, outer_t[...], (0, 0))
        norms[2:3] += jnp.sum(second_grad * hat, axis=0, keepdims=True)
        norms[3:4] += jnp.sum(second_grad, axis=0, keepdims=True)
        new = norm_backward(hat, rstd, scales[2:3], second_grad)
        new_part[...] = new
        out_grad = (back[0] + new).astype(BF16)
        heads_out_grad[...] += dot(attended[0], out_grad, (1, 0))
        attended_grad = dot(out_low[...], out_grad, (1, 1))
        sig = gate[0]
        gated = attended_grad * sig
        proj_grad[3 * width :] = (gated * mixed[0] * (1.0 - sig)).astype(BF16)
        for h in range(HEADS):
            span = slice(h * size, (h + 1) * size)
            grad = gated[span] * inverse[0, h]
            mixed_grad[span] = grad.astype(BF16)
            delta[h] = jnp.sum(grad * mixed[0, span], axis=0, keepdims=True)

    at = pl.multiple_of(head * size, size)
    keys = qkv[0, pl.ds(width + at, size), :]
    values = qkv[0, pl.ds(2 * width + at, size), :]
    key_grad = jnp.zeros((size, residues), F32)
    value_grad = jnp.zeros((size, residues), F32)
    for first in range(0, residues, chunk):
        span = slice(first, first + chunk)
        grad = mixed_grad[pl.ds(at, size), span]
        query = qkv[0, pl.ds(at, size), span]
        low = powers[0, 0, :, span]
        prob_grad = dot(values, grad, (0, 0))
        score_grad = low.astype(F32) * (prob_grad - delta[head, :, span])
        bias_total[head, :, span] += score_grad
        score_low = score_grad.astype(BF16)
        value_grad += dot(grad, low, (1, 1))
        key_grad += dot(query, score_low, (1, 1))
        proj_grad[pl.ds(at, size), span] = (dot(keys, score_low, (1, 0)) * size**-0.5).astype(BF16)
    proj_grad[pl.ds(width + at, size), :] = (key_grad / LOG2E).astype(BF16)
    proj_grad[pl.ds(2 * width + at, size), :] = value_grad.astype(BF16)

    @pl.when(last_row)
    def _():
        if not earlier:
            bias_grad[0] = bias_total[head]
        else:
            across, down, _, lines, cols = bias_grad.shape
            group = max(1, 128 // lines)
            for r in range(0, across, group):
                for c in range(down):
                    tile = bias_total[head, c * cols : (c + 1) * cols, r * lines : (r + group) * lines]
                    tile = tile.T.astype(BF16)
                    for g in range(group):
                        bias_grad[r + g, c, 0] = tile[g * lines : (g + 1) * lines]

    @pl.when(head == HEADS - 1)
    def _():
        hat, rstd = normalize(rows[0])
        normed = (hat * scales[0:1] + scales[1:2]).astype(BF16)
        grads = proj_grad[...]
        heads_in_grad[...] += dot(grads, normed, (1, 0))
        normed_grad = dot(grads, in_t[...], (0, 0))
        norms[0:1] += jnp.sum(normed_grad * hat, axis=0, keepdims=True)
        norms[1:2] += jnp.sum(normed_grad, axis=0, keepdims=True)
        part[0] = (new_part[...] + norm_backward(hat, rstd, scales[0:1], normed_grad)).astype(BF16)


def attention_backward(
    order, rows, update, back, scales, in_t, out_low, outer_t, sides_grad, kept, blocks,
    first, own, earlier=None, pieces=(), chunk=512,
):
    _, residues, width = rows.shape
    qkv, gate, powers, inverse, mixed, attended = kept
    sides = outer_t.shape[0]
    here = lambda s, h, order: (order[0] + first + s, 0, 0)
    by_row = lambda s, h, order: (first + s, 0, 0)
    whole = lambda s, h, order: (0, 0)
    one = pl.BlockSpec((1, residues, width), here)
    args = [rows, update, back, scales, in_t, out_low, outer_t, sides_grad]
    args += [qkv, gate, powers, inverse, mixed, attended]
    in_specs = [
        one,
        pl.BlockSpec((1, residues, width), by_row),
        one,
        pl.BlockSpec(scales.shape, whole),
        pl.BlockSpec(in_t.shape, whole),
        pl.BlockSpec(out_low.shape, whole),
        pl.BlockSpec(outer_t.shape, whole),
        pl.BlockSpec((1, sides, residues), by_row),
        pl.BlockSpec((1, 3 * width, residues), by_row),
        pl.BlockSpec((1, width, residues), by_row),
        pl.BlockSpec((1, 1, residues, residues), lambda s, h, order: (first + s, h, 0, 0)),
        pl.BlockSpec((1, HEADS, 1, residues), lambda s, h, order: (first + s, 0, 0, 0)),
        pl.BlockSpec((1, width, residues), by_row),
        pl.BlockSpec((1, width, residues), by_row),
    ]
    out_specs = [
        pl.BlockSpec((1, residues, width), lambda s, h, order: (s, 0, 0)),
        pl.BlockSpec((1, residues, residues), lambda s, h, order: (jnp.where(s == own - 1, h, 0), 0, 0)),
        pl.BlockSpec(in_t.shape, whole),
        pl.BlockSpec(out_low.shape, whole),
        pl.BlockSpec(outer_t.shape, whole),
        pl.BlockSpec((4, width), whole),
    ]
    out_shape = [
        jax.ShapeDtypeStruct((own, residues, width), BF16),
        jax.ShapeDtypeStruct((HEADS, residues, residues), F32),
        jax.ShapeDtypeStruct(in_t.shape, F32),
        jax.ShapeDtypeStruct(out_low.shape, F32),
        jax.ShapeDtypeStruct(outer_t.shape, F32),
        jax.ShapeDtypeStruct((4, width), F32),
    ]
    per = 1
    if earlier is not None:
        each = rows.shape[0] // (own * HEADS)
        per = pieces[0].shape[0] // each
        lines = pl.BlockSpec(
            (each, residues, width), lambda s, h, order: (order[(s * HEADS + h) * each] // each, 0, 0)
        )

        def changes(n):
            return pl.BlockSpec(
                (each, residues, width),
                lambda s, h, order: (jnp.clip(s * HEADS + h - n * per, 0, per - 1), 0, 0),
            )

        args += [earlier, rows] + list(pieces)
        in_specs += [
            pl.BlockSpec(
                (1, residues, residues), lambda s, h, order: (jnp.where(s == 0, h, HEADS - 1), 0, 0)
            ),
            lines,
        ] + [changes(n) for n in range(len(pieces))]
        out_specs[1] = pl.BlockSpec(
            blocks[:2] + (1,) + blocks[3:],
            lambda s, h, order: (0, 0, jnp.where(s == own - 1, h, 0), 0, 0),
        )
        out_shape[1] = jax.ShapeDtypeStruct(blocks, BF16)
        out_specs = [lines] + out_specs
        out_shape = [jax.ShapeDtypeStruct(rows.shape, F32)] + out_shape
    return pl.pallas_call(
        functools.partial(
            backward_kernel, chunk=chunk, earlier=earlier is not None, adds=len(pieces), per=per
        ),
        grid_spec=pltpu.PrefetchScalarGridSpec(
            num_scalar_prefetch=1,
            grid=(own, HEADS),
            in_specs=in_specs,
            out_specs=out_specs,
            scratch_shapes=[
                pltpu.VMEM((HEADS, residues, residues), F32),
                pltpu.VMEM((width, residues), BF16),
                pltpu.VMEM((HEADS, 1, residues), F32),
                pltpu.VMEM((4 * width, residues), BF16),
                pltpu.VMEM((residues, width), F32),
            ],
        ),
        out_shape=out_shape,
        compiler_params=pltpu.CompilerParams(vmem_limit_bytes=VMEM),
        cost_estimate=cost(22),
    )(order, *args)


def outer_kernel(
    left, right, pairs, back, table, table_t,
    total, left_grad, right_grad, table_grad,
    product, backed, *, scale, group,
):
    step = pl.program_id(0)
    rows = pairs.shape[0]
    cols = pairs.shape[1]
    channels = pairs.shape[2]
    width = left.shape[0] // rows
    wide = right.shape[1] // cols

    @pl.when(step == 0)
    def _():
        right_grad[...] = jnp.zeros_like(right_grad)
        table_grad[...] = jnp.zeros_like(table_grad)

    product[...] = dot(left[...], right[...], (1, 0)).astype(BF16)
    for first in range(0, rows, group):
        low = back[first : first + group].astype(BF16).reshape(group * cols, channels)
        both = jnp.concatenate(
            [
                jnp.concatenate(
                    [
                        product[(first + g) * width : (first + g + 1) * width, f * cols : (f + 1) * cols]
                        for f in range(wide)
                    ],
                    axis=0,
                )
                for g in range(group)
            ],
            axis=1,
        )
        out = dot(table_t[...], both, (1, 0)) * scale
        for g in range(group):
            total[first + g] = pairs[first + g] + out[:, g * cols : (g + 1) * cols].T
        table_grad[...] += dot(both, low, (1, 0)) * scale
        spread = dot(table[...], low, (1, 1)).astype(BF16)
        for g in range(group):
            for f in range(wide):
                backed[(first + g) * width : (first + g + 1) * width, f * cols : (f + 1) * cols] = spread[
                    f * width : (f + 1) * width, g * cols : (g + 1) * cols
                ]
    left_grad[...] = (dot(backed[...], right[...], (1, 1)) * scale).astype(BF16)
    right_grad[...] += dot(left[...], backed[...], (0, 0)) * scale


def outer_product(left, right, pairs, back, table, all_rows, block=8, group=2):
    rows, cols, channels = pairs.shape
    width = left.shape[0] // rows
    table_t = table.T
    by_row = lambda n: (n, 0, 0)
    whole = lambda n: (0, 0)
    return pl.pallas_call(
        functools.partial(outer_kernel, scale=1.0 / all_rows, group=group),
        grid=(rows // block,),
        in_specs=[
            pl.BlockSpec((block * width, left.shape[1]), lambda n: (n, 0)),
            pl.BlockSpec(right.shape, whole),
            pl.BlockSpec((block, cols, channels), by_row),
            pl.BlockSpec((block, cols, channels), by_row),
            pl.BlockSpec(table.shape, whole),
            pl.BlockSpec(table_t.shape, whole),
        ],
        out_specs=[
            pl.BlockSpec((block, cols, channels), by_row),
            pl.BlockSpec((block * width, left.shape[1]), lambda n: (n, 0)),
            pl.BlockSpec(right.shape, whole),
            pl.BlockSpec(table.shape, whole),
        ],
        out_shape=[
            jax.ShapeDtypeStruct(pairs.shape, F32),
            jax.ShapeDtypeStruct(left.shape, BF16),
            jax.ShapeDtypeStruct(right.shape, F32),
            jax.ShapeDtypeStruct(table.shape, F32),
        ],
        scratch_shapes=[
            pltpu.VMEM((block * width, right.shape[1]), BF16),
            pltpu.VMEM((block * width, right.shape[1]), BF16),
        ],
        cost_estimate=cost(29),
        compiler_params=pltpu.CompilerParams(vmem_limit_bytes=VMEM),
    )(left, right, pairs, back, table, table_t)


def outer_product_plain(left, right, pairs_back, table, all_rows):
    low = pairs_back.astype(BF16)
    product = mm("sei,sfj->eifj", left, right).astype(BF16)
    total = mm("eifj,efz->ijz", product, table) / all_rows
    table_grad = mm("eifj,ijz->efz", product, low) / all_rows
    back = mm("ijz,efz->eifj", low, table).astype(BF16)
    left_grad = mm("eifj,sfj->sei", back, right) / all_rows
    right_grad = mm("eifj,sei->sfj", back, left) / all_rows
    return total, table_grad, left_grad.astype(BF16), right_grad.astype(BF16)


def mm(spec, a, b):
    return jnp.einsum(spec, a, b, preferred_element_type=F32)


def pair_forward(pairs, gain, shift, bias_low):
    hat, _ = normalize(pairs)
    low = (hat * gain + shift).astype(BF16)
    return (mm("ijc,ch->hij", low, bias_low) * LOG2E).astype(BF16)


def pair_backward(pairs, pairs_back, gain, shift, bias_low, bias_grad):
    hat, rstd = normalize(pairs)
    low = (hat * gain + shift).astype(BF16)
    weight_grad = mm("ijc,hij->ch", low, bias_grad)
    in_grad = mm("hij,ch->ijc", bias_grad, bias_low)
    gain_grad = jnp.sum(in_grad * hat, axis=(0, 1))
    shift_grad = jnp.sum(in_grad, axis=(0, 1))
    return pairs_back + norm_backward(hat, rstd, gain, in_grad), weight_grad, gain_grad, shift_grad


MESH = pl.DeviceIdType.MESH
CORE, ACROSS, DOWN, CORNER = 1, 2, 4, 6


def place():
    return lax.axis_index("row"), lax.axis_index("head")


def flip(row, way):
    out = row
    for bit in (1, 2, 4):
        if way & bit:
            out = out + bit - 2 * bit * ((row // bit) % 2)
    return out


def greet(devices):
    barrier = pltpu.get_barrier_semaphore()
    for device in devices:
        pl.semaphore_signal(barrier, inc=1, device_id=device, device_id_type=MESH)
    pl.semaphore_wait(barrier, len(devices))


class Sends:
    def __init__(self, send_sem, recv_sem):
        self.send_sem, self.recv_sem, self.count, self.open = send_sem, recv_sem, 0, []

    def start(self, source, target, device):
        copy = pltpu.make_async_remote_copy(
            src_ref=source,
            dst_ref=target,
            send_sem=self.send_sem.at[self.count],
            recv_sem=self.recv_sem.at[self.count],
            device_id=device,
            device_id_type=MESH,
        )
        copy.start()
        self.count += 1
        self.open.append(copy)
        return copy

    def finish(self):
        for copy in self.open:
            copy.wait_send()


GATHER_SENDS = 6 + 3 + 31 + 3


def pair_bias_kernel(pairs, norm, weight, shard, bias, weights, block, low, local_sem, send_sem, recv_sem):
    row, head = place()
    rows, cols, channels = pairs.shape
    part = shard.shape[1] // 2
    core = row % 2
    beyond = [(head + k) % 4 for k in range(4)]
    behind = [(head + 4 - k) % 4 for k in range(4)]
    across, down, other = (flip(row, ACROSS), head), (flip(row, DOWN), head), (flip(row, CORE), head)
    greet([across, down, other] + [(row, beyond[k]) for k in (1, 2, 3)])
    sends = Sends(send_sem, recv_sem)

    def own_part(at, side):
        return weights.at[:, pl.ds(pl.multiple_of(at * 2 * part + side * part, part), part), :]

    half = shard.at[:, pl.ds(pl.multiple_of(core * part, part), part), :]
    keep = pltpu.make_async_copy(
        shard, weights.at[:, pl.ds(pl.multiple_of(head * 2 * part, 2 * part), 2 * part), :], local_sem.at[0]
    )
    keep.start()
    shards = [None] + [sends.start(half, own_part(head, core), (row, beyond[k])) for k in (1, 2, 3)]

    step = 8

    def norm_block(n, carry):
        first = pl.multiple_of(n * step, step)
        values = pairs[pl.ds(first, step)].reshape(step * cols, channels)
        center = values - jnp.mean(values, axis=-1, keepdims=True)
        rstd = lax.rsqrt(jnp.mean(center * center, axis=-1, keepdims=True) + 1e-05)
        normed = (center * rstd * norm[0:1] + norm[1:2]).astype(BF16)
        out = lax.dot_general(weight[...], normed, (((1,), (1,)), ((), ())), preferred_element_type=F32)
        for i in range(step):
            block[:, pl.ds(first + i, 1), :] = (out[:, i * cols : (i + 1) * cols] * LOG2E).reshape(
                HEADS, 1, cols
            )
        return carry

    lax.fori_loop(0, rows // step, norm_block, 0)
    low[...] = block[...].astype(BF16)

    mine = pltpu.make_async_copy(low, bias.at[row, head], local_sem.at[1])
    mine.start()
    stage = [None] * 4
    stage[0] = low
    along = [None] + [sends.start(low, bias.at[row, head], (row, beyond[k])) for k in (1, 2, 3)]
    from_across, from_down, from_corner, from_core = [None] * 4, [None] * 4, [None] * 4, []

    def spread(k, source):
        here = bias.at[row, behind[k]]
        from_across[k] = sends.start(source, here, across)
        from_down[k] = sends.start(source, here, down)
        from_core.append(sends.start(source, here, other))

    def relay(k):
        from_across[k].wait_recv()
        block_across = bias.at[flip(row, ACROSS), behind[k]]
        if k < 2:
            from_corner[k] = sends.start(block_across, block_across, down)
        from_core.append(sends.start(block_across, block_across, other))
        from_down[k].wait_recv()
        block_down = bias.at[flip(row, DOWN), behind[k]]
        if k >= 2:
            from_corner[k] = sends.start(block_down, block_down, across)
        from_core.append(sends.start(block_down, block_down, other))

    spread(0, low)
    for k in (1, 2, 3):
        along[k].wait_recv()
        spread(k, bias.at[row, behind[k]])
        relay(k - 1)
    relay(3)
    for k in range(4):
        from_corner[k].wait_recv()
        block_corner = bias.at[flip(row, CORNER), behind[k]]
        from_core.append(sends.start(block_corner, block_corner, other))
    for k in (1, 2, 3):
        shards[k].wait_recv()
        piece = own_part(behind[k], core)
        from_core.append(sends.start(piece, piece, other))
    for copy in from_core:
        copy.wait_recv()
    sends.finish()
    keep.wait()
    mine.wait()


def pair_bias(pairs, norm, weight, shard):
    rows, cols, channels = pairs.shape
    vmem = pl.BlockSpec(memory_space=pltpu.VMEM)
    hbm = pl.BlockSpec(memory_space=pl.ANY)
    return pl.pallas_call(
        pair_bias_kernel,
        out_shape=[
            jax.ShapeDtypeStruct((8, 4, HEADS, rows, cols), BF16),
            jax.ShapeDtypeStruct((shard.shape[0], 4 * shard.shape[1], shard.shape[2]), BF16),
        ],
        in_specs=[vmem, vmem, vmem, hbm],
        out_specs=[hbm, hbm],
        scratch_shapes=[
            pltpu.VMEM((HEADS, rows, cols), F32),
            pltpu.VMEM((HEADS, rows, cols), BF16),
            pltpu.SemaphoreType.DMA((2,)),
            pltpu.SemaphoreType.DMA((GATHER_SENDS,)),
            pltpu.SemaphoreType.DMA((GATHER_SENDS,)),
        ],
        cost_estimate=cost(34),
        compiler_params=pltpu.CompilerParams(
            collective_id=0, has_side_effects=True, vmem_limit_bytes=VMEM
        ),
    )(pairs, norm, weight, shard)


SIDES_SENDS = 6 + 28 + 16 + 12


def sides_kernel(left, right, left_all, right_all, left_on, right_on, local_sem, send_sem, recv_sem):
    row, head = place()
    beyond = [(head + k) % 4 for k in range(4)]
    behind = [(head + 4 - k) % 4 for k in range(4)]
    plane = [(flip(row, way), head) for way in range(8)]
    greet(plane[1:] + [(row, beyond[k]) for k in (1, 2, 3)])
    sends = Sends(send_sem, recv_sem)
    from_left, from_right = [None] * 4, [None] * 4
    for k in (1, 2, 3):
        from_right[k] = sends.start(right.at[beyond[k]], right_on.at[k], (row, beyond[k]))
        from_left[k] = sends.start(left, left_on.at[k], (row, beyond[k]))
    locals_ = []
    arrive, onward = [], []
    for k in range(4):
        if k:
            from_right[k].wait_recv()
        ours = right_on.at[k] if k else right.at[head]
        for way in (ACROSS, DOWN, CORNER):
            onward.append((way, k, sends.start(ours, right_all.at[row, behind[k]], plane[way])))
        arrive.append(sends.start(ours, right_all.at[row, behind[k]], plane[CORE]))
        copy = pltpu.make_async_copy(ours, right_all.at[row, behind[k]], local_sem.at[2 * k])
        copy.start()
        locals_.append(copy)
        if k:
            from_left[k].wait_recv()
        ours = left_on.at[k] if k else left
        for way in (2, 4, 6, 3, 5, 7, 1):
            arrive.append(sends.start(ours.at[plane[way][0]], left_all.at[row, behind[k]], plane[way]))
        copy = pltpu.make_async_copy(ours.at[row], left_all.at[row, behind[k]], local_sem.at[2 * k + 1])
        copy.start()
        locals_.append(copy)
    for way, k, copy in onward:
        copy.wait_recv()
        block = right_all.at[plane[way][0], behind[k]]
        arrive.append(sends.start(block, block, plane[CORE]))
    for copy in arrive:
        copy.wait_recv()
    sends.finish()
    for copy in locals_:
        copy.wait()


def share_sides(left, right):
    hbm = pl.BlockSpec(memory_space=pl.ANY)
    return pl.pallas_call(
        sides_kernel,
        out_shape=[
            jax.ShapeDtypeStruct((8, 4) + left.shape[1:], BF16),
            jax.ShapeDtypeStruct((8, 4) + right.shape[1:], BF16),
        ],
        in_specs=[hbm, hbm],
        out_specs=[hbm, hbm],
        scratch_shapes=[
            pltpu.VMEM((4,) + left.shape, BF16),
            pltpu.VMEM((4,) + right.shape[1:], BF16),
            pltpu.SemaphoreType.DMA((8,)),
            pltpu.SemaphoreType.DMA((SIDES_SENDS,)),
            pltpu.SemaphoreType.DMA((SIDES_SENDS,)),
        ],
        cost_estimate=cost(24),
        compiler_params=pltpu.CompilerParams(
            collective_id=1, has_side_effects=True, vmem_limit_bytes=VMEM
        ),
    )(left, right)


RETURN_SENDS = 1 + 7 + 3 + 6


def return_kernel(
    left, right, left_out, right_out, right_core, left_in, right_in, left_on, right_sum, local_sem, send_sem, recv_sem
):
    row, head = place()
    beyond = [(head + k) % 4 for k in range(4)]
    behind = [(head + 4 - k) % 4 for k in range(4)]
    plane = [(flip(row, way), head) for way in range(8)]
    greet(plane[1:] + [(row, beyond[k]) for k in (1, 2, 3)])
    sends = Sends(send_sem, recv_sem)
    core = row % 2
    swap = sends.start(right.at[:, 1 - core], right_core, plane[CORE])
    lefts = [sends.start(left.at[plane[way][0]], left_in.at[row], plane[way]) for way in (2, 4, 6, 3, 5, 7, 1)]
    copy = pltpu.make_async_copy(left.at[row], left_in.at[row], local_sem.at[0])
    copy.start()
    swap.wait_recv()
    chip = row // 2
    blocks = right.shape[2]
    for n in range(right.shape[0]):
        for b in range(blocks):
            right_sum[n, b] = (
                right[n, core, b].astype(F32) + right_core[n, b].astype(F32)
            ).astype(BF16)
    rights = []
    for slot, way in enumerate((ACROSS, DOWN, CORNER)):
        rights.append(sends.start(right_sum.at[plane[way][0] // 2], right_in.at[slot], plane[way]))
    for arrival in lefts:
        arrival.wait_recv()
    copy.wait()
    on = []
    for k in (1, 2, 3):
        on.append(sends.start(left_in.at[:, beyond[k]], left_on.at[k - 1], (row, beyond[k])))
    for arrival in rights:
        arrival.wait_recv()
    for b in range(blocks):
        total = right_sum[chip, b].astype(F32)
        for slot in range(3):
            total = total + right_in[slot, b].astype(F32)
        right_core[0, b] = total.astype(BF16)
    last = []
    for k in (1, 2, 3):
        last.append(sends.start(right_core.at[0, beyond[k]], right_out.at[head], (row, beyond[k])))
    mine = pltpu.make_async_copy(right_core.at[0, head], right_out.at[head], local_sem.at[1])
    mine.start()
    for arrival in on:
        arrival.wait_recv()
    for n in range(left_in.shape[0]):
        total = left_in[n, head].astype(F32)
        for k in range(3):
            total = total + left_on[k, n].astype(F32)
        left_out[n] = total.astype(BF16)
    for arrival in last:
        arrival.wait_recv()
    mine.wait()
    sends.finish()


def return_sides(left, right):
    vmem = pl.BlockSpec(memory_space=pltpu.VMEM)
    piece_left, piece_right = left.shape[2:], right.shape[2:]
    return pl.pallas_call(
        return_kernel,
        out_shape=[
            jax.ShapeDtypeStruct((8,) + piece_left, BF16),
            jax.ShapeDtypeStruct((4,) + piece_right, BF16),
        ],
        in_specs=[vmem, vmem],
        out_specs=[vmem, vmem],
        scratch_shapes=[
            pltpu.VMEM((4, 4) + piece_right, BF16),
            pltpu.VMEM((8, 4) + piece_left, BF16),
            pltpu.VMEM((3, 4) + piece_right, BF16),
            pltpu.VMEM((3, 8) + piece_left, BF16),
            pltpu.VMEM((4, 4) + piece_right, BF16),
            pltpu.SemaphoreType.DMA((2,)),
            pltpu.SemaphoreType.DMA((RETURN_SENDS,)),
            pltpu.SemaphoreType.DMA((RETURN_SENDS,)),
        ],
        cost_estimate=cost(27),
        compiler_params=pltpu.CompilerParams(
            collective_id=2, has_side_effects=True, vmem_limit_bytes=VMEM
        ),
    )(left, right.reshape((4, 2) + right.shape[1:]))


SUM_SENDS = 4 + 4 + 8 + 3 + 1 + 3 + 3


def sum_kernel(
    grads, parts, out, piece,
    swapped, chip_sum, by_across, by_down, from_across, from_down, down_sum, line_in,
    part_swapped, part_sum, part_plane, part_down, part_line,
    send_sem, recv_sem,
):
    row, head = place()
    beyond = [(head + k) % 4 for k in range(4)]
    core, chip = row % 2, row // 2
    ways = (CORNER, ACROSS, DOWN)
    plane = [(flip(row, way), head) for way in range(8)]
    other, across, down = plane[CORE], plane[ACROSS], plane[DOWN]
    greet([plane[way] for way in (CORE,) + ways] + [(row, beyond[k]) for k in (1, 2, 3)])
    sends = Sends(send_sem, recv_sem)
    chips = [plane[way][0] // 2 for way in ways] + [chip]
    swaps = [sends.start(grads.at[n, 1 - core], swapped.at[slot], other) for slot, n in enumerate(chips)]
    part_swap = sends.start(parts.at[1 - core], part_swapped, other)
    first, second = (2, 1), (3, 0)

    def add(slot, k):
        z = beyond[k]
        chip_sum[slot, k] = (
            grads[chips[slot], core, z].astype(F32) + swapped[slot, z].astype(F32)
        ).astype(BF16)

    swaps[0].wait_recv()
    relays_across, relays_down = [], []
    for n in range(2):
        add(0, first[n])
        relays_across.append(sends.start(chip_sum.at[0, first[n]], by_across.at[n], across))
        add(0, second[n])
        relays_down.append(sends.start(chip_sum.at[0, second[n]], by_down.at[n], down))
    last_across, last_down = [None] * 4, [None] * 4
    swaps[1].wait_recv()
    for k in first:
        add(1, k)
        last_across[k] = sends.start(chip_sum.at[1, k], from_across.at[k], across)
    swaps[2].wait_recv()
    for k in second:
        add(2, k)
        last_down[k] = sends.start(chip_sum.at[2, k], from_down.at[k], down)
    for n in range(2):
        add(1, second[n])
        add(2, first[n])
        relays_across[n].wait_recv()
        k = first[n]
        chip_sum[2, k] = (chip_sum[2, k].astype(F32) + by_across[n].astype(F32)).astype(BF16)
        last_down[k] = sends.start(chip_sum.at[2, k], from_down.at[k], down)
        relays_down[n].wait_recv()
        k = second[n]
        chip_sum[1, k] = (chip_sum[1, k].astype(F32) + by_down[n].astype(F32)).astype(BF16)
        last_across[k] = sends.start(chip_sum.at[1, k], from_across.at[k], across)
    part_swap.wait_recv()
    part_arrive = []
    for slot, n in enumerate(chips):
        for z in range(4):
            part_sum[slot, z] = (parts[core, n, z].astype(F32) + part_swapped[n, z].astype(F32)).astype(BF16)
        if slot < 3:
            part_arrive.append(sends.start(part_sum.at[slot], part_plane.at[slot], plane[ways[slot]]))
    swaps[3].wait_recv()
    line = []
    for k in first + second:
        add(3, k)
        last_across[k].wait_recv()
        last_down[k].wait_recv()
        total = chip_sum[3, k].astype(F32) + from_across[k].astype(F32) + from_down[k].astype(F32)
        if k:
            down_sum[k - 1] = total.astype(BF16)
            line.append(sends.start(down_sum.at[k - 1], line_in.at[k - 1], (row, beyond[k])))
        else:
            out[...] = total
    for copy in part_arrive:
        copy.wait_recv()
    for z in range(4):
        total = part_sum[3, z].astype(F32)
        for slot in range(3):
            total = total + part_plane[slot, z].astype(F32)
        part_down[z] = total.astype(BF16)
    part_arrive = [
        sends.start(part_down.at[beyond[k]], part_line.at[k - 1], (row, beyond[k])) for k in (1, 2, 3)
    ]
    for slot, copy in zip((1, 0, 2), line):
        copy.wait_recv()
        out[...] += line_in[slot].astype(F32)
    total = part_down[head].astype(F32)
    for slot, copy in enumerate(part_arrive):
        copy.wait_recv()
        total = total + part_line[slot].astype(F32)
    piece[...] = total.astype(BF16)
    sends.finish()


def sum_gradients(grads, parts):
    block = grads.shape[2:]
    lines = block[0] * block[1]
    rows, cols = parts.shape
    share = rows // 32
    vmem = pl.BlockSpec(memory_space=pltpu.VMEM)
    wide = lambda *first: pltpu.VMEM(first + (lines, block[2]), BF16)
    thin = lambda *first: pltpu.VMEM(first + (share, cols), BF16)
    out, piece = pl.pallas_call(
        sum_kernel,
        out_shape=[
            jax.ShapeDtypeStruct((lines, block[2]), F32),
            jax.ShapeDtypeStruct((share, cols), BF16),
        ],
        in_specs=[vmem, vmem],
        out_specs=[vmem, vmem],
        scratch_shapes=[
            wide(4, 4), wide(4, 4), wide(2), wide(2), wide(4), wide(4), wide(3), wide(3),
            thin(4, 4), thin(4, 4), thin(3, 4), thin(4), thin(3),
            pltpu.SemaphoreType.DMA((SUM_SENDS,)),
            pltpu.SemaphoreType.DMA((SUM_SENDS,)),
        ],
        compiler_params=pltpu.CompilerParams(
            collective_id=3, has_side_effects=True, vmem_limit_bytes=VMEM
        ),
        cost_estimate=cost(40),
    )(grads.reshape(4, 2, 4, lines, block[2]), parts.reshape(2, 4, 4, share, cols))
    return out.reshape(block), piece


SPREAD_SENDS = 3 + 12 + 16 + 3 + 7


def spread_kernel(
    piece, small, out, total, line_in, line_sum, plane_in, local_sem, send_sem, recv_sem
):
    row, head = place()
    beyond = [(head + k) % 4 for k in range(4)]
    behind = [(head + 4 - k) % 4 for k in range(4)]
    core, chip = row % 2, row // 2
    ways = (CORNER, ACROSS, DOWN)
    plane = [(flip(row, way), head) for way in range(8)]
    other = plane[CORE]
    greet(plane[1:] + [(row, beyond[k]) for k in (1, 2, 3)])
    sends = Sends(send_sem, recv_sem)
    small_line = [sends.start(small, line_in.at[head], (row, beyond[k])) for k in (1, 2, 3)]
    line = [None] + [sends.start(piece, out.at[core, chip, head], (row, beyond[k])) for k in (1, 2, 3)]
    mine = pltpu.make_async_copy(piece, out.at[core, chip, head], local_sem)
    mine.start()
    line_in[head] = small[...]
    across, end = [], []

    def forward(k):
        here = out.at[core, chip, behind[k]]
        source = here if k else piece
        for way in ways:
            across.append((plane[way][0] // 2, k, sends.start(source, here, plane[way])))
        end.append(sends.start(source, here, other))

    forward(0)
    for copy in small_line:
        copy.wait_recv()
    line_sum[...] = (line_in[0] + line_in[1]) + (line_in[2] + line_in[3])
    small_plane = [sends.start(line_sum, plane_in.at[row], plane[way]) for way in range(1, 8)]
    plane_in[row] = line_sum[...]
    for k in (1, 2, 3):
        line[k].wait_recv()
        forward(k)
    for n, k, copy in across:
        copy.wait_recv()
        block = out.at[core, n, behind[k]]
        end.append(sends.start(block, block, other))
    for copy in small_plane:
        copy.wait_recv()
    summed = plane_in[0]
    for n in range(1, 8):
        summed = summed + plane_in[n]
    total[...] = summed
    for copy in end:
        copy.wait_recv()
    mine.wait()
    sends.finish()


def spread_gradients(piece, small):
    lines, cols = piece.shape
    vmem = pl.BlockSpec(memory_space=pltpu.VMEM)
    out, total = pl.pallas_call(
        spread_kernel,
        out_shape=[
            jax.ShapeDtypeStruct((2, 4, 4, lines, cols), BF16),
            jax.ShapeDtypeStruct(small.shape, F32),
        ],
        in_specs=[vmem, vmem],
        out_specs=[vmem, vmem],
        scratch_shapes=[
            pltpu.VMEM((4,) + small.shape, F32),
            pltpu.VMEM(small.shape, F32),
            pltpu.VMEM((8,) + small.shape, F32),
            pltpu.SemaphoreType.DMA,
            pltpu.SemaphoreType.DMA((SPREAD_SENDS,)),
            pltpu.SemaphoreType.DMA((SPREAD_SENDS,)),
        ],
        compiler_params=pltpu.CompilerParams(
            collective_id=4, has_side_effects=True, vmem_limit_bytes=VMEM
        ),
        cost_estimate=cost(15),
    )(piece, small)
    return out.reshape(32 * lines, cols), total


def add_pieces(step, base, pieces, out):
    for n, piece in enumerate(pieces):
        @pl.when(step == n)
        def _():
            out[...] = base[...] + piece[...].astype(F32)


def added_specs(base, pieces):
    block = pieces[0].shape
    by_order = pl.BlockSpec(
        block, lambda n, order: (order[jnp.minimum(n, len(pieces) - 1) * block[0]] // block[0], 0, 0)
    )
    return by_order, [by_order] + [pl.BlockSpec(block, lambda n, order: (0, 0, 0))] * len(pieces)


def pair_backward_kernel(order, pairs, back, grads, norm, weight, base, *refs):
    pieces, (out, small, changed) = refs[:-3], refs[-3:]
    step = pl.program_id(0)
    rows, cols, channels = pairs.shape
    add_pieces(step, base, pieces, changed)

    @pl.when(step == 0)
    def _():
        small[...] = jnp.zeros_like(small)

    values = pairs[...].reshape(rows * cols, channels)
    hat, rstd = normalize(values)
    low = (hat * norm[0:1] + norm[1:2]).astype(BF16)
    bias = jnp.concatenate([grads[:, i, :] for i in range(rows)], axis=1).astype(BF16)
    small[0:HEADS] += dot(bias, low, (1, 0))
    in_grad = dot(bias, weight[...], (0, 0))
    small[HEADS : HEADS + 1] += jnp.sum(in_grad * hat, axis=0, keepdims=True)
    small[HEADS + 1 : HEADS + 2] += jnp.sum(in_grad, axis=0, keepdims=True)
    change = norm_backward(hat, rstd, norm[0:1], in_grad)
    out[...] = back[...] + change.reshape(rows, cols, channels)


def pair_norm_backward(order, pairs, back, grads, norm, weight, base, pieces, steps=8):
    rows, cols, channels = pairs.shape
    block = rows // steps
    by_row = lambda n, order: (n, 0, 0)
    whole = lambda n, order: (0, 0)
    by_order, added = added_specs(base, pieces)
    grads = grads.reshape(HEADS, steps, block, cols)
    return pl.pallas_call(
        pair_backward_kernel,
        grid_spec=pltpu.PrefetchScalarGridSpec(
            num_scalar_prefetch=1,
            grid=(steps,),
            in_specs=[
                pl.BlockSpec((block, cols, channels), by_row),
                pl.BlockSpec((block, cols, channels), by_row),
                pl.BlockSpec((HEADS, None, block, cols), lambda n, order: (0, n, 0, 0)),
                pl.BlockSpec(norm.shape, whole),
                pl.BlockSpec(weight.shape, whole),
            ]
            + added,
            out_specs=[
                pl.BlockSpec((block, cols, channels), by_row),
                pl.BlockSpec((2 * HEADS, channels), whole),
                by_order,
            ],
        ),
        out_shape=[
            jax.ShapeDtypeStruct(pairs.shape, F32),
            jax.ShapeDtypeStruct((2 * HEADS, channels), F32),
            jax.ShapeDtypeStruct(base.shape, F32),
        ],
        compiler_params=pltpu.CompilerParams(vmem_limit_bytes=VMEM),
        cost_estimate=cost(9),
    )(order, pairs, back, grads, norm, weight, base, *pieces)


def add_kernel(place_ref, base, piece, *refs):
    refs[-1][...] = base[...] + piece[...].astype(F32)


def add_rows(at, base, piece, into=None):
    own = piece.shape[0]
    block = (1,) + piece.shape[1:]
    spread = lambda n, at: (at[0] * own + n, 0, 0)
    return pl.pallas_call(
        add_kernel,
        grid_spec=pltpu.PrefetchScalarGridSpec(
            num_scalar_prefetch=1,
            grid=(own,),
            in_specs=[pl.BlockSpec(block, spread), pl.BlockSpec(block, lambda n, at: (n, 0, 0))]
            + ([] if into is None else [pl.BlockSpec(memory_space=pl.ANY)]),
            out_specs=pl.BlockSpec(block, spread),
        ),
        out_shape=jax.ShapeDtypeStruct(base.shape, F32),
        input_output_aliases={} if into is None else {3: 0},
        cost_estimate=cost(2),
    )(*((at, base, piece) if into is None else (at, base, piece, into)))


def hop(piece):
    count = lax.axis_size("head")
    return lax.ppermute(piece, "head", [(i, (i + 1) % count) for i in range(count)])


def together(moved, *values):
    return lax.optimization_barrier((moved,) + values)


def adam_kernel(at, packed, pair_side, *refs, rates, pieces):
    olds, base, adds, news = refs[:18], refs[18], refs[19 : 19 + pieces], refs[20 + pieces : 38 + pieces]
    changed, table = refs[38 + pieces :]
    step = pl.program_id(0)
    add_pieces(step, base, adds, changed)

    @pl.when(step == 0)
    def _():
        adam_step(at, packed, pair_side, olds, news, table, rates)


def adam_step(at, packed, pair_side, olds, news, table, rates):
    norms, heads_in, heads_out, bias_weight, outer_in, outer_out = [olds[3 * n : 3 * n + 3] for n in range(6)]
    count, local, all_heads = heads_in[0].shape
    sides, size = outer_in[0].shape[:2]

    def rows(first, lines):
        return packed[pl.ds(first, lines), :].astype(F32)

    def pair_of(first, offset, lines, span):
        return jnp.concatenate([rows(first + offset, lines), rows(first + span + offset, lines)], axis=1)

    def update(n, index, grad):
        weight, moment_one, moment_two = [ref[index] for ref in olds[3 * n : 3 * n + 3]]
        for ref, new in zip(
            news[3 * n : 3 * n + 3], adam_update(weight, grad, moment_one, moment_two, rates[n])
        ):
            ref[index] = new

    mine = pl.multiple_of(at[4], local)
    span = count * all_heads
    for k in range(count):
        update(1, k, pair_of(0, k * all_heads + mine, local, span))
    first = 2 * span
    update(2, slice(None), pair_of(first, mine, local, all_heads))
    first += 2 * all_heads
    for k in range(sides):
        update(4, k, pair_of(first, k * size, size, sides * size))
    first += 2 * sides * size
    table[...] = rows(first, size * size)
    for e in range(size):
        update(5, slice(e * size, (e + 1) * size), table[pl.ds(e, size, stride=size), :])
    first += size * size
    low = rows(first, 8)
    pair = pair_side[...]
    lines = [
        jnp.concatenate([low[n : n + 1], low[n + 4 : n + 5], low[n + 2 : n + 3], low[n + 6 : n + 7], pair[HEADS + n : HEADS + n + 1]], axis=1)
        for n in range(2)
    ]
    update(0, slice(None), jnp.concatenate(lines, axis=0))
    update(3, slice(None), pair[:HEADS])


def adam_all(at, packed, pair_side, olds, rates, base, pieces, into):
    turned = (1, 3, 4)
    flat = [array.swapaxes(-1, -2) if n in turned else array for n, triple in enumerate(olds) for array in triple]
    size = olds[4][0].shape[2]
    by_order, added = added_specs(base, pieces)
    whole = lambda array: pl.BlockSpec(array.shape, lambda n, at: (0,) * array.ndim)
    *news, changed = pl.pallas_call(
        functools.partial(adam_kernel, rates=rates, pieces=len(pieces)),
        grid_spec=pltpu.PrefetchScalarGridSpec(
            num_scalar_prefetch=1,
            grid=(len(pieces),),
            in_specs=[whole(array) for array in [packed, pair_side] + flat]
            + added
            + [pl.BlockSpec(memory_space=pl.ANY)],
            out_specs=[whole(array) for array in flat] + [by_order],
            scratch_shapes=[pltpu.VMEM((size * size, packed.shape[1]), F32)],
        ),
        out_shape=[jax.ShapeDtypeStruct(array.shape, F32) for array in flat + [base]],
        input_output_aliases={3 + len(flat) + 1 + len(pieces): len(flat)},
        compiler_params=pltpu.CompilerParams(vmem_limit_bytes=VMEM),
        cost_estimate=cost(5),
    )(at, packed, pair_side, *flat, base, *pieces, into)
    news = [array.swapaxes(-1, -2) if n // 3 in turned else array for n, array in enumerate(news)]
    return news + [changed]


def halves(array):
    return jnp.concatenate([array[:, :128], array[:, 128:]])


def per_device(
    alignment,
    pairs,
    residue_mask,
    row_mask,
    alignment_back,
    pairs_back,
    norm_scales,
    heads_in,
    heads_out,
    bias_weight,
    outer_in,
    outer_out,
    first_norms,
    second_norms,
    first_heads_in,
    second_heads_in,
    first_heads_out,
    second_heads_out,
    first_bias_weight,
    second_bias_weight,
    first_outer_in,
    second_outer_in,
    first_outer_out,
    second_outer_out,
):
    row_count = lax.axis_size("row")
    head_count = lax.axis_size("head")
    head_index = lax.axis_index("head")
    devices = row_count * head_count
    rows_here, residues, width = alignment.shape
    pair_rows, pair_cols, pair_width = pairs.shape
    size = width // HEADS
    outer_width = outer_in.shape[2]
    all_rows = rows_here * row_count
    own = rows_here // head_count
    start = head_index * own
    scales = norm_scales[:, : 2 * width].reshape(2, 2, width).swapaxes(0, 1).reshape(4, width)
    pair_gain = norm_scales[0:1, 2 * width :]
    pair_shift = norm_scales[1:2, 2 * width :]
    residue_live = residue_mask.astype(F32)
    key_mask = ((residue_live - 1.0) * (1e9 * LOG2E))[:, None]
    live = lax.dynamic_slice_in_dim(row_mask, start, own, 0).astype(F32)[:, None] * residue_live[None]
    bias_low = bias_weight.astype(BF16)

    fast = (row_count, head_count, pair_cols, own * outer_width) == (8, 4, 128, 128)

    local = heads_in.shape[2]
    shard = jnp.concatenate([heads_in.astype(BF16).swapaxes(1, 2), heads_out.astype(BF16)[None]])
    outer_t = outer_in.astype(BF16).swapaxes(1, 2).reshape(2 * outer_width, width)
    table = outer_out.astype(BF16).reshape(outer_width, outer_width, pair_width)
    if fast:
        bias, weights = pair_bias(pairs, norm_scales[:, 2 * width :], bias_low.T, shard)
    else:
        weights = lax.all_gather(shard, "head", axis=1, tiled=True)
        bias = pair_forward(pairs, pair_gain, pair_shift, bias_low)
        bias = lax.all_gather(bias, "head", axis=2, tiled=True)
        bias = lax.all_gather(bias, "row", axis=1, tiled=True)[None, None]
    in_t = weights[:4].reshape(4 * width, width)
    out_low = weights[4]

    update, sides, kept = attention_forward(
        start.astype(jnp.int32)[None], alignment, scales, in_t, out_low, outer_t, bias, key_mask, live[:, None]
    )

    left, right = sides[:, :outer_width], sides[:, outer_width:]
    if fast:
        left_all, right_all = share_sides(
            left.reshape(own * outer_width, residues).T.reshape(row_count, pair_rows, own * outer_width),
            right.reshape(own * outer_width, head_count, pair_cols).swapaxes(0, 1),
        )
        update, left_all, right_all = together(update, left_all, right_all)
        updates = [update, hop(update)]
        left_all = left_all.reshape(devices, pair_rows, own, outer_width).transpose(1, 3, 0, 2)
        pairs_new, left_grad, right_grad, table_grad = outer_product(
            left_all.reshape(pair_rows * outer_width, all_rows),
            right_all.reshape(all_rows, outer_width * pair_cols),
            pairs,
            pairs_back,
            table.swapaxes(0, 1).reshape(outer_width * outer_width, pair_width),
            all_rows,
        )
        left_grad = left_grad.reshape(pair_rows, outer_width, devices, own).transpose(2, 0, 3, 1)
        updates[1], left_grad, right_grad = together(updates[1], left_grad, right_grad)
        updates.append(hop(updates[1]))
        left_total, right_total = return_sides(
            left_grad.reshape(row_count, head_count, pair_rows, own * outer_width),
            right_grad.astype(BF16).reshape(row_count, head_count, own * outer_width, pair_cols),
        )
        updates[2], left_total, right_total = together(updates[2], left_total, right_total)
        updates.append(hop(updates[2]))
        left_total = left_total.reshape(residues, own * outer_width).T
        right_total = right_total.swapaxes(0, 1)
    else:
        updates = [update]
        for _ in range(head_count - 1):
            updates.append(hop(updates[-1]))
        left = left.reshape(own, outer_width, row_count, pair_rows).transpose(2, 0, 1, 3)
        right = right.reshape(own, outer_width, head_count, pair_cols).transpose(2, 0, 1, 3)
        both = (row_count, head_count, own, outer_width)
        send = jnp.concatenate(
            [
                jnp.broadcast_to(left[:, None], both + (pair_rows,)),
                jnp.broadcast_to(right[None], both + (pair_cols,)),
            ],
            axis=4,
        )
        flat = (devices, own, outer_width, pair_rows + pair_cols)
        got = lax.all_to_all(send.reshape(flat), EVERY, split_axis=0, concat_axis=0, tiled=True)
        got = got.reshape(all_rows, outer_width, pair_rows + pair_cols)
        total, table_grad, left_grad, right_grad = outer_product_plain(
            got[:, :, :pair_rows], got[:, :, pair_rows:], pairs_back, table, all_rows
        )
        pairs_new = pairs + total
        send = jnp.concatenate([left_grad, right_grad], axis=2).reshape(flat)
        got = lax.all_to_all(send, EVERY, split_axis=0, concat_axis=0, tiled=True)
        got = got.reshape(both + (pair_rows + pair_cols,)).astype(F32)
        left_total = jnp.sum(got[..., :pair_rows], axis=1).transpose(1, 2, 0, 3)
        right_total = jnp.sum(got[..., pair_rows:], axis=0).transpose(1, 2, 0, 3)
    sides_grad = jnp.concatenate(
        [
            left_total.reshape(own, outer_width, residues),
            right_total.reshape(own, outer_width, residues),
        ],
        axis=1,
    )
    sides_grad = (sides_grad * live[:, None, :]).astype(BF16)

    turns = (head_index + head_count - jnp.arange(head_count, dtype=jnp.int32)) % head_count
    order = (turns[:, None] * own + jnp.arange(own, dtype=jnp.int32)[None]).reshape(-1)
    half = own // 2

    def mine(first, hops, second, more):
        parts = [(first, step) for step in hops] + [(second, step) for step in more]
        return jnp.concatenate([order[step * own + n * half : step * own + (n + 1) * half] for n, step in parts])

    backward = functools.partial(
        attention_backward,
        order, alignment, update, alignment_back, scales, in_t, out_low, outer_t, sides_grad, kept, bias.shape,
    )
    part, bias_grad, *early = backward(first=0, own=half)
    updates[3:], (bias_grad, part) = together(updates[3:], (bias_grad, part))
    changes = [[part, hop(part)]]
    alignment_new, part, bias_grad, *late = backward(first=half, own=half, earlier=bias_grad, pieces=updates)
    if fast:
        changes[0][1], bias_grad, part, early, late = together(changes[0][1], bias_grad, part, early, late)
        sums = [one + two for one, two in zip(early, late)]
        changes[0].append(hop(changes[0][1]))
        changes.append([part, hop(part)])
        packed = [halves(sums[0]), halves(sums[1]), halves(sums[2]), table_grad, halves(sums[3])]
        rest = -sum(array.shape[0] for array in packed) % 512
        packed = jnp.concatenate([array.astype(BF16) for array in packed] + [jnp.zeros((rest, 128), BF16)])
        bias_grad, packed = sum_gradients(bias_grad, packed)
        changes[0][2], changes[1][1], bias_grad = together(changes[0][2], changes[1][1], bias_grad)
        changes[0].append(hop(changes[0][2]))
        changes[1].append(hop(changes[1][1]))
        pairs_grad, pair_side, alignment_grad = pair_norm_backward(
            mine(0, (0, 1, 2), 1, (0, 1)),
            pairs,
            pairs_back,
            bias_grad,
            norm_scales[:, 2 * width :],
            bias_low.T,
            alignment_back,
            changes[0][:3] + changes[1][:2],
        )
        packed, pair_side = spread_gradients(packed, pair_side)
        changes[0][3], changes[1][2], packed = together(changes[0][3], changes[1][2], packed)
        changes[1].append(hop(changes[1][2]))
    else:
        sums = [one + two for one, two in zip(early, late)]
        sums = (sums[0], sums[1], sums[2], table_grad, sums[3])
        for _ in range(head_count - 2):
            changes[0].append(hop(changes[0][-1]))
        changes.append([part])
        for _ in range(head_count - 1):
            changes[1].append(hop(changes[1][-1]))
        bias_grad = lax.psum_scatter(bias_grad[0, 0], "row", scatter_dimension=1, tiled=True)
        bias_grad = lax.psum_scatter(bias_grad, "head", scatter_dimension=2, tiled=True)
        pairs_grad, bias_weight_grad, pair_gain_grad, pair_shift_grad = pair_backward(
            pairs, pairs_back, pair_gain, pair_shift, bias_low, bias_grad
        )
        sums, bias_weight_total, pair_norms_total = lax.psum(
            (sums, bias_weight_grad, jnp.stack([pair_gain_grad, pair_shift_grad])), EVERY
        )
    olds = (
        (norm_scales, first_norms, second_norms),
        (heads_in, first_heads_in, second_heads_in),
        (heads_out, first_heads_out, second_heads_out),
        (bias_weight, first_bias_weight, second_bias_weight),
        (outer_in, first_outer_in, second_outer_in),
        (outer_out, first_outer_out, second_outer_out),
    )
    rates = (
        0.5,
        width ** (-0.5),
        max(2 * HEADS * size // residues, 1) ** (-0.5),
        pair_width ** (-0.5),
        width ** (-0.5),
        max(outer_width * outer_width // all_rows, 1) ** (-0.5),
    )
    if fast:
        at = (head_index * local).astype(jnp.int32)[None]
        *news, alignment_grad = adam_all(
            jnp.concatenate([mine(0, (3,), 1, (2,)), at]),
            packed, pair_side, olds, rates, alignment_back, [changes[0][3], changes[1][2]], alignment_grad,
        )
        at = (turns[3] * 2 + 1)[None]
        alignment_grad = add_rows(at, alignment_back, changes[1][3], alignment_grad)
        return (alignment_new, pairs_new, alignment_grad, pairs_grad, *news)
    alignment_grad = None
    for step in range(head_count):
        for n in range(2):
            at = (turns[step] * 2 + n)[None]
            alignment_grad = add_rows(at, alignment_back, changes[n][step], alignment_grad)
    heads_in_total = lax.dynamic_slice_in_dim(
        sums[0].reshape(4, width, width), head_index * local, local, 1
    ).swapaxes(1, 2)
    heads_out_total = lax.dynamic_slice_in_dim(sums[1], head_index * local, local, 0)
    outer_in_total = sums[2].reshape(2, outer_width, width).swapaxes(1, 2)
    table_total = sums[3].reshape(outer_width * outer_width, pair_width)
    norms_total = jnp.concatenate(
        [sums[4].reshape(2, 2, width).swapaxes(0, 1).reshape(2, 2 * width), pair_norms_total], axis=1
    )
    totals = (norms_total, heads_in_total, heads_out_total, bias_weight_total, outer_in_total, table_total)
    news = []
    for (weight, moment_one, moment_two), total, rate in zip(olds, totals, rates):
        news += adam_update(weight, total, moment_one, moment_two, rate)
    return (alignment_new, pairs_new, alignment_grad, pairs_grad, *news)


def solution(mesh):
    row_msa = P("row", None, None)
    pair = P("row", "head", None)
    columns = P(None, None, "head")
    lines = P("head", None)
    in_specs = (
        (row_msa, pair, P(), P("row"), row_msa, pair, P(), columns, lines)
        + (P(),) * 5
        + (columns,) * 2
        + (lines,) * 2
        + (P(),) * 6
    )
    out_specs = (row_msa, pair, row_msa, pair) + (P(),) * 3 + (columns,) * 3 + (lines,) * 3 + (P(),) * 9
    return jax.shard_map(
        per_device, mesh=mesh, in_specs=in_specs, out_specs=out_specs, check_vma=False
    )
```

```python
import functools

import jax
import jax.numpy as jnp
from jax import lax
from jax.experimental import pallas as pl
from jax.experimental.pallas import tpu as pltpu
from jax.sharding import PartitionSpec as P

HEADS = 8
STEP = 10
F32 = jnp.float32
BF16 = jnp.bfloat16
LOG2E = 1.4426950408889634
VMEM = 56 << 20
EVERY = ("row", "head")


def adam_update(weight, gradient, moment_one, moment_two, step_rate):
    first_new = 0.9 * moment_one + 0.1 * gradient
    second_new = 0.999 * moment_two + 0.001 * gradient * gradient
    first_hat = first_new / (1.0 - 0.9**STEP)
    second_hat = second_new / (1.0 - 0.999**STEP)
    updated = weight - step_rate * (first_hat / (jnp.sqrt(second_hat) + 1e-08) + 0.01 * weight)
    return (first_new, second_new, updated)


def cost(micros):
    return pl.CostEstimate(flops=0, bytes_accessed=int(micros * 3.5e6), transcendentals=0)


def dot(a, b, along):
    return lax.dot_general(a, b, (((along[0],), (along[1],)), ((), ())), preferred_element_type=F32)


def normalize(values):
    center = values - jnp.mean(values, axis=-1, keepdims=True)
    rstd = lax.rsqrt(jnp.mean(center * center, axis=-1, keepdims=True) + 1e-05)
    return center * rstd, rstd


def norm_backward(hat, rstd, gain, grad):
    scaled = grad * gain
    return rstd * (
        scaled
        - jnp.mean(scaled, axis=-1, keepdims=True)
        - hat * jnp.mean(scaled * hat, axis=-1, keepdims=True)
    )


QUADS = 4


def quad(outer_t, q):
    weights = outer_t[: outer_t.shape[0] // 2]
    zero = jnp.zeros_like(weights)
    return jnp.concatenate([weights if n == q else zero for n in range(QUADS)], axis=0)


def put(ref, value):
    for n in range(ref.shape[0]):
        ref[n] = value[:, n * 128 : (n + 1) * 128]


def take(ref, q):
    at = pl.ds(q, ref.shape[1] // QUADS, stride=QUADS)
    return jnp.concatenate([ref[n, at, :] for n in range(ref.shape[0])], axis=1)


def forward_kernel(
    at_ref, rows, scales, in_t, out_low, outer_t, bias, key_mask, live, row_live, flat_live,
    update, left, right, qkv, gate, powers, inverse, mixed, attended,
    bias_t, second, *, chunk,
):
    row = pl.program_id(0)
    width = rows.shape[2]
    residues = rows.shape[1]
    size = width // HEADS
    half = outer_t.shape[0] // 2

    @pl.when(row == 0)
    def _():
        across, down, _, lines, cols = bias.shape
        group = max(1, 128 // lines)

        def turn(head, carry):
            for r in range(0, across, group):
                for c in range(down):
                    tile = jnp.concatenate([bias[r + g, c, head] for g in range(group)], axis=0)
                    bias_t[head, c * cols : (c + 1) * cols, r * lines : (r + group) * lines] = (
                        tile.astype(F32).T + key_mask[c * cols : (c + 1) * cols]
                    )
            return carry

        lax.fori_loop(0, HEADS, turn, 0)

    hat, _ = normalize(rows[0])
    normed = (hat * scales[0:1] + scales[1:2]).astype(BF16)
    qkv[0, :width] = (dot(in_t[:width], normed, (1, 1)) * (size**-0.5 * LOG2E)).astype(BF16)
    qkv[0, width:] = dot(in_t[width : 3 * width], normed, (1, 1)).astype(BF16)
    gate[0] = jax.nn.sigmoid(dot(in_t[3 * width :], normed, (1, 1)))
    for head in range(HEADS):
        at = head * size
        keys = qkv[0, width + at : width + at + size]
        values = qkv[0, 2 * width + at : 2 * width + at + size]
        for first in range(0, residues, chunk):
            span = slice(first, first + chunk)
            query = qkv[0, at : at + size, span]
            scores = dot(keys, query, (0, 0)) + bias_t[head, :, span]
            exps = jnp.exp2(scores - jnp.max(scores, axis=0, keepdims=True))
            over = 1.0 / jnp.sum(exps, axis=0, keepdims=True)
            low = exps.astype(BF16)
            powers[0, head, :, span] = low
            inverse[0, head, :, span] = over
            mixed[0, at : at + size, span] = dot(values, low, (1, 0)) * over
    att = (gate[0] * mixed[0]).astype(BF16)
    attended[0] = att
    change = dot(att, out_low[...], (0, 0)).astype(BF16)
    update[0] = change
    hat, _ = normalize(rows[0] + change.astype(F32))
    normed = hat * scales[2:3] + scales[3:4]
    put(second, normed)
    right[0] = (dot(outer_t[half:], normed.astype(BF16), (1, 1)) * live[0]).astype(BF16)
    out = jnp.zeros(flat_live.shape, F32)
    for q in range(QUADS):
        out += dot(take(second, q).astype(BF16), quad(outer_t, q), (1, 1))
    left[0] = (out * flat_live[...] * row_live[0]).astype(BF16)


def attention_forward(start, rows, scales, in_t, out_low, outer_t, bias, key_mask, live, row_live, flat_live, chunk=512):
    _, residues, width = rows.shape
    own = live.shape[0]
    sides = outer_t.shape[0]
    by_row = lambda s, at: (s, 0, 0)
    by_row_four = lambda s, at: (s, 0, 0, 0)
    once = lambda array: pl.BlockSpec(
        array.shape, lambda s, at: (0,) * array.ndim, pipeline_mode=pl.Buffered(1)
    )
    out = pl.pallas_call(
        functools.partial(forward_kernel, chunk=chunk),
        grid_spec=pltpu.PrefetchScalarGridSpec(
            num_scalar_prefetch=1,
            grid=(own,),
            in_specs=[
                pl.BlockSpec((1, residues, width), lambda s, at: (at[0] + s, 0, 0)),
                once(scales),
                once(in_t),
                once(out_low),
                once(outer_t),
                once(bias),
                once(key_mask),
                pl.BlockSpec((1, 1, residues), by_row),
                pl.BlockSpec((1, 1, 128), by_row),
                once(flat_live),
            ],
            out_specs=[
                pl.BlockSpec((1, residues, width), by_row),
                pl.BlockSpec((1,) + flat_live.shape, by_row),
                pl.BlockSpec((1, sides // 2, residues), by_row),
                pl.BlockSpec((1, 3 * width, residues), by_row),
                pl.BlockSpec((1, width, residues), by_row),
                pl.BlockSpec((1, HEADS, residues, residues), by_row_four),
                pl.BlockSpec((1, HEADS, 1, residues), by_row_four),
                pl.BlockSpec((1, width, residues), by_row),
                pl.BlockSpec((1, width, residues), by_row),
            ],
            scratch_shapes=[
                pltpu.VMEM((HEADS, residues, residues), F32),
                pltpu.VMEM((width // 128, residues, 128), F32),
            ],
        ),
        out_shape=[
            jax.ShapeDtypeStruct((own, residues, width), BF16),
            jax.ShapeDtypeStruct((own,) + flat_live.shape, BF16),
            jax.ShapeDtypeStruct((own, sides // 2, residues), BF16),
            jax.ShapeDtypeStruct((own, 3 * width, residues), BF16),
            jax.ShapeDtypeStruct((own, width, residues), F32),
            jax.ShapeDtypeStruct((own, HEADS, residues, residues), BF16),
            jax.ShapeDtypeStruct((own, HEADS, 1, residues), F32),
            jax.ShapeDtypeStruct((own, width, residues), F32),
            jax.ShapeDtypeStruct((own, width, residues), BF16),
        ],
        cost_estimate=cost(36),
        compiler_params=pltpu.CompilerParams(vmem_limit_bytes=VMEM),
    )(start, rows, scales, in_t, out_low, outer_t, bias, key_mask, live, row_live, flat_live)
    return out[0], out[1], out[2], tuple(out[3:])


def backward_kernel(*refs, earlier, adds):
    (order, rows, update, back, scales, in_t, out_low, outer_t, left_grad, right_grad, live, row_live, flat_live,
     qkv, gate, powers, inverse, mixed, attended), refs = refs[:19], refs[19:]
    if earlier:
        so_far, early, table_grad, base = refs[0], refs[1:5], refs[5], refs[6]
        pieces, refs = refs[7 : 7 + adds], refs[7 + adds :]
        added, part, bias_grad, packed, norms = refs[:5]
        bias_low, base_in, piece_in, load_sem, piece_sem, store_sem = refs[-6:]
        heads_in_grad, heads_out_grad, outer_in_grad = refs[-9:-6]
        refs = refs[5:-9]
    else:
        part, bias_grad, heads_in_grad, heads_out_grad, outer_in_grad, norms = refs[:6]
        refs = refs[6:]
    bias_total, mixed_grad, proj_grad, spread, bias_sem = refs
    row = pl.program_id(0)
    own = pl.num_programs(0)
    width = rows.shape[2]
    residues = rows.shape[1]
    size = width // HEADS
    last_row = row == own - 1
    rows_here = base.shape[0] if earlier else 0
    if earlier:
        each = base_in.shape[1]
        per = pieces[0].shape[0] // each
        steps = adds * per

        def bias_load(head):
            return pltpu.make_async_copy(so_far.at[head], bias_total.at[head], bias_sem.at[head])

        def base_at(step):
            return base.at[pl.ds(order[step * each], each)], added.at[pl.ds(order[step * each], each)]

        def fetch(step, slot):
            pltpu.make_async_copy(base_at(step)[0], base_in.at[slot], load_sem.at[slot]).start()
            for n in range(adds):
                @pl.when(step // per == n)
                def _():
                    source = pieces[n].at[pl.ds((step - n * per) * each, each)]
                    pltpu.make_async_copy(source, piece_in.at[slot], piece_sem.at[slot]).start()

        def store(step, slot):
            return pltpu.make_async_copy(base_in.at[slot], base_at(step)[1], store_sem.at[slot])

        def add_step(head):
            step = row * HEADS + head
            slot = head % 2

            @pl.when(step < steps)
            def _():
                @pl.when(step + 1 < steps)
                def _():
                    @pl.when(step >= 1)
                    def _():
                        store(step - 1, 1 - slot).wait()
                    fetch(step + 1, 1 - slot)
                pltpu.make_async_copy(base_at(step)[0], base_in.at[slot], load_sem.at[slot]).wait()
                pltpu.make_async_copy(pieces[0].at[pl.ds(0, each)], piece_in.at[slot], piece_sem.at[slot]).wait()
                base_in[slot] = base_in[slot] + piece_in[slot].astype(F32)
                store(step, slot).start()

    @pl.when(row == 0)
    def _():
        for n, ref in enumerate((heads_in_grad, heads_out_grad, outer_in_grad, norms)):
            ref[...] = early[n][...] if earlier else jnp.zeros_like(ref)
        if earlier:
            for head in range(HEADS):
                bias_load(head).start()
            fetch(0, 0)

    half = outer_t.shape[0] // 2
    count = residues // QUADS
    hat, rstd = normalize(rows[0] + update[0].astype(F32))
    second = hat * scales[2:3] + scales[3:4]
    put(spread, second)
    grads = (right_grad[0].astype(F32) * live[0]).astype(BF16)
    outer_in_grad[half:] += dot(grads, second.astype(BF16), (1, 0))
    flat = (left_grad[0].astype(F32) * flat_live[...] * row_live[0]).astype(BF16).T
    for q in range(QUADS):
        mine = flat[q * half : (q + 1) * half]
        outer_in_grad[:half] += dot(mine, take(spread, q).astype(BF16), (1, 0))
        back_to = dot(mine, outer_t[:half], (0, 0))
        for n in range(spread.shape[0]):
            spread[n, pl.ds(q, count, stride=QUADS), :] = back_to[:, n * 128 : (n + 1) * 128]
    spread_grad = jnp.concatenate([spread[n] for n in range(spread.shape[0])], axis=1)
    second_grad = spread_grad + dot(grads, outer_t[half:], (0, 0))
    norms[2:3] += jnp.sum(second_grad * hat, axis=0, keepdims=True)
    norms[3:4] += jnp.sum(second_grad, axis=0, keepdims=True)
    new_part = norm_backward(hat, rstd, scales[2:3], second_grad)
    put(spread, new_part)
    out_grad = (back[0] + new_part).astype(BF16)
    heads_out_grad[...] += dot(attended[0], out_grad, (1, 0))
    attended_grad = dot(out_low[...], out_grad, (1, 1))
    sig = gate[0]
    gated = attended_grad * sig
    proj_grad[3 * width :] = (gated * mixed[0] * (1.0 - sig)).astype(BF16)
    deltas = []
    for head in range(HEADS):
        span = slice(head * size, (head + 1) * size)
        grad = gated[span] * inverse[0, head]
        mixed_grad[span] = grad.astype(BF16)
        deltas.append(jnp.sum(grad * mixed[0, span], axis=0, keepdims=True))

    for head in range(HEADS):
        at = head * size
        query = qkv[0, at : at + size]
        keys = qkv[0, width + at : width + at + size]
        values = qkv[0, 2 * width + at : 2 * width + at + size]
        grad = mixed_grad[at : at + size]
        low = powers[0, head]
        prob_grad = dot(values, grad, (0, 0))
        score_grad = low.astype(F32) * (prob_grad - deltas[head])
        if earlier:
            @pl.when(row == 0)
            def _():
                bias_load(head).wait()
            bias_total[head] += score_grad
        else:
            bias_total[head] = jnp.where(row == 0, 0.0, bias_total[head]) + score_grad
        score_low = score_grad.astype(BF16)
        proj_grad[2 * width + at : 2 * width + at + size] = dot(grad, low, (1, 1)).astype(BF16)
        proj_grad[width + at : width + at + size] = (dot(query, score_low, (1, 1)) / LOG2E).astype(BF16)
        proj_grad[at : at + size] = (dot(keys, score_low, (1, 0)) * size**-0.5).astype(BF16)
        if earlier:
            add_step(head)

        @pl.when(last_row)
        def _():
            if not earlier:
                pltpu.make_async_copy(bias_total.at[head], bias_grad.at[head], bias_sem.at[head]).start()
            else:
                across, down, _, lines, cols = bias_grad.shape
                group = max(1, 128 // lines)
                for r in range(0, across, group):
                    for c in range(down):
                        tile = bias_total[head, c * cols : (c + 1) * cols, r * lines : (r + group) * lines]
                        tile = tile.T.astype(BF16)
                        for g in range(group):
                            bias_low[head, r + g, c] = tile[g * lines : (g + 1) * lines]
                pltpu.make_async_copy(bias_low.at[head], bias_grad.at[:, :, head], bias_sem.at[head]).start()

    hat, rstd = normalize(rows[0])
    normed = (hat * scales[0:1] + scales[1:2]).astype(BF16)
    grads = proj_grad[...]
    heads_in_grad[...] += dot(grads, normed, (1, 0))
    normed_grad = dot(grads, in_t[...], (0, 0))
    norms[0:1] += jnp.sum(normed_grad * hat, axis=0, keepdims=True)
    norms[1:2] += jnp.sum(normed_grad, axis=0, keepdims=True)
    new_part = jnp.concatenate([spread[n] for n in range(spread.shape[0])], axis=1)
    part[0] = (new_part + norm_backward(hat, rstd, scales[0:1], normed_grad)).astype(BF16)

    @pl.when(last_row)
    def _():
        if earlier:
            first = 0
            for ref in (heads_in_grad, heads_out_grad, outer_in_grad):
                lines = ref.shape[0]
                packed[first : first + lines] = ref[:, :128].astype(BF16)
                packed[first + lines : first + 2 * lines] = ref[:, 128:].astype(BF16)
                first += 2 * lines
            lines = table_grad.shape[0]
            packed[first : first + lines] = table_grad[...].astype(BF16)
            first += lines
            packed[first:] = jnp.zeros((packed.shape[0] - first, 128), BF16)
            for step in range(max(0, steps - 2), steps):
                store(step, step % 2).wait()
            for head in range(HEADS):
                pltpu.make_async_copy(bias_low.at[head], bias_grad.at[:, :, head], bias_sem.at[head]).wait()
        else:
            for head in range(HEADS):
                pltpu.make_async_copy(bias_total.at[head], bias_grad.at[head], bias_sem.at[head]).wait()


def attention_backward(
    order, rows, update, back, scales, in_t, out_low, outer_t, left_grad, right_grad, live, row_live, flat_live,
    kept, blocks, first, own, earlier=None, early=(), table_grad=None, pieces=(),
):
    _, residues, width = rows.shape
    qkv, gate, powers, inverse, mixed, attended = kept
    here = lambda s, order: (order[0] + first + s, 0, 0)
    by_row = lambda s, order: (first + s, 0, 0)
    by_row_four = lambda s, order: (first + s, 0, 0, 0)
    hbm = pl.BlockSpec(memory_space=pl.ANY)
    once = lambda array: pl.BlockSpec(
        array.shape, lambda s, order: (0,) * array.ndim, pipeline_mode=pl.Buffered(1)
    )
    whole = lambda array: pl.BlockSpec(array.shape, lambda s, order: (0,) * array.ndim)
    one = pl.BlockSpec((1, residues, width), here)
    args = [rows, update, back, scales, in_t, out_low, outer_t, left_grad, right_grad, live, row_live, flat_live]
    args += [qkv, gate, powers, inverse, mixed, attended]
    in_specs = [
        one,
        pl.BlockSpec((1, residues, width), by_row),
        one,
        once(scales),
        once(in_t),
        once(out_low),
        once(outer_t),
        pl.BlockSpec((1,) + left_grad.shape[1:], by_row),
        pl.BlockSpec((1,) + right_grad.shape[1:], by_row),
        pl.BlockSpec((1, 1, residues), by_row),
        pl.BlockSpec((1, 1, 128), by_row),
        once(flat_live),
        pl.BlockSpec((1, 3 * width, residues), by_row),
        pl.BlockSpec((1, width, residues), by_row),
        pl.BlockSpec((1, HEADS, residues, residues), by_row_four),
        pl.BlockSpec((1, HEADS, 1, residues), by_row_four),
        pl.BlockSpec((1, width, residues), by_row),
        pl.BlockSpec((1, width, residues), by_row),
    ]
    part = jax.ShapeDtypeStruct((own, residues, width), BF16)
    part_spec = pl.BlockSpec((1, residues, width), lambda s, order: (s, 0, 0))
    weights = [jax.ShapeDtypeStruct(array.shape, F32) for array in (in_t, out_low, outer_t)]
    norms = jax.ShapeDtypeStruct((4, width), F32)
    scratch = [
        pltpu.VMEM((HEADS, residues, residues), F32),
        pltpu.VMEM((width, residues), BF16),
        pltpu.VMEM((4 * width, residues), BF16),
        pltpu.VMEM((width // 128, residues, 128), F32),
        pltpu.SemaphoreType.DMA((HEADS,)),
    ]
    if earlier is None:
        out_shape = [part, jax.ShapeDtypeStruct((HEADS, residues, residues), F32)] + weights + [norms]
        out_specs = [part_spec, hbm] + [whole(array) for array in weights + [norms]]
    else:
        each = max(1, rows.shape[0] // (own * HEADS))
        args += [earlier, *early, table_grad, rows] + list(pieces)
        in_specs += [hbm] + [once(array) for array in [*early, table_grad]] + [hbm] * (1 + len(pieces))
        count = 2 * sum(array.shape[0] for array in weights) + table_grad.shape[0]
        count += -count % 512
        packed = jax.ShapeDtypeStruct((count, 128), BF16)
        out_shape = [jax.ShapeDtypeStruct(rows.shape, F32), part, jax.ShapeDtypeStruct(blocks, BF16), packed, norms]
        out_specs = [hbm, part_spec, hbm, whole(packed), whole(norms)]
        scratch += [pltpu.VMEM(array.shape, F32) for array in weights] + [
            pltpu.VMEM((HEADS,) + blocks[:2] + blocks[3:], BF16),
            pltpu.VMEM((2, each, residues, width), F32),
            pltpu.VMEM((2, each, residues, width), BF16),
            pltpu.SemaphoreType.DMA((2,)),
            pltpu.SemaphoreType.DMA((2,)),
            pltpu.SemaphoreType.DMA((2,)),
        ]
    return pl.pallas_call(
        functools.partial(backward_kernel, earlier=earlier is not None, adds=len(pieces)),
        grid_spec=pltpu.PrefetchScalarGridSpec(
            num_scalar_prefetch=1, grid=(own,), in_specs=in_specs, out_specs=out_specs, scratch_shapes=scratch
        ),
        out_shape=out_shape,
        compiler_params=pltpu.CompilerParams(vmem_limit_bytes=VMEM),
        cost_estimate=cost(20),
    )(order, *args)


def outer_product_plain(left, right, pairs_back, table, all_rows):
    low = pairs_back.astype(BF16)
    product = mm("sei,sfj->eifj", left, right).astype(BF16)
    total = mm("eifj,efz->ijz", product, table) / all_rows
    table_grad = mm("eifj,ijz->efz", product, low) / all_rows
    back = mm("ijz,efz->eifj", low, table).astype(BF16)
    left_grad = mm("eifj,sfj->sei", back, right) / all_rows
    right_grad = mm("eifj,sei->sfj", back, left) / all_rows
    return total, table_grad, left_grad.astype(BF16), right_grad.astype(BF16)


def mm(spec, a, b):
    return jnp.einsum(spec, a, b, preferred_element_type=F32)


def pair_forward(pairs, gain, shift, bias_low):
    hat, _ = normalize(pairs)
    low = (hat * gain + shift).astype(BF16)
    return (mm("ijc,ch->hij", low, bias_low) * LOG2E).astype(BF16)


def pair_backward(pairs, pairs_back, gain, shift, bias_low, bias_grad):
    hat, rstd = normalize(pairs)
    low = (hat * gain + shift).astype(BF16)
    weight_grad = mm("ijc,hij->ch", low, bias_grad)
    in_grad = mm("hij,ch->ijc", bias_grad, bias_low)
    gain_grad = jnp.sum(in_grad * hat, axis=(0, 1))
    shift_grad = jnp.sum(in_grad, axis=(0, 1))
    return pairs_back + norm_backward(hat, rstd, gain, in_grad), weight_grad, gain_grad, shift_grad


MESH = pl.DeviceIdType.MESH
CORE, ACROSS, DOWN, CORNER = 1, 2, 4, 6


def place():
    return lax.axis_index("row"), lax.axis_index("head")


def flip(row, way):
    out = row
    for bit in (1, 2, 4):
        if way & bit:
            out = out + bit - 2 * bit * ((row // bit) % 2)
    return out


def greet(devices):
    barrier = pltpu.get_barrier_semaphore()
    for device in devices:
        pl.semaphore_signal(barrier, inc=1, device_id=device, device_id_type=MESH)
    pl.semaphore_wait(barrier, len(devices))


class Sends:
    def __init__(self, send_sem, recv_sem):
        self.send_sem, self.recv_sem, self.count, self.open = send_sem, recv_sem, 0, []

    def start(self, source, target, device):
        copy = pltpu.make_async_remote_copy(
            src_ref=source,
            dst_ref=target,
            send_sem=self.send_sem.at[self.count],
            recv_sem=self.recv_sem.at[self.count],
            device_id=device,
            device_id_type=MESH,
        )
        copy.start()
        self.count += 1
        self.open.append(copy)
        return copy

    def finish(self):
        for copy in self.open:
            copy.wait_send()


GATHER_SENDS = 6 + 3 + 31 + 3


def pair_bias_kernel(pairs, norm, weight, shard, bias, weights, block, low, local_sem, send_sem, recv_sem):
    row, head = place()
    rows, cols, channels = pairs.shape
    part = shard.shape[1] // 2
    core = row % 2
    beyond = [(head + k) % 4 for k in range(4)]
    behind = [(head + 4 - k) % 4 for k in range(4)]
    across, down, other = (flip(row, ACROSS), head), (flip(row, DOWN), head), (flip(row, CORE), head)
    greet([across, down, other] + [(row, beyond[k]) for k in (1, 2, 3)])
    sends = Sends(send_sem, recv_sem)

    def own_part(at, side):
        return weights.at[:, pl.ds(pl.multiple_of(at * 2 * part + side * part, part), part), :]

    half = shard.at[:, pl.ds(pl.multiple_of(core * part, part), part), :]
    keep = pltpu.make_async_copy(
        shard, weights.at[:, pl.ds(pl.multiple_of(head * 2 * part, 2 * part), 2 * part), :], local_sem.at[0]
    )
    keep.start()
    shards = [None] + [sends.start(half, own_part(head, core), (row, beyond[k])) for k in (1, 2, 3)]

    step = 8

    def norm_block(n, carry):
        first = pl.multiple_of(n * step, step)
        values = pairs[pl.ds(first, step)].reshape(step * cols, channels)
        center = values - jnp.mean(values, axis=-1, keepdims=True)
        rstd = lax.rsqrt(jnp.mean(center * center, axis=-1, keepdims=True) + 1e-05)
        normed = (center * rstd * norm[0:1] + norm[1:2]).astype(BF16)
        out = lax.dot_general(weight[...], normed, (((1,), (1,)), ((), ())), preferred_element_type=F32)
        for i in range(step):
            block[:, pl.ds(first + i, 1), :] = (out[:, i * cols : (i + 1) * cols] * LOG2E).reshape(
                HEADS, 1, cols
            )
        return carry

    lax.fori_loop(0, rows // step, norm_block, 0)
    low[...] = block[...].astype(BF16)

    mine = pltpu.make_async_copy(low, bias.at[row, head], local_sem.at[1])
    mine.start()
    stage = [None] * 4
    stage[0] = low
    along = [None] + [sends.start(low, bias.at[row, head], (row, beyond[k])) for k in (1, 2, 3)]
    from_across, from_down, from_corner, from_core = [None] * 4, [None] * 4, [None] * 4, []

    def spread(k, source):
        here = bias.at[row, behind[k]]
        from_across[k] = sends.start(source, here, across)
        from_down[k] = sends.start(source, here, down)
        from_core.append(sends.start(source, here, other))

    def relay(k):
        from_across[k].wait_recv()
        block_across = bias.at[flip(row, ACROSS), behind[k]]
        if k < 2:
            from_corner[k] = sends.start(block_across, block_across, down)
        from_core.append(sends.start(block_across, block_across, other))
        from_down[k].wait_recv()
        block_down = bias.at[flip(row, DOWN), behind[k]]
        if k >= 2:
            from_corner[k] = sends.start(block_down, block_down, across)
        from_core.append(sends.start(block_down, block_down, other))

    spread(0, low)
    for k in (1, 2, 3):
        along[k].wait_recv()
        spread(k, bias.at[row, behind[k]])
        relay(k - 1)
    relay(3)
    for k in range(4):
        from_corner[k].wait_recv()
        block_corner = bias.at[flip(row, CORNER), behind[k]]
        from_core.append(sends.start(block_corner, block_corner, other))
    for k in (1, 2, 3):
        shards[k].wait_recv()
        piece = own_part(behind[k], core)
        from_core.append(sends.start(piece, piece, other))
    for copy in from_core:
        copy.wait_recv()
    sends.finish()
    keep.wait()
    mine.wait()


def pair_bias(pairs, norm, weight, shard):
    rows, cols, channels = pairs.shape
    vmem = pl.BlockSpec(memory_space=pltpu.VMEM)
    hbm = pl.BlockSpec(memory_space=pl.ANY)
    return pl.pallas_call(
        pair_bias_kernel,
        out_shape=[
            jax.ShapeDtypeStruct((8, 4, HEADS, rows, cols), BF16),
            jax.ShapeDtypeStruct((shard.shape[0], 4 * shard.shape[1], shard.shape[2]), BF16),
        ],
        in_specs=[vmem, vmem, vmem, hbm],
        out_specs=[hbm, hbm],
        scratch_shapes=[
            pltpu.VMEM((HEADS, rows, cols), F32),
            pltpu.VMEM((HEADS, rows, cols), BF16),
            pltpu.SemaphoreType.DMA((2,)),
            pltpu.SemaphoreType.DMA((GATHER_SENDS,)),
            pltpu.SemaphoreType.DMA((GATHER_SENDS,)),
        ],
        cost_estimate=cost(34),
        compiler_params=pltpu.CompilerParams(
            collective_id=0, has_side_effects=True, vmem_limit_bytes=VMEM
        ),
    )(pairs, norm, weight, shard)


OUTER_SENDS = 6 + 28 + 16 + 12 + 1 + 7 + 3 + 3 + 3 + 3


def outer_kernel(
    left, right, pairs_back, outer_out, update,
    total, left_out, right_out, table_grad, hop_one, hop_two,
    left_on, right_on, left_all, right_all, left_wide, right_wide, left_rows, right_rows,
    backed, product, back, low, table, table_t, total_low,
    left_part, right_part, left_send, right_send, right_core, chip_sum, left_in, right_in, right_sum, left_line,
    load_sem, local_sem, out_sem, send_sem, recv_sem,
    *, scale, block, group,
):
    row, head = place()
    beyond = [(head + k) % 4 for k in range(4)]
    behind = [(head + 4 - k) % 4 for k in range(4)]
    plane = [(flip(row, way), head) for way in range(8)]
    core, chip = row % 2, row // 2
    own, wide, _ = right.shape
    rows, cols, channels = back.shape
    size = wide
    lines = left_all.shape[3]
    chunks = rows // block
    greet(plane[1:] + [(row, beyond[k]) for k in (1, 2, 3)])
    sends = Sends(send_sem, recv_sem)
    loads = []
    for n in range(chunks):
        copy = pltpu.make_async_copy(
            pairs_back.at[pl.ds(n * block, block)], back.at[pl.ds(n * block, block)], load_sem.at[n]
        )
        copy.start()
        loads.append(copy)

    def columns(h):
        return pl.ds(pl.multiple_of(h * cols, cols), cols)

    def strip(r):
        return pl.ds(pl.multiple_of(r * lines, lines), lines)

    from_left, from_right = [None] * 4, [None] * 4
    for k in (1, 2, 3):
        from_right[k] = sends.start(right.at[:, :, columns(beyond[k])], right_on.at[k - 1], (row, beyond[k]))
        from_left[k] = sends.start(left, left_on.at[k - 1], (row, beyond[k]))
    arrive, onward, locals_ = [], [], []

    def forward(k):
        ours = right_on.at[k - 1] if k else right.at[:, :, columns(head)]
        here = right_all.at[row, behind[k]]
        for way in (ACROSS, DOWN, CORNER):
            onward.append((way, k, sends.start(ours, here, plane[way])))
        arrive.append(sends.start(ours, here, plane[CORE]))
        copy = pltpu.make_async_copy(ours, here, local_sem.at[2 * k])
        copy.start()
        locals_.append(copy)
        ours = left_on.at[k - 1] if k else left
        here = left_all.at[row, behind[k]]
        for way in (2, 4, 6, 3, 5, 7, 1):
            arrive.append(sends.start(ours.at[:, strip(plane[way][0]), :], here, plane[way]))
        copy = pltpu.make_async_copy(ours.at[:, strip(row), :], here, local_sem.at[2 * k + 1])
        copy.start()
        locals_.append(copy)

    forward(0)
    for f in range(wide):
        table[f * size : (f + 1) * size] = outer_out[pl.ds(f, size, stride=wide), :].astype(BF16)
    for n in range(wide * size // 128):
        table_t[:, n * 128 : (n + 1) * 128] = table[n * 128 : (n + 1) * 128].T

    def spread_pair(p, carry):
        first = p * group
        both = back[pl.ds(first, group)].astype(BF16)
        low[pl.ds(first, group)] = both
        spread = dot(table[...], both.reshape(group * cols, channels), (1, 1)).astype(BF16)
        for g in range(group):
            at = pl.ds(pl.multiple_of((first + g) * size, size), size)
            for f in range(wide):
                backed[at, f * cols : (f + 1) * cols] = spread[
                    f * size : (f + 1) * size, g * cols : (g + 1) * cols
                ]
        return carry

    pairs_of = rows // group
    for k in range(4):
        for n in range(k * chunks // 4, (k + 1) * chunks // 4):
            loads[n].wait()
        if k:
            from_right[k].wait_recv()
            from_left[k].wait_recv()
            forward(k)
        if k == 3:
            half = update.shape[0] // 2
            hops = [
                sends.start(update.at[pl.ds(n * half, half)], hop_one.at[pl.ds(n * half, half)], (row, beyond[1]))
                for n in range(2)
            ]
        lax.fori_loop(k * pairs_of // 4, (k + 1) * pairs_of // 4, spread_pair, 0)
    for way, k, copy in onward:
        copy.wait_recv()
        slot = right_all.at[plane[way][0], behind[k]]
        arrive.append(sends.start(slot, slot, plane[CORE]))
    for copy in arrive:
        copy.wait_recv()
    for copy in locals_:
        copy.wait()

    count = 32
    left_wide[...] = left_all[...].astype(F32).reshape(left_wide.shape)
    right_wide[...] = right_all[...].astype(F32).reshape(right_wide.shape)
    for s in range(own):
        at = slice(s * count, (s + 1) * count)
        for n in range(lines):
            left_rows[at, n * 128 : (n + 1) * 128] = left_wide[:, s * lines + n, :].astype(BF16)
        for f in range(wide):
            right_rows[at, f * cols : (f + 1) * cols] = right_wide[:, s * wide + f, :].astype(BF16)

    step = 4 * cols

    def right_step(n, carry):
        at = pl.ds(pl.multiple_of(n * step, step), step)
        right_part[:, at] = dot(left_rows[...], backed[:, at], (1, 0)) * scale
        return carry

    lax.fori_loop(0, wide * cols // step, right_step, 0)
    for s in range(own):
        at = slice(s * count, (s + 1) * count)
        for f in range(wide):
            right_wide[:, s * wide + f, :] = right_part[at, f * cols : (f + 1) * cols]
    right_send[...] = right_wide[...].astype(BF16).reshape(right_send.shape)
    swap = sends.start(right_send.at[:, 1 - core], right_core, plane[CORE])
    deep = block * size

    def left_step(n, carry):
        at = pl.ds(pl.multiple_of(n * deep, deep), deep)
        left_part[:, at] = dot(right_rows[...], backed[at, :], (1, 1)) * scale
        return carry

    lax.fori_loop(0, chunks, left_step, 0)
    for s in range(own):
        at = slice(s * count, (s + 1) * count)
        for n in range(lines):
            left_wide[:, s * lines + n, :] = left_part[at, n * 128 : (n + 1) * 128]
    left_send[...] = left_wide[...].astype(BF16).reshape(left_send.shape)
    lefts = [
        sends.start(left_send.at[plane[way][0]], left_in.at[row], plane[way]) for way in (2, 4, 6, 3, 5, 7, 1)
    ]
    mine = pltpu.make_async_copy(left_send.at[row], left_in.at[row], local_sem.at[8])
    mine.start()

    table_grad[...] = jnp.zeros_like(table_grad)

    def outer_chunk(n, carry):
        at = pl.ds(pl.multiple_of(n * deep, deep), deep)
        product[...] = dot(left_rows[:, at], right_rows[...], (0, 0)).astype(BF16)
        for first in range(0, block, group):
            both = jnp.concatenate(
                [
                    jnp.concatenate(
                        [
                            product[(first + g) * size : (first + g + 1) * size, f * cols : (f + 1) * cols]
                            for f in range(wide)
                        ],
                        axis=0,
                    )
                    for g in range(group)
                ],
                axis=1,
            )
            out = dot(table_t[...], both, (1, 0)) * scale
            for g in range(group):
                total_low[n * block + first + g] = out[:, g * cols : (g + 1) * cols].T.astype(BF16)
            seen = low[pl.ds(n * block + first, group)].reshape(group * cols, channels)
            table_grad[...] += dot(both, seen, (1, 0)) * scale
        return carry

    stores = []

    def outer_part(n):
        first, last = n * chunks // 4, (n + 1) * chunks // 4
        lax.fori_loop(first, last, outer_chunk, 0)
        at = pl.ds(first * block, (last - first) * block)
        copy = pltpu.make_async_copy(total_low.at[at], total.at[at], out_sem.at[n])
        copy.start()
        stores.append(copy)

    outer_part(0)
    swap.wait_recv()
    rights = []
    for slot, way in enumerate((CORNER, ACROSS, DOWN)):
        n = plane[way][0] // 2
        for h in range(4):
            chip_sum[slot, h] = (right_send[n, core, h].astype(F32) + right_core[n, h].astype(F32)).astype(BF16)
        rights.append(sends.start(chip_sum.at[slot], right_in.at[slot], plane[way]))
    outer_part(1)
    for copy in lefts:
        copy.wait_recv()
    mine.wait()
    left_on_line = [
        sends.start(left_in.at[:, beyond[k]], left_line.at[k - 1], (row, beyond[k])) for k in (1, 2, 3)
    ]
    outer_part(2)
    for copy in rights:
        copy.wait_recv()
    for h in range(4):
        summed = right_send[chip, core, h].astype(F32) + right_core[chip, h].astype(F32)
        for slot in range(3):
            summed = summed + right_in[slot, h].astype(F32)
        right_sum[h] = summed.astype(BF16)
    last = [
        sends.start(right_sum.at[beyond[k]], right_out.at[:, :, columns(head)], (row, beyond[k])) for k in (1, 2, 3)
    ]
    own_right = pltpu.make_async_copy(right_sum.at[head], right_out.at[:, :, columns(head)], local_sem.at[9])
    own_right.start()
    hops[0].wait_recv()
    hops.append(sends.start(hop_one.at[pl.ds(0, half)], hop_two, (row, beyond[1])))
    outer_part(3)
    for copy in left_on_line:
        copy.wait_recv()
    for r in range(8):
        summed = left_in[r, head].astype(F32)
        for k in range(3):
            summed = summed + left_line[k, r].astype(F32)
        left_out[:, r * lines : (r + 1) * lines, :] = summed.astype(BF16)
    for copy in last:
        copy.wait_recv()
    own_right.wait()
    hops[1].wait_recv()
    hops[2].wait_recv()
    sends.finish()
    for copy in stores:
        copy.wait()


def outer_product(left, right, pairs_back, outer_out, update, all_rows, block=8, group=2):
    rows, cols, channels = pairs_back.shape
    own, wide, residues = right.shape
    size = left.shape[1] * left.shape[2] // residues
    lines = left.shape[1] // 8
    vmem = pl.BlockSpec(memory_space=pltpu.VMEM)
    hbm = pl.BlockSpec(memory_space=pl.ANY)
    low = lambda *shape: pltpu.VMEM(shape, BF16)
    full = lambda *shape: pltpu.VMEM(shape, F32)
    one = (own, lines, 128)
    other = (own, wide, cols)
    return pl.pallas_call(
        functools.partial(outer_kernel, scale=1.0 / all_rows, block=block, group=group),
        out_shape=[
            jax.ShapeDtypeStruct(pairs_back.shape, BF16),
            jax.ShapeDtypeStruct(left.shape, BF16),
            jax.ShapeDtypeStruct(right.shape, BF16),
            jax.ShapeDtypeStruct((wide * size, channels), F32),
            jax.ShapeDtypeStruct(update.shape, BF16),
            jax.ShapeDtypeStruct((update.shape[0] // 2,) + update.shape[1:], BF16),
        ],
        in_specs=[hbm, hbm, hbm, vmem, hbm],
        out_specs=[hbm, vmem, vmem, vmem, hbm, hbm],
        scratch_shapes=[
            low(3, *left.shape), low(3, *other), low(8, 4, *one), low(8, 4, *other),
            full(32, own * lines, 128), full(32, own * wide, cols), low(all_rows, rows * size), low(all_rows, wide * cols),
            low(rows * size, wide * cols), low(block * size, wide * cols), full(rows, cols, channels),
            low(rows, cols, channels), low(wide * size, channels), low(channels, wide * size), low(rows, cols, channels),
            full(all_rows, rows * size), full(all_rows, wide * cols), low(8, 4, *one), low(4, 2, 4, *other),
            low(4, 4, *other), low(3, 4, *other), low(8, 4, *one), low(3, 4, *other), low(4, *other), low(3, 8, *one),
            pltpu.SemaphoreType.DMA((rows // block,)),
            pltpu.SemaphoreType.DMA((10,)),
            pltpu.SemaphoreType.DMA((4,)),
            pltpu.SemaphoreType.DMA((OUTER_SENDS,)),
            pltpu.SemaphoreType.DMA((OUTER_SENDS,)),
        ],
        compiler_params=pltpu.CompilerParams(
            collective_id=1, has_side_effects=True, vmem_limit_bytes=VMEM
        ),
        cost_estimate=cost(65),
    )(left, right, pairs_back, outer_out, update)


SUM_SENDS = 4 + 4 + 8 + 3 + 1 + 3 + 3


def sum_kernel(
    grads, parts, out, piece,
    swapped, chip_sum, by_across, by_down, from_across, from_down, down_sum, line_in,
    part_swapped, part_sum, part_plane, part_down, part_line,
    send_sem, recv_sem,
):
    row, head = place()
    beyond = [(head + k) % 4 for k in range(4)]
    core, chip = row % 2, row // 2
    ways = (CORNER, ACROSS, DOWN)
    plane = [(flip(row, way), head) for way in range(8)]
    other, across, down = plane[CORE], plane[ACROSS], plane[DOWN]
    greet([plane[way] for way in (CORE,) + ways] + [(row, beyond[k]) for k in (1, 2, 3)])
    sends = Sends(send_sem, recv_sem)
    chips = [plane[way][0] // 2 for way in ways] + [chip]
    swaps = [sends.start(grads.at[n, 1 - core], swapped.at[slot], other) for slot, n in enumerate(chips)]
    part_swap = sends.start(parts.at[1 - core], part_swapped, other)
    first, second = (2, 1), (3, 0)

    def add(slot, k):
        z = beyond[k]
        chip_sum[slot, k] = (
            grads[chips[slot], core, z].astype(F32) + swapped[slot, z].astype(F32)
        ).astype(BF16)

    swaps[0].wait_recv()
    relays_across, relays_down = [], []
    for n in range(2):
        add(0, first[n])
        relays_across.append(sends.start(chip_sum.at[0, first[n]], by_across.at[n], across))
        add(0, second[n])
        relays_down.append(sends.start(chip_sum.at[0, second[n]], by_down.at[n], down))
    last_across, last_down = [None] * 4, [None] * 4
    swaps[1].wait_recv()
    for k in first:
        add(1, k)
        last_across[k] = sends.start(chip_sum.at[1, k], from_across.at[k], across)
    swaps[2].wait_recv()
    for k in second:
        add(2, k)
        last_down[k] = sends.start(chip_sum.at[2, k], from_down.at[k], down)
    for n in range(2):
        add(1, second[n])
        add(2, first[n])
        relays_across[n].wait_recv()
        k = first[n]
        chip_sum[2, k] = (chip_sum[2, k].astype(F32) + by_across[n].astype(F32)).astype(BF16)
        last_down[k] = sends.start(chip_sum.at[2, k], from_down.at[k], down)
        relays_down[n].wait_recv()
        k = second[n]
        chip_sum[1, k] = (chip_sum[1, k].astype(F32) + by_down[n].astype(F32)).astype(BF16)
        last_across[k] = sends.start(chip_sum.at[1, k], from_across.at[k], across)
    part_swap.wait_recv()
    part_arrive = []
    for slot, n in enumerate(chips):
        for z in range(4):
            part_sum[slot, z] = (parts[core, n, z].astype(F32) + part_swapped[n, z].astype(F32)).astype(BF16)
        if slot < 3:
            part_arrive.append(sends.start(part_sum.at[slot], part_plane.at[slot], plane[ways[slot]]))
    swaps[3].wait_recv()
    line = []
    for k in first + second:
        add(3, k)
        last_across[k].wait_recv()
        last_down[k].wait_recv()
        total = chip_sum[3, k].astype(F32) + from_across[k].astype(F32) + from_down[k].astype(F32)
        if k:
            down_sum[k - 1] = total.astype(BF16)
            line.append(sends.start(down_sum.at[k - 1], line_in.at[k - 1], (row, beyond[k])))
        else:
            out[...] = total
    for copy in part_arrive:
        copy.wait_recv()
    for z in range(4):
        total = part_sum[3, z].astype(F32)
        for slot in range(3):
            total = total + part_plane[slot, z].astype(F32)
        part_down[z] = total.astype(BF16)
    part_arrive = [
        sends.start(part_down.at[beyond[k]], part_line.at[k - 1], (row, beyond[k])) for k in (1, 2, 3)
    ]
    for slot, copy in zip((1, 0, 2), line):
        copy.wait_recv()
        out[...] += line_in[slot].astype(F32)
    total = part_down[head].astype(F32)
    for slot, copy in enumerate(part_arrive):
        copy.wait_recv()
        total = total + part_line[slot].astype(F32)
    piece[...] = total.astype(BF16)
    sends.finish()


def sum_gradients(grads, parts):
    block = grads.shape[2:]
    lines = block[0] * block[1]
    rows, cols = parts.shape
    share = rows // 32
    vmem = pl.BlockSpec(memory_space=pltpu.VMEM)
    wide = lambda *first: pltpu.VMEM(first + (lines, block[2]), BF16)
    thin = lambda *first: pltpu.VMEM(first + (share, cols), BF16)
    out, piece = pl.pallas_call(
        sum_kernel,
        out_shape=[
            jax.ShapeDtypeStruct((lines, block[2]), F32),
            jax.ShapeDtypeStruct((share, cols), BF16),
        ],
        in_specs=[vmem, vmem],
        out_specs=[vmem, vmem],
        scratch_shapes=[
            wide(4, 4), wide(4, 4), wide(2), wide(2), wide(4), wide(4), wide(3), wide(3),
            thin(4, 4), thin(4, 4), thin(3, 4), thin(4), thin(3),
            pltpu.SemaphoreType.DMA((SUM_SENDS,)),
            pltpu.SemaphoreType.DMA((SUM_SENDS,)),
        ],
        compiler_params=pltpu.CompilerParams(
            collective_id=3, has_side_effects=True, vmem_limit_bytes=VMEM
        ),
        cost_estimate=cost(40),
    )(grads.reshape(4, 2, 4, lines, block[2]), parts.reshape(2, 4, 4, share, cols))
    return out.reshape(block), piece


SPREAD_SENDS = 3 + 12 + 16 + 3 + 7


def spread_kernel(
    piece, small, out, total, line_in, line_sum, plane_in, local_sem, send_sem, recv_sem
):
    row, head = place()
    beyond = [(head + k) % 4 for k in range(4)]
    behind = [(head + 4 - k) % 4 for k in range(4)]
    core, chip = row % 2, row // 2
    ways = (CORNER, ACROSS, DOWN)
    plane = [(flip(row, way), head) for way in range(8)]
    other = plane[CORE]
    greet(plane[1:] + [(row, beyond[k]) for k in (1, 2, 3)])
    sends = Sends(send_sem, recv_sem)
    small_line = [sends.start(small, line_in.at[head], (row, beyond[k])) for k in (1, 2, 3)]
    line = [None] + [sends.start(piece, out.at[core, chip, head], (row, beyond[k])) for k in (1, 2, 3)]
    mine = pltpu.make_async_copy(piece, out.at[core, chip, head], local_sem)
    mine.start()
    line_in[head] = small[...]
    across, end = [], []

    def forward(k):
        here = out.at[core, chip, behind[k]]
        source = here if k else piece
        for way in ways:
            across.append((plane[way][0] // 2, k, sends.start(source, here, plane[way])))
        end.append(sends.start(source, here, other))

    forward(0)
    for copy in small_line:
        copy.wait_recv()
    line_sum[...] = (line_in[0] + line_in[1]) + (line_in[2] + line_in[3])
    small_plane = [sends.start(line_sum, plane_in.at[row], plane[way]) for way in range(1, 8)]
    plane_in[row] = line_sum[...]
    for k in (1, 2, 3):
        line[k].wait_recv()
        forward(k)
    for n, k, copy in across:
        copy.wait_recv()
        block = out.at[core, n, behind[k]]
        end.append(sends.start(block, block, other))
    for copy in small_plane:
        copy.wait_recv()
    summed = plane_in[0]
    for n in range(1, 8):
        summed = summed + plane_in[n]
    total[...] = summed
    for copy in end:
        copy.wait_recv()
    mine.wait()
    sends.finish()


def spread_gradients(piece, small):
    lines, cols = piece.shape
    vmem = pl.BlockSpec(memory_space=pltpu.VMEM)
    out, total = pl.pallas_call(
        spread_kernel,
        out_shape=[
            jax.ShapeDtypeStruct((2, 4, 4, lines, cols), BF16),
            jax.ShapeDtypeStruct(small.shape, F32),
        ],
        in_specs=[vmem, vmem],
        out_specs=[vmem, vmem],
        scratch_shapes=[
            pltpu.VMEM((4,) + small.shape, F32),
            pltpu.VMEM(small.shape, F32),
            pltpu.VMEM((8,) + small.shape, F32),
            pltpu.SemaphoreType.DMA,
            pltpu.SemaphoreType.DMA((SPREAD_SENDS,)),
            pltpu.SemaphoreType.DMA((SPREAD_SENDS,)),
        ],
        compiler_params=pltpu.CompilerParams(
            collective_id=4, has_side_effects=True, vmem_limit_bytes=VMEM
        ),
        cost_estimate=cost(15),
    )(piece, small)
    return out.reshape(32 * lines, cols), total


def add_pieces(step, base, pieces, out):
    for n, piece in enumerate(pieces):
        @pl.when(step == n)
        def _():
            out[...] = base[...] + piece[...].astype(F32)


def added_specs(base, pieces):
    block = pieces[0].shape
    by_order = pl.BlockSpec(
        block, lambda n, order: (order[jnp.minimum(n, len(pieces) - 1) * block[0]] // block[0], 0, 0)
    )
    return by_order, [by_order] + [pl.BlockSpec(block, lambda n, order: (0, 0, 0))] * len(pieces)


def pair_backward_kernel(order, pairs, back, total, grads, norm, weight, norms, base, *refs):
    pieces, (out, new, small, changed) = refs[:-4], refs[-4:]
    step = pl.program_id(0)
    rows, cols, channels = pairs.shape
    add_pieces(step, base, pieces, changed)

    @pl.when(step == 0)
    def _():
        small[...] = jnp.zeros_like(small)
        small[2 * HEADS :] = jnp.concatenate([norms[:, :128], norms[:, 128:]], axis=0)

    values = pairs[...].reshape(rows * cols, channels)
    hat, rstd = normalize(values)
    low = (hat * norm[0:1] + norm[1:2]).astype(BF16)
    bias = jnp.concatenate([grads[:, i, :] for i in range(rows)], axis=1).astype(BF16)
    small[0:HEADS] += dot(bias, low, (1, 0))
    in_grad = dot(bias, weight[...], (0, 0))
    small[HEADS : HEADS + 1] += jnp.sum(in_grad * hat, axis=0, keepdims=True)
    small[HEADS + 1 : HEADS + 2] += jnp.sum(in_grad, axis=0, keepdims=True)
    change = norm_backward(hat, rstd, norm[0:1], in_grad)
    out[...] = back[...] + change.reshape(rows, cols, channels)
    new[...] = pairs[...] + total[...].astype(F32)


def pair_norm_backward(order, pairs, back, total, grads, norm, weight, norms, base, pieces, steps=8):
    rows, cols, channels = pairs.shape
    block = rows // steps
    by_row = lambda n, order: (n, 0, 0)
    whole = lambda n, order: (0, 0)
    by_order, added = added_specs(base, pieces)
    grads = grads.reshape(HEADS, steps, block, cols)
    return pl.pallas_call(
        pair_backward_kernel,
        grid_spec=pltpu.PrefetchScalarGridSpec(
            num_scalar_prefetch=1,
            grid=(steps,),
            in_specs=[
                pl.BlockSpec((block, cols, channels), by_row),
                pl.BlockSpec((block, cols, channels), by_row),
                pl.BlockSpec((block, cols, channels), by_row),
                pl.BlockSpec((HEADS, None, block, cols), lambda n, order: (0, n, 0, 0)),
                pl.BlockSpec(norm.shape, whole),
                pl.BlockSpec(weight.shape, whole),
                pl.BlockSpec(norms.shape, whole),
            ]
            + added,
            out_specs=[
                pl.BlockSpec((block, cols, channels), by_row),
                pl.BlockSpec((block, cols, channels), by_row),
                pl.BlockSpec((3 * HEADS, channels), whole),
                by_order,
            ],
        ),
        out_shape=[
            jax.ShapeDtypeStruct(pairs.shape, F32),
            jax.ShapeDtypeStruct(pairs.shape, F32),
            jax.ShapeDtypeStruct((3 * HEADS, channels), F32),
            jax.ShapeDtypeStruct(base.shape, F32),
        ],
        compiler_params=pltpu.CompilerParams(vmem_limit_bytes=VMEM),
        cost_estimate=cost(9),
    )(order, pairs, back, total, grads, norm, weight, norms, base, *pieces)


def add_kernel(place_ref, base, piece, *refs):
    refs[-1][...] = base[...] + piece[...].astype(F32)


def add_rows(at, base, piece, into=None):
    own = piece.shape[0]
    block = (1,) + piece.shape[1:]
    spread = lambda n, at: (at[0] * own + n, 0, 0)
    return pl.pallas_call(
        add_kernel,
        grid_spec=pltpu.PrefetchScalarGridSpec(
            num_scalar_prefetch=1,
            grid=(own,),
            in_specs=[pl.BlockSpec(block, spread), pl.BlockSpec(block, lambda n, at: (n, 0, 0))]
            + ([] if into is None else [pl.BlockSpec(memory_space=pl.ANY)]),
            out_specs=pl.BlockSpec(block, spread),
        ),
        out_shape=jax.ShapeDtypeStruct(base.shape, F32),
        input_output_aliases={} if into is None else {3: 0},
        cost_estimate=cost(2),
    )(*((at, base, piece) if into is None else (at, base, piece, into)))


def hop(piece):
    count = lax.axis_size("head")
    return lax.ppermute(piece, "head", [(i, (i + 1) % count) for i in range(count)])


def together(moved, *values):
    return lax.optimization_barrier((moved,) + values)


def adam_kernel(at, packed, pair_side, *refs, rates, pieces):
    olds, base, adds, news = refs[:18], refs[18], refs[19 : 19 + pieces], refs[20 + pieces : 38 + pieces]
    changed, table = refs[38 + pieces :]
    step = pl.program_id(0)
    add_pieces(step, base, adds, changed)

    @pl.when(step == 0)
    def _():
        adam_step(at, packed, pair_side, olds, news, table, rates)


def adam_step(at, packed, pair_side, olds, news, table, rates):
    norms, heads_in, heads_out, bias_weight, outer_in, outer_out = [olds[3 * n : 3 * n + 3] for n in range(6)]
    count, local, all_heads = heads_in[0].shape
    sides, size = outer_in[0].shape[:2]

    def rows(first, lines):
        return packed[pl.ds(first, lines), :].astype(F32)

    def pair_of(first, offset, lines, span):
        return jnp.concatenate([rows(first + offset, lines), rows(first + span + offset, lines)], axis=1)

    def update(n, index, grad):
        weight, moment_one, moment_two = [ref[index] for ref in olds[3 * n : 3 * n + 3]]
        for ref, new in zip(
            news[3 * n : 3 * n + 3], adam_update(weight, grad, moment_one, moment_two, rates[n])
        ):
            ref[index] = new

    mine = pl.multiple_of(at[4], local)
    span = count * all_heads
    for k in range(count):
        update(1, k, pair_of(0, k * all_heads + mine, local, span))
    first = 2 * span
    update(2, slice(None), pair_of(first, mine, local, all_heads))
    first += 2 * all_heads
    for k in range(sides):
        update(4, k, pair_of(first, k * size, size, sides * size))
    first += 2 * sides * size
    table[...] = rows(first, size * size)
    for e in range(size):
        update(5, slice(e * size, (e + 1) * size), table[pl.ds(e, size, stride=size), :])
    pair = pair_side[...]
    low = pair[2 * HEADS :]
    lines = [
        jnp.concatenate([low[n : n + 1], low[n + 4 : n + 5], low[n + 2 : n + 3], low[n + 6 : n + 7], pair[HEADS + n : HEADS + n + 1]], axis=1)
        for n in range(2)
    ]
    update(0, slice(None), jnp.concatenate(lines, axis=0))
    update(3, slice(None), pair[:HEADS])


def adam_all(at, packed, pair_side, olds, rates, base, pieces, into):
    turned = (1, 3, 4)
    flat = [array.swapaxes(-1, -2) if n in turned else array for n, triple in enumerate(olds) for array in triple]
    size = olds[4][0].shape[2]
    by_order, added = added_specs(base, pieces)
    whole = lambda array: pl.BlockSpec(array.shape, lambda n, at: (0,) * array.ndim)
    *news, changed = pl.pallas_call(
        functools.partial(adam_kernel, rates=rates, pieces=len(pieces)),
        grid_spec=pltpu.PrefetchScalarGridSpec(
            num_scalar_prefetch=1,
            grid=(len(pieces),),
            in_specs=[whole(array) for array in [packed, pair_side] + flat]
            + added
            + [pl.BlockSpec(memory_space=pl.ANY)],
            out_specs=[whole(array) for array in flat] + [by_order],
            scratch_shapes=[pltpu.VMEM((size * size, packed.shape[1]), F32)],
        ),
        out_shape=[jax.ShapeDtypeStruct(array.shape, F32) for array in flat + [base]],
        input_output_aliases={3 + len(flat) + 1 + len(pieces): len(flat)},
        compiler_params=pltpu.CompilerParams(vmem_limit_bytes=VMEM),
        cost_estimate=cost(5),
    )(at, packed, pair_side, *flat, base, *pieces, into)
    news = [array.swapaxes(-1, -2) if n // 3 in turned else array for n, array in enumerate(news)]
    return news + [changed]


def per_device(
    alignment,
    pairs,
    residue_mask,
    row_mask,
    alignment_back,
    pairs_back,
    norm_scales,
    heads_in,
    heads_out,
    bias_weight,
    outer_in,
    outer_out,
    first_norms,
    second_norms,
    first_heads_in,
    second_heads_in,
    first_heads_out,
    second_heads_out,
    first_bias_weight,
    second_bias_weight,
    first_outer_in,
    second_outer_in,
    first_outer_out,
    second_outer_out,
):
    row_count = lax.axis_size("row")
    head_count = lax.axis_size("head")
    head_index = lax.axis_index("head")
    devices = row_count * head_count
    rows_here, residues, width = alignment.shape
    pair_rows, pair_cols, pair_width = pairs.shape
    size = width // HEADS
    outer_width = outer_in.shape[2]
    all_rows = rows_here * row_count
    own = rows_here // head_count
    start = head_index * own
    scales = norm_scales[:, : 2 * width].reshape(2, 2, width).swapaxes(0, 1).reshape(4, width)
    pair_gain = norm_scales[0:1, 2 * width :]
    pair_shift = norm_scales[1:2, 2 * width :]
    residue_live = residue_mask.astype(F32)
    key_mask = ((residue_live - 1.0) * (1e9 * LOG2E))[:, None]
    row_live = lax.dynamic_slice_in_dim(row_mask, start, own, 0).astype(F32)
    live = (row_live[:, None] * residue_live[None])[:, None]
    flat_live = jnp.repeat(residue_live.reshape(-1, QUADS), outer_in.shape[2], axis=1)
    row_live = jnp.broadcast_to(row_live[:, None, None], (own, 1, 128))
    bias_low = bias_weight.astype(BF16)

    fast = (row_count, head_count, pair_cols, own * outer_width) == (8, 4, 128, 128)

    local = heads_in.shape[2]
    shard = jnp.concatenate([heads_in.astype(BF16).swapaxes(1, 2), heads_out.astype(BF16)[None]])
    outer_t = outer_in.astype(BF16).swapaxes(1, 2).reshape(2 * outer_width, width)
    if fast:
        bias, weights = pair_bias(pairs, norm_scales[:, 2 * width :], bias_low.T, shard)
    else:
        weights = lax.all_gather(shard, "head", axis=1, tiled=True)
        bias = pair_forward(pairs, pair_gain, pair_shift, bias_low)
        bias = lax.all_gather(bias, "head", axis=2, tiled=True)
        bias = lax.all_gather(bias, "row", axis=1, tiled=True)[None, None]
    in_t = weights[:4].reshape(4 * width, width)
    out_low = weights[4]

    update, left, right, kept = attention_forward(
        start.astype(jnp.int32)[None],
        alignment, scales, in_t, out_low, outer_t, bias, key_mask, live, row_live, flat_live,
    )

    split = own // 2
    if fast:
        total, left_grad, right_grad, table_grad, one, two = outer_product(
            left, right, pairs_back, outer_out, update, all_rows
        )
        updates = [update[:split], update[split:], one[:split], one[split:], two]
    else:
        table = outer_out.astype(BF16).reshape(outer_width, outer_width, pair_width)
        updates = [update]
        for _ in range(head_count - 1):
            updates.append(hop(updates[-1]))
        left = left.reshape(own, residues, outer_width).swapaxes(1, 2)
        left = left.reshape(own, outer_width, row_count, pair_rows).transpose(2, 0, 1, 3)
        right = right.reshape(own, outer_width, head_count, pair_cols).transpose(2, 0, 1, 3)
        both = (row_count, head_count, own, outer_width)
        send = jnp.concatenate(
            [
                jnp.broadcast_to(left[:, None], both + (pair_rows,)),
                jnp.broadcast_to(right[None], both + (pair_cols,)),
            ],
            axis=4,
        )
        flat = (devices, own, outer_width, pair_rows + pair_cols)
        got = lax.all_to_all(send.reshape(flat), EVERY, split_axis=0, concat_axis=0, tiled=True)
        got = got.reshape(all_rows, outer_width, pair_rows + pair_cols)
        total, table_grad, left_grad, right_grad = outer_product_plain(
            got[:, :, :pair_rows], got[:, :, pair_rows:], pairs_back, table, all_rows
        )
        pairs_new = pairs + total
        send = jnp.concatenate([left_grad, right_grad], axis=2).reshape(flat)
        got = lax.all_to_all(send, EVERY, split_axis=0, concat_axis=0, tiled=True)
        got = got.reshape(both + (pair_rows + pair_cols,)).astype(F32)
        left_grad = jnp.sum(got[..., :pair_rows], axis=1).transpose(1, 0, 3, 2).astype(BF16)
        left_grad = left_grad.reshape(own, residues // QUADS, QUADS * outer_width)
        right_grad = jnp.sum(got[..., pair_rows:], axis=0).transpose(1, 2, 0, 3).astype(BF16)
        right_grad = right_grad.reshape(own, outer_width, residues)
        table_grad = table_grad.swapaxes(0, 1).reshape(outer_width * outer_width, pair_width)

    turns = (head_index + head_count - jnp.arange(head_count, dtype=jnp.int32)) % head_count
    order = (turns[:, None] * own + jnp.arange(own, dtype=jnp.int32)[None]).reshape(-1)
    half = own // 2

    def mine(first, hops, second, more):
        parts = [(first, step) for step in hops] + [(second, step) for step in more]
        return jnp.concatenate([order[step * own + n * half : step * own + (n + 1) * half] for n, step in parts])

    backward = functools.partial(
        attention_backward,
        order, alignment, update, alignment_back, scales, in_t, out_low, outer_t, left_grad, right_grad,
        live, row_live, flat_live, kept, bias.shape,
    )
    if fast:
        moved = [hop(updates[3]), hop(updates[4])]
    part, bias_grad, *early = backward(first=0, own=half)
    if fast:
        moved, bias_grad, part, early = together(moved, bias_grad, part, early)
        updates += moved
        left_over = hop(updates[5])
    changes = [[part, hop(part)]]
    alignment_new, part, bias_grad, packed, norms = backward(
        first=half, own=half, earlier=bias_grad, early=early, table_grad=table_grad, pieces=updates
    )
    if fast:
        left_over, changes[0][1], bias_grad, part, packed, norms = together(
            left_over, changes[0][1], bias_grad, part, packed, norms
        )
        changes[0].append(hop(changes[0][1]))
        changes.append([part, hop(part)])
        bias_grad, packed = sum_gradients(bias_grad, packed)
        changes[0][2], changes[1][1], bias_grad = together(changes[0][2], changes[1][1], bias_grad)
        changes[0].append(hop(changes[0][2]))
        changes[1].append(hop(changes[1][1]))
        pairs_grad, pairs_new, pair_side, alignment_grad = pair_norm_backward(
            mine(0, (0, 1, 2), 1, (0, 1)),
            pairs,
            pairs_back,
            total,
            bias_grad,
            norm_scales[:, 2 * width :],
            bias_low.T,
            norms,
            alignment_back,
            changes[0][:3] + changes[1][:2],
        )
        packed, pair_side = spread_gradients(packed, pair_side)
        changes[0][3], changes[1][2], packed = together(changes[0][3], changes[1][2], packed)
        changes[1].append(hop(changes[1][2]))
    else:
        for _ in range(head_count - 2):
            changes[0].append(hop(changes[0][-1]))
        changes.append([part])
        for _ in range(head_count - 1):
            changes[1].append(hop(changes[1][-1]))
        bias_grad = lax.psum_scatter(bias_grad[0, 0], "row", scatter_dimension=1, tiled=True)
        bias_grad = lax.psum_scatter(bias_grad, "head", scatter_dimension=2, tiled=True)
        pairs_grad, bias_weight_grad, pair_gain_grad, pair_shift_grad = pair_backward(
            pairs, pairs_back, pair_gain, pair_shift, bias_low, bias_grad
        )
        packed, norms, bias_weight_total, pair_norms_total = lax.psum(
            (packed.astype(F32), norms, bias_weight_grad, jnp.stack([pair_gain_grad, pair_shift_grad])), EVERY
        )
    olds = (
        (norm_scales, first_norms, second_norms),
        (heads_in, first_heads_in, second_heads_in),
        (heads_out, first_heads_out, second_heads_out),
        (bias_weight, first_bias_weight, second_bias_weight),
        (outer_in, first_outer_in, second_outer_in),
        (outer_out, first_outer_out, second_outer_out),
    )
    rates = (
        0.5,
        width ** (-0.5),
        max(2 * HEADS * size // residues, 1) ** (-0.5),
        pair_width ** (-0.5),
        width ** (-0.5),
        max(outer_width * outer_width // all_rows, 1) ** (-0.5),
    )
    if fast:
        at = (head_index * local).astype(jnp.int32)[None]
        *news, alignment_grad = adam_all(
            jnp.concatenate([mine(0, (3,), 1, (2,)), at]),
            packed, pair_side, olds, rates, alignment_back, [changes[0][3], changes[1][2]], alignment_grad,
        )
        at = (turns[3] * 2 + 1)[None]
        alignment_new = add_rows(at, alignment, left_over, alignment_new)
        alignment_grad = add_rows(at, alignment_back, changes[1][3], alignment_grad)
        return (alignment_new, pairs_new, alignment_grad, pairs_grad, *news)
    alignment_grad = None
    for step in range(head_count):
        for n in range(2):
            at = (turns[step] * 2 + n)[None]
            alignment_grad = add_rows(at, alignment_back, changes[n][step], alignment_grad)
    def unpack(first, lines):
        return jnp.concatenate([packed[first : first + lines], packed[first + lines : first + 2 * lines]], axis=1)

    lines = 4 * width
    heads_in_total = lax.dynamic_slice_in_dim(
        unpack(0, lines).reshape(4, width, width), head_index * local, local, 1
    ).swapaxes(1, 2)
    heads_out_total = lax.dynamic_slice_in_dim(unpack(2 * lines, width), head_index * local, local, 0)
    lines = 2 * (lines + width)
    outer_in_total = unpack(lines, 2 * outer_width).reshape(2, outer_width, width).swapaxes(1, 2)
    lines += 4 * outer_width
    table_total = packed[lines : lines + outer_width * outer_width]
    table_total = table_total.reshape(outer_width, outer_width, pair_width).swapaxes(0, 1)
    table_total = table_total.reshape(outer_width * outer_width, pair_width)
    norms_total = jnp.concatenate(
        [norms.reshape(2, 2, width).swapaxes(0, 1).reshape(2, 2 * width), pair_norms_total], axis=1
    )
    totals = (norms_total, heads_in_total, heads_out_total, bias_weight_total, outer_in_total, table_total)
    news = []
    for (weight, moment_one, moment_two), total, rate in zip(olds, totals, rates):
        news += adam_update(weight, total, moment_one, moment_two, rate)
    return (alignment_new, pairs_new, alignment_grad, pairs_grad, *news)


def solution(mesh):
    row_msa = P("row", None, None)
    pair = P("row", "head", None)
    columns = P(None, None, "head")
    lines = P("head", None)
    in_specs = (
        (row_msa, pair, P(), P("row"), row_msa, pair, P(), columns, lines)
        + (P(),) * 5
        + (columns,) * 2
        + (lines,) * 2
        + (P(),) * 6
    )
    out_specs = (row_msa, pair, row_msa, pair) + (P(),) * 3 + (columns,) * 3 + (lines,) * 3 + (P(),) * 9
    return jax.shard_map(
        per_device, mesh=mesh, in_specs=in_specs, out_specs=out_specs, check_vma=False
    )
```

```python
import functools

import jax
import jax.numpy as jnp
from jax import lax
from jax.experimental import pallas as pl
from jax.experimental.pallas import tpu as pltpu
from jax.sharding import PartitionSpec as P

HEADS = 8
STEP = 10
F32 = jnp.float32
BF16 = jnp.bfloat16
LOG2E = 1.4426950408889634
VMEM = 56 << 20
EVERY = ("row", "head")


def adam_update(weight, gradient, moment_one, moment_two, step_rate):
    first_new = 0.9 * moment_one + 0.1 * gradient
    second_new = 0.999 * moment_two + 0.001 * gradient * gradient
    first_hat = first_new / (1.0 - 0.9**STEP)
    second_hat = second_new / (1.0 - 0.999**STEP)
    updated = weight - step_rate * (first_hat / (jnp.sqrt(second_hat) + 1e-08) + 0.01 * weight)
    return (first_new, second_new, updated)


def cost(micros):
    return pl.CostEstimate(flops=0, bytes_accessed=int(micros * 3.5e6), transcendentals=0)


def dot(a, b, along):
    return lax.dot_general(a, b, (((along[0],), (along[1],)), ((), ())), preferred_element_type=F32)


def normalize(values):
    center = values - jnp.mean(values, axis=-1, keepdims=True)
    rstd = lax.rsqrt(jnp.mean(center * center, axis=-1, keepdims=True) + 1e-05)
    return center * rstd, rstd


def norm_backward(hat, rstd, gain, grad):
    scaled = grad * gain
    return rstd * (
        scaled
        - jnp.mean(scaled, axis=-1, keepdims=True)
        - hat * jnp.mean(scaled * hat, axis=-1, keepdims=True)
    )


QUADS = 4


def quad(outer_t, q):
    weights = outer_t[: outer_t.shape[0] // 2]
    zero = jnp.zeros_like(weights)
    return jnp.concatenate([weights if n == q else zero for n in range(QUADS)], axis=0)


def put(ref, value):
    for n in range(ref.shape[0]):
        ref[n] = value[:, n * 128 : (n + 1) * 128]


def take(ref, q):
    at = pl.ds(q, ref.shape[1] // QUADS, stride=QUADS)
    return jnp.concatenate([ref[n, at, :] for n in range(ref.shape[0])], axis=1)


ROW_SENDS = 20


class Exchange:
    def __init__(
        self, left, right, left_stage, right_stage, left_plane, right_line, left_all, right_all,
        local_sem, send_sem, recv_sem,
    ):
        self.left, self.right, self.left_stage, self.right_stage = left, right, left_stage, right_stage
        self.left_plane, self.right_line, self.left_all, self.right_all = left_plane, right_line, left_all, right_all
        self.local_sem, self.send_sem, self.recv_sem = local_sem, send_sem, recv_sem
        self.row, self.head = place()
        self.beyond = [(self.head + k) % 4 for k in range(4)]
        self.behind = [(self.head + 4 - k) % 4 for k in range(4)]
        self.plane = [(flip(self.row, way), self.head) for way in range(8)]
        self.lines = left_plane.shape[2]
        self.cols = right_line.shape[3]

    def copy(self, n, source, target, device):
        return pltpu.make_async_remote_copy(
            src_ref=source,
            dst_ref=target,
            send_sem=self.send_sem.at[n],
            recv_sem=self.recv_sem.at[n],
            device_id=device,
            device_id_type=MESH,
        )

    def first(self):
        out = [
            self.copy(7 + k, self.right_stage.at[self.beyond[k + 1]], self.right_line.at[self.head],
                      (self.row, self.beyond[k + 1]))
            for k in range(3)
        ]
        out += [
            self.copy(n, self.left_stage.at[self.plane[way][0]], self.left_plane.at[self.row], self.plane[way])
            for n, way in enumerate((2, 4, 6, 3, 5, 7, 1))
        ]
        return out

    def second(self, which):
        if which == "left":
            return [
                self.copy(10 + k, self.left_plane, self.left_all.at[self.head], (self.row, self.beyond[k + 1]))
                for k in range(3)
            ]
        if which == "core":
            return [self.copy(16, self.right_line, self.right_all.at[self.row], self.plane[CORE])]
        return [
            self.copy(13 + n, self.right_line, self.right_all.at[self.row], self.plane[way])
            for n, way in enumerate((ACROSS, DOWN, CORNER))
        ]

    def third(self):
        out = []
        for n, way in enumerate((ACROSS, DOWN, CORNER)):
            block = self.right_all.at[self.plane[way][0]]
            out.append(self.copy(17 + n, block, block, self.plane[CORE]))
        return out

    def locals(self):
        return [
            pltpu.make_async_copy(self.left_plane, self.left_all.at[self.head], self.local_sem.at[0]),
            pltpu.make_async_copy(self.right_line, self.right_all.at[self.row], self.local_sem.at[1]),
        ]

    def begin(self):
        for r in range(8):
            self.left_stage[r] = self.left[:, r * self.lines : (r + 1) * self.lines, :]
        for h in range(4):
            self.right_stage[h] = self.right[:, :, h * self.cols : (h + 1) * self.cols]
        self.left_plane[self.row] = self.left_stage[self.row]
        self.right_line[self.head] = self.right_stage[self.head]
        for copy in self.first():
            copy.start()

    def go_on(self):
        for copy in self.first():
            copy.wait_recv()
        for copy in self.second("chips") + self.second("core") + self.second("left") + self.locals():
            copy.start()

    def core(self):
        for copy in self.second("chips"):
            copy.wait_recv()
        for copy in self.third():
            copy.start()

    def end(self):
        for copy in self.second("left") + self.second("core") + self.third():
            copy.wait()
        for copy in self.locals():
            copy.wait()
        for copy in self.first() + self.second("chips"):
            copy.wait_send()


def forward_kernel(*refs, share):
    (rows, scales, in_t, out_low, outer_t, bias, key_mask, live, row_live, flat_live), refs = refs[:10], refs[10:]
    (update, left, right, qkv, gate, powers, inverse, mixed, attended), refs = refs[:9], refs[9:]
    if share:
        (left_all, right_all, hop_one), refs = refs[:3], refs[3:]
        left_stage, right_stage, left_plane, right_line, local_sem, send_sem, recv_sem, hop_sem = refs[-8:]
    bias_t, second, rows_in, load_sem = refs[:4]
    row = pl.program_id(0)
    own = update.shape[0]
    width = rows.shape[2]
    residues = rows.shape[1]
    size = width // HEADS
    half = outer_t.shape[0] // 2
    start = lax.axis_index("head") * own
    device_row, device_head = place()

    def load(n):
        return pltpu.make_async_copy(rows.at[start + n], rows_in.at[n % 2], load_sem.at[n % 2])

    def exchange():
        return Exchange(
            left.at[pl.ds(0, own - 1)], right.at[pl.ds(0, own - 1)], left_stage, right_stage,
            left_plane, right_line, left_all, right_all, local_sem, send_sem, recv_sem,
        )

    def hop_copy(n):
        return pltpu.make_async_remote_copy(
            src_ref=update.at[n],
            dst_ref=hop_one.at[n],
            send_sem=hop_sem.at[0, n],
            recv_sem=hop_sem.at[1, n],
            device_id=(device_row, (device_head + 1) % 4),
            device_id_type=MESH,
        )

    @pl.when(row == 0)
    def _():
        load(0).start()
        if own > 1:
            load(1).start()
        if share:
            greet(
                [(flip(device_row, way), device_head) for way in range(1, 8)]
                + [(device_row, (device_head + k) % 4) for k in (1, 2, 3)]
            )
        across, down, _, lines, cols = bias.shape
        group = max(1, 128 // lines)

        def turn(head, carry):
            for r in range(0, across, group):
                for c in range(down):
                    tile = jnp.concatenate([bias[r + g, c, head] for g in range(group)], axis=0)
                    bias_t[head, c * cols : (c + 1) * cols, r * lines : (r + group) * lines] = (
                        tile.astype(F32).T + key_mask[c * cols : (c + 1) * cols]
                    )
            return carry

        lax.fori_loop(0, HEADS, turn, 0)

    load(row).wait()
    values_in = rows_in[row % 2]
    hat, _ = normalize(values_in)
    normed = (hat * scales[0:1] + scales[1:2]).astype(BF16)
    qkv[0, :width] = (dot(in_t[:width], normed, (1, 1)) * (size**-0.5 * LOG2E)).astype(BF16)
    qkv[0, width:] = dot(in_t[width : 3 * width], normed, (1, 1)).astype(BF16)
    gate[0] = jax.nn.sigmoid(dot(in_t[3 * width :], normed, (1, 1)))
    for head in range(HEADS):
        at = head * size
        keys = qkv[0, width + at : width + at + size]
        values = qkv[0, 2 * width + at : 2 * width + at + size]
        query = qkv[0, at : at + size]
        scores = dot(keys, query, (0, 0)) + bias_t[head]
        exps = jnp.exp2(scores - jnp.max(scores, axis=0, keepdims=True))
        over = 1.0 / jnp.sum(exps, axis=0, keepdims=True)
        low = exps.astype(BF16)
        powers[0, head] = low
        inverse[0, head] = over
        mixed[0, at : at + size] = dot(values, low, (1, 0)) * over
        if share and head == HEADS // 2 - 1:
            @pl.when(row == own - 1)
            def _():
                exchange().go_on()
    att = (gate[0] * mixed[0]).astype(BF16)
    attended[0] = att
    change = dot(att, out_low[...], (0, 0)).astype(BF16)
    update[row] = change
    hat, _ = normalize(rows_in[row % 2] + change.astype(F32))
    normed = hat * scales[2:3] + scales[3:4]
    put(second, normed)
    right[row] = (dot(outer_t[half:], normed.astype(BF16), (1, 1)) * live[0]).astype(BF16)
    out = jnp.zeros(flat_live.shape, F32)
    for q in range(QUADS):
        out += dot(take(second, q).astype(BF16), quad(outer_t, q), (1, 1))
    left[row] = (out * flat_live[...] * row_live[0]).astype(BF16)

    @pl.when(row + 2 < own)
    def _():
        load(row + 2).start()

    if share:
        @pl.when(row == own - 2)
        def _():
            exchange().begin()

        @pl.when(row < own // 2)
        def _():
            hop_copy(row).start()

        @pl.when(row == own - 1)
        def _():
            exchange().core()
            for n in range(own // 2):
                hop_copy(n).wait()
            exchange().end()


def attention_forward(rows, scales, in_t, out_low, outer_t, bias, key_mask, live, row_live, flat_live, share):
    _, residues, width = rows.shape
    own = live.shape[0]
    sides = outer_t.shape[0] // 2
    by_row = lambda s: (s, 0, 0)
    by_row_four = lambda s: (s, 0, 0, 0)
    hbm = pl.BlockSpec(memory_space=pl.ANY)
    once = lambda array: pl.BlockSpec(array.shape, lambda s: (0,) * array.ndim, pipeline_mode=pl.Buffered(1))
    whole = lambda *shape: pl.BlockSpec(shape, lambda s: (0,) * len(shape))
    lines, cols = flat_live.shape[0] // 8, residues // 4
    early = own - 1
    out_specs = [
        whole(own, residues, width),
        whole(own, *flat_live.shape),
        whole(own, sides, residues),
        pl.BlockSpec((1, 3 * width, residues), by_row),
        pl.BlockSpec((1, width, residues), by_row),
        pl.BlockSpec((1, HEADS, residues, residues), by_row_four),
        pl.BlockSpec((1, HEADS, 1, residues), by_row_four),
        pl.BlockSpec((1, width, residues), by_row),
        pl.BlockSpec((1, width, residues), by_row),
    ]
    out_shape = [
        jax.ShapeDtypeStruct((own, residues, width), BF16),
        jax.ShapeDtypeStruct((own,) + flat_live.shape, BF16),
        jax.ShapeDtypeStruct((own, sides, residues), BF16),
        jax.ShapeDtypeStruct((own, 3 * width, residues), BF16),
        jax.ShapeDtypeStruct((own, width, residues), F32),
        jax.ShapeDtypeStruct((own, HEADS, residues, residues), BF16),
        jax.ShapeDtypeStruct((own, HEADS, 1, residues), F32),
        jax.ShapeDtypeStruct((own, width, residues), F32),
        jax.ShapeDtypeStruct((own, width, residues), BF16),
    ]
    scratch = [
        pltpu.VMEM((HEADS, residues, residues), F32),
        pltpu.VMEM((width // 128, residues, 128), F32),
        pltpu.VMEM((2, residues, width), F32),
        pltpu.SemaphoreType.DMA((2,)),
    ]
    params = dict(vmem_limit_bytes=VMEM)
    if share:
        params.update(collective_id=2, has_side_effects=True)
        out_specs += [hbm] * 3
        out_shape += [
            jax.ShapeDtypeStruct((4, 8, early, lines, 128), BF16),
            jax.ShapeDtypeStruct((8, 4, early, sides, cols), BF16),
            jax.ShapeDtypeStruct((own // 2, residues, width), BF16),
        ]
        scratch += [
            pltpu.VMEM((8, early, lines, 128), BF16),
            pltpu.VMEM((4, early, sides, cols), BF16),
            pltpu.VMEM((8, early, lines, 128), BF16),
            pltpu.VMEM((4, early, sides, cols), BF16),
            pltpu.SemaphoreType.DMA((2,)),
            pltpu.SemaphoreType.DMA((ROW_SENDS,)),
            pltpu.SemaphoreType.DMA((ROW_SENDS,)),
            pltpu.SemaphoreType.DMA((2, own // 2)),
        ]
    out = pl.pallas_call(
        functools.partial(forward_kernel, share=share),
        grid=(own,),
        in_specs=[
            hbm,
            once(scales),
            once(in_t),
            once(out_low),
            once(outer_t),
            once(bias),
            once(key_mask),
            pl.BlockSpec((1, 1, residues), by_row),
            pl.BlockSpec((1, 1, 128), by_row),
            once(flat_live),
        ],
        out_specs=out_specs,
        scratch_shapes=scratch,
        out_shape=out_shape,
        cost_estimate=cost(30),
        compiler_params=pltpu.CompilerParams(**params),
    )(rows, scales, in_t, out_low, outer_t, bias, key_mask, live, row_live, flat_live)
    return out[0], out[1], out[2], tuple(out[3:9]), tuple(out[9:])


def backward_kernel(*refs, earlier, adds):
    (order, rows, update, back, scales, in_t, out_low, outer_t, left_grad, right_grad, live, row_live, flat_live,
     qkv, gate, powers, inverse, mixed, attended), refs = refs[:19], refs[19:]
    if earlier:
        so_far, early, table_grad, base = refs[0], refs[1:5], refs[5], refs[6]
        pieces, refs = refs[7 : 7 + adds], refs[7 + adds :]
        added, part, bias_grad, packed, norms = refs[:5]
        bias_low, base_in, piece_in, load_sem, piece_sem, store_sem = refs[-6:]
        heads_in_grad, heads_out_grad, outer_in_grad = refs[-9:-6]
        refs = refs[5:-9]
    else:
        part, bias_grad, heads_in_grad, heads_out_grad, outer_in_grad, norms = refs[:6]
        refs = refs[6:]
    bias_total, mixed_grad, proj_grad, spread, bias_sem = refs
    row = pl.program_id(0)
    own = pl.num_programs(0)
    width = rows.shape[2]
    residues = rows.shape[1]
    size = width // HEADS
    last_row = row == own - 1
    rows_here = base.shape[0] if earlier else 0
    if earlier:
        per, each = base_in.shape[1:3]
        bounds = [0]
        for piece in pieces:
            bounds.append(bounds[-1] + piece.shape[0] // each)
        steps = bounds[-1]

        def bias_load(head):
            return pltpu.make_async_copy(so_far.at[head], bias_total.at[head], bias_sem.at[head])

        def row_of(step):
            return pl.ds(order[step * each], each)

        def fetch(batch, slot):
            for n in range(per):
                step = batch * per + n
                for piece in range(adds):
                    low, high = bounds[piece], bounds[piece + 1]

                    @pl.when((step >= low) & (step < high))
                    def _():
                        pltpu.make_async_copy(base.at[row_of(step)], base_in.at[slot, n], load_sem.at[slot, n]).start()
                        source = pieces[piece].at[pl.ds((step - low) * each, each)]
                        pltpu.make_async_copy(source, piece_in.at[slot, n], piece_sem.at[slot, n]).start()

        def store(batch, slot, n):
            return pltpu.make_async_copy(base_in.at[slot, n], added.at[row_of(batch * per + n)], store_sem.at[slot, n])

        def add_batch(batch, slot):
            for n in range(per):
                step = batch * per + n

                @pl.when((batch >= 1) & (step - per < steps))
                def _():
                    store(batch - 1, 1 - slot, n).wait()
            fetch(batch + 1, 1 - slot)
            for n in range(per):
                step = batch * per + n

                @pl.when(step < steps)
                def _():
                    pltpu.make_async_copy(base.at[row_of(step)], base_in.at[slot, n], load_sem.at[slot, n]).wait()
                    source = pieces[0].at[pl.ds(0, each)]
                    pltpu.make_async_copy(source, piece_in.at[slot, n], piece_sem.at[slot, n]).wait()
                    base_in[slot, n] = base_in[slot, n] + piece_in[slot, n].astype(F32)
                    store(batch, slot, n).start()

    @pl.when(row == 0)
    def _():
        for n, ref in enumerate((heads_in_grad, heads_out_grad, outer_in_grad, norms)):
            ref[...] = early[n][...] if earlier else jnp.zeros_like(ref)
        if earlier:
            for head in range(HEADS):
                bias_load(head).start()
            fetch(0, 0)

    half = outer_t.shape[0] // 2
    count = residues // QUADS
    hat, rstd = normalize(rows[0] + update[0].astype(F32))
    second = hat * scales[2:3] + scales[3:4]
    put(spread, second)
    grads = (right_grad[0].astype(F32) * live[0]).astype(BF16)
    outer_in_grad[half:] += dot(grads, second.astype(BF16), (1, 0))
    flat = (left_grad[0].astype(F32) * flat_live[...] * row_live[0]).astype(BF16).T
    for q in range(QUADS):
        mine = flat[q * half : (q + 1) * half]
        outer_in_grad[:half] += dot(mine, take(spread, q).astype(BF16), (1, 0))
        back_to = dot(mine, outer_t[:half], (0, 0))
        for n in range(spread.shape[0]):
            spread[n, pl.ds(q, count, stride=QUADS), :] = back_to[:, n * 128 : (n + 1) * 128]
    spread_grad = jnp.concatenate([spread[n] for n in range(spread.shape[0])], axis=1)
    second_grad = spread_grad + dot(grads, outer_t[half:], (0, 0))
    norms[2:3] += jnp.sum(second_grad * hat, axis=0, keepdims=True)
    norms[3:4] += jnp.sum(second_grad, axis=0, keepdims=True)
    new_part = norm_backward(hat, rstd, scales[2:3], second_grad)
    put(spread, new_part)
    out_grad = (back[0] + new_part).astype(BF16)
    heads_out_grad[...] += dot(attended[0], out_grad, (1, 0))
    attended_grad = dot(out_low[...], out_grad, (1, 1))
    sig = gate[0]
    gated = attended_grad * sig
    proj_grad[3 * width :] = (gated * mixed[0] * (1.0 - sig)).astype(BF16)
    deltas = []
    for head in range(HEADS):
        span = slice(head * size, (head + 1) * size)
        grad = gated[span] * inverse[0, head]
        mixed_grad[span] = grad.astype(BF16)
        deltas.append(jnp.sum(grad * mixed[0, span], axis=0, keepdims=True))

    if earlier:
        @pl.when(row == 0)
        def _():
            for head in range(HEADS):
                bias_load(head).wait()

    for head in range(HEADS):
        at = head * size
        query = qkv[0, at : at + size]
        keys = qkv[0, width + at : width + at + size]
        values = qkv[0, 2 * width + at : 2 * width + at + size]
        grad = mixed_grad[at : at + size]
        low = powers[0, head]
        prob_grad = dot(values, grad, (0, 0))
        score_grad = low.astype(F32) * (prob_grad - deltas[head])
        if earlier:
            bias_total[head] += score_grad
        else:
            bias_total[head] = jnp.where(row == 0, 0.0, bias_total[head]) + score_grad
        score_low = score_grad.astype(BF16)
        proj_grad[2 * width + at : 2 * width + at + size] = dot(grad, low, (1, 1)).astype(BF16)
        proj_grad[width + at : width + at + size] = (dot(query, score_low, (1, 1)) / LOG2E).astype(BF16)
        proj_grad[at : at + size] = (dot(keys, score_low, (1, 0)) * size**-0.5).astype(BF16)
        if earlier and (head + 1) % per == 0:
            add_batch(row * (HEADS // per) + head // per, head // per % 2)
        if not earlier:
            @pl.when(last_row)
            def _():
                pltpu.make_async_copy(bias_total.at[head], bias_grad.at[head], bias_sem.at[head]).start()

    if earlier:
        @pl.when(last_row)
        def _():
            across, down, _, lines, cols = bias_grad.shape
            group = max(1, 128 // lines)
            for head in range(HEADS):
                for r in range(0, across, group):
                    for c in range(down):
                        tile = bias_total[head, c * cols : (c + 1) * cols, r * lines : (r + group) * lines]
                        tile = tile.T.astype(BF16)
                        for g in range(group):
                            bias_low[head, r + g, c] = tile[g * lines : (g + 1) * lines]
                pltpu.make_async_copy(bias_low.at[head], bias_grad.at[:, :, head], bias_sem.at[head]).start()

    hat, rstd = normalize(rows[0])
    normed = (hat * scales[0:1] + scales[1:2]).astype(BF16)
    grads = proj_grad[...]
    heads_in_grad[...] += dot(grads, normed, (1, 0))
    normed_grad = dot(grads, in_t[...], (0, 0))
    norms[0:1] += jnp.sum(normed_grad * hat, axis=0, keepdims=True)
    norms[1:2] += jnp.sum(normed_grad, axis=0, keepdims=True)
    new_part = jnp.concatenate([spread[n] for n in range(spread.shape[0])], axis=1)
    part[0] = (new_part + norm_backward(hat, rstd, scales[0:1], normed_grad)).astype(BF16)

    @pl.when(last_row)
    def _():
        if earlier:
            first = 0
            for ref in (heads_in_grad, heads_out_grad, outer_in_grad):
                lines = ref.shape[0]
                packed[first : first + lines] = ref[:, :128].astype(BF16)
                packed[first + lines : first + 2 * lines] = ref[:, 128:].astype(BF16)
                first += 2 * lines
            lines = table_grad.shape[0]
            packed[first : first + lines] = table_grad[...].astype(BF16)
            first += lines
            packed[first:] = jnp.zeros((packed.shape[0] - first, 128), BF16)
            batch = rows_here // each // per - 1
            for n in range(per):
                if batch * per + n < steps:
                    store(batch, batch % 2, n).wait()
            for head in range(HEADS):
                pltpu.make_async_copy(bias_low.at[head], bias_grad.at[:, :, head], bias_sem.at[head]).wait()
        else:
            for head in range(HEADS):
                pltpu.make_async_copy(bias_total.at[head], bias_grad.at[head], bias_sem.at[head]).wait()


def attention_backward(
    order, rows, update, back, scales, in_t, out_low, outer_t, left_grad, right_grad, live, row_live, flat_live,
    kept, blocks, first, own, earlier=None, early=(), table_grad=None, pieces=(),
):
    _, residues, width = rows.shape
    qkv, gate, powers, inverse, mixed, attended = kept
    here = lambda s, order: (order[0] + first + s, 0, 0)
    by_row = lambda s, order: (first + s, 0, 0)
    by_row_four = lambda s, order: (first + s, 0, 0, 0)
    hbm = pl.BlockSpec(memory_space=pl.ANY)
    once = lambda array: pl.BlockSpec(
        array.shape, lambda s, order: (0,) * array.ndim, pipeline_mode=pl.Buffered(1)
    )
    whole = lambda array: pl.BlockSpec(array.shape, lambda s, order: (0,) * array.ndim)
    one = pl.BlockSpec((1, residues, width), here)
    args = [rows, update, back, scales, in_t, out_low, outer_t, left_grad, right_grad, live, row_live, flat_live]
    args += [qkv, gate, powers, inverse, mixed, attended]
    in_specs = [
        one,
        pl.BlockSpec((1, residues, width), by_row),
        one,
        once(scales),
        once(in_t),
        once(out_low),
        once(outer_t),
        pl.BlockSpec((1,) + left_grad.shape[1:], by_row),
        pl.BlockSpec((1,) + right_grad.shape[1:], by_row),
        pl.BlockSpec((1, 1, residues), by_row),
        pl.BlockSpec((1, 1, 128), by_row),
        once(flat_live),
        pl.BlockSpec((1, 3 * width, residues), by_row),
        pl.BlockSpec((1, width, residues), by_row),
        pl.BlockSpec((1, HEADS, residues, residues), by_row_four),
        pl.BlockSpec((1, HEADS, 1, residues), by_row_four),
        pl.BlockSpec((1, width, residues), by_row),
        pl.BlockSpec((1, width, residues), by_row),
    ]
    part = jax.ShapeDtypeStruct((own, residues, width), BF16)
    part_spec = pl.BlockSpec((1, residues, width), lambda s, order: (s, 0, 0))
    weights = [jax.ShapeDtypeStruct(array.shape, F32) for array in (in_t, out_low, outer_t)]
    norms = jax.ShapeDtypeStruct((4, width), F32)
    scratch = [
        pltpu.VMEM((HEADS, residues, residues), F32),
        pltpu.VMEM((width, residues), BF16),
        pltpu.VMEM((4 * width, residues), BF16),
        pltpu.VMEM((width // 128, residues, 128), F32),
        pltpu.SemaphoreType.DMA((HEADS,)),
    ]
    if earlier is None:
        out_shape = [part, jax.ShapeDtypeStruct((HEADS, residues, residues), F32)] + weights + [norms]
        out_specs = [part_spec, hbm] + [whole(array) for array in weights + [norms]]
    else:
        each = max(1, rows.shape[0] // (own * HEADS))
        args += [earlier, *early, table_grad, rows] + list(pieces)
        in_specs += [hbm] + [once(array) for array in [*early, table_grad]] + [hbm] * (1 + len(pieces))
        count = 2 * sum(array.shape[0] for array in weights) + table_grad.shape[0]
        count += -count % 512
        packed = jax.ShapeDtypeStruct((count, 128), BF16)
        out_shape = [jax.ShapeDtypeStruct(rows.shape, F32), part, jax.ShapeDtypeStruct(blocks, BF16), packed, norms]
        out_specs = [hbm, part_spec, hbm, whole(packed), whole(norms)]
        scratch += [pltpu.VMEM(array.shape, F32) for array in weights] + [
            pltpu.VMEM((HEADS,) + blocks[:2] + blocks[3:], BF16),
            pltpu.VMEM((2, HEADS // 2, each, residues, width), F32),
            pltpu.VMEM((2, HEADS // 2, each, residues, width), BF16),
            pltpu.SemaphoreType.DMA((2, HEADS // 2)),
            pltpu.SemaphoreType.DMA((2, HEADS // 2)),
            pltpu.SemaphoreType.DMA((2, HEADS // 2)),
        ]
    return pl.pallas_call(
        functools.partial(backward_kernel, earlier=earlier is not None, adds=len(pieces)),
        grid_spec=pltpu.PrefetchScalarGridSpec(
            num_scalar_prefetch=1, grid=(own,), in_specs=in_specs, out_specs=out_specs, scratch_shapes=scratch
        ),
        out_shape=out_shape,
        compiler_params=pltpu.CompilerParams(vmem_limit_bytes=VMEM),
        cost_estimate=cost(20),
    )(order, *args)


def outer_product_plain(left, right, pairs_back, table, all_rows):
    low = pairs_back.astype(BF16)
    product = mm("sei,sfj->eifj", left, right).astype(BF16)
    total = mm("eifj,efz->ijz", product, table) / all_rows
    table_grad = mm("eifj,ijz->efz", product, low) / all_rows
    back = mm("ijz,efz->eifj", low, table).astype(BF16)
    left_grad = mm("eifj,sfj->sei", back, right) / all_rows
    right_grad = mm("eifj,sei->sfj", back, left) / all_rows
    return total, table_grad, left_grad.astype(BF16), right_grad.astype(BF16)


def mm(spec, a, b):
    return jnp.einsum(spec, a, b, preferred_element_type=F32)


def pair_forward(pairs, gain, shift, bias_low):
    hat, _ = normalize(pairs)
    low = (hat * gain + shift).astype(BF16)
    return (mm("ijc,ch->hij", low, bias_low) * LOG2E).astype(BF16)


def pair_backward(pairs, pairs_back, gain, shift, bias_low, bias_grad):
    hat, rstd = normalize(pairs)
    low = (hat * gain + shift).astype(BF16)
    weight_grad = mm("ijc,hij->ch", low, bias_grad)
    in_grad = mm("hij,ch->ijc", bias_grad, bias_low)
    gain_grad = jnp.sum(in_grad * hat, axis=(0, 1))
    shift_grad = jnp.sum(in_grad, axis=(0, 1))
    return pairs_back + norm_backward(hat, rstd, gain, in_grad), weight_grad, gain_grad, shift_grad


MESH = pl.DeviceIdType.MESH
CORE, ACROSS, DOWN, CORNER = 1, 2, 4, 6


def place():
    return lax.axis_index("row"), lax.axis_index("head")


def flip(row, way):
    out = row
    for bit in (1, 2, 4):
        if way & bit:
            out = out + bit - 2 * bit * ((row // bit) % 2)
    return out


def greet(devices):
    barrier = pltpu.get_barrier_semaphore()
    for device in devices:
        pl.semaphore_signal(barrier, inc=1, device_id=device, device_id_type=MESH)
    pl.semaphore_wait(barrier, len(devices))


class Sends:
    def __init__(self, send_sem, recv_sem):
        self.send_sem, self.recv_sem, self.count, self.open = send_sem, recv_sem, 0, []

    def start(self, source, target, device):
        copy = pltpu.make_async_remote_copy(
            src_ref=source,
            dst_ref=target,
            send_sem=self.send_sem.at[self.count],
            recv_sem=self.recv_sem.at[self.count],
            device_id=device,
            device_id_type=MESH,
        )
        copy.start()
        self.count += 1
        self.open.append(copy)
        return copy

    def finish(self):
        for copy in self.open:
            copy.wait_send()


GATHER_SENDS = 6 + 3 + 31 + 3


def pair_bias_kernel(pairs, norm, weight, shard, bias, weights, block, low, local_sem, send_sem, recv_sem):
    row, head = place()
    rows, cols, channels = pairs.shape
    part = shard.shape[1] // 2
    core = row % 2
    beyond = [(head + k) % 4 for k in range(4)]
    behind = [(head + 4 - k) % 4 for k in range(4)]
    across, down, other = (flip(row, ACROSS), head), (flip(row, DOWN), head), (flip(row, CORE), head)
    greet([across, down, other] + [(row, beyond[k]) for k in (1, 2, 3)])
    sends = Sends(send_sem, recv_sem)

    def own_part(at, side):
        return weights.at[:, pl.ds(pl.multiple_of(at * 2 * part + side * part, part), part), :]

    half = shard.at[:, pl.ds(pl.multiple_of(core * part, part), part), :]
    keep = pltpu.make_async_copy(
        shard, weights.at[:, pl.ds(pl.multiple_of(head * 2 * part, 2 * part), 2 * part), :], local_sem.at[0]
    )
    keep.start()
    shards = [None] + [sends.start(half, own_part(head, core), (row, beyond[k])) for k in (1, 2, 3)]

    step = 8

    def norm_block(n, carry):
        first = pl.multiple_of(n * step, step)
        values = pairs[pl.ds(first, step)].reshape(step * cols, channels)
        center = values - jnp.mean(values, axis=-1, keepdims=True)
        rstd = lax.rsqrt(jnp.mean(center * center, axis=-1, keepdims=True) + 1e-05)
        normed = (center * rstd * norm[0:1] + norm[1:2]).astype(BF16)
        out = lax.dot_general(weight[...], normed, (((1,), (1,)), ((), ())), preferred_element_type=F32)
        for i in range(step):
            block[:, pl.ds(first + i, 1), :] = (out[:, i * cols : (i + 1) * cols] * LOG2E).reshape(
                HEADS, 1, cols
            )
        return carry

    lax.fori_loop(0, rows // step, norm_block, 0)
    low[...] = block[...].astype(BF16)

    mine = pltpu.make_async_copy(low, bias.at[row, head], local_sem.at[1])
    mine.start()
    stage = [None] * 4
    stage[0] = low
    along = [None] + [sends.start(low, bias.at[row, head], (row, beyond[k])) for k in (1, 2, 3)]
    from_across, from_down, from_corner, from_core = [None] * 4, [None] * 4, [None] * 4, []

    def spread(k, source):
        here = bias.at[row, behind[k]]
        from_across[k] = sends.start(source, here, across)
        from_down[k] = sends.start(source, here, down)
        from_core.append(sends.start(source, here, other))

    def relay(k):
        from_across[k].wait_recv()
        block_across = bias.at[flip(row, ACROSS), behind[k]]
        if k < 2:
            from_corner[k] = sends.start(block_across, block_across, down)
        from_core.append(sends.start(block_across, block_across, other))
        from_down[k].wait_recv()
        block_down = bias.at[flip(row, DOWN), behind[k]]
        if k >= 2:
            from_corner[k] = sends.start(block_down, block_down, across)
        from_core.append(sends.start(block_down, block_down, other))

    spread(0, low)
    for k in (1, 2, 3):
        along[k].wait_recv()
        spread(k, bias.at[row, behind[k]])
        relay(k - 1)
    relay(3)
    for k in range(4):
        from_corner[k].wait_recv()
        block_corner = bias.at[flip(row, CORNER), behind[k]]
        from_core.append(sends.start(block_corner, block_corner, other))
    for k in (1, 2, 3):
        shards[k].wait_recv()
        piece = own_part(behind[k], core)
        from_core.append(sends.start(piece, piece, other))
    for copy in from_core:
        copy.wait_recv()
    sends.finish()
    keep.wait()
    mine.wait()


def pair_bias(pairs, norm, weight, shard):
    rows, cols, channels = pairs.shape
    vmem = pl.BlockSpec(memory_space=pltpu.VMEM)
    hbm = pl.BlockSpec(memory_space=pl.ANY)
    return pl.pallas_call(
        pair_bias_kernel,
        out_shape=[
            jax.ShapeDtypeStruct((8, 4, HEADS, rows, cols), BF16),
            jax.ShapeDtypeStruct((shard.shape[0], 4 * shard.shape[1], shard.shape[2]), BF16),
        ],
        in_specs=[vmem, vmem, vmem, hbm],
        out_specs=[hbm, hbm],
        scratch_shapes=[
            pltpu.VMEM((HEADS, rows, cols), F32),
            pltpu.VMEM((HEADS, rows, cols), BF16),
            pltpu.SemaphoreType.DMA((2,)),
            pltpu.SemaphoreType.DMA((GATHER_SENDS,)),
            pltpu.SemaphoreType.DMA((GATHER_SENDS,)),
        ],
        cost_estimate=cost(34),
        compiler_params=pltpu.CompilerParams(
            collective_id=0, has_side_effects=True, vmem_limit_bytes=VMEM
        ),
    )(pairs, norm, weight, shard)


OUTER_SENDS = 2 + 3 + 7 + 1 + 3 + 3


def outer_kernel(
    left, right, left_early, right_early, pairs_back, outer_out, update, hop_early,
    total, left_out, right_out, table_grad, hop_one, hop_two,
    left_stage, right_stage, left_plane, right_line, left_all, right_all, left_last, right_last, left_wide, right_wide, left_rows, right_rows,
    backed, product, back, low, table, table_t, total_low,
    left_part, right_part, left_send, right_send, right_core, chip_sum, right_in, right_sum, left_line, left_sum, left_land, right_land,
    load_sem, local_sem, out_sem, row_local, row_send, row_recv, send_sem, recv_sem,
    *, scale, block, group,
):
    row, head = place()
    beyond = [(head + k) % 4 for k in range(4)]
    plane = [(flip(row, way), head) for way in range(8)]
    core, chip = row % 2, row // 2
    own, wide, _ = right.shape
    rows, cols, channels = back.shape
    size = wide
    lines = left_all.shape[3]
    chunks = rows // block
    half, most = own // 2, own - 1
    greet(plane[1:] + [(row, beyond[k]) for k in (1, 2, 3)])
    sends = Sends(send_sem, recv_sem)
    sides = Exchange(
        left.at[pl.ds(most, own - most)], right.at[pl.ds(most, own - most)], left_stage, right_stage,
        left_plane, right_line, left_last, right_last, row_local, row_send, row_recv,
    )
    sides.begin()
    gather = [
        pltpu.make_async_copy(left_early, left_all, local_sem.at[0]),
        pltpu.make_async_copy(right_early, right_all, local_sem.at[1]),
    ]
    loads = []
    for n in range(chunks):
        copy = pltpu.make_async_copy(
            pairs_back.at[pl.ds(n * block, block)], back.at[pl.ds(n * block, block)], load_sem.at[n]
        )
        copy.start()
        loads.append(copy)
    for copy in gather:
        copy.start()

    for f in range(wide):
        table[f * size : (f + 1) * size] = outer_out[pl.ds(f, size, stride=wide), :].astype(BF16)
    for n in range(wide * size // 128):
        table_t[:, n * 128 : (n + 1) * 128] = table[n * 128 : (n + 1) * 128].T

    def spread_pair(p, carry):
        first = p * group
        both = back[pl.ds(first, group)].astype(BF16)
        low[pl.ds(first, group)] = both
        spread = dot(table[...], both.reshape(group * cols, channels), (1, 1)).astype(BF16)
        for g in range(group):
            at = pl.ds(pl.multiple_of((first + g) * size, size), size)
            for f in range(wide):
                backed[at, f * cols : (f + 1) * cols] = spread[
                    f * size : (f + 1) * size, g * cols : (g + 1) * cols
                ]
        return carry

    pairs_of = rows // group

    def spread_part(k):
        for n in range(k * chunks // 4, (k + 1) * chunks // 4):
            loads[n].wait()
        lax.fori_loop(k * pairs_of // 4, (k + 1) * pairs_of // 4, spread_pair, 0)

    spread_part(0)
    sides.go_on()
    hops = [
        sends.start(update.at[pl.ds(half, own - half)], hop_one, (row, beyond[1])),
        sends.start(hop_early, hop_two, (row, beyond[1])),
    ]
    spread_part(1)
    spread_part(2)
    sides.core()
    spread_part(3)
    sides.end()
    for copy in gather:
        copy.wait()

    count = 32
    for r in range(8):
        for h in range(4):
            left_wide[r * 4 + h, :most] = left_all[h, r].astype(F32)
            left_wide[r * 4 + h, most:] = left_last[h, r].astype(F32)
    right_wide[:, :most] = right_all[...].astype(F32).reshape((count, most) + right_wide.shape[2:])
    right_wide[:, most:] = right_last[...].astype(F32).reshape((count, own - most) + right_wide.shape[2:])
    for s in range(own):
        at = slice(s * count, (s + 1) * count)
        for n in range(lines):
            left_rows[at, n * 128 : (n + 1) * 128] = left_wide[:, s, n, :].astype(BF16)
        for f in range(wide):
            right_rows[at, f * cols : (f + 1) * cols] = right_wide[:, s, f, :].astype(BF16)

    deep = block * size

    def left_step(n, carry):
        at = pl.ds(pl.multiple_of(n * deep, deep), deep)
        left_part[:, at] = dot(right_rows[...], backed[at, :], (1, 1)) * scale
        return carry

    lax.fori_loop(0, chunks, left_step, 0)
    for s in range(own):
        at = slice(s * count, (s + 1) * count)
        for n in range(lines):
            left_wide[:, s, n, :] = left_part[at, n * 128 : (n + 1) * 128]
    for r in range(8):
        for h in range(4):
            left_send[h, r] = left_wide[r * 4 + h].astype(BF16)
    lefts = [
        sends.start(left_send.at[beyond[k]], left_line.at[k - 1], (row, beyond[k])) for k in (2, 1, 3)
    ]
    step = 4 * cols

    def right_step(n, carry):
        at = pl.ds(pl.multiple_of(n * step, step), step)
        right_part[:, at] = dot(left_rows[...], backed[:, at], (1, 0)) * scale
        return carry

    lax.fori_loop(0, wide * cols // step, right_step, 0)
    for s in range(own):
        at = slice(s * count, (s + 1) * count)
        for f in range(wide):
            right_wide[:, s, f, :] = right_part[at, f * cols : (f + 1) * cols]
    right_send[...] = right_wide[...].astype(BF16).reshape(right_send.shape)
    swap = sends.start(right_send.at[:, 1 - core], right_core, plane[CORE])
    table_grad[...] = jnp.zeros_like(table_grad)

    def outer_chunk(n, carry):
        at = pl.ds(pl.multiple_of(n * deep, deep), deep)
        product[...] = dot(left_rows[:, at], right_rows[...], (0, 0)).astype(BF16)
        for first in range(0, block, group):
            both = jnp.concatenate(
                [
                    jnp.concatenate(
                        [
                            product[(first + g) * size : (first + g + 1) * size, f * cols : (f + 1) * cols]
                            for f in range(wide)
                        ],
                        axis=0,
                    )
                    for g in range(group)
                ],
                axis=1,
            )
            out = dot(table_t[...], both, (1, 0)) * scale
            for g in range(group):
                total_low[n * block + first + g] = out[:, g * cols : (g + 1) * cols].T.astype(BF16)
            seen = low[pl.ds(n * block + first, group)].reshape(group * cols, channels)
            table_grad[...] += dot(both, seen, (1, 0)) * scale
        return carry

    stores = []

    def outer_part(n):
        first, last = n * chunks // 4, (n + 1) * chunks // 4
        lax.fori_loop(first, last, outer_chunk, 0)
        at = pl.ds(first * block, (last - first) * block)
        copy = pltpu.make_async_copy(total_low.at[at], total.at[at], out_sem.at[n])
        copy.start()
        stores.append(copy)

    swap.wait_recv()
    rights = []
    for slot, way in enumerate((CORNER, ACROSS, DOWN)):
        n = plane[way][0] // 2
        for h in range(4):
            chip_sum[slot, h] = (
                right_send[n, core, h].astype(F32) + right_core[n, h].astype(F32)
            ).astype(BF16)
        rights.append(sends.start(chip_sum.at[slot], right_in.at[slot], plane[way]))
    outer_part(0)
    for copy in lefts:
        copy.wait_recv()
    for r in range(8):
        summed = left_send[head, r].astype(F32)
        for k in range(3):
            summed = summed + left_line[k, r].astype(F32)
        left_sum[r] = summed.astype(BF16)
    across = [
        sends.start(left_sum.at[plane[way][0]], left_land.at[row], plane[way])
        for way in (2, 4, 6, 3, 5, 7, 1)
    ]
    left_land[row] = left_sum[row]
    outer_part(1)
    for copy in rights:
        copy.wait_recv()
    for h in range(4):
        summed = right_send[chip, core, h].astype(F32) + right_core[chip, h].astype(F32)
        for slot in range(3):
            summed = summed + right_in[slot, h].astype(F32)
        right_sum[h] = summed.astype(BF16)
    line = [
        sends.start(right_sum.at[beyond[k]], right_land.at[head], (row, beyond[k])) for k in (1, 2, 3)
    ]
    right_land[head] = right_sum[head]
    outer_part(2)
    outer_part(3)
    for copy in across + line:
        copy.wait_recv()
    for r in range(8):
        left_out[:, r * lines : (r + 1) * lines, :] = left_land[r]
    for h in range(4):
        right_out[:, :, h * cols : (h + 1) * cols] = right_land[h]
    for copy in hops:
        copy.wait_recv()
    sends.finish()
    for copy in stores:
        copy.wait()


def outer_product(left, right, early, pairs_back, outer_out, update, all_rows, block=8, group=2):
    left_early, right_early, hop_early = early
    rows, cols, channels = pairs_back.shape
    own, wide, residues = right.shape
    size = left.shape[1] * left.shape[2] // residues
    lines = left.shape[1] // 8
    vmem = pl.BlockSpec(memory_space=pltpu.VMEM)
    hbm = pl.BlockSpec(memory_space=pl.ANY)
    low = lambda *shape: pltpu.VMEM(shape, BF16)
    full = lambda *shape: pltpu.VMEM(shape, F32)
    one = (lines, 128)
    other = (wide, cols)
    rest = 1
    dma = pltpu.SemaphoreType.DMA
    return pl.pallas_call(
        functools.partial(outer_kernel, scale=1.0 / all_rows, block=block, group=group),
        out_shape=[
            jax.ShapeDtypeStruct(pairs_back.shape, BF16),
            jax.ShapeDtypeStruct(left.shape, BF16),
            jax.ShapeDtypeStruct(right.shape, BF16),
            jax.ShapeDtypeStruct((wide * size, channels), F32),
            jax.ShapeDtypeStruct((own - own // 2,) + update.shape[1:], BF16),
            jax.ShapeDtypeStruct(hop_early.shape, BF16),
        ],
        in_specs=[vmem, vmem, hbm, hbm, hbm, vmem, hbm, hbm],
        out_specs=[hbm, vmem, vmem, vmem, hbm, hbm],
        scratch_shapes=[
            low(8, rest, *one), low(4, rest, *other), low(8, rest, *one), low(4, rest, *other),
            low(4, 8, own - rest, *one), low(8, 4, own - rest, *other),
            low(4, 8, rest, *one), low(8, 4, rest, *other), full(32, own, *one), full(32, own, *other),
            low(all_rows, rows * size), low(all_rows, wide * cols),
            low(rows * size, wide * cols), low(block * size, wide * cols), full(rows, cols, channels),
            low(rows, cols, channels), low(wide * size, channels), low(channels, wide * size), low(rows, cols, channels),
            full(all_rows, rows * size), full(all_rows, wide * cols), low(4, 8, own, *one), low(4, 2, 4, own, *other),
            low(4, 4, own, *other), low(3, 4, own, *other), low(3, 4, own, *other), low(4, own, *other),
            low(3, 8, own, *one), low(8, own, *one), low(8, own, *one), low(4, own, *other),
            dma((rows // block,)), dma((2,)), dma((4,)), dma((2,)), dma((ROW_SENDS,)), dma((ROW_SENDS,)),
            dma((OUTER_SENDS,)), dma((OUTER_SENDS,)),
        ],
        compiler_params=pltpu.CompilerParams(
            collective_id=1, has_side_effects=True, vmem_limit_bytes=VMEM
        ),
        cost_estimate=cost(50),
    )(left, right, left_early, right_early, pairs_back, outer_out, update, hop_early)


SUM_SENDS = 4 + 4 + 8 + 3 + 1 + 3 + 3


def sum_kernel(
    grads, parts, out, piece,
    swapped, chip_sum, by_across, by_down, from_across, from_down, down_sum, line_in,
    part_swapped, part_sum, part_plane, part_down, part_line,
    send_sem, recv_sem,
):
    row, head = place()
    beyond = [(head + k) % 4 for k in range(4)]
    core, chip = row % 2, row // 2
    ways = (CORNER, ACROSS, DOWN)
    plane = [(flip(row, way), head) for way in range(8)]
    other, across, down = plane[CORE], plane[ACROSS], plane[DOWN]
    greet([plane[way] for way in (CORE,) + ways] + [(row, beyond[k]) for k in (1, 2, 3)])
    sends = Sends(send_sem, recv_sem)
    chips = [plane[way][0] // 2 for way in ways] + [chip]
    swaps = [sends.start(grads.at[n, 1 - core], swapped.at[slot], other) for slot, n in enumerate(chips)]
    part_swap = sends.start(parts.at[1 - core], part_swapped, other)
    first, second = (2, 1), (3, 0)

    def add(slot, k):
        z = beyond[k]
        chip_sum[slot, k] = (
            grads[chips[slot], core, z].astype(F32) + swapped[slot, z].astype(F32)
        ).astype(BF16)

    swaps[0].wait_recv()
    relays_across, relays_down = [], []
    for n in range(2):
        add(0, first[n])
        relays_across.append(sends.start(chip_sum.at[0, first[n]], by_across.at[n], across))
        add(0, second[n])
        relays_down.append(sends.start(chip_sum.at[0, second[n]], by_down.at[n], down))
    last_across, last_down = [None] * 4, [None] * 4
    swaps[1].wait_recv()
    for k in first:
        add(1, k)
        last_across[k] = sends.start(chip_sum.at[1, k], from_across.at[k], across)
    swaps[2].wait_recv()
    for k in second:
        add(2, k)
        last_down[k] = sends.start(chip_sum.at[2, k], from_down.at[k], down)
    for n in range(2):
        add(1, second[n])
        add(2, first[n])
        relays_across[n].wait_recv()
        k = first[n]
        chip_sum[2, k] = (chip_sum[2, k].astype(F32) + by_across[n].astype(F32)).astype(BF16)
        last_down[k] = sends.start(chip_sum.at[2, k], from_down.at[k], down)
        relays_down[n].wait_recv()
        k = second[n]
        chip_sum[1, k] = (chip_sum[1, k].astype(F32) + by_down[n].astype(F32)).astype(BF16)
        last_across[k] = sends.start(chip_sum.at[1, k], from_across.at[k], across)
    part_swap.wait_recv()
    part_arrive = []
    for slot, n in enumerate(chips):
        for z in range(4):
            part_sum[slot, z] = (parts[core, n, z].astype(F32) + part_swapped[n, z].astype(F32)).astype(BF16)
        if slot < 3:
            part_arrive.append(sends.start(part_sum.at[slot], part_plane.at[slot], plane[ways[slot]]))
    swaps[3].wait_recv()
    line = []
    for k in first + second:
        add(3, k)
        last_across[k].wait_recv()
        last_down[k].wait_recv()
        total = chip_sum[3, k].astype(F32) + from_across[k].astype(F32) + from_down[k].astype(F32)
        if k:
            down_sum[k - 1] = total.astype(BF16)
            line.append(sends.start(down_sum.at[k - 1], line_in.at[k - 1], (row, beyond[k])))
        else:
            out[...] = total
    for copy in part_arrive:
        copy.wait_recv()
    for z in range(4):
        total = part_sum[3, z].astype(F32)
        for slot in range(3):
            total = total + part_plane[slot, z].astype(F32)
        part_down[z] = total.astype(BF16)
    part_arrive = [
        sends.start(part_down.at[beyond[k]], part_line.at[k - 1], (row, beyond[k])) for k in (1, 2, 3)
    ]
    for slot, copy in zip((1, 0, 2), line):
        copy.wait_recv()
        out[...] += line_in[slot].astype(F32)
    total = part_down[head].astype(F32)
    for slot, copy in enumerate(part_arrive):
        copy.wait_recv()
        total = total + part_line[slot].astype(F32)
    piece[...] = total.astype(BF16)
    sends.finish()


def sum_gradients(grads, parts):
    block = grads.shape[2:]
    lines = block[0] * block[1]
    rows, cols = parts.shape
    share = rows // 32
    vmem = pl.BlockSpec(memory_space=pltpu.VMEM)
    wide = lambda *first: pltpu.VMEM(first + (lines, block[2]), BF16)
    thin = lambda *first: pltpu.VMEM(first + (share, cols), BF16)
    out, piece = pl.pallas_call(
        sum_kernel,
        out_shape=[
            jax.ShapeDtypeStruct((lines, block[2]), F32),
            jax.ShapeDtypeStruct((share, cols), BF16),
        ],
        in_specs=[vmem, vmem],
        out_specs=[vmem, vmem],
        scratch_shapes=[
            wide(4, 4), wide(4, 4), wide(2), wide(2), wide(4), wide(4), wide(3), wide(3),
            thin(4, 4), thin(4, 4), thin(3, 4), thin(4), thin(3),
            pltpu.SemaphoreType.DMA((SUM_SENDS,)),
            pltpu.SemaphoreType.DMA((SUM_SENDS,)),
        ],
        compiler_params=pltpu.CompilerParams(
            collective_id=3, has_side_effects=True, vmem_limit_bytes=VMEM
        ),
        cost_estimate=cost(40),
    )(grads.reshape(4, 2, 4, lines, block[2]), parts.reshape(2, 4, 4, share, cols))
    return out.reshape(block), piece


SPREAD_SENDS = 3 + 12 + 16 + 3 + 7


def spread_kernel(
    piece, small, out, total, line_in, line_sum, plane_in, local_sem, send_sem, recv_sem
):
    row, head = place()
    beyond = [(head + k) % 4 for k in range(4)]
    behind = [(head + 4 - k) % 4 for k in range(4)]
    core, chip = row % 2, row // 2
    ways = (CORNER, ACROSS, DOWN)
    plane = [(flip(row, way), head) for way in range(8)]
    other = plane[CORE]
    greet(plane[1:] + [(row, beyond[k]) for k in (1, 2, 3)])
    sends = Sends(send_sem, recv_sem)
    small_line = [sends.start(small, line_in.at[head], (row, beyond[k])) for k in (1, 2, 3)]
    line = [None] + [sends.start(piece, out.at[core, chip, head], (row, beyond[k])) for k in (1, 2, 3)]
    mine = pltpu.make_async_copy(piece, out.at[core, chip, head], local_sem)
    mine.start()
    line_in[head] = small[...]
    across, end = [], []

    def forward(k):
        here = out.at[core, chip, behind[k]]
        source = here if k else piece
        for way in ways:
            across.append((plane[way][0] // 2, k, sends.start(source, here, plane[way])))
        end.append(sends.start(source, here, other))

    forward(0)
    for copy in small_line:
        copy.wait_recv()
    line_sum[...] = (line_in[0] + line_in[1]) + (line_in[2] + line_in[3])
    small_plane = [sends.start(line_sum, plane_in.at[row], plane[way]) for way in range(1, 8)]
    plane_in[row] = line_sum[...]
    for k in (1, 2, 3):
        line[k].wait_recv()
        forward(k)
    for n, k, copy in across:
        copy.wait_recv()
        block = out.at[core, n, behind[k]]
        end.append(sends.start(block, block, other))
    for copy in small_plane:
        copy.wait_recv()
    summed = plane_in[0]
    for n in range(1, 8):
        summed = summed + plane_in[n]
    total[...] = summed
    for copy in end:
        copy.wait_recv()
    mine.wait()
    sends.finish()


def spread_gradients(piece, small):
    lines, cols = piece.shape
    vmem = pl.BlockSpec(memory_space=pltpu.VMEM)
    out, total = pl.pallas_call(
        spread_kernel,
        out_shape=[
            jax.ShapeDtypeStruct((2, 4, 4, lines, cols), BF16),
            jax.ShapeDtypeStruct(small.shape, F32),
        ],
        in_specs=[vmem, vmem],
        out_specs=[vmem, vmem],
        scratch_shapes=[
            pltpu.VMEM((4,) + small.shape, F32),
            pltpu.VMEM(small.shape, F32),
            pltpu.VMEM((8,) + small.shape, F32),
            pltpu.SemaphoreType.DMA,
            pltpu.SemaphoreType.DMA((SPREAD_SENDS,)),
            pltpu.SemaphoreType.DMA((SPREAD_SENDS,)),
        ],
        compiler_params=pltpu.CompilerParams(
            collective_id=4, has_side_effects=True, vmem_limit_bytes=VMEM
        ),
        cost_estimate=cost(15),
    )(piece, small)
    return out.reshape(32 * lines, cols), total


def add_pieces(step, base, pieces, out):
    for n, piece in enumerate(pieces):
        @pl.when(step == n)
        def _():
            out[...] = base[...] + piece[...].astype(F32)


def added_specs(base, pieces):
    block = pieces[0].shape
    by_order = pl.BlockSpec(
        block, lambda n, order: (order[jnp.minimum(n, len(pieces) - 1) * block[0]] // block[0], 0, 0)
    )
    return by_order, [by_order] + [pl.BlockSpec(block, lambda n, order: (0, 0, 0))] * len(pieces)


def pair_backward_kernel(order, pairs, back, total, grads, norm, weight, norms, base, *refs):
    pieces, (out, new, small, changed) = refs[:-4], refs[-4:]
    step = pl.program_id(0)
    rows, cols, channels = pairs.shape
    add_pieces(step, base, pieces, changed)

    @pl.when(step == 0)
    def _():
        small[...] = jnp.zeros_like(small)
        small[2 * HEADS :] = jnp.concatenate([norms[:, :128], norms[:, 128:]], axis=0)

    values = pairs[...].reshape(rows * cols, channels)
    hat, rstd = normalize(values)
    low = (hat * norm[0:1] + norm[1:2]).astype(BF16)
    bias = jnp.concatenate([grads[:, i, :] for i in range(rows)], axis=1).astype(BF16)
    small[0:HEADS] += dot(bias, low, (1, 0))
    in_grad = dot(bias, weight[...], (0, 0))
    small[HEADS : HEADS + 1] += jnp.sum(in_grad * hat, axis=0, keepdims=True)
    small[HEADS + 1 : HEADS + 2] += jnp.sum(in_grad, axis=0, keepdims=True)
    change = norm_backward(hat, rstd, norm[0:1], in_grad)
    out[...] = back[...] + change.reshape(rows, cols, channels)
    new[...] = pairs[...] + total[...].astype(F32)


def pair_norm_backward(order, pairs, back, total, grads, norm, weight, norms, base, pieces, steps=8):
    rows, cols, channels = pairs.shape
    block = rows // steps
    by_row = lambda n, order: (n, 0, 0)
    whole = lambda n, order: (0, 0)
    by_order, added = added_specs(base, pieces)
    grads = grads.reshape(HEADS, steps, block, cols)
    return pl.pallas_call(
        pair_backward_kernel,
        grid_spec=pltpu.PrefetchScalarGridSpec(
            num_scalar_prefetch=1,
            grid=(steps,),
            in_specs=[
                pl.BlockSpec((block, cols, channels), by_row),
                pl.BlockSpec((block, cols, channels), by_row),
                pl.BlockSpec((block, cols, channels), by_row),
                pl.BlockSpec((HEADS, None, block, cols), lambda n, order: (0, n, 0, 0)),
                pl.BlockSpec(norm.shape, whole),
                pl.BlockSpec(weight.shape, whole),
                pl.BlockSpec(norms.shape, whole),
            ]
            + added,
            out_specs=[
                pl.BlockSpec((block, cols, channels), by_row),
                pl.BlockSpec((block, cols, channels), by_row),
                pl.BlockSpec((3 * HEADS, channels), whole),
                by_order,
            ],
        ),
        out_shape=[
            jax.ShapeDtypeStruct(pairs.shape, F32),
            jax.ShapeDtypeStruct(pairs.shape, F32),
            jax.ShapeDtypeStruct((3 * HEADS, channels), F32),
            jax.ShapeDtypeStruct(base.shape, F32),
        ],
        compiler_params=pltpu.CompilerParams(vmem_limit_bytes=VMEM),
        cost_estimate=cost(9),
    )(order, pairs, back, total, grads, norm, weight, norms, base, *pieces)


def add_kernel(place_ref, base, piece, *refs):
    refs[-1][...] = base[...] + piece[...].astype(F32)


def add_rows(at, base, piece, into=None):
    own = piece.shape[0]
    block = (1,) + piece.shape[1:]
    spread = lambda n, at: (at[0] * own + n, 0, 0)
    return pl.pallas_call(
        add_kernel,
        grid_spec=pltpu.PrefetchScalarGridSpec(
            num_scalar_prefetch=1,
            grid=(own,),
            in_specs=[pl.BlockSpec(block, spread), pl.BlockSpec(block, lambda n, at: (n, 0, 0))]
            + ([] if into is None else [pl.BlockSpec(memory_space=pl.ANY)]),
            out_specs=pl.BlockSpec(block, spread),
        ),
        out_shape=jax.ShapeDtypeStruct(base.shape, F32),
        input_output_aliases={} if into is None else {3: 0},
        cost_estimate=cost(2),
    )(*((at, base, piece) if into is None else (at, base, piece, into)))


def hop(piece):
    count = lax.axis_size("head")
    return lax.ppermute(piece, "head", [(i, (i + 1) % count) for i in range(count)])


def together(moved, *values):
    return lax.optimization_barrier((moved,) + values)


def adam_kernel(at, packed, pair_side, *refs, rates, pieces):
    olds, base, adds, news = refs[:18], refs[18], refs[19 : 19 + pieces], refs[20 + pieces : 38 + pieces]
    changed, table = refs[38 + pieces :]
    step = pl.program_id(0)
    add_pieces(step, base, adds, changed)

    @pl.when(step == 0)
    def _():
        adam_step(at, packed, pair_side, olds, news, table, rates)


def adam_step(at, packed, pair_side, olds, news, table, rates):
    norms, heads_in, heads_out, bias_weight, outer_in, outer_out = [olds[3 * n : 3 * n + 3] for n in range(6)]
    count, local, all_heads = heads_in[0].shape
    sides, size = outer_in[0].shape[:2]

    def rows(first, lines):
        return packed[pl.ds(first, lines), :].astype(F32)

    def pair_of(first, offset, lines, span):
        return jnp.concatenate([rows(first + offset, lines), rows(first + span + offset, lines)], axis=1)

    def update(n, index, grad):
        weight, moment_one, moment_two = [ref[index] for ref in olds[3 * n : 3 * n + 3]]
        for ref, new in zip(
            news[3 * n : 3 * n + 3], adam_update(weight, grad, moment_one, moment_two, rates[n])
        ):
            ref[index] = new

    mine = pl.multiple_of(at[4], local)
    span = count * all_heads
    for k in range(count):
        update(1, k, pair_of(0, k * all_heads + mine, local, span))
    first = 2 * span
    update(2, slice(None), pair_of(first, mine, local, all_heads))
    first += 2 * all_heads
    for k in range(sides):
        update(4, k, pair_of(first, k * size, size, sides * size))
    first += 2 * sides * size
    table[...] = rows(first, size * size)
    for e in range(size):
        update(5, slice(e * size, (e + 1) * size), table[pl.ds(e, size, stride=size), :])
    pair = pair_side[...]
    low = pair[2 * HEADS :]
    lines = [
        jnp.concatenate([low[n : n + 1], low[n + 4 : n + 5], low[n + 2 : n + 3], low[n + 6 : n + 7], pair[HEADS + n : HEADS + n + 1]], axis=1)
        for n in range(2)
    ]
    update(0, slice(None), jnp.concatenate(lines, axis=0))
    update(3, slice(None), pair[:HEADS])


def adam_all(at, packed, pair_side, olds, rates, base, pieces, into):
    turned = (1, 3, 4)
    flat = [array.swapaxes(-1, -2) if n in turned else array for n, triple in enumerate(olds) for array in triple]
    size = olds[4][0].shape[2]
    by_order, added = added_specs(base, pieces)
    whole = lambda array: pl.BlockSpec(array.shape, lambda n, at: (0,) * array.ndim)
    *news, changed = pl.pallas_call(
        functools.partial(adam_kernel, rates=rates, pieces=len(pieces)),
        grid_spec=pltpu.PrefetchScalarGridSpec(
            num_scalar_prefetch=1,
            grid=(len(pieces),),
            in_specs=[whole(array) for array in [packed, pair_side] + flat]
            + added
            + [pl.BlockSpec(memory_space=pl.ANY)],
            out_specs=[whole(array) for array in flat] + [by_order],
            scratch_shapes=[pltpu.VMEM((size * size, packed.shape[1]), F32)],
        ),
        out_shape=[jax.ShapeDtypeStruct(array.shape, F32) for array in flat + [base]],
        input_output_aliases={3 + len(flat) + 1 + len(pieces): len(flat)},
        compiler_params=pltpu.CompilerParams(vmem_limit_bytes=VMEM),
        cost_estimate=cost(5),
    )(at, packed, pair_side, *flat, base, *pieces, into)
    news = [array.swapaxes(-1, -2) if n // 3 in turned else array for n, array in enumerate(news)]
    return news + [changed]


def per_device(
    alignment,
    pairs,
    residue_mask,
    row_mask,
    alignment_back,
    pairs_back,
    norm_scales,
    heads_in,
    heads_out,
    bias_weight,
    outer_in,
    outer_out,
    first_norms,
    second_norms,
    first_heads_in,
    second_heads_in,
    first_heads_out,
    second_heads_out,
    first_bias_weight,
    second_bias_weight,
    first_outer_in,
    second_outer_in,
    first_outer_out,
    second_outer_out,
):
    row_count = lax.axis_size("row")
    head_count = lax.axis_size("head")
    head_index = lax.axis_index("head")
    devices = row_count * head_count
    rows_here, residues, width = alignment.shape
    pair_rows, pair_cols, pair_width = pairs.shape
    size = width // HEADS
    outer_width = outer_in.shape[2]
    all_rows = rows_here * row_count
    own = rows_here // head_count
    start = head_index * own
    scales = norm_scales[:, : 2 * width].reshape(2, 2, width).swapaxes(0, 1).reshape(4, width)
    pair_gain = norm_scales[0:1, 2 * width :]
    pair_shift = norm_scales[1:2, 2 * width :]
    residue_live = residue_mask.astype(F32)
    key_mask = ((residue_live - 1.0) * (1e9 * LOG2E))[:, None]
    row_live = lax.dynamic_slice_in_dim(row_mask, start, own, 0).astype(F32)
    live = (row_live[:, None] * residue_live[None])[:, None]
    flat_live = jnp.repeat(residue_live.reshape(-1, QUADS), outer_in.shape[2], axis=1)
    row_live = jnp.broadcast_to(row_live[:, None, None], (own, 1, 128))
    bias_low = bias_weight.astype(BF16)

    fast = (row_count, head_count, pair_cols, own * outer_width) == (8, 4, 128, 128)

    local = heads_in.shape[2]
    shard = jnp.concatenate([heads_in.astype(BF16).swapaxes(1, 2), heads_out.astype(BF16)[None]])
    outer_t = outer_in.astype(BF16).swapaxes(1, 2).reshape(2 * outer_width, width)
    if fast:
        bias, weights = pair_bias(pairs, norm_scales[:, 2 * width :], bias_low.T, shard)
    else:
        weights = lax.all_gather(shard, "head", axis=1, tiled=True)
        bias = pair_forward(pairs, pair_gain, pair_shift, bias_low)
        bias = lax.all_gather(bias, "head", axis=2, tiled=True)
        bias = lax.all_gather(bias, "row", axis=1, tiled=True)[None, None]
    in_t = weights[:4].reshape(4 * width, width)
    out_low = weights[4]

    update, left, right, kept, early = attention_forward(
        alignment, scales, in_t, out_low, outer_t, bias, key_mask, live, row_live, flat_live, fast
    )

    if fast:
        total, left_grad, right_grad, table_grad, hop_one, hop_two = outer_product(
            left, right, early, pairs_back, outer_out, update, all_rows
        )
        updates = [update, early[2], hop_one, hop_two]
    else:
        table = outer_out.astype(BF16).reshape(outer_width, outer_width, pair_width)
        updates = [update]
        for _ in range(head_count - 1):
            updates.append(hop(updates[-1]))
        left = left.reshape(own, residues, outer_width).swapaxes(1, 2)
        left = left.reshape(own, outer_width, row_count, pair_rows).transpose(2, 0, 1, 3)
        right = right.reshape(own, outer_width, head_count, pair_cols).transpose(2, 0, 1, 3)
        both = (row_count, head_count, own, outer_width)
        send = jnp.concatenate(
            [
                jnp.broadcast_to(left[:, None], both + (pair_rows,)),
                jnp.broadcast_to(right[None], both + (pair_cols,)),
            ],
            axis=4,
        )
        flat = (devices, own, outer_width, pair_rows + pair_cols)
        got = lax.all_to_all(send.reshape(flat), EVERY, split_axis=0, concat_axis=0, tiled=True)
        got = got.reshape(all_rows, outer_width, pair_rows + pair_cols)
        total, table_grad, left_grad, right_grad = outer_product_plain(
            got[:, :, :pair_rows], got[:, :, pair_rows:], pairs_back, table, all_rows
        )
        pairs_new = pairs + total
        send = jnp.concatenate([left_grad, right_grad], axis=2).reshape(flat)
        got = lax.all_to_all(send, EVERY, split_axis=0, concat_axis=0, tiled=True)
        got = got.reshape(both + (pair_rows + pair_cols,)).astype(F32)
        left_grad = jnp.sum(got[..., :pair_rows], axis=1).transpose(1, 0, 3, 2).astype(BF16)
        left_grad = left_grad.reshape(own, residues // QUADS, QUADS * outer_width)
        right_grad = jnp.sum(got[..., pair_rows:], axis=0).transpose(1, 2, 0, 3).astype(BF16)
        right_grad = right_grad.reshape(own, outer_width, residues)
        table_grad = table_grad.swapaxes(0, 1).reshape(outer_width * outer_width, pair_width)

    turns = (head_index + head_count - jnp.arange(head_count, dtype=jnp.int32)) % head_count
    order = (turns[:, None] * own + jnp.arange(own, dtype=jnp.int32)[None]).reshape(-1)
    half = own // 2

    def mine(first, hops, second, more):
        parts = [(first, step) for step in hops] + [(second, step) for step in more]
        return jnp.concatenate([order[step * own + n * half : step * own + (n + 1) * half] for n, step in parts])

    backward = functools.partial(
        attention_backward,
        order, alignment, update, alignment_back, scales, in_t, out_low, outer_t, left_grad, right_grad,
        live, row_live, flat_live, kept, bias.shape,
    )
    if fast:
        moved = [hop(hop_one), hop(hop_two)]
    part, bias_grad, *early = backward(first=0, own=half)
    if fast:
        moved, bias_grad, part, early = together(moved, bias_grad, part, early)
        updates += moved
        left_over = hop(moved[0])
    changes = [[part, hop(part)]]
    alignment_new, part, bias_grad, packed, norms = backward(
        first=half, own=half, earlier=bias_grad, early=early, table_grad=table_grad, pieces=updates
    )
    if fast:
        left_over, changes[0][1], bias_grad, part, packed, norms = together(
            left_over, changes[0][1], bias_grad, part, packed, norms
        )
        changes[0].append(hop(changes[0][1]))
        changes.append([part, hop(part)])
        bias_grad, packed = sum_gradients(bias_grad, packed)
        changes[0][2], changes[1][1], bias_grad = together(changes[0][2], changes[1][1], bias_grad)
        changes[0].append(hop(changes[0][2]))
        changes[1].append(hop(changes[1][1]))
        pairs_grad, pairs_new, pair_side, alignment_grad = pair_norm_backward(
            mine(0, (0, 1, 2), 1, (0, 1)),
            pairs,
            pairs_back,
            total,
            bias_grad,
            norm_scales[:, 2 * width :],
            bias_low.T,
            norms,
            alignment_back,
            changes[0][:3] + changes[1][:2],
        )
        packed, pair_side = spread_gradients(packed, pair_side)
        changes[0][3], changes[1][2], packed = together(changes[0][3], changes[1][2], packed)
        changes[1].append(hop(changes[1][2]))
    else:
        for _ in range(head_count - 2):
            changes[0].append(hop(changes[0][-1]))
        changes.append([part])
        for _ in range(head_count - 1):
            changes[1].append(hop(changes[1][-1]))
        bias_grad = lax.psum_scatter(bias_grad[0, 0], "row", scatter_dimension=1, tiled=True)
        bias_grad = lax.psum_scatter(bias_grad, "head", scatter_dimension=2, tiled=True)
        pairs_grad, bias_weight_grad, pair_gain_grad, pair_shift_grad = pair_backward(
            pairs, pairs_back, pair_gain, pair_shift, bias_low, bias_grad
        )
        packed, norms, bias_weight_total, pair_norms_total = lax.psum(
            (packed.astype(F32), norms, bias_weight_grad, jnp.stack([pair_gain_grad, pair_shift_grad])), EVERY
        )
    olds = (
        (norm_scales, first_norms, second_norms),
        (heads_in, first_heads_in, second_heads_in),
        (heads_out, first_heads_out, second_heads_out),
        (bias_weight, first_bias_weight, second_bias_weight),
        (outer_in, first_outer_in, second_outer_in),
        (outer_out, first_outer_out, second_outer_out),
    )
    rates = (
        0.5,
        width ** (-0.5),
        max(2 * HEADS * size // residues, 1) ** (-0.5),
        pair_width ** (-0.5),
        width ** (-0.5),
        max(outer_width * outer_width // all_rows, 1) ** (-0.5),
    )
    if fast:
        at = (head_index * local).astype(jnp.int32)[None]
        *news, alignment_grad = adam_all(
            jnp.concatenate([mine(0, (3,), 1, (2,)), at]),
            packed, pair_side, olds, rates, alignment_back, [changes[0][3], changes[1][2]], alignment_grad,
        )
        at = (turns[3] * 2 + 1)[None]
        alignment_new = add_rows(at, alignment, left_over, alignment_new)
        alignment_grad = add_rows(at, alignment_back, changes[1][3], alignment_grad)
        return (alignment_new, pairs_new, alignment_grad, pairs_grad, *news)
    alignment_grad = None
    for step in range(head_count):
        for n in range(2):
            at = (turns[step] * 2 + n)[None]
            alignment_grad = add_rows(at, alignment_back, changes[n][step], alignment_grad)
    def unpack(first, lines):
        return jnp.concatenate([packed[first : first + lines], packed[first + lines : first + 2 * lines]], axis=1)

    lines = 4 * width
    heads_in_total = lax.dynamic_slice_in_dim(
        unpack(0, lines).reshape(4, width, width), head_index * local, local, 1
    ).swapaxes(1, 2)
    heads_out_total = lax.dynamic_slice_in_dim(unpack(2 * lines, width), head_index * local, local, 0)
    lines = 2 * (lines + width)
    outer_in_total = unpack(lines, 2 * outer_width).reshape(2, outer_width, width).swapaxes(1, 2)
    lines += 4 * outer_width
    table_total = packed[lines : lines + outer_width * outer_width]
    table_total = table_total.reshape(outer_width, outer_width, pair_width).swapaxes(0, 1)
    table_total = table_total.reshape(outer_width * outer_width, pair_width)
    norms_total = jnp.concatenate(
        [norms.reshape(2, 2, width).swapaxes(0, 1).reshape(2, 2 * width), pair_norms_total], axis=1
    )
    totals = (norms_total, heads_in_total, heads_out_total, bias_weight_total, outer_in_total, table_total)
    news = []
    for (weight, moment_one, moment_two), total, rate in zip(olds, totals, rates):
        news += adam_update(weight, total, moment_one, moment_two, rate)
    return (alignment_new, pairs_new, alignment_grad, pairs_grad, *news)


def solution(mesh):
    row_msa = P("row", None, None)
    pair = P("row", "head", None)
    columns = P(None, None, "head")
    lines = P("head", None)
    in_specs = (
        (row_msa, pair, P(), P("row"), row_msa, pair, P(), columns, lines)
        + (P(),) * 5
        + (columns,) * 2
        + (lines,) * 2
        + (P(),) * 6
    )
    out_specs = (row_msa, pair, row_msa, pair) + (P(),) * 3 + (columns,) * 3 + (lines,) * 3 + (P(),) * 9
    return jax.shard_map(
        per_device, mesh=mesh, in_specs=in_specs, out_specs=out_specs, check_vma=False
    )
```

```python
import functools

import jax
import jax.numpy as jnp
from jax import lax
from jax.experimental import pallas as pl
from jax.experimental.pallas import tpu as pltpu
from jax.sharding import PartitionSpec as P

HEADS = 8
STEP = 10
F32 = jnp.float32
BF16 = jnp.bfloat16
LOG2E = 1.4426950408889634
VMEM = 56 << 20
EVERY = ("row", "head")


def adam_update(weight, gradient, moment_one, moment_two, step_rate):
    first_new = 0.9 * moment_one + 0.1 * gradient
    second_new = 0.999 * moment_two + 0.001 * gradient * gradient
    first_hat = first_new / (1.0 - 0.9**STEP)
    second_hat = second_new / (1.0 - 0.999**STEP)
    updated = weight - step_rate * (first_hat / (jnp.sqrt(second_hat) + 1e-08) + 0.01 * weight)
    return (first_new, second_new, updated)


def cost(micros):
    return pl.CostEstimate(flops=0, bytes_accessed=int(micros * 3.5e6), transcendentals=0)


def dot(a, b, along):
    return lax.dot_general(a, b, (((along[0],), (along[1],)), ((), ())), preferred_element_type=F32)


def normalize(values):
    center = values - jnp.mean(values, axis=-1, keepdims=True)
    rstd = lax.rsqrt(jnp.mean(center * center, axis=-1, keepdims=True) + 1e-05)
    return center * rstd, rstd


def norm_backward(hat, rstd, gain, grad):
    scaled = grad * gain
    return rstd * (
        scaled
        - jnp.mean(scaled, axis=-1, keepdims=True)
        - hat * jnp.mean(scaled * hat, axis=-1, keepdims=True)
    )


QUADS = 4


def quad(outer_t, q):
    weights = outer_t[: outer_t.shape[0] // 2]
    zero = jnp.zeros_like(weights)
    return jnp.concatenate([weights if n == q else zero for n in range(QUADS)], axis=0)


def put(ref, value):
    for n in range(ref.shape[0]):
        ref[n] = value[:, n * 128 : (n + 1) * 128]


def take(ref, q):
    at = pl.ds(q, ref.shape[1] // QUADS, stride=QUADS)
    return jnp.concatenate([ref[n, at, :] for n in range(ref.shape[0])], axis=1)


ROW_SENDS = 20


class Exchange:
    def __init__(
        self, left, right, left_stage, right_stage, left_plane, right_line, left_all, right_all,
        local_sem, send_sem, recv_sem,
    ):
        self.left, self.right, self.left_stage, self.right_stage = left, right, left_stage, right_stage
        self.left_plane, self.right_line, self.left_all, self.right_all = left_plane, right_line, left_all, right_all
        self.local_sem, self.send_sem, self.recv_sem = local_sem, send_sem, recv_sem
        self.row, self.head = place()
        self.beyond = [(self.head + k) % 4 for k in range(4)]
        self.behind = [(self.head + 4 - k) % 4 for k in range(4)]
        self.plane = [(flip(self.row, way), self.head) for way in range(8)]
        self.lines = left_plane.shape[2]
        self.cols = right_line.shape[3]

    def copy(self, n, source, target, device):
        return pltpu.make_async_remote_copy(
            src_ref=source,
            dst_ref=target,
            send_sem=self.send_sem.at[n],
            recv_sem=self.recv_sem.at[n],
            device_id=device,
            device_id_type=MESH,
        )

    def first(self):
        out = [
            self.copy(7 + k, self.right_stage.at[self.beyond[k + 1]], self.right_line.at[self.head],
                      (self.row, self.beyond[k + 1]))
            for k in range(3)
        ]
        out += [
            self.copy(n, self.left_stage.at[self.plane[way][0]], self.left_plane.at[self.row], self.plane[way])
            for n, way in enumerate((2, 4, 6, 3, 5, 7, 1))
        ]
        return out

    def second(self, which):
        if which == "left":
            return [
                self.copy(10 + k, self.left_plane, self.left_all.at[self.head], (self.row, self.beyond[k + 1]))
                for k in range(3)
            ]
        if which == "core":
            return [self.copy(16, self.right_line, self.right_all.at[self.row], self.plane[CORE])]
        return [
            self.copy(13 + n, self.right_line, self.right_all.at[self.row], self.plane[way])
            for n, way in enumerate((ACROSS, DOWN, CORNER))
        ]

    def third(self):
        out = []
        for n, way in enumerate((ACROSS, DOWN, CORNER)):
            block = self.right_all.at[self.plane[way][0]]
            out.append(self.copy(17 + n, block, block, self.plane[CORE]))
        return out

    def locals(self):
        return [
            pltpu.make_async_copy(self.left_plane, self.left_all.at[self.head], self.local_sem.at[0]),
            pltpu.make_async_copy(self.right_line, self.right_all.at[self.row], self.local_sem.at[1]),
        ]

    def begin(self):
        for r in range(8):
            self.left_stage[r] = self.left[:, r * self.lines : (r + 1) * self.lines, :]
        for h in range(4):
            self.right_stage[h] = self.right[:, :, h * self.cols : (h + 1) * self.cols]
        self.left_plane[self.row] = self.left_stage[self.row]
        self.right_line[self.head] = self.right_stage[self.head]
        for copy in self.first():
            copy.start()

    def go_on(self):
        for copy in self.first():
            copy.wait_recv()
        for copy in self.second("chips") + self.second("core") + self.second("left") + self.locals():
            copy.start()

    def core(self):
        for copy in self.second("chips"):
            copy.wait_recv()
        for copy in self.third():
            copy.start()

    def end(self):
        for copy in self.second("left") + self.second("core") + self.third():
            copy.wait()
        for copy in self.locals():
            copy.wait()
        for copy in self.first() + self.second("chips"):
            copy.wait_send()


def forward_kernel(*refs, share):
    (rows, scales, weights, outer_t, bias, residue, row_live, flat_live), refs = refs[:8], refs[8:]
    (update, left, right, qkv, gate, powers, inverse, mixed, attended), refs = refs[:9], refs[9:]
    if share:
        (left_all, right_all, hop_one), refs = refs[:3], refs[3:]
        left_stage, right_stage, left_plane, right_line, local_sem, send_sem, recv_sem, hop_sem = refs[-8:]
    bias_t, second, rows_in, load_sem = refs[:4]
    row = pl.program_id(0)
    own = update.shape[0]
    width = rows.shape[2]
    residues = rows.shape[1]
    size = width // HEADS
    half = outer_t.shape[0] // 2
    start = lax.axis_index("head") * own
    device_row, device_head = place()

    def load(n):
        return pltpu.make_async_copy(rows.at[start + n], rows_in.at[n % 2], load_sem.at[n % 2])

    def exchange():
        return Exchange(
            left.at[pl.ds(0, own - 1)], right.at[pl.ds(0, own - 1)], left_stage, right_stage,
            left_plane, right_line, left_all, right_all, local_sem, send_sem, recv_sem,
        )

    def hop_copy(n):
        return pltpu.make_async_remote_copy(
            src_ref=update.at[n],
            dst_ref=hop_one.at[n],
            send_sem=hop_sem.at[0, n],
            recv_sem=hop_sem.at[1, n],
            device_id=(device_row, (device_head + 1) % 4),
            device_id_type=MESH,
        )

    @pl.when(row == 0)
    def _():
        load(0).start()
        if own > 1:
            load(1).start()
        if share:
            greet(
                [(flip(device_row, way), device_head) for way in range(1, 8)]
                + [(device_row, (device_head + k) % 4) for k in (1, 2, 3)]
            )
        key_mask = (residue[...] - 1.0) * (1e9 * LOG2E)
        across, down, _, lines, cols = bias.shape
        group = max(1, 128 // lines)

        def turn(head, carry):
            for r in range(0, across, group):
                for c in range(down):
                    tile = jnp.concatenate([bias[r + g, c, head] for g in range(group)], axis=0)
                    bias_t[head, c * cols : (c + 1) * cols, r * lines : (r + group) * lines] = (
                        tile.astype(F32) + key_mask[:, c * cols : (c + 1) * cols]
                    ).T
            return carry

        lax.fori_loop(0, HEADS, turn, 0)

    load(row).wait()
    values_in = rows_in[row % 2]
    hat, _ = normalize(values_in)
    normed = (hat * scales[0:1] + scales[1:2]).astype(BF16)
    qkv[0, :width] = (dot(weights[0], normed, (1, 1)) * (size**-0.5 * LOG2E)).astype(BF16)
    qkv[0, width:] = dot(weights[1:3].reshape(2 * width, width), normed, (1, 1)).astype(BF16)
    gate[0] = jax.nn.sigmoid(dot(weights[3], normed, (1, 1)))
    for head in range(HEADS):
        at = head * size
        keys = qkv[0, width + at : width + at + size]
        values = qkv[0, 2 * width + at : 2 * width + at + size]
        query = qkv[0, at : at + size]
        scores = dot(keys, query, (0, 0)) + bias_t[head]
        exps = jnp.exp2(scores - jnp.max(scores, axis=0, keepdims=True))
        over = 1.0 / jnp.sum(exps, axis=0, keepdims=True)
        low = exps.astype(BF16)
        powers[0, head] = low
        inverse[0, head] = over
        mixed[0, at : at + size] = dot(values, low, (1, 0)) * over
        if share and head == HEADS // 2 - 1:
            @pl.when(row == own - 1)
            def _():
                exchange().go_on()
    att = (gate[0] * mixed[0]).astype(BF16)
    attended[0] = att
    change = dot(att, weights[4], (0, 0)).astype(BF16)
    update[row] = change
    hat, _ = normalize(rows_in[row % 2] + change.astype(F32))
    normed = hat * scales[2:3] + scales[3:4]
    put(second, normed)
    right[row] = (dot(outer_t[half:], normed.astype(BF16), (1, 1)) * (residue[...] * row_live[0][:, :1])).astype(BF16)
    out = jnp.zeros(flat_live.shape, F32)
    for q in range(QUADS):
        out += dot(take(second, q).astype(BF16), quad(outer_t, q), (1, 1))
    left[row] = (out * flat_live[...] * row_live[0]).astype(BF16)

    @pl.when(row + 2 < own)
    def _():
        load(row + 2).start()

    if share:
        @pl.when(row == own - 2)
        def _():
            exchange().begin()

        @pl.when(row < own // 2)
        def _():
            hop_copy(row).start()

        @pl.when(row == own - 1)
        def _():
            exchange().core()
            for n in range(own // 2):
                hop_copy(n).wait()
            exchange().end()


def attention_forward(rows, scales, weights, outer_t, bias, residue, row_live, flat_live, share):
    _, residues, width = rows.shape
    own = row_live.shape[0]
    sides = outer_t.shape[0] // 2
    by_row = lambda s: (s, 0, 0)
    by_row_four = lambda s: (s, 0, 0, 0)
    hbm = pl.BlockSpec(memory_space=pl.ANY)
    once = lambda array: pl.BlockSpec(array.shape, lambda s: (0,) * array.ndim, pipeline_mode=pl.Buffered(1))
    whole = lambda *shape: pl.BlockSpec(shape, lambda s: (0,) * len(shape))
    lines, cols = flat_live.shape[0] // 8, residues // 4
    early = own - 1
    out_specs = [
        whole(own, residues, width),
        whole(own, *flat_live.shape),
        whole(own, sides, residues),
        pl.BlockSpec((1, 3 * width, residues), by_row),
        pl.BlockSpec((1, width, residues), by_row),
        pl.BlockSpec((1, HEADS, residues, residues), by_row_four),
        pl.BlockSpec((1, HEADS, 1, residues), by_row_four),
        pl.BlockSpec((1, width, residues), by_row),
        pl.BlockSpec((1, width, residues), by_row),
    ]
    out_shape = [
        jax.ShapeDtypeStruct((own, residues, width), BF16),
        jax.ShapeDtypeStruct((own,) + flat_live.shape, BF16),
        jax.ShapeDtypeStruct((own, sides, residues), BF16),
        jax.ShapeDtypeStruct((own, 3 * width, residues), BF16),
        jax.ShapeDtypeStruct((own, width, residues), F32),
        jax.ShapeDtypeStruct((own, HEADS, residues, residues), BF16),
        jax.ShapeDtypeStruct((own, HEADS, 1, residues), F32),
        jax.ShapeDtypeStruct((own, width, residues), F32),
        jax.ShapeDtypeStruct((own, width, residues), BF16),
    ]
    scratch = [
        pltpu.VMEM((HEADS, residues, residues), F32),
        pltpu.VMEM((width // 128, residues, 128), F32),
        pltpu.VMEM((2, residues, width), F32),
        pltpu.SemaphoreType.DMA((2,)),
    ]
    params = dict(vmem_limit_bytes=VMEM)
    if share:
        params.update(collective_id=2, has_side_effects=True)
        out_specs += [hbm] * 3
        out_shape += [
            jax.ShapeDtypeStruct((4, 8, early, lines, 128), BF16),
            jax.ShapeDtypeStruct((8, 4, early, sides, cols), BF16),
            jax.ShapeDtypeStruct((own // 2, residues, width), BF16),
        ]
        scratch += [
            pltpu.VMEM((8, early, lines, 128), BF16),
            pltpu.VMEM((4, early, sides, cols), BF16),
            pltpu.VMEM((8, early, lines, 128), BF16),
            pltpu.VMEM((4, early, sides, cols), BF16),
            pltpu.SemaphoreType.DMA((2,)),
            pltpu.SemaphoreType.DMA((ROW_SENDS,)),
            pltpu.SemaphoreType.DMA((ROW_SENDS,)),
            pltpu.SemaphoreType.DMA((2, own // 2)),
        ]
    out = pl.pallas_call(
        functools.partial(forward_kernel, share=share),
        grid=(own,),
        in_specs=[
            hbm,
            once(scales),
            once(weights),
            once(outer_t),
            once(bias),
            once(residue),
            pl.BlockSpec((1, 1, 128), by_row),
            once(flat_live),
        ],
        out_specs=out_specs,
        scratch_shapes=scratch,
        out_shape=out_shape,
        cost_estimate=cost(30),
        compiler_params=pltpu.CompilerParams(**params),
    )(rows, scales, weights, outer_t, bias, residue, row_live, flat_live)
    return out[0], out[1], out[2], tuple(out[3:9]), tuple(out[9:])


def backward_kernel(*refs, earlier, adds):
    (order, rows, update, back, scales, weights, outer_t, left_grad, right_grad, residue, row_live, flat_live,
     qkv, gate, powers, inverse, mixed, attended), refs = refs[:18], refs[18:]
    if earlier:
        so_far, early, table_grad, base = refs[0], refs[1:5], refs[5], refs[6]
        pieces, refs = refs[7 : 7 + adds], refs[7 + adds :]
        added, part, bias_grad, packed, norms = refs[:5]
        bias_low, base_in, piece_in, load_sem, piece_sem, store_sem = refs[-6:]
        heads_in_grad, heads_out_grad, outer_in_grad = refs[-9:-6]
        refs = refs[5:-9]
    else:
        if adds:
            pairs, total, pairs_new = refs[0], refs[1], refs[8]
            pairs_new[...] = pairs[...] + total[...].astype(F32)
            refs = refs[2:8] + refs[9:]
        part, bias_grad, heads_in_grad, heads_out_grad, outer_in_grad, norms = refs[:6]
        refs = refs[6:]
    bias_total, mixed_grad, proj_grad, spread, bias_sem = refs
    row = pl.program_id(0)
    own = pl.num_programs(0)
    width = rows.shape[2]
    residues = rows.shape[1]
    size = width // HEADS
    last_row = row == own - 1
    rows_here = base.shape[0] if earlier else 0
    if earlier:
        per, each = base_in.shape[1:3]
        bounds = [0]
        for piece in pieces:
            bounds.append(bounds[-1] + piece.shape[0] // each)
        steps = bounds[-1]

        def bias_load(head):
            return pltpu.make_async_copy(so_far.at[head], bias_total.at[head], bias_sem.at[head])

        def row_of(step):
            return pl.ds(order[step * each], each)

        def fetch(batch, slot):
            for n in range(per):
                step = batch * per + n
                for piece in range(adds):
                    low, high = bounds[piece], bounds[piece + 1]

                    @pl.when((step >= low) & (step < high))
                    def _():
                        pltpu.make_async_copy(base.at[row_of(step)], base_in.at[slot, n], load_sem.at[slot, n]).start()
                        source = pieces[piece].at[pl.ds((step - low) * each, each)]
                        pltpu.make_async_copy(source, piece_in.at[slot, n], piece_sem.at[slot, n]).start()

        def store(batch, slot, n):
            return pltpu.make_async_copy(base_in.at[slot, n], added.at[row_of(batch * per + n)], store_sem.at[slot, n])

        def add_batch(batch, slot):
            for n in range(per):
                step = batch * per + n

                @pl.when((batch >= 1) & (step - per < steps))
                def _():
                    store(batch - 1, 1 - slot, n).wait()
            fetch(batch + 1, 1 - slot)
            for n in range(per):
                step = batch * per + n

                @pl.when(step < steps)
                def _():
                    pltpu.make_async_copy(base.at[row_of(step)], base_in.at[slot, n], load_sem.at[slot, n]).wait()
                    source = pieces[0].at[pl.ds(0, each)]
                    pltpu.make_async_copy(source, piece_in.at[slot, n], piece_sem.at[slot, n]).wait()
                    base_in[slot, n] = base_in[slot, n] + piece_in[slot, n].astype(F32)
                    store(batch, slot, n).start()

    @pl.when(row == 0)
    def _():
        for n, ref in enumerate((heads_in_grad, heads_out_grad, outer_in_grad, norms)):
            ref[...] = early[n][...] if earlier else jnp.zeros_like(ref)
        if earlier:
            for head in range(HEADS):
                bias_load(head).start()
            fetch(0, 0)

    half = outer_t.shape[0] // 2
    count = residues // QUADS
    hat, rstd = normalize(rows[0] + update[0].astype(F32))
    second = hat * scales[2:3] + scales[3:4]
    put(spread, second)
    grads = (right_grad[0].astype(F32) * (residue[...] * row_live[0][:, :1])).astype(BF16)
    outer_in_grad[half:] += dot(grads, second.astype(BF16), (1, 0))
    flat = (left_grad[0].astype(F32) * flat_live[...] * row_live[0]).astype(BF16).T
    for q in range(QUADS):
        mine = flat[q * half : (q + 1) * half]
        outer_in_grad[:half] += dot(mine, take(spread, q).astype(BF16), (1, 0))
        back_to = dot(mine, outer_t[:half], (0, 0))
        for n in range(spread.shape[0]):
            spread[n, pl.ds(q, count, stride=QUADS), :] = back_to[:, n * 128 : (n + 1) * 128]
    spread_grad = jnp.concatenate([spread[n] for n in range(spread.shape[0])], axis=1)
    second_grad = spread_grad + dot(grads, outer_t[half:], (0, 0))
    norms[2:3] += jnp.sum(second_grad * hat, axis=0, keepdims=True)
    norms[3:4] += jnp.sum(second_grad, axis=0, keepdims=True)
    new_part = norm_backward(hat, rstd, scales[2:3], second_grad)
    put(spread, new_part)
    out_grad = (back[0] + new_part).astype(BF16)
    heads_out_grad[...] += dot(attended[0], out_grad, (1, 0))
    attended_grad = dot(weights[4], out_grad, (1, 1))
    sig = gate[0]
    gated = attended_grad * sig
    proj_grad[3 * width :] = (gated * mixed[0] * (1.0 - sig)).astype(BF16)
    deltas = []
    for head in range(HEADS):
        span = slice(head * size, (head + 1) * size)
        grad = gated[span] * inverse[0, head]
        mixed_grad[span] = grad.astype(BF16)
        deltas.append(jnp.sum(grad * mixed[0, span], axis=0, keepdims=True))

    if earlier:
        @pl.when(row == 0)
        def _():
            for head in range(HEADS):
                bias_load(head).wait()

    for head in range(HEADS):
        at = head * size
        query = qkv[0, at : at + size]
        keys = qkv[0, width + at : width + at + size]
        values = qkv[0, 2 * width + at : 2 * width + at + size]
        grad = mixed_grad[at : at + size]
        low = powers[0, head]
        prob_grad = dot(values, grad, (0, 0))
        score_grad = low.astype(F32) * (prob_grad - deltas[head])
        if earlier:
            bias_total[head] += score_grad
        else:
            bias_total[head] = jnp.where(row == 0, 0.0, bias_total[head]) + score_grad
        score_low = score_grad.astype(BF16)
        proj_grad[2 * width + at : 2 * width + at + size] = dot(grad, low, (1, 1)).astype(BF16)
        proj_grad[width + at : width + at + size] = (dot(query, score_low, (1, 1)) / LOG2E).astype(BF16)
        proj_grad[at : at + size] = (dot(keys, score_low, (1, 0)) * size**-0.5).astype(BF16)
        if earlier and (head + 1) % per == 0:
            add_batch(row * (HEADS // per) + head // per, head // per % 2)
        if not earlier:
            @pl.when(last_row)
            def _():
                pltpu.make_async_copy(bias_total.at[head], bias_grad.at[head], bias_sem.at[head]).start()

    if earlier:
        @pl.when(last_row)
        def _():
            across, down, _, lines, cols = bias_grad.shape
            group = max(1, 128 // lines)
            for head in range(HEADS):
                for r in range(0, across, group):
                    for c in range(down):
                        tile = bias_total[head, c * cols : (c + 1) * cols, r * lines : (r + group) * lines]
                        tile = tile.T.astype(BF16)
                        for g in range(group):
                            bias_low[head, r + g, c] = tile[g * lines : (g + 1) * lines]
                pltpu.make_async_copy(bias_low.at[head], bias_grad.at[:, :, head], bias_sem.at[head]).start()

    hat, rstd = normalize(rows[0])
    normed = (hat * scales[0:1] + scales[1:2]).astype(BF16)
    grads = proj_grad[...]
    heads_in_grad[...] += dot(grads, normed, (1, 0))
    normed_grad = dot(grads, weights[:4].reshape(4 * width, width), (0, 0))
    norms[0:1] += jnp.sum(normed_grad * hat, axis=0, keepdims=True)
    norms[1:2] += jnp.sum(normed_grad, axis=0, keepdims=True)
    new_part = jnp.concatenate([spread[n] for n in range(spread.shape[0])], axis=1)
    part[0] = (new_part + norm_backward(hat, rstd, scales[0:1], normed_grad)).astype(BF16)

    @pl.when(last_row)
    def _():
        if earlier:
            first = 0
            for ref in (heads_in_grad, heads_out_grad, outer_in_grad):
                lines = ref.shape[0]
                packed[first : first + lines] = ref[:, :128].astype(BF16)
                packed[first + lines : first + 2 * lines] = ref[:, 128:].astype(BF16)
                first += 2 * lines
            lines = table_grad.shape[0]
            packed[first : first + lines] = table_grad[...].astype(BF16)
            first += lines
            packed[first:] = jnp.zeros((packed.shape[0] - first, 128), BF16)
            batch = rows_here // each // per - 1
            for n in range(per):
                if batch * per + n < steps:
                    store(batch, batch % 2, n).wait()
            for head in range(HEADS):
                pltpu.make_async_copy(bias_low.at[head], bias_grad.at[:, :, head], bias_sem.at[head]).wait()
        else:
            for head in range(HEADS):
                pltpu.make_async_copy(bias_total.at[head], bias_grad.at[head], bias_sem.at[head]).wait()


def attention_backward(
    order, rows, update, back, scales, weights, outer_t, left_grad, right_grad, residue, row_live, flat_live,
    kept, blocks, first, own, earlier=None, early=(), table_grad=None, pieces=(), pairs=(),
):
    _, residues, width = rows.shape
    qkv, gate, powers, inverse, mixed, attended = kept
    here = lambda s, order: (order[0] + first + s, 0, 0)
    by_row = lambda s, order: (first + s, 0, 0)
    by_row_four = lambda s, order: (first + s, 0, 0, 0)
    hbm = pl.BlockSpec(memory_space=pl.ANY)
    once = lambda array: pl.BlockSpec(
        array.shape, lambda s, order: (0,) * array.ndim, pipeline_mode=pl.Buffered(1)
    )
    whole = lambda array: pl.BlockSpec(array.shape, lambda s, order: (0,) * array.ndim)
    one = pl.BlockSpec((1, residues, width), here)
    args = [rows, update, back, scales, weights, outer_t, left_grad, right_grad, residue, row_live, flat_live]
    args += [qkv, gate, powers, inverse, mixed, attended]
    in_specs = [
        one,
        pl.BlockSpec((1, residues, width), by_row),
        one,
        once(scales),
        once(weights),
        once(outer_t),
        pl.BlockSpec((1,) + left_grad.shape[1:], by_row),
        pl.BlockSpec((1,) + right_grad.shape[1:], by_row),
        once(residue),
        pl.BlockSpec((1, 1, 128), by_row),
        once(flat_live),
        pl.BlockSpec((1, 3 * width, residues), by_row),
        pl.BlockSpec((1, width, residues), by_row),
        pl.BlockSpec((1, HEADS, residues, residues), by_row_four),
        pl.BlockSpec((1, HEADS, 1, residues), by_row_four),
        pl.BlockSpec((1, width, residues), by_row),
        pl.BlockSpec((1, width, residues), by_row),
    ]
    part = jax.ShapeDtypeStruct((own, residues, width), BF16)
    part_spec = pl.BlockSpec((1, residues, width), lambda s, order: (s, 0, 0))
    grads = [jax.ShapeDtypeStruct(shape, F32) for shape in ((4 * width, width), (width, width), outer_t.shape)]
    norms = jax.ShapeDtypeStruct((4, width), F32)
    scratch = [
        pltpu.VMEM((HEADS, residues, residues), F32),
        pltpu.VMEM((width, residues), BF16),
        pltpu.VMEM((4 * width, residues), BF16),
        pltpu.VMEM((width // 128, residues, 128), F32),
        pltpu.SemaphoreType.DMA((HEADS,)),
    ]
    if earlier is None:
        out_shape = [part, jax.ShapeDtypeStruct((HEADS, residues, residues), F32)] + grads + [norms]
        out_specs = [part_spec, hbm] + [whole(array) for array in grads + [norms]]
        if pairs:
            slab = pl.BlockSpec((pairs[0].shape[0] // own,) + pairs[0].shape[1:], lambda s, order: (s, 0, 0))
            args += pairs
            in_specs += [slab, slab]
            out_specs.append(slab)
            out_shape.append(jax.ShapeDtypeStruct(pairs[0].shape, F32))
    else:
        each = max(1, rows.shape[0] // (own * HEADS))
        args += [earlier, *early, table_grad, rows] + list(pieces)
        in_specs += [hbm] + [once(array) for array in [*early, table_grad]] + [hbm] * (1 + len(pieces))
        count = 2 * sum(array.shape[0] for array in grads) + table_grad.shape[0]
        count += -count % 512
        packed = jax.ShapeDtypeStruct((count, 128), BF16)
        out_shape = [jax.ShapeDtypeStruct(rows.shape, F32), part, jax.ShapeDtypeStruct(blocks, BF16), packed, norms]
        out_specs = [hbm, part_spec, hbm, whole(packed), whole(norms)]
        scratch += [pltpu.VMEM(array.shape, F32) for array in grads] + [
            pltpu.VMEM((HEADS,) + blocks[:2] + blocks[3:], BF16),
            pltpu.VMEM((2, HEADS // 2, each, residues, width), F32),
            pltpu.VMEM((2, HEADS // 2, each, residues, width), BF16),
            pltpu.SemaphoreType.DMA((2, HEADS // 2)),
            pltpu.SemaphoreType.DMA((2, HEADS // 2)),
            pltpu.SemaphoreType.DMA((2, HEADS // 2)),
        ]
    return pl.pallas_call(
        functools.partial(backward_kernel, earlier=earlier is not None, adds=len(pieces) + len(pairs)),
        grid_spec=pltpu.PrefetchScalarGridSpec(
            num_scalar_prefetch=1, grid=(own,), in_specs=in_specs, out_specs=out_specs, scratch_shapes=scratch
        ),
        out_shape=out_shape,
        compiler_params=pltpu.CompilerParams(vmem_limit_bytes=VMEM),
        cost_estimate=cost(20),
    )(order, *args)


def outer_product_plain(left, right, pairs_back, table, all_rows):
    low = pairs_back.astype(BF16)
    product = mm("sei,sfj->eifj", left, right).astype(BF16)
    total = mm("eifj,efz->ijz", product, table) / all_rows
    table_grad = mm("eifj,ijz->efz", product, low) / all_rows
    back = mm("ijz,efz->eifj", low, table).astype(BF16)
    left_grad = mm("eifj,sfj->sei", back, right) / all_rows
    right_grad = mm("eifj,sei->sfj", back, left) / all_rows
    return total, table_grad, left_grad.astype(BF16), right_grad.astype(BF16)


def mm(spec, a, b):
    return jnp.einsum(spec, a, b, preferred_element_type=F32)


def pair_forward(pairs, gain, shift, bias_low):
    hat, _ = normalize(pairs)
    low = (hat * gain + shift).astype(BF16)
    return (mm("ijc,ch->hij", low, bias_low) * LOG2E).astype(BF16)


def pair_backward(pairs, pairs_back, gain, shift, bias_low, bias_grad):
    hat, rstd = normalize(pairs)
    low = (hat * gain + shift).astype(BF16)
    weight_grad = mm("ijc,hij->ch", low, bias_grad)
    in_grad = mm("hij,ch->ijc", bias_grad, bias_low)
    gain_grad = jnp.sum(in_grad * hat, axis=(0, 1))
    shift_grad = jnp.sum(in_grad, axis=(0, 1))
    return pairs_back + norm_backward(hat, rstd, gain, in_grad), weight_grad, gain_grad, shift_grad


MESH = pl.DeviceIdType.MESH
CORE, ACROSS, DOWN, CORNER = 1, 2, 4, 6


def place():
    return lax.axis_index("row"), lax.axis_index("head")


def flip(row, way):
    out = row
    for bit in (1, 2, 4):
        if way & bit:
            out = out + bit - 2 * bit * ((row // bit) % 2)
    return out


def greet(devices):
    barrier = pltpu.get_barrier_semaphore()
    for device in devices:
        pl.semaphore_signal(barrier, inc=1, device_id=device, device_id_type=MESH)
    pl.semaphore_wait(barrier, len(devices))


class Sends:
    def __init__(self, send_sem, recv_sem):
        self.send_sem, self.recv_sem, self.count, self.open = send_sem, recv_sem, 0, []

    def start(self, source, target, device):
        copy = pltpu.make_async_remote_copy(
            src_ref=source,
            dst_ref=target,
            send_sem=self.send_sem.at[self.count],
            recv_sem=self.recv_sem.at[self.count],
            device_id=device,
            device_id_type=MESH,
        )
        copy.start()
        self.count += 1
        self.open.append(copy)
        return copy

    def finish(self):
        for copy in self.open:
            copy.wait_send()


PARTS = 2
GATHER_SENDS = 6 + PARTS * (3 + 12 + 16)


def pair_bias_kernel(
    pairs, norm, weight, heads_in, heads_out, bias, weights, values_in, shard, block, low,
    load_sem, local_sem, send_sem, recv_sem,
):
    row, head = place()
    rows, cols, channels = pairs.shape
    part = shard.shape[1] // 2
    core = row % 2
    lines = rows // PARTS
    loads = []
    for n in range(PARTS):
        at = pl.ds(n * lines, lines)
        loads.append(pltpu.make_async_copy(pairs.at[at], values_in.at[at], load_sem.at[n]))
        loads[n].start()
    shard[:4] = heads_in[...].astype(BF16)
    shard[4] = heads_out[...].astype(BF16)
    beyond = [(head + k) % 4 for k in range(4)]
    behind = [(head + 4 - k) % 4 for k in range(4)]
    across, down, other = (flip(row, ACROSS), head), (flip(row, DOWN), head), (flip(row, CORE), head)
    greet([across, down, other] + [(row, beyond[k]) for k in (1, 2, 3)])
    sends = Sends(send_sem, recv_sem)

    def own_part(at, side):
        return weights.at[:, pl.ds(pl.multiple_of(at * 2 * part + side * part, part), part), :]

    keep = pltpu.make_async_copy(
        shard, weights.at[:, pl.ds(pl.multiple_of(head * 2 * part, 2 * part), 2 * part), :], local_sem.at[PARTS]
    )
    keep.start()
    step = 8

    def norm_block(n, carry):
        first = pl.multiple_of(n * step, step)
        values = values_in[pl.ds(first, step)].reshape(step * cols, channels)
        center = values - jnp.mean(values, axis=-1, keepdims=True)
        rstd = lax.rsqrt(jnp.mean(center * center, axis=-1, keepdims=True) + 1e-05)
        normed = (center * rstd * norm[0:1] + norm[1:2]).astype(BF16)
        out = lax.dot_general(weight[...], normed, (((1,), (1,)), ((), ())), preferred_element_type=F32)
        for i in range(step):
            block[:, pl.ds(first + i, 1), :] = (out[:, i * cols : (i + 1) * cols] * LOG2E).reshape(
                HEADS, 1, cols
            )
        return carry

    ends, mine = [], []

    class Part:
        def __init__(self, n):
            self.at = pl.ds(n * lines, lines)
            loads[n].wait()
            lax.fori_loop(n * lines // step, (n + 1) * lines // step, norm_block, 0)
            low[n] = block[:, n * lines : (n + 1) * lines].astype(BF16)
            self.own = low.at[n]
            copy = pltpu.make_async_copy(self.own, self.slot(row, 0), local_sem.at[n])
            copy.start()
            mine.append(copy)
            self.along = [None] + [
                sends.start(self.own, self.slot(row, 0), (row, beyond[k])) for k in (1, 2, 3)
            ]
            self.across, self.down, self.corner = [None] * 4, [None] * 4, [None] * 4
            self.spread(0)

        def slot(self, at, k):
            return bias.at[at, behind[k], :, self.at]

        def spread(self, k):
            if k:
                self.along[k].wait_recv()
            here = self.slot(row, k)
            source = here if k else self.own
            self.across[k] = sends.start(source, here, across)
            self.down[k] = sends.start(source, here, down)
            ends.append(sends.start(source, here, other))

        def relay(self, k):
            self.across[k].wait_recv()
            here = self.slot(flip(row, ACROSS), k)
            if k < 2:
                self.corner[k] = sends.start(here, here, down)
            ends.append(sends.start(here, here, other))
            self.down[k].wait_recv()
            here = self.slot(flip(row, DOWN), k)
            if k >= 2:
                self.corner[k] = sends.start(here, here, across)
            ends.append(sends.start(here, here, other))

        def finish(self, k):
            self.corner[k].wait_recv()
            here = self.slot(flip(row, CORNER), k)
            ends.append(sends.start(here, here, other))

    parts = [Part(n) for n in range(PARTS)]
    half = shard.at[:, pl.ds(pl.multiple_of(core * part, part), part), :]
    shards = [None] + [sends.start(half, own_part(head, core), (row, beyond[k])) for k in (1, 2, 3)]
    for k in range(4):
        for one in parts:
            if k:
                one.spread(k)
                one.relay(k - 1)
    for one in parts:
        one.relay(3)
    for k in range(4):
        for one in parts:
            one.finish(k)
    for k in (1, 2, 3):
        shards[k].wait_recv()
        piece = own_part(behind[k], core)
        ends.append(sends.start(piece, piece, other))
    for copy in ends:
        copy.wait_recv()
    sends.finish()
    keep.wait()
    for copy in mine:
        copy.wait()


def pair_bias(pairs, norm, weight, heads_in, heads_out):
    rows, cols, channels = pairs.shape
    vmem = pl.BlockSpec(memory_space=pltpu.VMEM)
    hbm = pl.BlockSpec(memory_space=pl.ANY)
    shard = (heads_in.shape[0] + 1,) + heads_out.shape
    return pl.pallas_call(
        pair_bias_kernel,
        out_shape=[
            jax.ShapeDtypeStruct((8, 4, HEADS, rows, cols), BF16),
            jax.ShapeDtypeStruct((shard[0], 4 * shard[1], shard[2]), BF16),
        ],
        in_specs=[hbm, vmem, vmem, vmem, vmem],
        out_specs=[hbm, hbm],
        scratch_shapes=[
            pltpu.VMEM(pairs.shape, F32),
            pltpu.VMEM(shard, BF16),
            pltpu.VMEM((HEADS, rows, cols), F32),
            pltpu.VMEM((PARTS, HEADS, rows // PARTS, cols), BF16),
            pltpu.SemaphoreType.DMA((PARTS,)),
            pltpu.SemaphoreType.DMA((PARTS + 1,)),
            pltpu.SemaphoreType.DMA((GATHER_SENDS,)),
            pltpu.SemaphoreType.DMA((GATHER_SENDS,)),
        ],
        compiler_params=pltpu.CompilerParams(
            collective_id=0, has_side_effects=True, vmem_limit_bytes=VMEM
        ),
        cost_estimate=cost(34),
    )(pairs, norm, weight, heads_in, heads_out)


OUTER_SENDS = 2 + 3 + 7 + 1 + 3 + 3


def outer_kernel(
    left, right, left_early, right_early, pairs_back, outer_out, update, hop_early,
    total, left_out, right_out, table_grad, hop_one, hop_two,
    left_stage, right_stage, left_plane, right_line, left_all, right_all, left_last, right_last, left_wide, right_wide, left_rows, right_rows,
    backed, product, back, low, table, table_t, total_low,
    left_part, right_part, left_send, right_send, right_core, chip_sum, right_in, right_sum, left_line, left_sum, left_land, right_land,
    load_sem, local_sem, out_sem, row_local, row_send, row_recv, send_sem, recv_sem,
    *, scale, block, group,
):
    row, head = place()
    beyond = [(head + k) % 4 for k in range(4)]
    plane = [(flip(row, way), head) for way in range(8)]
    core, chip = row % 2, row // 2
    own, wide, _ = right.shape
    rows, cols, channels = back.shape
    size = wide
    lines = left_all.shape[3]
    chunks = rows // block
    half, most = own // 2, own - 1
    greet(plane[1:] + [(row, beyond[k]) for k in (1, 2, 3)])
    sends = Sends(send_sem, recv_sem)
    sides = Exchange(
        left.at[pl.ds(most, own - most)], right.at[pl.ds(most, own - most)], left_stage, right_stage,
        left_plane, right_line, left_last, right_last, row_local, row_send, row_recv,
    )
    sides.begin()
    gather = [
        pltpu.make_async_copy(left_early, left_all, local_sem.at[0]),
        pltpu.make_async_copy(right_early, right_all, local_sem.at[1]),
    ]
    loads = []
    for n in range(chunks):
        copy = pltpu.make_async_copy(
            pairs_back.at[pl.ds(n * block, block)], back.at[pl.ds(n * block, block)], load_sem.at[n]
        )
        copy.start()
        loads.append(copy)
    for copy in gather:
        copy.start()

    for f in range(wide):
        table[f * size : (f + 1) * size] = outer_out[pl.ds(f, size, stride=wide), :].astype(BF16)
    for n in range(wide * size // 128):
        table_t[:, n * 128 : (n + 1) * 128] = table[n * 128 : (n + 1) * 128].T

    def spread_pair(p, carry):
        first = p * group
        both = back[pl.ds(first, group)].astype(BF16)
        low[pl.ds(first, group)] = both
        spread = dot(table[...], both.reshape(group * cols, channels), (1, 1)).astype(BF16)
        for g in range(group):
            at = pl.ds(pl.multiple_of((first + g) * size, size), size)
            for f in range(wide):
                backed[at, f * cols : (f + 1) * cols] = spread[
                    f * size : (f + 1) * size, g * cols : (g + 1) * cols
                ]
        return carry

    pairs_of = rows // group

    def spread_part(k):
        for n in range(k * chunks // 4, (k + 1) * chunks // 4):
            loads[n].wait()
        lax.fori_loop(k * pairs_of // 4, (k + 1) * pairs_of // 4, spread_pair, 0)

    spread_part(0)
    sides.go_on()
    hops = [
        sends.start(update.at[pl.ds(half, own - half)], hop_one, (row, beyond[1])),
        sends.start(hop_early, hop_two, (row, beyond[1])),
    ]
    spread_part(1)
    spread_part(2)
    sides.core()
    spread_part(3)
    sides.end()
    for copy in gather:
        copy.wait()

    count = 32
    for r in range(8):
        for h in range(4):
            left_wide[r * 4 + h, :most] = left_all[h, r].astype(F32)
            left_wide[r * 4 + h, most:] = left_last[h, r].astype(F32)
    right_wide[:, :most] = right_all[...].astype(F32).reshape((count, most) + right_wide.shape[2:])
    right_wide[:, most:] = right_last[...].astype(F32).reshape((count, own - most) + right_wide.shape[2:])
    for s in range(own):
        at = slice(s * count, (s + 1) * count)
        for n in range(lines):
            left_rows[at, n * 128 : (n + 1) * 128] = left_wide[:, s, n, :].astype(BF16)
        for f in range(wide):
            right_rows[at, f * cols : (f + 1) * cols] = right_wide[:, s, f, :].astype(BF16)

    deep = block * size

    def left_step(n, carry):
        at = pl.ds(pl.multiple_of(n * deep, deep), deep)
        left_part[:, at] = dot(right_rows[...], backed[at, :], (1, 1)) * scale
        return carry

    lax.fori_loop(0, chunks, left_step, 0)
    for s in range(own):
        at = slice(s * count, (s + 1) * count)
        for n in range(lines):
            left_wide[:, s, n, :] = left_part[at, n * 128 : (n + 1) * 128]
    for r in range(8):
        for h in range(4):
            left_send[h, r] = left_wide[r * 4 + h].astype(BF16)
    lefts = [
        sends.start(left_send.at[beyond[k]], left_line.at[k - 1], (row, beyond[k])) for k in (2, 1, 3)
    ]
    step = 4 * cols

    def right_step(n, carry):
        at = pl.ds(pl.multiple_of(n * step, step), step)
        right_part[:, at] = dot(left_rows[...], backed[:, at], (1, 0)) * scale
        return carry

    lax.fori_loop(0, wide * cols // step, right_step, 0)
    for s in range(own):
        at = slice(s * count, (s + 1) * count)
        for f in range(wide):
            right_wide[:, s, f, :] = right_part[at, f * cols : (f + 1) * cols]
    right_send[...] = right_wide[...].astype(BF16).reshape(right_send.shape)
    swap = sends.start(right_send.at[:, 1 - core], right_core, plane[CORE])
    table_grad[...] = jnp.zeros_like(table_grad)

    def outer_chunk(n, carry):
        at = pl.ds(pl.multiple_of(n * deep, deep), deep)
        product[...] = dot(left_rows[:, at], right_rows[...], (0, 0)).astype(BF16)
        for first in range(0, block, group):
            both = jnp.concatenate(
                [
                    jnp.concatenate(
                        [
                            product[(first + g) * size : (first + g + 1) * size, f * cols : (f + 1) * cols]
                            for f in range(wide)
                        ],
                        axis=0,
                    )
                    for g in range(group)
                ],
                axis=1,
            )
            out = dot(table_t[...], both, (1, 0)) * scale
            for g in range(group):
                total_low[n * block + first + g] = out[:, g * cols : (g + 1) * cols].T.astype(BF16)
            seen = low[pl.ds(n * block + first, group)].reshape(group * cols, channels)
            table_grad[...] += dot(both, seen, (1, 0)) * scale
        return carry

    stores = []

    def outer_part(n):
        first, last = n * chunks // 4, (n + 1) * chunks // 4
        lax.fori_loop(first, last, outer_chunk, 0)
        at = pl.ds(first * block, (last - first) * block)
        copy = pltpu.make_async_copy(total_low.at[at], total.at[at], out_sem.at[n])
        copy.start()
        stores.append(copy)

    swap.wait_recv()
    rights = []
    for slot, way in enumerate((CORNER, ACROSS, DOWN)):
        n = plane[way][0] // 2
        for h in range(4):
            chip_sum[slot, h] = (
                right_send[n, core, h].astype(F32) + right_core[n, h].astype(F32)
            ).astype(BF16)
        rights.append(sends.start(chip_sum.at[slot], right_in.at[slot], plane[way]))
    outer_part(0)
    for copy in lefts:
        copy.wait_recv()
    for r in range(8):
        summed = left_send[head, r].astype(F32)
        for k in range(3):
            summed = summed + left_line[k, r].astype(F32)
        left_sum[r] = summed.astype(BF16)
    across = [
        sends.start(left_sum.at[plane[way][0]], left_land.at[row], plane[way])
        for way in (2, 4, 6, 3, 5, 7, 1)
    ]
    left_land[row] = left_sum[row]
    outer_part(1)
    for copy in rights:
        copy.wait_recv()
    for h in range(4):
        summed = right_send[chip, core, h].astype(F32) + right_core[chip, h].astype(F32)
        for slot in range(3):
            summed = summed + right_in[slot, h].astype(F32)
        right_sum[h] = summed.astype(BF16)
    line = [
        sends.start(right_sum.at[beyond[k]], right_land.at[head], (row, beyond[k])) for k in (1, 2, 3)
    ]
    right_land[head] = right_sum[head]
    outer_part(2)
    outer_part(3)
    for copy in across + line:
        copy.wait_recv()
    for r in range(8):
        left_out[:, r * lines : (r + 1) * lines, :] = left_land[r]
    for h in range(4):
        right_out[:, :, h * cols : (h + 1) * cols] = right_land[h]
    for copy in hops:
        copy.wait_recv()
    sends.finish()
    for copy in stores:
        copy.wait()


def outer_product(left, right, early, pairs_back, outer_out, update, all_rows, block=8, group=2):
    left_early, right_early, hop_early = early
    rows, cols, channels = pairs_back.shape
    own, wide, residues = right.shape
    size = left.shape[1] * left.shape[2] // residues
    lines = left.shape[1] // 8
    vmem = pl.BlockSpec(memory_space=pltpu.VMEM)
    hbm = pl.BlockSpec(memory_space=pl.ANY)
    low = lambda *shape: pltpu.VMEM(shape, BF16)
    full = lambda *shape: pltpu.VMEM(shape, F32)
    one = (lines, 128)
    other = (wide, cols)
    rest = 1
    dma = pltpu.SemaphoreType.DMA
    return pl.pallas_call(
        functools.partial(outer_kernel, scale=1.0 / all_rows, block=block, group=group),
        out_shape=[
            jax.ShapeDtypeStruct(pairs_back.shape, BF16),
            jax.ShapeDtypeStruct(left.shape, BF16),
            jax.ShapeDtypeStruct(right.shape, BF16),
            jax.ShapeDtypeStruct((wide * size, channels), F32),
            jax.ShapeDtypeStruct((own - own // 2,) + update.shape[1:], BF16),
            jax.ShapeDtypeStruct(hop_early.shape, BF16),
        ],
        in_specs=[vmem, vmem, hbm, hbm, hbm, vmem, hbm, hbm],
        out_specs=[hbm, vmem, vmem, vmem, hbm, hbm],
        scratch_shapes=[
            low(8, rest, *one), low(4, rest, *other), low(8, rest, *one), low(4, rest, *other),
            low(4, 8, own - rest, *one), low(8, 4, own - rest, *other),
            low(4, 8, rest, *one), low(8, 4, rest, *other), full(32, own, *one), full(32, own, *other),
            low(all_rows, rows * size), low(all_rows, wide * cols),
            low(rows * size, wide * cols), low(block * size, wide * cols), full(rows, cols, channels),
            low(rows, cols, channels), low(wide * size, channels), low(channels, wide * size), low(rows, cols, channels),
            full(all_rows, rows * size), full(all_rows, wide * cols), low(4, 8, own, *one), low(4, 2, 4, own, *other),
            low(4, 4, own, *other), low(3, 4, own, *other), low(3, 4, own, *other), low(4, own, *other),
            low(3, 8, own, *one), low(8, own, *one), low(8, own, *one), low(4, own, *other),
            dma((rows // block,)), dma((2,)), dma((4,)), dma((2,)), dma((ROW_SENDS,)), dma((ROW_SENDS,)),
            dma((OUTER_SENDS,)), dma((OUTER_SENDS,)),
        ],
        compiler_params=pltpu.CompilerParams(
            collective_id=1, has_side_effects=True, vmem_limit_bytes=VMEM
        ),
        cost_estimate=cost(50),
    )(left, right, left_early, right_early, pairs_back, outer_out, update, hop_early)


SUM_SENDS = 4 + 4 + 8 + 3 + 1 + 3 + 3 + 3 + 12 + 16


def sum_kernel(
    grads, parts, out, spread,
    swapped, chip_sum, by_across, by_down, from_across, from_down, down_sum, line_in,
    part_swapped, part_sum, part_plane, part_down, part_line, piece,
    local_sem, send_sem, recv_sem,
):
    row, head = place()
    beyond = [(head + k) % 4 for k in range(4)]
    core, chip = row % 2, row // 2
    ways = (CORNER, ACROSS, DOWN)
    plane = [(flip(row, way), head) for way in range(8)]
    other, across, down = plane[CORE], plane[ACROSS], plane[DOWN]
    greet([plane[way] for way in (CORE,) + ways] + [(row, beyond[k]) for k in (1, 2, 3)])
    sends = Sends(send_sem, recv_sem)
    chips = [plane[way][0] // 2 for way in ways] + [chip]
    part_swap = sends.start(parts.at[1 - core], part_swapped, other)
    swaps = [sends.start(grads.at[n, 1 - core], swapped.at[slot], other) for slot, n in enumerate(chips)]
    first, second = (2, 1), (3, 0)

    def add(slot, k):
        z = beyond[k]
        chip_sum[slot, k] = (
            grads[chips[slot], core, z].astype(F32) + swapped[slot, z].astype(F32)
        ).astype(BF16)

    part_swap.wait_recv()
    part_arrive = []
    for slot, n in enumerate(chips):
        for z in range(4):
            part_sum[slot, z] = (parts[core, n, z].astype(F32) + part_swapped[n, z].astype(F32)).astype(BF16)
        if slot < 3:
            part_arrive.append(sends.start(part_sum.at[slot], part_plane.at[slot], plane[ways[slot]]))
    swaps[0].wait_recv()
    relays_across, relays_down = [], []
    for n in range(2):
        add(0, first[n])
        relays_across.append(sends.start(chip_sum.at[0, first[n]], by_across.at[n], across))
        add(0, second[n])
        relays_down.append(sends.start(chip_sum.at[0, second[n]], by_down.at[n], down))
    last_across, last_down = [None] * 4, [None] * 4
    swaps[1].wait_recv()
    for k in first:
        add(1, k)
        last_across[k] = sends.start(chip_sum.at[1, k], from_across.at[k], across)
    swaps[2].wait_recv()
    for k in second:
        add(2, k)
        last_down[k] = sends.start(chip_sum.at[2, k], from_down.at[k], down)
    for n in range(2):
        add(1, second[n])
        add(2, first[n])
        relays_across[n].wait_recv()
        k = first[n]
        chip_sum[2, k] = (chip_sum[2, k].astype(F32) + by_across[n].astype(F32)).astype(BF16)
        last_down[k] = sends.start(chip_sum.at[2, k], from_down.at[k], down)
        relays_down[n].wait_recv()
        k = second[n]
        chip_sum[1, k] = (chip_sum[1, k].astype(F32) + by_down[n].astype(F32)).astype(BF16)
        last_across[k] = sends.start(chip_sum.at[1, k], from_across.at[k], across)
    for copy in part_arrive:
        copy.wait_recv()
    for z in range(4):
        total = part_sum[3, z].astype(F32)
        for slot in range(3):
            total = total + part_plane[slot, z].astype(F32)
        part_down[z] = total.astype(BF16)
    part_arrive = [
        sends.start(part_down.at[beyond[k]], part_line.at[k - 1], (row, beyond[k])) for k in (1, 2, 3)
    ]
    swaps[3].wait_recv()
    for k in first + second:
        add(3, k)
    total = part_down[head].astype(F32)
    for slot, copy in enumerate(part_arrive):
        copy.wait_recv()
        total = total + part_line[slot].astype(F32)
    piece[...] = total.astype(BF16)
    behind = [(head + 4 - k) % 4 for k in range(4)]
    part_line_all = [None] + [sends.start(piece, spread.at[core, chip, head], (row, beyond[k])) for k in (1, 2, 3)]
    mine = pltpu.make_async_copy(piece, spread.at[core, chip, head], local_sem)
    mine.start()
    wide, end = [], []

    def forward(k):
        here = spread.at[core, chip, behind[k]]
        source = here if k else piece
        for way in ways:
            wide.append((plane[way][0] // 2, k, sends.start(source, here, plane[way])))
        end.append(sends.start(source, here, other))

    forward(0)
    line = []
    for k in first + second:
        last_across[k].wait_recv()
        last_down[k].wait_recv()
        total = chip_sum[3, k].astype(F32) + from_across[k].astype(F32) + from_down[k].astype(F32)
        if k:
            down_sum[k - 1] = total.astype(BF16)
            line.append(sends.start(down_sum.at[k - 1], line_in.at[k - 1], (row, beyond[k])))
        else:
            out[...] = total
        if k == first[0]:
            for n in (1, 2, 3):
                part_line_all[n].wait_recv()
                forward(n)
    for n, k, copy in wide:
        copy.wait_recv()
        block = spread.at[core, n, behind[k]]
        end.append(sends.start(block, block, other))
    for slot, copy in zip((1, 0, 2), line):
        copy.wait_recv()
        out[...] += line_in[slot].astype(F32)
    for copy in end:
        copy.wait_recv()
    mine.wait()
    sends.finish()


def sum_gradients(grads, parts):
    block = grads.shape[2:]
    lines = block[0] * block[1]
    rows, cols = parts.shape
    share = rows // 32
    vmem = pl.BlockSpec(memory_space=pltpu.VMEM)
    wide = lambda *first: pltpu.VMEM(first + (lines, block[2]), BF16)
    thin = lambda *first: pltpu.VMEM(first + (share, cols), BF16)
    out, spread = pl.pallas_call(
        sum_kernel,
        out_shape=[
            jax.ShapeDtypeStruct((lines, block[2]), F32),
            jax.ShapeDtypeStruct((2, 4, 4, share, cols), BF16),
        ],
        in_specs=[vmem, vmem],
        out_specs=[vmem, vmem],
        scratch_shapes=[
            wide(4, 4), wide(4, 4), wide(2), wide(2), wide(4), wide(4), wide(3), wide(3),
            thin(4, 4), thin(4, 4), thin(3, 4), thin(4), thin(3), thin(),
            pltpu.SemaphoreType.DMA,
            pltpu.SemaphoreType.DMA((SUM_SENDS,)),
            pltpu.SemaphoreType.DMA((SUM_SENDS,)),
        ],
        compiler_params=pltpu.CompilerParams(
            collective_id=3, has_side_effects=True, vmem_limit_bytes=VMEM
        ),
        cost_estimate=cost(40),
    )(grads.reshape(4, 2, 4, lines, block[2]), parts.reshape(2, 4, 4, share, cols))
    return out.reshape(block), spread.reshape(rows, cols)


SMALL_SENDS = 3 + 7


def small_kernel(small, total, line_in, line_sum, plane_in, send_sem, recv_sem):
    row, head = place()
    line = [(row, (head + k) % 4) for k in (1, 2, 3)]
    plane = [(flip(row, way), head) for way in range(1, 8)]
    greet(plane + line)
    sends = Sends(send_sem, recv_sem)
    arrive = [sends.start(small, line_in.at[head], device) for device in line]
    line_in[head] = small[...]
    for copy in arrive:
        copy.wait_recv()
    line_sum[...] = (line_in[0] + line_in[1]) + (line_in[2] + line_in[3])
    arrive = [sends.start(line_sum, plane_in.at[row], device) for device in plane]
    plane_in[row] = line_sum[...]
    for copy in arrive:
        copy.wait_recv()
    summed = plane_in[0]
    for n in range(1, 8):
        summed = summed + plane_in[n]
    total[...] = summed
    sends.finish()


def small_sum(small):
    vmem = pl.BlockSpec(memory_space=pltpu.VMEM)
    return pl.pallas_call(
        small_kernel,
        out_shape=jax.ShapeDtypeStruct(small.shape, F32),
        in_specs=[vmem],
        out_specs=vmem,
        scratch_shapes=[
            pltpu.VMEM((4,) + small.shape, F32),
            pltpu.VMEM(small.shape, F32),
            pltpu.VMEM((8,) + small.shape, F32),
            pltpu.SemaphoreType.DMA((SMALL_SENDS,)),
            pltpu.SemaphoreType.DMA((SMALL_SENDS,)),
        ],
        compiler_params=pltpu.CompilerParams(
            collective_id=4, has_side_effects=True, vmem_limit_bytes=VMEM
        ),
        cost_estimate=cost(9),
    )(small)


def add_pieces(step, base, pieces, out):
    for n, piece in enumerate(pieces):
        @pl.when(step == n)
        def _():
            out[...] = base[...] + piece[...].astype(F32)


def added_specs(base, pieces):
    block = pieces[0].shape
    by_order = pl.BlockSpec(
        block, lambda n, order: (order[jnp.minimum(n, len(pieces) - 1) * block[0]] // block[0], 0, 0)
    )
    return by_order, [by_order] + [pl.BlockSpec(block, lambda n, order: (0, 0, 0))] * len(pieces)


def pair_backward_kernel(order, pairs, back, grads, norm, weight, norms, base, *refs):
    pieces, (out, small, changed) = refs[:-3], refs[-3:]
    step = pl.program_id(0)
    rows, cols, channels = pairs.shape
    add_pieces(step, base, pieces, changed)

    @pl.when(step == 0)
    def _():
        small[...] = jnp.zeros_like(small)
        small[2 * HEADS :] = jnp.concatenate([norms[:, :128], norms[:, 128:]], axis=0)

    values = pairs[...].reshape(rows * cols, channels)
    hat, rstd = normalize(values)
    low = (hat * norm[0:1] + norm[1:2]).astype(BF16)
    bias = jnp.concatenate([grads[:, i, :] for i in range(rows)], axis=1).astype(BF16)
    small[0:HEADS] += dot(bias, low, (1, 0))
    in_grad = dot(bias, weight[...], (0, 0))
    small[HEADS : HEADS + 1] += jnp.sum(in_grad * hat, axis=0, keepdims=True)
    small[HEADS + 1 : HEADS + 2] += jnp.sum(in_grad, axis=0, keepdims=True)
    change = norm_backward(hat, rstd, norm[0:1], in_grad)
    out[...] = back[...] + change.reshape(rows, cols, channels)


def pair_norm_backward(order, pairs, back, grads, norm, weight, norms, base, pieces, steps=8):
    rows, cols, channels = pairs.shape
    block = rows // steps
    by_row = lambda n, order: (n, 0, 0)
    whole = lambda n, order: (0, 0)
    by_order, added = added_specs(base, pieces)
    grads = grads.reshape(HEADS, steps, block, cols)
    return pl.pallas_call(
        pair_backward_kernel,
        grid_spec=pltpu.PrefetchScalarGridSpec(
            num_scalar_prefetch=1,
            grid=(steps,),
            in_specs=[
                pl.BlockSpec((block, cols, channels), by_row),
                pl.BlockSpec((block, cols, channels), by_row),
                pl.BlockSpec((HEADS, None, block, cols), lambda n, order: (0, n, 0, 0)),
                pl.BlockSpec(norm.shape, whole),
                pl.BlockSpec(weight.shape, whole),
                pl.BlockSpec(norms.shape, whole),
            ]
            + added,
            out_specs=[
                pl.BlockSpec((block, cols, channels), by_row),
                pl.BlockSpec((3 * HEADS, channels), whole),
                by_order,
            ],
        ),
        out_shape=[
            jax.ShapeDtypeStruct(pairs.shape, F32),
            jax.ShapeDtypeStruct((3 * HEADS, channels), F32),
            jax.ShapeDtypeStruct(base.shape, F32),
        ],
        compiler_params=pltpu.CompilerParams(vmem_limit_bytes=VMEM),
        cost_estimate=cost(9),
    )(order, pairs, back, grads, norm, weight, norms, base, *pieces)


def add_kernel(place_ref, base, piece, *refs):
    refs[-1][...] = base[...] + piece[...].astype(F32)


def add_rows(at, base, piece, into=None):
    own = piece.shape[0]
    block = (1,) + piece.shape[1:]
    spread = lambda n, at: (at[0] * own + n, 0, 0)
    return pl.pallas_call(
        add_kernel,
        grid_spec=pltpu.PrefetchScalarGridSpec(
            num_scalar_prefetch=1,
            grid=(own,),
            in_specs=[pl.BlockSpec(block, spread), pl.BlockSpec(block, lambda n, at: (n, 0, 0))]
            + ([] if into is None else [pl.BlockSpec(memory_space=pl.ANY)]),
            out_specs=pl.BlockSpec(block, spread),
        ),
        out_shape=jax.ShapeDtypeStruct(base.shape, F32),
        input_output_aliases={} if into is None else {3: 0},
        cost_estimate=cost(2),
    )(*((at, base, piece) if into is None else (at, base, piece, into)))


def hop(piece):
    count = lax.axis_size("head")
    return lax.ppermute(piece, "head", [(i, (i + 1) % count) for i in range(count)])


def together(moved, *values):
    return lax.optimization_barrier((moved,) + values)


def adam_kernel(at, packed, pair_side, *refs, rates, pieces):
    olds, base, adds, news = refs[:18], refs[18], refs[19 : 19 + pieces], refs[20 + pieces : 38 + pieces]
    changed, table = refs[38 + pieces :]
    step = pl.program_id(0)
    add_pieces(step, base, adds, changed)

    @pl.when(step == 0)
    def _():
        adam_step(at, packed, pair_side, olds, news, table, rates)


def adam_step(at, packed, pair_side, olds, news, table, rates):
    norms, heads_in, heads_out, bias_weight, outer_in, outer_out = [olds[3 * n : 3 * n + 3] for n in range(6)]
    count, local, all_heads = heads_in[0].shape
    sides, size = outer_in[0].shape[:2]

    def rows(first, lines):
        return packed[pl.ds(first, lines), :].astype(F32)

    def pair_of(first, offset, lines, span):
        return jnp.concatenate([rows(first + offset, lines), rows(first + span + offset, lines)], axis=1)

    def update(n, index, grad):
        weight, moment_one, moment_two = [ref[index] for ref in olds[3 * n : 3 * n + 3]]
        for ref, new in zip(
            news[3 * n : 3 * n + 3], adam_update(weight, grad, moment_one, moment_two, rates[n])
        ):
            ref[index] = new

    mine = pl.multiple_of(at[4], local)
    span = count * all_heads
    for k in range(count):
        update(1, k, pair_of(0, k * all_heads + mine, local, span))
    first = 2 * span
    update(2, slice(None), pair_of(first, mine, local, all_heads))
    first += 2 * all_heads
    for k in range(sides):
        update(4, k, pair_of(first, k * size, size, sides * size))
    first += 2 * sides * size
    table[...] = rows(first, size * size)
    for e in range(size):
        update(5, slice(e * size, (e + 1) * size), table[pl.ds(e, size, stride=size), :])
    pair = pair_side[...]
    low = pair[2 * HEADS :]
    lines = [
        jnp.concatenate([low[n : n + 1], low[n + 4 : n + 5], low[n + 2 : n + 3], low[n + 6 : n + 7], pair[HEADS + n : HEADS + n + 1]], axis=1)
        for n in range(2)
    ]
    update(0, slice(None), jnp.concatenate(lines, axis=0))
    update(3, slice(None), pair[:HEADS])


def adam_all(at, packed, pair_side, olds, rates, base, pieces, into):
    turned = (1, 3, 4)
    flat = [array.swapaxes(-1, -2) if n in turned else array for n, triple in enumerate(olds) for array in triple]
    size = olds[4][0].shape[2]
    by_order, added = added_specs(base, pieces)
    whole = lambda array: pl.BlockSpec(array.shape, lambda n, at: (0,) * array.ndim)
    *news, changed = pl.pallas_call(
        functools.partial(adam_kernel, rates=rates, pieces=len(pieces)),
        grid_spec=pltpu.PrefetchScalarGridSpec(
            num_scalar_prefetch=1,
            grid=(len(pieces),),
            in_specs=[whole(array) for array in [packed, pair_side] + flat]
            + added
            + [pl.BlockSpec(memory_space=pl.ANY)],
            out_specs=[whole(array) for array in flat] + [by_order],
            scratch_shapes=[pltpu.VMEM((size * size, packed.shape[1]), F32)],
        ),
        out_shape=[jax.ShapeDtypeStruct(array.shape, F32) for array in flat + [base]],
        input_output_aliases={3 + len(flat) + 1 + len(pieces): len(flat)},
        compiler_params=pltpu.CompilerParams(vmem_limit_bytes=VMEM),
        cost_estimate=cost(5),
    )(at, packed, pair_side, *flat, base, *pieces, into)
    news = [array.swapaxes(-1, -2) if n // 3 in turned else array for n, array in enumerate(news)]
    return news + [changed]


def per_device(
    alignment,
    pairs,
    residue_mask,
    row_mask,
    alignment_back,
    pairs_back,
    norm_scales,
    heads_in,
    heads_out,
    bias_weight,
    outer_in,
    outer_out,
    first_norms,
    second_norms,
    first_heads_in,
    second_heads_in,
    first_heads_out,
    second_heads_out,
    first_bias_weight,
    second_bias_weight,
    first_outer_in,
    second_outer_in,
    first_outer_out,
    second_outer_out,
):
    row_count = lax.axis_size("row")
    head_count = lax.axis_size("head")
    head_index = lax.axis_index("head")
    devices = row_count * head_count
    rows_here, residues, width = alignment.shape
    pair_rows, pair_cols, pair_width = pairs.shape
    size = width // HEADS
    outer_width = outer_in.shape[2]
    all_rows = rows_here * row_count
    own = rows_here // head_count
    start = head_index * own
    scales = norm_scales[:, : 2 * width].reshape(2, 2, width).swapaxes(0, 1).reshape(4, width)
    pair_gain = norm_scales[0:1, 2 * width :]
    pair_shift = norm_scales[1:2, 2 * width :]
    residue_live = residue_mask.astype(F32)
    row_live = lax.dynamic_slice_in_dim(row_mask, start, own, 0).astype(F32)
    flat_live = jnp.repeat(residue_live.reshape(-1, QUADS), outer_in.shape[2], axis=1)
    row_live = jnp.broadcast_to(row_live[:, None, None], (own, 1, 128))
    bias_low = bias_weight.astype(BF16)

    fast = (row_count, head_count, pair_cols, own * outer_width) == (8, 4, 128, 128)

    local = heads_in.shape[2]
    outer_t = outer_in.astype(BF16).swapaxes(1, 2).reshape(2 * outer_width, width)
    if fast:
        bias, weights = pair_bias(
            pairs, norm_scales[:, 2 * width :], bias_low.T, heads_in.swapaxes(1, 2), heads_out
        )
    else:
        shard = jnp.concatenate([heads_in.astype(BF16).swapaxes(1, 2), heads_out.astype(BF16)[None]])
        weights = lax.all_gather(shard, "head", axis=1, tiled=True)
        bias = pair_forward(pairs, pair_gain, pair_shift, bias_low)
        bias = lax.all_gather(bias, "head", axis=2, tiled=True)
        bias = lax.all_gather(bias, "row", axis=1, tiled=True)[None, None]

    update, left, right, kept, early = attention_forward(
        alignment, scales, weights, outer_t, bias, residue_live[None], row_live, flat_live, fast
    )

    if fast:
        total, left_grad, right_grad, table_grad, hop_one, hop_two = outer_product(
            left, right, early, pairs_back, outer_out, update, all_rows
        )
        updates = [update, early[2], hop_one, hop_two]
    else:
        table = outer_out.astype(BF16).reshape(outer_width, outer_width, pair_width)
        updates = [update]
        for _ in range(head_count - 1):
            updates.append(hop(updates[-1]))
        left = left.reshape(own, residues, outer_width).swapaxes(1, 2)
        left = left.reshape(own, outer_width, row_count, pair_rows).transpose(2, 0, 1, 3)
        right = right.reshape(own, outer_width, head_count, pair_cols).transpose(2, 0, 1, 3)
        both = (row_count, head_count, own, outer_width)
        send = jnp.concatenate(
            [
                jnp.broadcast_to(left[:, None], both + (pair_rows,)),
                jnp.broadcast_to(right[None], both + (pair_cols,)),
            ],
            axis=4,
        )
        flat = (devices, own, outer_width, pair_rows + pair_cols)
        got = lax.all_to_all(send.reshape(flat), EVERY, split_axis=0, concat_axis=0, tiled=True)
        got = got.reshape(all_rows, outer_width, pair_rows + pair_cols)
        total, table_grad, left_grad, right_grad = outer_product_plain(
            got[:, :, :pair_rows], got[:, :, pair_rows:], pairs_back, table, all_rows
        )
        pairs_new = pairs + total
        send = jnp.concatenate([left_grad, right_grad], axis=2).reshape(flat)
        got = lax.all_to_all(send, EVERY, split_axis=0, concat_axis=0, tiled=True)
        got = got.reshape(both + (pair_rows + pair_cols,)).astype(F32)
        left_grad = jnp.sum(got[..., :pair_rows], axis=1).transpose(1, 0, 3, 2).astype(BF16)
        left_grad = left_grad.reshape(own, residues // QUADS, QUADS * outer_width)
        right_grad = jnp.sum(got[..., pair_rows:], axis=0).transpose(1, 2, 0, 3).astype(BF16)
        right_grad = right_grad.reshape(own, outer_width, residues)
        table_grad = table_grad.swapaxes(0, 1).reshape(outer_width * outer_width, pair_width)

    turns = (head_index + head_count - jnp.arange(head_count, dtype=jnp.int32)) % head_count
    order = (turns[:, None] * own + jnp.arange(own, dtype=jnp.int32)[None]).reshape(-1)
    half = own // 2

    def mine(first, hops, second, more):
        parts = [(first, step) for step in hops] + [(second, step) for step in more]
        return jnp.concatenate([order[step * own + n * half : step * own + (n + 1) * half] for n, step in parts])

    backward = functools.partial(
        attention_backward,
        order, alignment, update, alignment_back, scales, weights, outer_t, left_grad, right_grad,
        residue_live[None], row_live, flat_live, kept, bias.shape,
    )
    if fast:
        moved = [hop(hop_one), hop(hop_two)]
    part, bias_grad, *early = backward(first=0, own=half, pairs=[pairs, total] if fast else ())
    if fast:
        pairs_new = early.pop()
        moved, bias_grad, part, early = together(moved, bias_grad, part, early)
        updates += moved
        left_over = hop(moved[0])
    changes = [[part, hop(part)]]
    alignment_new, part, bias_grad, packed, norms = backward(
        first=half, own=half, earlier=bias_grad, early=early, table_grad=table_grad, pieces=updates
    )
    if fast:
        left_over, changes[0][1], bias_grad, part, packed, norms = together(
            left_over, changes[0][1], bias_grad, part, packed, norms
        )
        changes[0].append(hop(changes[0][1]))
        changes.append([part, hop(part)])
        bias_grad, packed = sum_gradients(bias_grad, packed)
        changes[0][2], changes[1][1], bias_grad = together(changes[0][2], changes[1][1], bias_grad)
        changes[0].append(hop(changes[0][2]))
        changes[1].append(hop(changes[1][1]))
        pairs_grad, pair_side, alignment_grad = pair_norm_backward(
            mine(0, (0, 1, 2), 1, (0, 1)),
            pairs,
            pairs_back,
            bias_grad,
            norm_scales[:, 2 * width :],
            bias_low.T,
            norms,
            alignment_back,
            changes[0][:3] + changes[1][:2],
        )
        pair_side = small_sum(pair_side)
        changes[0][3], changes[1][2], pair_side = together(changes[0][3], changes[1][2], pair_side)
        changes[1].append(hop(changes[1][2]))
    else:
        for _ in range(head_count - 2):
            changes[0].append(hop(changes[0][-1]))
        changes.append([part])
        for _ in range(head_count - 1):
            changes[1].append(hop(changes[1][-1]))
        bias_grad = lax.psum_scatter(bias_grad[0, 0], "row", scatter_dimension=1, tiled=True)
        bias_grad = lax.psum_scatter(bias_grad, "head", scatter_dimension=2, tiled=True)
        pairs_grad, bias_weight_grad, pair_gain_grad, pair_shift_grad = pair_backward(
            pairs, pairs_back, pair_gain, pair_shift, bias_low, bias_grad
        )
        packed, norms, bias_weight_total, pair_norms_total = lax.psum(
            (packed.astype(F32), norms, bias_weight_grad, jnp.stack([pair_gain_grad, pair_shift_grad])), EVERY
        )
    olds = (
        (norm_scales, first_norms, second_norms),
        (heads_in, first_heads_in, second_heads_in),
        (heads_out, first_heads_out, second_heads_out),
        (bias_weight, first_bias_weight, second_bias_weight),
        (outer_in, first_outer_in, second_outer_in),
        (outer_out, first_outer_out, second_outer_out),
    )
    rates = (
        0.5,
        width ** (-0.5),
        max(2 * HEADS * size // residues, 1) ** (-0.5),
        pair_width ** (-0.5),
        width ** (-0.5),
        max(outer_width * outer_width // all_rows, 1) ** (-0.5),
    )
    if fast:
        at = (head_index * local).astype(jnp.int32)[None]
        *news, alignment_grad = adam_all(
            jnp.concatenate([mine(0, (3,), 1, (2,)), at]),
            packed, pair_side, olds, rates, alignment_back, [changes[0][3], changes[1][2]], alignment_grad,
        )
        at = (turns[3] * 2 + 1)[None]
        alignment_new = add_rows(at, alignment, left_over, alignment_new)
        alignment_grad = add_rows(at, alignment_back, changes[1][3], alignment_grad)
        return (alignment_new, pairs_new, alignment_grad, pairs_grad, *news)
    alignment_grad = None
    for step in range(head_count):
        for n in range(2):
            at = (turns[step] * 2 + n)[None]
            alignment_grad = add_rows(at, alignment_back, changes[n][step], alignment_grad)
    def unpack(first, lines):
        return jnp.concatenate([packed[first : first + lines], packed[first + lines : first + 2 * lines]], axis=1)

    lines = 4 * width
    heads_in_total = lax.dynamic_slice_in_dim(
        unpack(0, lines).reshape(4, width, width), head_index * local, local, 1
    ).swapaxes(1, 2)
    heads_out_total = lax.dynamic_slice_in_dim(unpack(2 * lines, width), head_index * local, local, 0)
    lines = 2 * (lines + width)
    outer_in_total = unpack(lines, 2 * outer_width).reshape(2, outer_width, width).swapaxes(1, 2)
    lines += 4 * outer_width
    table_total = packed[lines : lines + outer_width * outer_width]
    table_total = table_total.reshape(outer_width, outer_width, pair_width).swapaxes(0, 1)
    table_total = table_total.reshape(outer_width * outer_width, pair_width)
    norms_total = jnp.concatenate(
        [norms.reshape(2, 2, width).swapaxes(0, 1).reshape(2, 2 * width), pair_norms_total], axis=1
    )
    totals = (norms_total, heads_in_total, heads_out_total, bias_weight_total, outer_in_total, table_total)
    news = []
    for (weight, moment_one, moment_two), total, rate in zip(olds, totals, rates):
        news += adam_update(weight, total, moment_one, moment_two, rate)
    return (alignment_new, pairs_new, alignment_grad, pairs_grad, *news)


def solution(mesh):
    row_msa = P("row", None, None)
    pair = P("row", "head", None)
    columns = P(None, None, "head")
    lines = P("head", None)
    in_specs = (
        (row_msa, pair, P(), P("row"), row_msa, pair, P(), columns, lines)
        + (P(),) * 5
        + (columns,) * 2
        + (lines,) * 2
        + (P(),) * 6
    )
    out_specs = (row_msa, pair, row_msa, pair) + (P(),) * 3 + (columns,) * 3 + (lines,) * 3 + (P(),) * 9
    return jax.shard_map(
        per_device, mesh=mesh, in_specs=in_specs, out_specs=out_specs, check_vma=False
    )
```

```python
import functools

import jax
import jax.numpy as jnp
from jax import lax
from jax.experimental import pallas as pl
from jax.experimental.pallas import tpu as pltpu
from jax.sharding import PartitionSpec as P

HEADS = 8
STEP = 10
F32 = jnp.float32
BF16 = jnp.bfloat16
LOG2E = 1.4426950408889634
VMEM = 56 << 20
EVERY = ("row", "head")


def adam_update(weight, gradient, moment_one, moment_two, step_rate):
    first_new = 0.9 * moment_one + 0.1 * gradient
    second_new = 0.999 * moment_two + 0.001 * gradient * gradient
    first_hat = first_new / (1.0 - 0.9**STEP)
    second_hat = second_new / (1.0 - 0.999**STEP)
    updated = weight - step_rate * (first_hat / (jnp.sqrt(second_hat) + 1e-08) + 0.01 * weight)
    return (first_new, second_new, updated)


def cost(micros):
    return pl.CostEstimate(flops=0, bytes_accessed=int(micros * 3.5e6), transcendentals=0)


def dot(a, b, along):
    return lax.dot_general(a, b, (((along[0],), (along[1],)), ((), ())), preferred_element_type=F32)


def normalize(values):
    center = values - jnp.mean(values, axis=-1, keepdims=True)
    rstd = lax.rsqrt(jnp.mean(center * center, axis=-1, keepdims=True) + 1e-05)
    return center * rstd, rstd


def norm_backward(hat, rstd, gain, grad):
    scaled = grad * gain
    return rstd * (
        scaled
        - jnp.mean(scaled, axis=-1, keepdims=True)
        - hat * jnp.mean(scaled * hat, axis=-1, keepdims=True)
    )


QUADS = 4


def quad(outer_t, q):
    weights = outer_t[: outer_t.shape[0] // 2]
    zero = jnp.zeros_like(weights)
    return jnp.concatenate([weights if n == q else zero for n in range(QUADS)], axis=0)


def put(ref, value):
    for n in range(ref.shape[0]):
        ref[n] = value[:, n * 128 : (n + 1) * 128]


def take(ref, q):
    at = pl.ds(q, ref.shape[1] // QUADS, stride=QUADS)
    return jnp.concatenate([ref[n, at, :] for n in range(ref.shape[0])], axis=1)


ROW_SENDS = 20


class Exchange:
    def __init__(
        self, left, right, left_stage, right_stage, left_plane, right_line, left_all, right_all,
        local_sem, send_sem, recv_sem,
    ):
        self.left, self.right, self.left_stage, self.right_stage = left, right, left_stage, right_stage
        self.left_plane, self.right_line, self.left_all, self.right_all = left_plane, right_line, left_all, right_all
        self.local_sem, self.send_sem, self.recv_sem = local_sem, send_sem, recv_sem
        self.row, self.head = place()
        self.beyond = [(self.head + k) % 4 for k in range(4)]
        self.behind = [(self.head + 4 - k) % 4 for k in range(4)]
        self.plane = [(flip(self.row, way), self.head) for way in range(8)]
        self.lines = left_plane.shape[2]
        self.cols = right_line.shape[3]

    def copy(self, n, source, target, device):
        return pltpu.make_async_remote_copy(
            src_ref=source,
            dst_ref=target,
            send_sem=self.send_sem.at[n],
            recv_sem=self.recv_sem.at[n],
            device_id=device,
            device_id_type=MESH,
        )

    def first(self):
        out = [
            self.copy(7 + k, self.right_stage.at[self.beyond[k + 1]], self.right_line.at[self.head],
                      (self.row, self.beyond[k + 1]))
            for k in range(3)
        ]
        out += [
            self.copy(n, self.left_stage.at[self.plane[way][0]], self.left_plane.at[self.row], self.plane[way])
            for n, way in enumerate((2, 4, 6, 3, 5, 7, 1))
        ]
        return out

    def second(self, which):
        if which == "left":
            return [
                self.copy(10 + k, self.left_plane, self.left_all.at[self.head], (self.row, self.beyond[k + 1]))
                for k in range(3)
            ]
        if which == "core":
            return [self.copy(16, self.right_line, self.right_all.at[self.row], self.plane[CORE])]
        return [
            self.copy(13 + n, self.right_line, self.right_all.at[self.row], self.plane[way])
            for n, way in enumerate((ACROSS, DOWN, CORNER))
        ]

    def third(self):
        out = []
        for n, way in enumerate((ACROSS, DOWN, CORNER)):
            block = self.right_all.at[self.plane[way][0]]
            out.append(self.copy(17 + n, block, block, self.plane[CORE]))
        return out

    def locals(self):
        return [
            pltpu.make_async_copy(self.left_plane, self.left_all.at[self.head], self.local_sem.at[0]),
            pltpu.make_async_copy(self.right_line, self.right_all.at[self.row], self.local_sem.at[1]),
        ]

    def begin(self):
        for r in range(8):
            self.left_stage[r] = self.left[:, r * self.lines : (r + 1) * self.lines, :]
        for h in range(4):
            self.right_stage[h] = self.right[:, :, h * self.cols : (h + 1) * self.cols]
        self.left_plane[self.row] = self.left_stage[self.row]
        self.right_line[self.head] = self.right_stage[self.head]
        for copy in self.first():
            copy.start()

    def go_on(self):
        for copy in self.first():
            copy.wait_recv()
        for copy in self.second("chips") + self.second("core") + self.second("left") + self.locals():
            copy.start()

    def core(self):
        for copy in self.second("chips"):
            copy.wait_recv()
        for copy in self.third():
            copy.start()

    def end(self):
        for copy in self.second("left") + self.second("core") + self.third():
            copy.wait()
        for copy in self.locals():
            copy.wait()
        for copy in self.first() + self.second("chips"):
            copy.wait_send()


def norm_rows(scales, width):
    return (
        scales[0:1, :width],
        scales[1:2, :width],
        scales[0:1, width : 2 * width],
        scales[1:2, width : 2 * width],
    )


def forward_kernel(*refs, share):
    (rows, scales, weights, outer_w, bias, residue, row_live, flat_live), refs = refs[:8], refs[8:]
    (update, left, right, qkv, gate, powers, inverse, mixed, attended), refs = refs[:9], refs[9:]
    if share:
        (left_all, right_all, hop_one), refs = refs[:3], refs[3:]
        left_stage, right_stage, left_plane, right_line, local_sem, send_sem, recv_sem, hop_sem = refs[-8:]
    bias_t, second, rows_in, load_sem = refs[:4]
    row = pl.program_id(0)
    own = update.shape[0]
    width = rows.shape[2]
    residues = rows.shape[1]
    size = width // HEADS
    half = outer_w.shape[0] // 2
    outer_t = outer_w[...].astype(BF16)
    gain_one, shift_one, gain_two, shift_two = norm_rows(scales, width)
    start = lax.axis_index("head") * own
    device_row, device_head = place()

    def load(n):
        return pltpu.make_async_copy(rows.at[start + n], rows_in.at[n % 2], load_sem.at[n % 2])

    def exchange():
        return Exchange(
            left.at[pl.ds(0, own - 1)], right.at[pl.ds(0, own - 1)], left_stage, right_stage,
            left_plane, right_line, left_all, right_all, local_sem, send_sem, recv_sem,
        )

    def hop_copy(n):
        return pltpu.make_async_remote_copy(
            src_ref=update.at[n],
            dst_ref=hop_one.at[n],
            send_sem=hop_sem.at[0, n],
            recv_sem=hop_sem.at[1, n],
            device_id=(device_row, (device_head + 1) % 4),
            device_id_type=MESH,
        )

    @pl.when(row == 0)
    def _():
        load(0).start()
        if own > 1:
            load(1).start()
        if share:
            greet(
                [(flip(device_row, way), device_head) for way in range(1, 8)]
                + [(device_row, (device_head + k) % 4) for k in (1, 2, 3)]
            )
        key_mask = (residue[...] - 1.0) * (1e9 * LOG2E)
        across, down, _, lines, cols = bias.shape
        group = max(1, 128 // lines)

        def turn(head, carry):
            for r in range(0, across, group):
                for c in range(down):
                    tile = jnp.concatenate([bias[r + g, c, head] for g in range(group)], axis=0)
                    bias_t[head, c * cols : (c + 1) * cols, r * lines : (r + group) * lines] = (
                        tile.astype(F32) + key_mask[:, c * cols : (c + 1) * cols]
                    ).T
            return carry

        lax.fori_loop(0, HEADS, turn, 0)

    load(row).wait()
    values_in = rows_in[row % 2]
    hat, _ = normalize(values_in)
    normed = (hat * gain_one + shift_one).astype(BF16)
    qkv[0, :width] = (dot(weights[0], normed, (1, 1)) * (size**-0.5 * LOG2E)).astype(BF16)
    qkv[0, width:] = dot(weights[1:3].reshape(2 * width, width), normed, (1, 1)).astype(BF16)
    gate[0] = jax.nn.sigmoid(dot(weights[3], normed, (1, 1)))
    for head in range(HEADS):
        at = head * size
        keys = qkv[0, width + at : width + at + size]
        values = qkv[0, 2 * width + at : 2 * width + at + size]
        query = qkv[0, at : at + size]
        scores = dot(keys, query, (0, 0)) + bias_t[head]
        exps = jnp.exp2(scores - jnp.max(scores, axis=0, keepdims=True))
        over = 1.0 / jnp.sum(exps, axis=0, keepdims=True)
        low = exps.astype(BF16)
        powers[0, head] = low
        inverse[0, head] = over
        mixed[0, at : at + size] = dot(values, low, (1, 0)) * over
        if share and head == HEADS // 2 - 1:
            @pl.when(row == own - 1)
            def _():
                exchange().go_on()
    att = (gate[0] * mixed[0]).astype(BF16)
    attended[0] = att
    change = dot(att, weights[4], (0, 0)).astype(BF16)
    update[row] = change
    hat, _ = normalize(rows_in[row % 2] + change.astype(F32))
    normed = hat * gain_two + shift_two
    put(second, normed)
    right[row] = (dot(outer_t[half:], normed.astype(BF16), (1, 1)) * (residue[...] * row_live[0][:, :1])).astype(BF16)
    out = jnp.zeros(flat_live.shape, F32)
    for q in range(QUADS):
        out += dot(take(second, q).astype(BF16), quad(outer_t, q), (1, 1))
    left[row] = (out * flat_live[...] * row_live[0]).astype(BF16)

    @pl.when(row + 2 < own)
    def _():
        load(row + 2).start()

    if share:
        @pl.when(row == own - 2)
        def _():
            exchange().begin()

        @pl.when(row < own // 2)
        def _():
            hop_copy(row).start()

        @pl.when(row == own - 1)
        def _():
            exchange().core()
            for n in range(own // 2):
                hop_copy(n).wait()
            exchange().end()


def attention_forward(rows, scales, weights, outer_t, bias, residue, row_live, flat_live, share):
    _, residues, width = rows.shape
    own = row_live.shape[0]
    sides = outer_t.shape[0] // 2
    by_row = lambda s: (s, 0, 0)
    by_row_four = lambda s: (s, 0, 0, 0)
    hbm = pl.BlockSpec(memory_space=pl.ANY)
    once = lambda array: pl.BlockSpec(array.shape, lambda s: (0,) * array.ndim, pipeline_mode=pl.Buffered(1))
    whole = lambda *shape: pl.BlockSpec(shape, lambda s: (0,) * len(shape))
    lines, cols = flat_live.shape[0] // 8, residues // 4
    early = own - 1
    out_specs = [
        whole(own, residues, width),
        whole(own, *flat_live.shape),
        whole(own, sides, residues),
        pl.BlockSpec((1, 3 * width, residues), by_row),
        pl.BlockSpec((1, width, residues), by_row),
        pl.BlockSpec((1, HEADS, residues, residues), by_row_four),
        pl.BlockSpec((1, HEADS, 1, residues), by_row_four),
        pl.BlockSpec((1, width, residues), by_row),
        pl.BlockSpec((1, width, residues), by_row),
    ]
    out_shape = [
        jax.ShapeDtypeStruct((own, residues, width), BF16),
        jax.ShapeDtypeStruct((own,) + flat_live.shape, BF16),
        jax.ShapeDtypeStruct((own, sides, residues), BF16),
        jax.ShapeDtypeStruct((own, 3 * width, residues), BF16),
        jax.ShapeDtypeStruct((own, width, residues), F32),
        jax.ShapeDtypeStruct((own, HEADS, residues, residues), BF16),
        jax.ShapeDtypeStruct((own, HEADS, 1, residues), F32),
        jax.ShapeDtypeStruct((own, width, residues), F32),
        jax.ShapeDtypeStruct((own, width, residues), BF16),
    ]
    scratch = [
        pltpu.VMEM((HEADS, residues, residues), F32),
        pltpu.VMEM((width // 128, residues, 128), F32),
        pltpu.VMEM((2, residues, width), F32),
        pltpu.SemaphoreType.DMA((2,)),
    ]
    params = dict(vmem_limit_bytes=VMEM)
    if share:
        params.update(collective_id=2, has_side_effects=True)
        out_specs += [hbm] * 3
        out_shape += [
            jax.ShapeDtypeStruct((4, 8, early, lines, 128), BF16),
            jax.ShapeDtypeStruct((8, 4, early, sides, cols), BF16),
            jax.ShapeDtypeStruct((own // 2, residues, width), BF16),
        ]
        scratch += [
            pltpu.VMEM((8, early, lines, 128), BF16),
            pltpu.VMEM((4, early, sides, cols), BF16),
            pltpu.VMEM((8, early, lines, 128), BF16),
            pltpu.VMEM((4, early, sides, cols), BF16),
            pltpu.SemaphoreType.DMA((2,)),
            pltpu.SemaphoreType.DMA((ROW_SENDS,)),
            pltpu.SemaphoreType.DMA((ROW_SENDS,)),
            pltpu.SemaphoreType.DMA((2, own // 2)),
        ]
    out = pl.pallas_call(
        functools.partial(forward_kernel, share=share),
        grid=(own,),
        in_specs=[
            hbm,
            once(scales),
            once(weights),
            once(outer_t),
            once(bias),
            once(residue),
            pl.BlockSpec((1, 1, 128), by_row),
            once(flat_live),
        ],
        out_specs=out_specs,
        scratch_shapes=scratch,
        out_shape=out_shape,
        cost_estimate=cost(30),
        compiler_params=pltpu.CompilerParams(**params),
    )(rows, scales, weights, outer_t, bias, residue, row_live, flat_live)
    return out[0], out[1], out[2], tuple(out[3:9]), tuple(out[9:])


def backward_kernel(*refs, earlier, adds):
    (order, rows, update, back, scales, weights, outer_w, left_grad, right_grad, residue, row_live, flat_live,
     qkv, gate, powers, inverse, mixed, attended), refs = refs[:18], refs[18:]
    if earlier:
        so_far, early, table_grad, base = refs[0], refs[1:5], refs[5], refs[6]
        pieces, refs = refs[7 : 7 + adds], refs[7 + adds :]
        added, part, bias_grad, packed, norms = refs[:5]
        bias_low, base_in, piece_in, load_sem, piece_sem, store_sem = refs[-6:]
        heads_in_grad, heads_out_grad, outer_in_grad = refs[-9:-6]
        refs = refs[5:-9]
    else:
        if adds:
            pairs, total, pairs_new = refs[0], refs[1], refs[8]
            pairs_new[...] = pairs[...] + total[...].astype(F32)
            refs = refs[2:8] + refs[9:]
        part, bias_grad, heads_in_grad, heads_out_grad, outer_in_grad, norms = refs[:6]
        refs = refs[6:]
    bias_total, mixed_grad, proj_grad, spread, bias_sem = refs
    row = pl.program_id(0)
    own = pl.num_programs(0)
    width = rows.shape[2]
    residues = rows.shape[1]
    size = width // HEADS
    last_row = row == own - 1
    rows_here = base.shape[0] if earlier else 0
    if earlier:
        per, each = base_in.shape[1:3]
        bounds = [0]
        for piece in pieces:
            bounds.append(bounds[-1] + piece.shape[0] // each)
        steps = bounds[-1]

        def bias_load(head):
            return pltpu.make_async_copy(so_far.at[head], bias_total.at[head], bias_sem.at[head])

        def row_of(step):
            return pl.ds(order[step * each], each)

        def fetch(batch, slot):
            for n in range(per):
                step = batch * per + n
                for piece in range(adds):
                    low, high = bounds[piece], bounds[piece + 1]

                    @pl.when((step >= low) & (step < high))
                    def _():
                        pltpu.make_async_copy(base.at[row_of(step)], base_in.at[slot, n], load_sem.at[slot, n]).start()
                        source = pieces[piece].at[pl.ds((step - low) * each, each)]
                        pltpu.make_async_copy(source, piece_in.at[slot, n], piece_sem.at[slot, n]).start()

        def store(batch, slot, n):
            return pltpu.make_async_copy(base_in.at[slot, n], added.at[row_of(batch * per + n)], store_sem.at[slot, n])

        def add_batch(batch, slot):
            for n in range(per):
                step = batch * per + n

                @pl.when((batch >= 1) & (step - per < steps))
                def _():
                    store(batch - 1, 1 - slot, n).wait()
            fetch(batch + 1, 1 - slot)
            for n in range(per):
                step = batch * per + n

                @pl.when(step < steps)
                def _():
                    pltpu.make_async_copy(base.at[row_of(step)], base_in.at[slot, n], load_sem.at[slot, n]).wait()
                    source = pieces[0].at[pl.ds(0, each)]
                    pltpu.make_async_copy(source, piece_in.at[slot, n], piece_sem.at[slot, n]).wait()
                    base_in[slot, n] = base_in[slot, n] + piece_in[slot, n].astype(F32)
                    store(batch, slot, n).start()

    @pl.when(row == 0)
    def _():
        for n, ref in enumerate((heads_in_grad, heads_out_grad, outer_in_grad, norms)):
            ref[...] = early[n][...] if earlier else jnp.zeros_like(ref)
        if earlier:
            for head in range(HEADS):
                bias_load(head).start()
            fetch(0, 0)

    half = outer_w.shape[0] // 2
    outer_t = outer_w[...].astype(BF16)
    gain_one, shift_one, gain_two, shift_two = norm_rows(scales, width)
    count = residues // QUADS
    hat, rstd = normalize(rows[0] + update[0].astype(F32))
    second = hat * gain_two + shift_two
    put(spread, second)
    grads = (right_grad[0].astype(F32) * (residue[...] * row_live[0][:, :1])).astype(BF16)
    outer_in_grad[half:] += dot(grads, second.astype(BF16), (1, 0))
    flat = (left_grad[0].astype(F32) * flat_live[...] * row_live[0]).astype(BF16).T
    for q in range(QUADS):
        mine = flat[q * half : (q + 1) * half]
        outer_in_grad[:half] += dot(mine, take(spread, q).astype(BF16), (1, 0))
        back_to = dot(mine, outer_t[:half], (0, 0))
        for n in range(spread.shape[0]):
            spread[n, pl.ds(q, count, stride=QUADS), :] = back_to[:, n * 128 : (n + 1) * 128]
    spread_grad = jnp.concatenate([spread[n] for n in range(spread.shape[0])], axis=1)
    second_grad = spread_grad + dot(grads, outer_t[half:], (0, 0))
    norms[2:3] += jnp.sum(second_grad * hat, axis=0, keepdims=True)
    norms[3:4] += jnp.sum(second_grad, axis=0, keepdims=True)
    new_part = norm_backward(hat, rstd, gain_two, second_grad)
    put(spread, new_part)
    out_grad = (back[0] + new_part).astype(BF16)
    heads_out_grad[...] += dot(attended[0], out_grad, (1, 0))
    attended_grad = dot(weights[4], out_grad, (1, 1))
    sig = gate[0]
    gated = attended_grad * sig
    proj_grad[3 * width :] = (gated * mixed[0] * (1.0 - sig)).astype(BF16)
    deltas = []
    for head in range(HEADS):
        span = slice(head * size, (head + 1) * size)
        grad = gated[span] * inverse[0, head]
        mixed_grad[span] = grad.astype(BF16)
        deltas.append(jnp.sum(grad * mixed[0, span], axis=0, keepdims=True))

    if earlier:
        @pl.when(row == 0)
        def _():
            for head in range(HEADS):
                bias_load(head).wait()

    for head in range(HEADS):
        at = head * size
        query = qkv[0, at : at + size]
        keys = qkv[0, width + at : width + at + size]
        values = qkv[0, 2 * width + at : 2 * width + at + size]
        grad = mixed_grad[at : at + size]
        low = powers[0, head]
        prob_grad = dot(values, grad, (0, 0))
        score_grad = low.astype(F32) * (prob_grad - deltas[head])
        if earlier:
            bias_total[head] += score_grad
        else:
            bias_total[head] = jnp.where(row == 0, 0.0, bias_total[head]) + score_grad
        score_low = score_grad.astype(BF16)
        proj_grad[2 * width + at : 2 * width + at + size] = dot(grad, low, (1, 1)).astype(BF16)
        proj_grad[width + at : width + at + size] = (dot(query, score_low, (1, 1)) / LOG2E).astype(BF16)
        proj_grad[at : at + size] = (dot(keys, score_low, (1, 0)) * size**-0.5).astype(BF16)
        if earlier and (head + 1) % per == 0:
            add_batch(row * (HEADS // per) + head // per, head // per % 2)
        if not earlier:
            @pl.when(last_row)
            def _():
                pltpu.make_async_copy(bias_total.at[head], bias_grad.at[head], bias_sem.at[head]).start()

    if earlier:
        @pl.when(last_row)
        def _():
            across, down, _, lines, cols = bias_grad.shape
            group = max(1, 128 // lines)
            for head in range(HEADS):
                for r in range(0, across, group):
                    for c in range(down):
                        tile = bias_total[head, c * cols : (c + 1) * cols, r * lines : (r + group) * lines]
                        tile = tile.T.astype(BF16)
                        for g in range(group):
                            bias_low[head, r + g, c] = tile[g * lines : (g + 1) * lines]
                pltpu.make_async_copy(bias_low.at[head], bias_grad.at[:, :, head], bias_sem.at[head]).start()

    hat, rstd = normalize(rows[0])
    normed = (hat * gain_one + shift_one).astype(BF16)
    grads = proj_grad[...]
    heads_in_grad[...] += dot(grads, normed, (1, 0))
    normed_grad = dot(grads, weights[:4].reshape(4 * width, width), (0, 0))
    norms[0:1] += jnp.sum(normed_grad * hat, axis=0, keepdims=True)
    norms[1:2] += jnp.sum(normed_grad, axis=0, keepdims=True)
    new_part = jnp.concatenate([spread[n] for n in range(spread.shape[0])], axis=1)
    part[0] = (new_part + norm_backward(hat, rstd, gain_one, normed_grad)).astype(BF16)

    @pl.when(last_row)
    def _():
        if earlier:
            first = 0
            for ref in (heads_in_grad, heads_out_grad, outer_in_grad):
                lines = ref.shape[0]
                packed[first : first + lines] = ref[:, :128].astype(BF16)
                packed[first + lines : first + 2 * lines] = ref[:, 128:].astype(BF16)
                first += 2 * lines
            lines = table_grad.shape[0]
            packed[first : first + lines] = table_grad[...].astype(BF16)
            first += lines
            packed[first:] = jnp.zeros((packed.shape[0] - first, 128), BF16)
            batch = rows_here // each // per - 1
            for n in range(per):
                if batch * per + n < steps:
                    store(batch, batch % 2, n).wait()
            for head in range(HEADS):
                pltpu.make_async_copy(bias_low.at[head], bias_grad.at[:, :, head], bias_sem.at[head]).wait()
        else:
            for head in range(HEADS):
                pltpu.make_async_copy(bias_total.at[head], bias_grad.at[head], bias_sem.at[head]).wait()


def attention_backward(
    order, rows, update, back, scales, weights, outer_t, left_grad, right_grad, residue, row_live, flat_live,
    kept, blocks, first, own, earlier=None, early=(), table_grad=None, pieces=(), pairs=(),
):
    _, residues, width = rows.shape
    qkv, gate, powers, inverse, mixed, attended = kept
    here = lambda s, order: (order[0] + first + s, 0, 0)
    by_row = lambda s, order: (first + s, 0, 0)
    by_row_four = lambda s, order: (first + s, 0, 0, 0)
    hbm = pl.BlockSpec(memory_space=pl.ANY)
    once = lambda array: pl.BlockSpec(
        array.shape, lambda s, order: (0,) * array.ndim, pipeline_mode=pl.Buffered(1)
    )
    whole = lambda array: pl.BlockSpec(array.shape, lambda s, order: (0,) * array.ndim)
    one = pl.BlockSpec((1, residues, width), here)
    args = [rows, update, back, scales, weights, outer_t, left_grad, right_grad, residue, row_live, flat_live]
    args += [qkv, gate, powers, inverse, mixed, attended]
    in_specs = [
        one,
        pl.BlockSpec((1, residues, width), by_row),
        one,
        once(scales),
        once(weights),
        once(outer_t),
        pl.BlockSpec((1,) + left_grad.shape[1:], by_row),
        pl.BlockSpec((1,) + right_grad.shape[1:], by_row),
        once(residue),
        pl.BlockSpec((1, 1, 128), by_row),
        once(flat_live),
        pl.BlockSpec((1, 3 * width, residues), by_row),
        pl.BlockSpec((1, width, residues), by_row),
        pl.BlockSpec((1, HEADS, residues, residues), by_row_four),
        pl.BlockSpec((1, HEADS, 1, residues), by_row_four),
        pl.BlockSpec((1, width, residues), by_row),
        pl.BlockSpec((1, width, residues), by_row),
    ]
    part = jax.ShapeDtypeStruct((own, residues, width), BF16)
    part_spec = pl.BlockSpec((1, residues, width), lambda s, order: (s, 0, 0))
    grads = [jax.ShapeDtypeStruct(shape, F32) for shape in ((4 * width, width), (width, width), outer_t.shape)]
    norms = jax.ShapeDtypeStruct((4, width), F32)
    scratch = [
        pltpu.VMEM((HEADS, residues, residues), F32),
        pltpu.VMEM((width, residues), BF16),
        pltpu.VMEM((4 * width, residues), BF16),
        pltpu.VMEM((width // 128, residues, 128), F32),
        pltpu.SemaphoreType.DMA((HEADS,)),
    ]
    if earlier is None:
        out_shape = [part, jax.ShapeDtypeStruct((HEADS, residues, residues), F32)] + grads + [norms]
        out_specs = [part_spec, hbm] + [whole(array) for array in grads + [norms]]
        if pairs:
            slab = pl.BlockSpec((pairs[0].shape[0] // own,) + pairs[0].shape[1:], lambda s, order: (s, 0, 0))
            args += pairs
            in_specs += [slab, slab]
            out_specs.append(slab)
            out_shape.append(jax.ShapeDtypeStruct(pairs[0].shape, F32))
    else:
        each = max(1, rows.shape[0] // (own * HEADS))
        args += [earlier, *early, table_grad, rows] + list(pieces)
        in_specs += [hbm] + [once(array) for array in [*early, table_grad]] + [hbm] * (1 + len(pieces))
        count = 2 * sum(array.shape[0] for array in grads) + table_grad.shape[0]
        count += -count % 512
        packed = jax.ShapeDtypeStruct((count, 128), BF16)
        out_shape = [jax.ShapeDtypeStruct(rows.shape, F32), part, jax.ShapeDtypeStruct(blocks, BF16), packed, norms]
        out_specs = [hbm, part_spec, hbm, whole(packed), whole(norms)]
        scratch += [pltpu.VMEM(array.shape, F32) for array in grads] + [
            pltpu.VMEM((HEADS,) + blocks[:2] + blocks[3:], BF16),
            pltpu.VMEM((2, HEADS // 2, each, residues, width), F32),
            pltpu.VMEM((2, HEADS // 2, each, residues, width), BF16),
            pltpu.SemaphoreType.DMA((2, HEADS // 2)),
            pltpu.SemaphoreType.DMA((2, HEADS // 2)),
            pltpu.SemaphoreType.DMA((2, HEADS // 2)),
        ]
    return pl.pallas_call(
        functools.partial(backward_kernel, earlier=earlier is not None, adds=len(pieces) + len(pairs)),
        grid_spec=pltpu.PrefetchScalarGridSpec(
            num_scalar_prefetch=1, grid=(own,), in_specs=in_specs, out_specs=out_specs, scratch_shapes=scratch
        ),
        out_shape=out_shape,
        compiler_params=pltpu.CompilerParams(vmem_limit_bytes=VMEM),
        cost_estimate=cost(20),
    )(order, *args)


def outer_product_plain(left, right, pairs_back, table, all_rows):
    low = pairs_back.astype(BF16)
    product = mm("sei,sfj->eifj", left, right).astype(BF16)
    total = mm("eifj,efz->ijz", product, table) / all_rows
    table_grad = mm("eifj,ijz->efz", product, low) / all_rows
    back = mm("ijz,efz->eifj", low, table).astype(BF16)
    left_grad = mm("eifj,sfj->sei", back, right) / all_rows
    right_grad = mm("eifj,sei->sfj", back, left) / all_rows
    return total, table_grad, left_grad.astype(BF16), right_grad.astype(BF16)


def mm(spec, a, b):
    return jnp.einsum(spec, a, b, preferred_element_type=F32)


def pair_forward(pairs, gain, shift, bias_low):
    hat, _ = normalize(pairs)
    low = (hat * gain + shift).astype(BF16)
    return (mm("ijc,ch->hij", low, bias_low) * LOG2E).astype(BF16)


def pair_backward(pairs, pairs_back, gain, shift, bias_low, bias_grad):
    hat, rstd = normalize(pairs)
    low = (hat * gain + shift).astype(BF16)
    weight_grad = mm("ijc,hij->ch", low, bias_grad)
    in_grad = mm("hij,ch->ijc", bias_grad, bias_low)
    gain_grad = jnp.sum(in_grad * hat, axis=(0, 1))
    shift_grad = jnp.sum(in_grad, axis=(0, 1))
    return pairs_back + norm_backward(hat, rstd, gain, in_grad), weight_grad, gain_grad, shift_grad


MESH = pl.DeviceIdType.MESH
CORE, ACROSS, DOWN, CORNER = 1, 2, 4, 6


def place():
    return lax.axis_index("row"), lax.axis_index("head")


def flip(row, way):
    out = row
    for bit in (1, 2, 4):
        if way & bit:
            out = out + bit - 2 * bit * ((row // bit) % 2)
    return out


def greet(devices):
    barrier = pltpu.get_barrier_semaphore()
    for device in devices:
        pl.semaphore_signal(barrier, inc=1, device_id=device, device_id_type=MESH)
    pl.semaphore_wait(barrier, len(devices))


class Sends:
    def __init__(self, send_sem, recv_sem):
        self.send_sem, self.recv_sem, self.count, self.open = send_sem, recv_sem, 0, []

    def start(self, source, target, device):
        copy = pltpu.make_async_remote_copy(
            src_ref=source,
            dst_ref=target,
            send_sem=self.send_sem.at[self.count],
            recv_sem=self.recv_sem.at[self.count],
            device_id=device,
            device_id_type=MESH,
        )
        copy.start()
        self.count += 1
        self.open.append(copy)
        return copy

    def finish(self):
        for copy in self.open:
            copy.wait_send()


PARTS = 2
GATHER_SENDS = 6 + PARTS * (3 + 12 + 16)


def pair_bias_kernel(
    pairs, norm, weight, heads_in, heads_out, bias, weights, values_in, shard, block, low,
    load_sem, local_sem, send_sem, recv_sem,
):
    row, head = place()
    rows, cols, channels = pairs.shape
    part = shard.shape[1] // 2
    core = row % 2
    lines = rows // PARTS
    loads = []
    for n in range(PARTS):
        at = pl.ds(n * lines, lines)
        loads.append(pltpu.make_async_copy(pairs.at[at], values_in.at[at], load_sem.at[n]))
        loads[n].start()
    shard[:4] = heads_in[...].astype(BF16)
    shard[4] = heads_out[...].astype(BF16)
    beyond = [(head + k) % 4 for k in range(4)]
    behind = [(head + 4 - k) % 4 for k in range(4)]
    across, down, other = (flip(row, ACROSS), head), (flip(row, DOWN), head), (flip(row, CORE), head)
    greet([across, down, other] + [(row, beyond[k]) for k in (1, 2, 3)])
    sends = Sends(send_sem, recv_sem)

    def own_part(at, side):
        return weights.at[:, pl.ds(pl.multiple_of(at * 2 * part + side * part, part), part), :]

    keep = pltpu.make_async_copy(
        shard, weights.at[:, pl.ds(pl.multiple_of(head * 2 * part, 2 * part), 2 * part), :], local_sem.at[PARTS]
    )
    keep.start()
    step = 8
    first_pair = norm.shape[1] - channels
    gain, shift = norm[0:1, first_pair:], norm[1:2, first_pair:]
    low_weight = weight[...].astype(BF16)

    def norm_block(n, carry):
        first = pl.multiple_of(n * step, step)
        values = values_in[pl.ds(first, step)].reshape(step * cols, channels)
        center = values - jnp.mean(values, axis=-1, keepdims=True)
        rstd = lax.rsqrt(jnp.mean(center * center, axis=-1, keepdims=True) + 1e-05)
        normed = (center * rstd * gain + shift).astype(BF16)
        out = lax.dot_general(low_weight, normed, (((1,), (1,)), ((), ())), preferred_element_type=F32)
        for i in range(step):
            block[:, pl.ds(first + i, 1), :] = (out[:, i * cols : (i + 1) * cols] * LOG2E).reshape(
                HEADS, 1, cols
            )
        return carry

    ends, mine = [], []

    class Part:
        def __init__(self, n):
            self.at = pl.ds(n * lines, lines)
            loads[n].wait()
            lax.fori_loop(n * lines // step, (n + 1) * lines // step, norm_block, 0)
            low[n] = block[:, n * lines : (n + 1) * lines].astype(BF16)
            self.own = low.at[n]
            copy = pltpu.make_async_copy(self.own, self.slot(row, 0), local_sem.at[n])
            copy.start()
            mine.append(copy)
            self.along = [None] + [
                sends.start(self.own, self.slot(row, 0), (row, beyond[k])) for k in (1, 2, 3)
            ]
            self.across, self.down, self.corner = [None] * 4, [None] * 4, [None] * 4
            self.spread(0)

        def slot(self, at, k):
            return bias.at[at, behind[k], :, self.at]

        def spread(self, k):
            if k:
                self.along[k].wait_recv()
            here = self.slot(row, k)
            source = here if k else self.own
            self.across[k] = sends.start(source, here, across)
            self.down[k] = sends.start(source, here, down)
            ends.append(sends.start(source, here, other))

        def relay(self, k):
            self.across[k].wait_recv()
            here = self.slot(flip(row, ACROSS), k)
            if k < 2:
                self.corner[k] = sends.start(here, here, down)
            ends.append(sends.start(here, here, other))
            self.down[k].wait_recv()
            here = self.slot(flip(row, DOWN), k)
            if k >= 2:
                self.corner[k] = sends.start(here, here, across)
            ends.append(sends.start(here, here, other))

        def finish(self, k):
            self.corner[k].wait_recv()
            here = self.slot(flip(row, CORNER), k)
            ends.append(sends.start(here, here, other))

    parts = [Part(n) for n in range(PARTS)]
    half = shard.at[:, pl.ds(pl.multiple_of(core * part, part), part), :]
    shards = [None] + [sends.start(half, own_part(head, core), (row, beyond[k])) for k in (1, 2, 3)]
    for k in range(4):
        for one in parts:
            if k:
                one.spread(k)
                one.relay(k - 1)
    for one in parts:
        one.relay(3)
    for k in range(4):
        for one in parts:
            one.finish(k)
    for k in (1, 2, 3):
        shards[k].wait_recv()
        piece = own_part(behind[k], core)
        ends.append(sends.start(piece, piece, other))
    for copy in ends:
        copy.wait_recv()
    sends.finish()
    keep.wait()
    for copy in mine:
        copy.wait()


def pair_bias(pairs, norm, weight, heads_in, heads_out):
    rows, cols, channels = pairs.shape
    vmem = pl.BlockSpec(memory_space=pltpu.VMEM)
    hbm = pl.BlockSpec(memory_space=pl.ANY)
    shard = (heads_in.shape[0] + 1,) + heads_out.shape
    return pl.pallas_call(
        pair_bias_kernel,
        out_shape=[
            jax.ShapeDtypeStruct((8, 4, HEADS, rows, cols), BF16),
            jax.ShapeDtypeStruct((shard[0], 4 * shard[1], shard[2]), BF16),
        ],
        in_specs=[hbm, vmem, vmem, vmem, vmem],
        out_specs=[hbm, hbm],
        scratch_shapes=[
            pltpu.VMEM(pairs.shape, F32),
            pltpu.VMEM(shard, BF16),
            pltpu.VMEM((HEADS, rows, cols), F32),
            pltpu.VMEM((PARTS, HEADS, rows // PARTS, cols), BF16),
            pltpu.SemaphoreType.DMA((PARTS,)),
            pltpu.SemaphoreType.DMA((PARTS + 1,)),
            pltpu.SemaphoreType.DMA((GATHER_SENDS,)),
            pltpu.SemaphoreType.DMA((GATHER_SENDS,)),
        ],
        compiler_params=pltpu.CompilerParams(
            collective_id=0, has_side_effects=True, vmem_limit_bytes=VMEM
        ),
        cost_estimate=cost(34),
    )(pairs, norm, weight, heads_in, heads_out)


OUTER_SENDS = 2 + 3 + 7 + 1 + 3 + 3


def outer_kernel(
    left, right, left_early, right_early, pairs_back, outer_out, update, hop_early,
    total, left_out, right_out, table_grad, hop_one, hop_two,
    left_stage, right_stage, left_plane, right_line, left_all, right_all, left_last, right_last, left_wide, right_wide, left_rows, right_rows,
    backed, product, back, low, table, table_t, total_low,
    left_part, right_part, left_send, right_send, right_core, chip_sum, right_in, right_sum, left_line, left_sum, left_land, right_land,
    load_sem, local_sem, out_sem, row_local, row_send, row_recv, send_sem, recv_sem,
    *, scale, block, group,
):
    row, head = place()
    beyond = [(head + k) % 4 for k in range(4)]
    plane = [(flip(row, way), head) for way in range(8)]
    core, chip = row % 2, row // 2
    own, wide, _ = right.shape
    rows, cols, channels = back.shape
    size = wide
    lines = left_all.shape[3]
    chunks = rows // block
    half, most = own // 2, own - 1
    greet(plane[1:] + [(row, beyond[k]) for k in (1, 2, 3)])
    sends = Sends(send_sem, recv_sem)
    sides = Exchange(
        left.at[pl.ds(most, own - most)], right.at[pl.ds(most, own - most)], left_stage, right_stage,
        left_plane, right_line, left_last, right_last, row_local, row_send, row_recv,
    )
    sides.begin()
    gather = [
        pltpu.make_async_copy(left_early, left_all, local_sem.at[0]),
        pltpu.make_async_copy(right_early, right_all, local_sem.at[1]),
    ]
    loads = []
    for n in range(chunks):
        copy = pltpu.make_async_copy(
            pairs_back.at[pl.ds(n * block, block)], back.at[pl.ds(n * block, block)], load_sem.at[n]
        )
        copy.start()
        loads.append(copy)
    for copy in gather:
        copy.start()

    for f in range(wide):
        table[f * size : (f + 1) * size] = outer_out[pl.ds(f, size, stride=wide), :].astype(BF16)
    for n in range(wide * size // 128):
        table_t[:, n * 128 : (n + 1) * 128] = table[n * 128 : (n + 1) * 128].T

    def spread_pair(p, carry):
        first = p * group
        both = back[pl.ds(first, group)].astype(BF16)
        low[pl.ds(first, group)] = both
        spread = dot(table[...], both.reshape(group * cols, channels), (1, 1)).astype(BF16)
        for g in range(group):
            at = pl.ds(pl.multiple_of((first + g) * size, size), size)
            for f in range(wide):
                backed[at, f * cols : (f + 1) * cols] = spread[
                    f * size : (f + 1) * size, g * cols : (g + 1) * cols
                ]
        return carry

    pairs_of = rows // group

    def spread_part(k):
        for n in range(k * chunks // 4, (k + 1) * chunks // 4):
            loads[n].wait()
        lax.fori_loop(k * pairs_of // 4, (k + 1) * pairs_of // 4, spread_pair, 0)

    spread_part(0)
    sides.go_on()
    hops = [
        sends.start(update.at[pl.ds(half, own - half)], hop_one, (row, beyond[1])),
        sends.start(hop_early, hop_two, (row, beyond[1])),
    ]
    spread_part(1)
    spread_part(2)
    sides.core()
    spread_part(3)
    sides.end()
    for copy in gather:
        copy.wait()

    count = 32
    for r in range(8):
        for h in range(4):
            left_wide[r * 4 + h, :most] = left_all[h, r].astype(F32)
            left_wide[r * 4 + h, most:] = left_last[h, r].astype(F32)
    right_wide[:, :most] = right_all[...].astype(F32).reshape((count, most) + right_wide.shape[2:])
    right_wide[:, most:] = right_last[...].astype(F32).reshape((count, own - most) + right_wide.shape[2:])
    for s in range(own):
        at = slice(s * count, (s + 1) * count)
        for n in range(lines):
            left_rows[at, n * 128 : (n + 1) * 128] = left_wide[:, s, n, :].astype(BF16)
        for f in range(wide):
            right_rows[at, f * cols : (f + 1) * cols] = right_wide[:, s, f, :].astype(BF16)

    deep = block * size

    def left_step(n, carry):
        at = pl.ds(pl.multiple_of(n * deep, deep), deep)
        left_part[:, at] = dot(right_rows[...], backed[at, :], (1, 1)) * scale
        return carry

    lax.fori_loop(0, chunks, left_step, 0)
    for s in range(own):
        at = slice(s * count, (s + 1) * count)
        for n in range(lines):
            left_wide[:, s, n, :] = left_part[at, n * 128 : (n + 1) * 128]
    for r in range(8):
        for h in range(4):
            left_send[h, r] = left_wide[r * 4 + h].astype(BF16)
    lefts = [
        sends.start(left_send.at[beyond[k]], left_line.at[k - 1], (row, beyond[k])) for k in (2, 1, 3)
    ]
    step = 4 * cols

    def right_step(n, carry):
        at = pl.ds(pl.multiple_of(n * step, step), step)
        right_part[:, at] = dot(left_rows[...], backed[:, at], (1, 0)) * scale
        return carry

    lax.fori_loop(0, wide * cols // step, right_step, 0)
    for s in range(own):
        at = slice(s * count, (s + 1) * count)
        for f in range(wide):
            right_wide[:, s, f, :] = right_part[at, f * cols : (f + 1) * cols]
    right_send[...] = right_wide[...].astype(BF16).reshape(right_send.shape)
    swap = sends.start(right_send.at[:, 1 - core], right_core, plane[CORE])
    table_grad[...] = jnp.zeros_like(table_grad)

    def outer_chunk(n, carry):
        at = pl.ds(pl.multiple_of(n * deep, deep), deep)
        product[...] = dot(left_rows[:, at], right_rows[...], (0, 0)).astype(BF16)
        for first in range(0, block, group):
            both = jnp.concatenate(
                [
                    jnp.concatenate(
                        [
                            product[(first + g) * size : (first + g + 1) * size, f * cols : (f + 1) * cols]
                            for f in range(wide)
                        ],
                        axis=0,
                    )
                    for g in range(group)
                ],
                axis=1,
            )
            out = dot(table_t[...], both, (1, 0)) * scale
            for g in range(group):
                total_low[n * block + first + g] = out[:, g * cols : (g + 1) * cols].T.astype(BF16)
            seen = low[pl.ds(n * block + first, group)].reshape(group * cols, channels)
            table_grad[...] += dot(both, seen, (1, 0)) * scale
        return carry

    stores = []

    def outer_part(n):
        first, last = n * chunks // 4, (n + 1) * chunks // 4
        lax.fori_loop(first, last, outer_chunk, 0)
        at = pl.ds(first * block, (last - first) * block)
        copy = pltpu.make_async_copy(total_low.at[at], total.at[at], out_sem.at[n])
        copy.start()
        stores.append(copy)

    swap.wait_recv()
    rights = []
    for slot, way in enumerate((CORNER, ACROSS, DOWN)):
        n = plane[way][0] // 2
        for h in range(4):
            chip_sum[slot, h] = (
                right_send[n, core, h].astype(F32) + right_core[n, h].astype(F32)
            ).astype(BF16)
        rights.append(sends.start(chip_sum.at[slot], right_in.at[slot], plane[way]))
    outer_part(0)
    for copy in lefts:
        copy.wait_recv()
    for r in range(8):
        summed = left_send[head, r].astype(F32)
        for k in range(3):
            summed = summed + left_line[k, r].astype(F32)
        left_sum[r] = summed.astype(BF16)
    across = [
        sends.start(left_sum.at[plane[way][0]], left_land.at[row], plane[way])
        for way in (2, 4, 6, 3, 5, 7, 1)
    ]
    left_land[row] = left_sum[row]
    outer_part(1)
    for copy in rights:
        copy.wait_recv()
    for h in range(4):
        summed = right_send[chip, core, h].astype(F32) + right_core[chip, h].astype(F32)
        for slot in range(3):
            summed = summed + right_in[slot, h].astype(F32)
        right_sum[h] = summed.astype(BF16)
    line = [
        sends.start(right_sum.at[beyond[k]], right_land.at[head], (row, beyond[k])) for k in (1, 2, 3)
    ]
    right_land[head] = right_sum[head]
    outer_part(2)
    outer_part(3)
    for copy in across + line:
        copy.wait_recv()
    for r in range(8):
        left_out[:, r * lines : (r + 1) * lines, :] = left_land[r]
    for h in range(4):
        right_out[:, :, h * cols : (h + 1) * cols] = right_land[h]
    for copy in hops:
        copy.wait_recv()
    sends.finish()
    for copy in stores:
        copy.wait()


def outer_product(left, right, early, pairs_back, outer_out, update, all_rows, block=8, group=2):
    left_early, right_early, hop_early = early
    rows, cols, channels = pairs_back.shape
    own, wide, residues = right.shape
    size = left.shape[1] * left.shape[2] // residues
    lines = left.shape[1] // 8
    vmem = pl.BlockSpec(memory_space=pltpu.VMEM)
    hbm = pl.BlockSpec(memory_space=pl.ANY)
    low = lambda *shape: pltpu.VMEM(shape, BF16)
    full = lambda *shape: pltpu.VMEM(shape, F32)
    one = (lines, 128)
    other = (wide, cols)
    rest = 1
    dma = pltpu.SemaphoreType.DMA
    return pl.pallas_call(
        functools.partial(outer_kernel, scale=1.0 / all_rows, block=block, group=group),
        out_shape=[
            jax.ShapeDtypeStruct(pairs_back.shape, BF16),
            jax.ShapeDtypeStruct(left.shape, BF16),
            jax.ShapeDtypeStruct(right.shape, BF16),
            jax.ShapeDtypeStruct((wide * size, channels), F32),
            jax.ShapeDtypeStruct((own - own // 2,) + update.shape[1:], BF16),
            jax.ShapeDtypeStruct(hop_early.shape, BF16),
        ],
        in_specs=[vmem, vmem, hbm, hbm, hbm, vmem, hbm, hbm],
        out_specs=[hbm, vmem, vmem, vmem, hbm, hbm],
        scratch_shapes=[
            low(8, rest, *one), low(4, rest, *other), low(8, rest, *one), low(4, rest, *other),
            low(4, 8, own - rest, *one), low(8, 4, own - rest, *other),
            low(4, 8, rest, *one), low(8, 4, rest, *other), full(32, own, *one), full(32, own, *other),
            low(all_rows, rows * size), low(all_rows, wide * cols),
            low(rows * size, wide * cols), low(block * size, wide * cols), full(rows, cols, channels),
            low(rows, cols, channels), low(wide * size, channels), low(channels, wide * size), low(rows, cols, channels),
            full(all_rows, rows * size), full(all_rows, wide * cols), low(4, 8, own, *one), low(4, 2, 4, own, *other),
            low(4, 4, own, *other), low(3, 4, own, *other), low(3, 4, own, *other), low(4, own, *other),
            low(3, 8, own, *one), low(8, own, *one), low(8, own, *one), low(4, own, *other),
            dma((rows // block,)), dma((2,)), dma((4,)), dma((2,)), dma((ROW_SENDS,)), dma((ROW_SENDS,)),
            dma((OUTER_SENDS,)), dma((OUTER_SENDS,)),
        ],
        compiler_params=pltpu.CompilerParams(
            collective_id=1, has_side_effects=True, vmem_limit_bytes=VMEM
        ),
        cost_estimate=cost(50),
    )(left, right, left_early, right_early, pairs_back, outer_out, update, hop_early)


SUM_SENDS = 4 + 4 + 8 + 3 + 1 + 3 + 3 + 3 + 12 + 16


def sum_kernel(
    grads, parts, out, spread,
    swapped, chip_sum, by_across, by_down, from_across, from_down, down_sum, line_in,
    part_swapped, part_sum, part_plane, part_down, part_line, piece,
    local_sem, send_sem, recv_sem,
):
    row, head = place()
    beyond = [(head + k) % 4 for k in range(4)]
    core, chip = row % 2, row // 2
    ways = (CORNER, ACROSS, DOWN)
    plane = [(flip(row, way), head) for way in range(8)]
    other, across, down = plane[CORE], plane[ACROSS], plane[DOWN]
    greet([plane[way] for way in (CORE,) + ways] + [(row, beyond[k]) for k in (1, 2, 3)])
    sends = Sends(send_sem, recv_sem)
    chips = [plane[way][0] // 2 for way in ways] + [chip]
    part_swap = sends.start(parts.at[1 - core], part_swapped, other)
    swaps = [sends.start(grads.at[n, 1 - core], swapped.at[slot], other) for slot, n in enumerate(chips)]
    first, second = (2, 1), (3, 0)

    def add(slot, k):
        z = beyond[k]
        chip_sum[slot, k] = (
            grads[chips[slot], core, z].astype(F32) + swapped[slot, z].astype(F32)
        ).astype(BF16)

    part_swap.wait_recv()
    part_arrive = []
    for slot, n in enumerate(chips):
        for z in range(4):
            part_sum[slot, z] = (parts[core, n, z].astype(F32) + part_swapped[n, z].astype(F32)).astype(BF16)
        if slot < 3:
            part_arrive.append(sends.start(part_sum.at[slot], part_plane.at[slot], plane[ways[slot]]))
    swaps[0].wait_recv()
    relays_across, relays_down = [], []
    for n in range(2):
        add(0, first[n])
        relays_across.append(sends.start(chip_sum.at[0, first[n]], by_across.at[n], across))
        add(0, second[n])
        relays_down.append(sends.start(chip_sum.at[0, second[n]], by_down.at[n], down))
    last_across, last_down = [None] * 4, [None] * 4
    swaps[1].wait_recv()
    for k in first:
        add(1, k)
        last_across[k] = sends.start(chip_sum.at[1, k], from_across.at[k], across)
    swaps[2].wait_recv()
    for k in second:
        add(2, k)
        last_down[k] = sends.start(chip_sum.at[2, k], from_down.at[k], down)
    for n in range(2):
        add(1, second[n])
        add(2, first[n])
        relays_across[n].wait_recv()
        k = first[n]
        chip_sum[2, k] = (chip_sum[2, k].astype(F32) + by_across[n].astype(F32)).astype(BF16)
        last_down[k] = sends.start(chip_sum.at[2, k], from_down.at[k], down)
        relays_down[n].wait_recv()
        k = second[n]
        chip_sum[1, k] = (chip_sum[1, k].astype(F32) + by_down[n].astype(F32)).astype(BF16)
        last_across[k] = sends.start(chip_sum.at[1, k], from_across.at[k], across)
    for copy in part_arrive:
        copy.wait_recv()
    for z in range(4):
        total = part_sum[3, z].astype(F32)
        for slot in range(3):
            total = total + part_plane[slot, z].astype(F32)
        part_down[z] = total.astype(BF16)
    part_arrive = [
        sends.start(part_down.at[beyond[k]], part_line.at[k - 1], (row, beyond[k])) for k in (1, 2, 3)
    ]
    swaps[3].wait_recv()
    for k in first + second:
        add(3, k)
    total = part_down[head].astype(F32)
    for slot, copy in enumerate(part_arrive):
        copy.wait_recv()
        total = total + part_line[slot].astype(F32)
    piece[...] = total.astype(BF16)
    behind = [(head + 4 - k) % 4 for k in range(4)]
    part_line_all = [None] + [sends.start(piece, spread.at[core, chip, head], (row, beyond[k])) for k in (1, 2, 3)]
    mine = pltpu.make_async_copy(piece, spread.at[core, chip, head], local_sem)
    mine.start()
    wide, end = [], []

    def forward(k):
        here = spread.at[core, chip, behind[k]]
        source = here if k else piece
        for way in ways:
            wide.append((plane[way][0] // 2, k, sends.start(source, here, plane[way])))
        end.append(sends.start(source, here, other))

    forward(0)
    line = []
    for k in first + second:
        last_across[k].wait_recv()
        last_down[k].wait_recv()
        total = chip_sum[3, k].astype(F32) + from_across[k].astype(F32) + from_down[k].astype(F32)
        if k:
            down_sum[k - 1] = total.astype(BF16)
            line.append(sends.start(down_sum.at[k - 1], line_in.at[k - 1], (row, beyond[k])))
        else:
            out[...] = total
        if k == first[0]:
            for n in (1, 2, 3):
                part_line_all[n].wait_recv()
                forward(n)
    for n, k, copy in wide:
        copy.wait_recv()
        block = spread.at[core, n, behind[k]]
        end.append(sends.start(block, block, other))
    for slot, copy in zip((1, 0, 2), line):
        copy.wait_recv()
        out[...] += line_in[slot].astype(F32)
    for copy in end:
        copy.wait_recv()
    mine.wait()
    sends.finish()


def sum_gradients(grads, parts):
    block = grads.shape[2:]
    lines = block[0] * block[1]
    rows, cols = parts.shape
    share = rows // 32
    vmem = pl.BlockSpec(memory_space=pltpu.VMEM)
    wide = lambda *first: pltpu.VMEM(first + (lines, block[2]), BF16)
    thin = lambda *first: pltpu.VMEM(first + (share, cols), BF16)
    out, spread = pl.pallas_call(
        sum_kernel,
        out_shape=[
            jax.ShapeDtypeStruct((lines, block[2]), F32),
            jax.ShapeDtypeStruct((2, 4, 4, share, cols), BF16),
        ],
        in_specs=[vmem, vmem],
        out_specs=[vmem, vmem],
        scratch_shapes=[
            wide(4, 4), wide(4, 4), wide(2), wide(2), wide(4), wide(4), wide(3), wide(3),
            thin(4, 4), thin(4, 4), thin(3, 4), thin(4), thin(3), thin(),
            pltpu.SemaphoreType.DMA,
            pltpu.SemaphoreType.DMA((SUM_SENDS,)),
            pltpu.SemaphoreType.DMA((SUM_SENDS,)),
        ],
        compiler_params=pltpu.CompilerParams(
            collective_id=3, has_side_effects=True, vmem_limit_bytes=VMEM
        ),
        cost_estimate=cost(40),
    )(grads.reshape(4, 2, 4, lines, block[2]), parts.reshape(2, 4, 4, share, cols))
    return out.reshape(block), spread.reshape(rows, cols)


SMALL_SENDS = 3 + 7


def small_kernel(small, total, line_in, line_sum, plane_in, send_sem, recv_sem):
    row, head = place()
    line = [(row, (head + k) % 4) for k in (1, 2, 3)]
    plane = [(flip(row, way), head) for way in range(1, 8)]
    greet(plane + line)
    sends = Sends(send_sem, recv_sem)
    arrive = [sends.start(small, line_in.at[head], device) for device in line]
    line_in[head] = small[...]
    for copy in arrive:
        copy.wait_recv()
    line_sum[...] = (line_in[0] + line_in[1]) + (line_in[2] + line_in[3])
    arrive = [sends.start(line_sum, plane_in.at[row], device) for device in plane]
    plane_in[row] = line_sum[...]
    for copy in arrive:
        copy.wait_recv()
    summed = plane_in[0]
    for n in range(1, 8):
        summed = summed + plane_in[n]
    total[...] = summed
    sends.finish()


def small_sum(small):
    vmem = pl.BlockSpec(memory_space=pltpu.VMEM)
    return pl.pallas_call(
        small_kernel,
        out_shape=jax.ShapeDtypeStruct(small.shape, F32),
        in_specs=[vmem],
        out_specs=vmem,
        scratch_shapes=[
            pltpu.VMEM((4,) + small.shape, F32),
            pltpu.VMEM(small.shape, F32),
            pltpu.VMEM((8,) + small.shape, F32),
            pltpu.SemaphoreType.DMA((SMALL_SENDS,)),
            pltpu.SemaphoreType.DMA((SMALL_SENDS,)),
        ],
        compiler_params=pltpu.CompilerParams(
            collective_id=4, has_side_effects=True, vmem_limit_bytes=VMEM
        ),
        cost_estimate=cost(9),
    )(small)


def add_pieces(step, base, pieces, out):
    for n, piece in enumerate(pieces):
        @pl.when(step == n)
        def _():
            out[...] = base[...] + piece[...].astype(F32)


def added_specs(base, pieces):
    block = pieces[0].shape
    by_order = pl.BlockSpec(
        block, lambda n, order: (order[jnp.minimum(n, len(pieces) - 1) * block[0]] // block[0], 0, 0)
    )
    return by_order, [by_order] + [pl.BlockSpec(block, lambda n, order: (0, 0, 0))] * len(pieces)


def pair_backward_kernel(order, pairs, back, grads, norm, weight, norms, base, *refs):
    pieces, (out, small, changed) = refs[:-3], refs[-3:]
    step = pl.program_id(0)
    rows, cols, channels = pairs.shape
    add_pieces(step, base, pieces, changed)

    @pl.when(step == 0)
    def _():
        small[...] = jnp.zeros_like(small)
        small[2 * HEADS :] = jnp.concatenate([norms[:, :128], norms[:, 128:]], axis=0)

    values = pairs[...].reshape(rows * cols, channels)
    hat, rstd = normalize(values)
    gain, shift = norm[0:1, norm.shape[1] - channels :], norm[1:2, norm.shape[1] - channels :]
    low = (hat * gain + shift).astype(BF16)
    bias = jnp.concatenate([grads[:, i, :] for i in range(rows)], axis=1).astype(BF16)
    small[0:HEADS] += dot(bias, low, (1, 0))
    in_grad = dot(bias, weight[...].astype(BF16), (0, 0))
    small[HEADS : HEADS + 1] += jnp.sum(in_grad * hat, axis=0, keepdims=True)
    small[HEADS + 1 : HEADS + 2] += jnp.sum(in_grad, axis=0, keepdims=True)
    change = norm_backward(hat, rstd, gain, in_grad)
    out[...] = back[...] + change.reshape(rows, cols, channels)


def pair_norm_backward(order, pairs, back, grads, norm, weight, norms, base, pieces, steps=8):
    rows, cols, channels = pairs.shape
    block = rows // steps
    by_row = lambda n, order: (n, 0, 0)
    whole = lambda n, order: (0, 0)
    by_order, added = added_specs(base, pieces)
    grads = grads.reshape(HEADS, steps, block, cols)
    return pl.pallas_call(
        pair_backward_kernel,
        grid_spec=pltpu.PrefetchScalarGridSpec(
            num_scalar_prefetch=1,
            grid=(steps,),
            in_specs=[
                pl.BlockSpec((block, cols, channels), by_row),
                pl.BlockSpec((block, cols, channels), by_row),
                pl.BlockSpec((HEADS, None, block, cols), lambda n, order: (0, n, 0, 0)),
                pl.BlockSpec(norm.shape, whole),
                pl.BlockSpec(weight.shape, whole),
                pl.BlockSpec(norms.shape, whole),
            ]
            + added,
            out_specs=[
                pl.BlockSpec((block, cols, channels), by_row),
                pl.BlockSpec((3 * HEADS, channels), whole),
                by_order,
            ],
        ),
        out_shape=[
            jax.ShapeDtypeStruct(pairs.shape, F32),
            jax.ShapeDtypeStruct((3 * HEADS, channels), F32),
            jax.ShapeDtypeStruct(base.shape, F32),
        ],
        compiler_params=pltpu.CompilerParams(vmem_limit_bytes=VMEM),
        cost_estimate=cost(9),
    )(order, pairs, back, grads, norm, weight, norms, base, *pieces)


def add_kernel(place_ref, base, piece, *refs):
    refs[-1][...] = base[...] + piece[...].astype(F32)


def add_rows(at, base, piece, into=None):
    own = piece.shape[0]
    block = (1,) + piece.shape[1:]
    spread = lambda n, at: (at[0] * own + n, 0, 0)
    return pl.pallas_call(
        add_kernel,
        grid_spec=pltpu.PrefetchScalarGridSpec(
            num_scalar_prefetch=1,
            grid=(own,),
            in_specs=[pl.BlockSpec(block, spread), pl.BlockSpec(block, lambda n, at: (n, 0, 0))]
            + ([] if into is None else [pl.BlockSpec(memory_space=pl.ANY)]),
            out_specs=pl.BlockSpec(block, spread),
        ),
        out_shape=jax.ShapeDtypeStruct(base.shape, F32),
        input_output_aliases={} if into is None else {3: 0},
        cost_estimate=cost(2),
    )(*((at, base, piece) if into is None else (at, base, piece, into)))


def hop(piece):
    count = lax.axis_size("head")
    return lax.ppermute(piece, "head", [(i, (i + 1) % count) for i in range(count)])


def together(moved, *values):
    return lax.optimization_barrier((moved,) + values)


def adam_kernel(at, packed, pair_side, *refs, rates, pieces):
    olds, base, adds, news = refs[:18], refs[18], refs[19 : 19 + pieces], refs[20 + pieces : 38 + pieces]
    changed, table = refs[38 + pieces :]
    step = pl.program_id(0)
    add_pieces(step, base, adds, changed)

    @pl.when(step == 0)
    def _():
        adam_step(at, packed, pair_side, olds, news, table, rates)


def adam_step(at, packed, pair_side, olds, news, table, rates):
    norms, heads_in, heads_out, bias_weight, outer_in, outer_out = [olds[3 * n : 3 * n + 3] for n in range(6)]
    count, local, all_heads = heads_in[0].shape
    sides, size = outer_in[0].shape[:2]

    def rows(first, lines):
        return packed[pl.ds(first, lines), :].astype(F32)

    def pair_of(first, offset, lines, span):
        return jnp.concatenate([rows(first + offset, lines), rows(first + span + offset, lines)], axis=1)

    def update(n, index, grad):
        weight, moment_one, moment_two = [ref[index] for ref in olds[3 * n : 3 * n + 3]]
        for ref, new in zip(
            news[3 * n : 3 * n + 3], adam_update(weight, grad, moment_one, moment_two, rates[n])
        ):
            ref[index] = new

    mine = pl.multiple_of(at[4], local)
    span = count * all_heads
    for k in range(count):
        update(1, k, pair_of(0, k * all_heads + mine, local, span))
    first = 2 * span
    update(2, slice(None), pair_of(first, mine, local, all_heads))
    first += 2 * all_heads
    for k in range(sides):
        update(4, k, pair_of(first, k * size, size, sides * size))
    first += 2 * sides * size
    table[...] = rows(first, size * size)
    for e in range(size):
        update(5, slice(e * size, (e + 1) * size), table[pl.ds(e, size, stride=size), :])
    pair = pair_side[...]
    low = pair[2 * HEADS :]
    lines = [
        jnp.concatenate([low[n : n + 1], low[n + 4 : n + 5], low[n + 2 : n + 3], low[n + 6 : n + 7], pair[HEADS + n : HEADS + n + 1]], axis=1)
        for n in range(2)
    ]
    update(0, slice(None), jnp.concatenate(lines, axis=0))
    update(3, slice(None), pair[:HEADS])


def adam_all(at, packed, pair_side, olds, rates, base, pieces, into):
    turned = (1, 3, 4)
    flat = [array.swapaxes(-1, -2) if n in turned else array for n, triple in enumerate(olds) for array in triple]
    size = olds[4][0].shape[2]
    by_order, added = added_specs(base, pieces)
    whole = lambda array: pl.BlockSpec(array.shape, lambda n, at: (0,) * array.ndim)
    *news, changed = pl.pallas_call(
        functools.partial(adam_kernel, rates=rates, pieces=len(pieces)),
        grid_spec=pltpu.PrefetchScalarGridSpec(
            num_scalar_prefetch=1,
            grid=(len(pieces),),
            in_specs=[whole(array) for array in [packed, pair_side] + flat]
            + added
            + [pl.BlockSpec(memory_space=pl.ANY)],
            out_specs=[whole(array) for array in flat] + [by_order],
            scratch_shapes=[pltpu.VMEM((size * size, packed.shape[1]), F32)],
        ),
        out_shape=[jax.ShapeDtypeStruct(array.shape, F32) for array in flat + [base]],
        input_output_aliases={3 + len(flat) + 1 + len(pieces): len(flat)},
        compiler_params=pltpu.CompilerParams(vmem_limit_bytes=VMEM),
        cost_estimate=cost(5),
    )(at, packed, pair_side, *flat, base, *pieces, into)
    news = [array.swapaxes(-1, -2) if n // 3 in turned else array for n, array in enumerate(news)]
    return news + [changed]


def per_device(
    alignment,
    pairs,
    residue_mask,
    row_mask,
    alignment_back,
    pairs_back,
    norm_scales,
    heads_in,
    heads_out,
    bias_weight,
    outer_in,
    outer_out,
    first_norms,
    second_norms,
    first_heads_in,
    second_heads_in,
    first_heads_out,
    second_heads_out,
    first_bias_weight,
    second_bias_weight,
    first_outer_in,
    second_outer_in,
    first_outer_out,
    second_outer_out,
):
    row_count = lax.axis_size("row")
    head_count = lax.axis_size("head")
    head_index = lax.axis_index("head")
    devices = row_count * head_count
    rows_here, residues, width = alignment.shape
    pair_rows, pair_cols, pair_width = pairs.shape
    size = width // HEADS
    outer_width = outer_in.shape[2]
    all_rows = rows_here * row_count
    own = rows_here // head_count
    start = head_index * own
    pair_gain = norm_scales[0:1, 2 * width :]
    pair_shift = norm_scales[1:2, 2 * width :]
    residue_live = residue_mask.astype(F32)
    row_live = lax.dynamic_slice_in_dim(row_mask, start, own, 0).astype(F32)
    flat_live = jnp.repeat(residue_live.reshape(-1, QUADS), outer_in.shape[2], axis=1)
    row_live = jnp.broadcast_to(row_live[:, None, None], (own, 1, 128))
    bias_low = bias_weight.astype(BF16)

    fast = (row_count, head_count, pair_cols, own * outer_width) == (8, 4, 128, 128)

    local = heads_in.shape[2]
    outer_t = outer_in.swapaxes(1, 2).reshape(2 * outer_width, width)
    if fast:
        bias, weights = pair_bias(
            pairs, norm_scales, bias_weight.T, heads_in.swapaxes(1, 2), heads_out
        )
    else:
        shard = jnp.concatenate([heads_in.astype(BF16).swapaxes(1, 2), heads_out.astype(BF16)[None]])
        weights = lax.all_gather(shard, "head", axis=1, tiled=True)
        bias = pair_forward(pairs, pair_gain, pair_shift, bias_low)
        bias = lax.all_gather(bias, "head", axis=2, tiled=True)
        bias = lax.all_gather(bias, "row", axis=1, tiled=True)[None, None]

    update, left, right, kept, early = attention_forward(
        alignment, norm_scales, weights, outer_t, bias, residue_live[None], row_live, flat_live, fast
    )

    if fast:
        total, left_grad, right_grad, table_grad, hop_one, hop_two = outer_product(
            left, right, early, pairs_back, outer_out, update, all_rows
        )
        updates = [update, early[2], hop_one, hop_two]
    else:
        table = outer_out.astype(BF16).reshape(outer_width, outer_width, pair_width)
        updates = [update]
        for _ in range(head_count - 1):
            updates.append(hop(updates[-1]))
        left = left.reshape(own, residues, outer_width).swapaxes(1, 2)
        left = left.reshape(own, outer_width, row_count, pair_rows).transpose(2, 0, 1, 3)
        right = right.reshape(own, outer_width, head_count, pair_cols).transpose(2, 0, 1, 3)
        both = (row_count, head_count, own, outer_width)
        send = jnp.concatenate(
            [
                jnp.broadcast_to(left[:, None], both + (pair_rows,)),
                jnp.broadcast_to(right[None], both + (pair_cols,)),
            ],
            axis=4,
        )
        flat = (devices, own, outer_width, pair_rows + pair_cols)
        got = lax.all_to_all(send.reshape(flat), EVERY, split_axis=0, concat_axis=0, tiled=True)
        got = got.reshape(all_rows, outer_width, pair_rows + pair_cols)
        total, table_grad, left_grad, right_grad = outer_product_plain(
            got[:, :, :pair_rows], got[:, :, pair_rows:], pairs_back, table, all_rows
        )
        pairs_new = pairs + total
        send = jnp.concatenate([left_grad, right_grad], axis=2).reshape(flat)
        got = lax.all_to_all(send, EVERY, split_axis=0, concat_axis=0, tiled=True)
        got = got.reshape(both + (pair_rows + pair_cols,)).astype(F32)
        left_grad = jnp.sum(got[..., :pair_rows], axis=1).transpose(1, 0, 3, 2).astype(BF16)
        left_grad = left_grad.reshape(own, residues // QUADS, QUADS * outer_width)
        right_grad = jnp.sum(got[..., pair_rows:], axis=0).transpose(1, 2, 0, 3).astype(BF16)
        right_grad = right_grad.reshape(own, outer_width, residues)
        table_grad = table_grad.swapaxes(0, 1).reshape(outer_width * outer_width, pair_width)

    turns = (head_index + head_count - jnp.arange(head_count, dtype=jnp.int32)) % head_count
    order = (turns[:, None] * own + jnp.arange(own, dtype=jnp.int32)[None]).reshape(-1)
    half = own // 2

    def mine(first, hops, second, more):
        parts = [(first, step) for step in hops] + [(second, step) for step in more]
        return jnp.concatenate([order[step * own + n * half : step * own + (n + 1) * half] for n, step in parts])

    backward = functools.partial(
        attention_backward,
        order, alignment, update, alignment_back, norm_scales, weights, outer_t, left_grad, right_grad,
        residue_live[None], row_live, flat_live, kept, bias.shape,
    )
    if fast:
        moved = [hop(hop_one), hop(hop_two)]
    part, bias_grad, *early = backward(first=0, own=half, pairs=[pairs, total] if fast else ())
    if fast:
        pairs_new = early.pop()
        moved, bias_grad, part, early = together(moved, bias_grad, part, early)
        updates += moved
        left_over = hop(moved[0])
    changes = [[part, hop(part)]]
    alignment_new, part, bias_grad, packed, norms = backward(
        first=half, own=half, earlier=bias_grad, early=early, table_grad=table_grad, pieces=updates
    )
    if fast:
        left_over, changes[0][1], bias_grad, part, packed, norms = together(
            left_over, changes[0][1], bias_grad, part, packed, norms
        )
        changes[0].append(hop(changes[0][1]))
        changes.append([part, hop(part)])
        bias_grad, packed = sum_gradients(bias_grad, packed)
        changes[0][2], changes[1][1], bias_grad = together(changes[0][2], changes[1][1], bias_grad)
        changes[0].append(hop(changes[0][2]))
        changes[1].append(hop(changes[1][1]))
        pairs_grad, pair_side, alignment_grad = pair_norm_backward(
            mine(0, (0, 1, 2), 1, (0, 1)),
            pairs,
            pairs_back,
            bias_grad,
            norm_scales,
            bias_weight.T,
            norms,
            alignment_back,
            changes[0][:3] + changes[1][:2],
        )
        pair_side = small_sum(pair_side)
        changes[0][3], changes[1][2], pair_side = together(changes[0][3], changes[1][2], pair_side)
        changes[1].append(hop(changes[1][2]))
    else:
        for _ in range(head_count - 2):
            changes[0].append(hop(changes[0][-1]))
        changes.append([part])
        for _ in range(head_count - 1):
            changes[1].append(hop(changes[1][-1]))
        bias_grad = lax.psum_scatter(bias_grad[0, 0], "row", scatter_dimension=1, tiled=True)
        bias_grad = lax.psum_scatter(bias_grad, "head", scatter_dimension=2, tiled=True)
        pairs_grad, bias_weight_grad, pair_gain_grad, pair_shift_grad = pair_backward(
            pairs, pairs_back, pair_gain, pair_shift, bias_low, bias_grad
        )
        packed, norms, bias_weight_total, pair_norms_total = lax.psum(
            (packed.astype(F32), norms, bias_weight_grad, jnp.stack([pair_gain_grad, pair_shift_grad])), EVERY
        )
    olds = (
        (norm_scales, first_norms, second_norms),
        (heads_in, first_heads_in, second_heads_in),
        (heads_out, first_heads_out, second_heads_out),
        (bias_weight, first_bias_weight, second_bias_weight),
        (outer_in, first_outer_in, second_outer_in),
        (outer_out, first_outer_out, second_outer_out),
    )
    rates = (
        0.5,
        width ** (-0.5),
        max(2 * HEADS * size // residues, 1) ** (-0.5),
        pair_width ** (-0.5),
        width ** (-0.5),
        max(outer_width * outer_width // all_rows, 1) ** (-0.5),
    )
    if fast:
        at = (head_index * local).astype(jnp.int32)[None]
        *news, alignment_grad = adam_all(
            jnp.concatenate([mine(0, (3,), 1, (2,)), at]),
            packed, pair_side, olds, rates, alignment_back, [changes[0][3], changes[1][2]], alignment_grad,
        )
        at = (turns[3] * 2 + 1)[None]
        alignment_new = add_rows(at, alignment, left_over, alignment_new)
        alignment_grad = add_rows(at, alignment_back, changes[1][3], alignment_grad)
        return (alignment_new, pairs_new, alignment_grad, pairs_grad, *news)
    alignment_grad = None
    for step in range(head_count):
        for n in range(2):
            at = (turns[step] * 2 + n)[None]
            alignment_grad = add_rows(at, alignment_back, changes[n][step], alignment_grad)
    def unpack(first, lines):
        return jnp.concatenate([packed[first : first + lines], packed[first + lines : first + 2 * lines]], axis=1)

    lines = 4 * width
    heads_in_total = lax.dynamic_slice_in_dim(
        unpack(0, lines).reshape(4, width, width), head_index * local, local, 1
    ).swapaxes(1, 2)
    heads_out_total = lax.dynamic_slice_in_dim(unpack(2 * lines, width), head_index * local, local, 0)
    lines = 2 * (lines + width)
    outer_in_total = unpack(lines, 2 * outer_width).reshape(2, outer_width, width).swapaxes(1, 2)
    lines += 4 * outer_width
    table_total = packed[lines : lines + outer_width * outer_width]
    table_total = table_total.reshape(outer_width, outer_width, pair_width).swapaxes(0, 1)
    table_total = table_total.reshape(outer_width * outer_width, pair_width)
    norms_total = jnp.concatenate(
        [norms.reshape(2, 2, width).swapaxes(0, 1).reshape(2, 2 * width), pair_norms_total], axis=1
    )
    totals = (norms_total, heads_in_total, heads_out_total, bias_weight_total, outer_in_total, table_total)
    news = []
    for (weight, moment_one, moment_two), total, rate in zip(olds, totals, rates):
        news += adam_update(weight, total, moment_one, moment_two, rate)
    return (alignment_new, pairs_new, alignment_grad, pairs_grad, *news)


def solution(mesh):
    row_msa = P("row", None, None)
    pair = P("row", "head", None)
    columns = P(None, None, "head")
    lines = P("head", None)
    in_specs = (
        (row_msa, pair, P(), P("row"), row_msa, pair, P(), columns, lines)
        + (P(),) * 5
        + (columns,) * 2
        + (lines,) * 2
        + (P(),) * 6
    )
    out_specs = (row_msa, pair, row_msa, pair) + (P(),) * 3 + (columns,) * 3 + (lines,) * 3 + (P(),) * 9
    return jax.shard_map(
        per_device, mesh=mesh, in_specs=in_specs, out_specs=out_specs, check_vma=False
    )
```

```python
import functools

import jax
import jax.numpy as jnp
from jax import lax
from jax.experimental import pallas as pl
from jax.experimental.pallas import tpu as pltpu
from jax.sharding import PartitionSpec as P

HEADS = 8
STEP = 10
F32 = jnp.float32
BF16 = jnp.bfloat16
LOG2E = 1.4426950408889634
VMEM = 56 << 20
EVERY = ("row", "head")


def adam_update(weight, gradient, moment_one, moment_two, step_rate):
    first_new = 0.9 * moment_one + 0.1 * gradient
    second_new = 0.999 * moment_two + 0.001 * gradient * gradient
    first_hat = first_new / (1.0 - 0.9**STEP)
    second_hat = second_new / (1.0 - 0.999**STEP)
    updated = weight - step_rate * (first_hat / (jnp.sqrt(second_hat) + 1e-08) + 0.01 * weight)
    return (first_new, second_new, updated)


def cost(micros):
    return pl.CostEstimate(flops=0, bytes_accessed=int(micros * 3.5e6), transcendentals=0)


def dot(a, b, along):
    return lax.dot_general(a, b, (((along[0],), (along[1],)), ((), ())), preferred_element_type=F32)


def normalize(values):
    center = values - jnp.mean(values, axis=-1, keepdims=True)
    rstd = lax.rsqrt(jnp.mean(center * center, axis=-1, keepdims=True) + 1e-05)
    return center * rstd, rstd


def norm_backward(hat, rstd, gain, grad):
    scaled = grad * gain
    return rstd * (
        scaled
        - jnp.mean(scaled, axis=-1, keepdims=True)
        - hat * jnp.mean(scaled * hat, axis=-1, keepdims=True)
    )


QUADS = 4


def quad(outer_t, q):
    weights = outer_t[: outer_t.shape[0] // 2]
    zero = jnp.zeros_like(weights)
    return jnp.concatenate([weights if n == q else zero for n in range(QUADS)], axis=0)


def put(ref, value):
    for n in range(ref.shape[0]):
        ref[n] = value[:, n * 128 : (n + 1) * 128]


def take(ref, q):
    at = pl.ds(q, ref.shape[1] // QUADS, stride=QUADS)
    return jnp.concatenate([ref[n, at, :] for n in range(ref.shape[0])], axis=1)


ROW_SENDS = 20


class Exchange:
    def __init__(
        self, left, right, left_stage, right_stage, left_plane, right_line, left_all, right_all,
        local_sem, send_sem, recv_sem,
    ):
        self.left, self.right, self.left_stage, self.right_stage = left, right, left_stage, right_stage
        self.left_plane, self.right_line, self.left_all, self.right_all = left_plane, right_line, left_all, right_all
        self.local_sem, self.send_sem, self.recv_sem = local_sem, send_sem, recv_sem
        self.row, self.head = place()
        self.beyond = [(self.head + k) % 4 for k in range(4)]
        self.behind = [(self.head + 4 - k) % 4 for k in range(4)]
        self.plane = [(flip(self.row, way), self.head) for way in range(8)]
        self.lines = left_plane.shape[2]
        self.cols = right_line.shape[3]

    def copy(self, n, source, target, device):
        return pltpu.make_async_remote_copy(
            src_ref=source,
            dst_ref=target,
            send_sem=self.send_sem.at[n],
            recv_sem=self.recv_sem.at[n],
            device_id=device,
            device_id_type=MESH,
        )

    def first(self):
        out = [
            self.copy(7 + k, self.right_stage.at[self.beyond[k + 1]], self.right_line.at[self.head],
                      (self.row, self.beyond[k + 1]))
            for k in range(3)
        ]
        out += [
            self.copy(n, self.left_stage.at[self.plane[way][0]], self.left_plane.at[self.row], self.plane[way])
            for n, way in enumerate((2, 4, 6, 3, 5, 7, 1))
        ]
        return out

    def second(self, which):
        if which == "left":
            return [
                self.copy(10 + k, self.left_plane, self.left_all.at[self.head], (self.row, self.beyond[k + 1]))
                for k in range(3)
            ]
        if which == "core":
            return [self.copy(16, self.right_line, self.right_all.at[self.row], self.plane[CORE])]
        return [
            self.copy(13 + n, self.right_line, self.right_all.at[self.row], self.plane[way])
            for n, way in enumerate((ACROSS, DOWN, CORNER))
        ]

    def third(self):
        out = []
        for n, way in enumerate((ACROSS, DOWN, CORNER)):
            block = self.right_all.at[self.plane[way][0]]
            out.append(self.copy(17 + n, block, block, self.plane[CORE]))
        return out

    def locals(self):
        return [
            pltpu.make_async_copy(self.left_plane, self.left_all.at[self.head], self.local_sem.at[0]),
            pltpu.make_async_copy(self.right_line, self.right_all.at[self.row], self.local_sem.at[1]),
        ]

    def begin(self):
        for r in range(8):
            self.left_stage[r] = self.left[:, r * self.lines : (r + 1) * self.lines, :]
        for h in range(4):
            self.right_stage[h] = self.right[:, :, h * self.cols : (h + 1) * self.cols]
        self.left_plane[self.row] = self.left_stage[self.row]
        self.right_line[self.head] = self.right_stage[self.head]
        for copy in self.first():
            copy.start()

    def go_on(self):
        for copy in self.first():
            copy.wait_recv()
        for copy in self.second("chips") + self.second("core") + self.second("left") + self.locals():
            copy.start()

    def core(self):
        for copy in self.second("chips"):
            copy.wait_recv()
        for copy in self.third():
            copy.start()

    def end(self):
        for copy in self.second("left") + self.second("core") + self.third():
            copy.wait()
        for copy in self.locals():
            copy.wait()
        for copy in self.first() + self.second("chips"):
            copy.wait_send()


def norm_rows(scales, width):
    return (
        scales[0:1, :width],
        scales[1:2, :width],
        scales[0:1, width : 2 * width],
        scales[1:2, width : 2 * width],
    )


def forward_kernel(*refs, share):
    (rows, scales, weights, outer_w, bias, residue, row_live, flat_live), refs = refs[:8], refs[8:]
    (update, left, right, qkv, gate, powers, inverse, mixed, attended), refs = refs[:9], refs[9:]
    if share:
        (left_all, right_all, hop_one), refs = refs[:3], refs[3:]
        left_stage, right_stage, left_plane, right_line, local_sem, send_sem, recv_sem, hop_sem = refs[-8:]
    bias_t, second, rows_in, load_sem = refs[:4]
    row = pl.program_id(0)
    own = update.shape[0]
    width = rows.shape[2]
    residues = rows.shape[1]
    size = width // HEADS
    half = outer_w.shape[0] // 2
    outer_t = outer_w[...].astype(BF16)
    gain_one, shift_one, gain_two, shift_two = norm_rows(scales, width)
    start = lax.axis_index("head") * own
    device_row, device_head = place()

    def load(n):
        return pltpu.make_async_copy(rows.at[start + n], rows_in.at[n % 2], load_sem.at[n % 2])

    def exchange():
        return Exchange(
            left.at[pl.ds(0, own - 1)], right.at[pl.ds(0, own - 1)], left_stage, right_stage,
            left_plane, right_line, left_all, right_all, local_sem, send_sem, recv_sem,
        )

    def hop_copy(n):
        return pltpu.make_async_remote_copy(
            src_ref=update.at[n],
            dst_ref=hop_one.at[n],
            send_sem=hop_sem.at[0, n],
            recv_sem=hop_sem.at[1, n],
            device_id=(device_row, (device_head + 1) % 4),
            device_id_type=MESH,
        )

    @pl.when(row == 0)
    def _():
        load(0).start()
        if own > 1:
            load(1).start()
        if share:
            greet(
                [(flip(device_row, way), device_head) for way in range(1, 8)]
                + [(device_row, (device_head + k) % 4) for k in (1, 2, 3)]
            )
        key_mask = (residue[...] - 1.0) * (1e9 * LOG2E)
        key_mask = jnp.broadcast_to(key_mask, (8, residues)).T[:, :1]
        across, down, _, lines, cols = bias.shape
        group = max(1, 128 // lines)

        def turn(head, carry):
            for r in range(0, across, group):
                for c in range(down):
                    tile = jnp.concatenate([bias[r + g, c, head] for g in range(group)], axis=0)
                    bias_t[head, c * cols : (c + 1) * cols, r * lines : (r + group) * lines] = (
                        tile.T.astype(F32) + key_mask[c * cols : (c + 1) * cols]
                    )
            return carry

        lax.fori_loop(0, HEADS, turn, 0)

    load(row).wait()
    values_in = rows_in[row % 2]
    hat, _ = normalize(values_in)
    normed = (hat * gain_one + shift_one).astype(BF16)
    qkv[0, :width] = (dot(weights[0], normed, (1, 1)) * (size**-0.5 * LOG2E)).astype(BF16)
    qkv[0, width:] = dot(weights[1:3].reshape(2 * width, width), normed, (1, 1)).astype(BF16)
    gate[0] = jax.nn.sigmoid(dot(weights[3], normed, (1, 1)))
    for head in range(HEADS):
        at = head * size
        keys = qkv[0, width + at : width + at + size]
        values = qkv[0, 2 * width + at : 2 * width + at + size]
        query = qkv[0, at : at + size]
        scores = dot(keys, query, (0, 0)) + bias_t[head]
        exps = jnp.exp2(scores - jnp.max(scores, axis=0, keepdims=True))
        over = 1.0 / jnp.sum(exps, axis=0, keepdims=True)
        low = exps.astype(BF16)
        powers[0, head] = low
        inverse[0, head] = over
        mixed[0, at : at + size] = dot(values, low, (1, 0)) * over
        if share and head == HEADS // 2 - 1:
            @pl.when(row == own - 1)
            def _():
                exchange().go_on()
    att = (gate[0] * mixed[0]).astype(BF16)
    attended[0] = att
    change = dot(att, weights[4], (0, 0)).astype(BF16)
    update[row] = change
    hat, _ = normalize(rows_in[row % 2] + change.astype(F32))
    normed = hat * gain_two + shift_two
    put(second, normed)
    right[row] = (dot(outer_t[half:], normed.astype(BF16), (1, 1)) * (residue[...] * row_live[0][:, :1])).astype(BF16)
    out = jnp.zeros(flat_live.shape, F32)
    for q in range(QUADS):
        out += dot(take(second, q).astype(BF16), quad(outer_t, q), (1, 1))
    left[row] = (out * flat_live[...] * row_live[0]).astype(BF16)

    @pl.when(row + 2 < own)
    def _():
        load(row + 2).start()

    if share:
        @pl.when(row == own - 2)
        def _():
            exchange().begin()

        @pl.when(row < own // 2)
        def _():
            hop_copy(row).start()

        @pl.when(row == own - 1)
        def _():
            exchange().core()
            for n in range(own // 2):
                hop_copy(n).wait()
            exchange().end()


def attention_forward(rows, scales, weights, outer_t, bias, residue, row_live, flat_live, share):
    _, residues, width = rows.shape
    own = row_live.shape[0]
    sides = outer_t.shape[0] // 2
    by_row = lambda s: (s, 0, 0)
    by_row_four = lambda s: (s, 0, 0, 0)
    hbm = pl.BlockSpec(memory_space=pl.ANY)
    once = lambda array: pl.BlockSpec(array.shape, lambda s: (0,) * array.ndim, pipeline_mode=pl.Buffered(1))
    whole = lambda *shape: pl.BlockSpec(shape, lambda s: (0,) * len(shape))
    lines, cols = flat_live.shape[0] // 8, residues // 4
    early = own - 1
    out_specs = [
        whole(own, residues, width),
        whole(own, *flat_live.shape),
        whole(own, sides, residues),
        pl.BlockSpec((1, 3 * width, residues), by_row),
        pl.BlockSpec((1, width, residues), by_row),
        pl.BlockSpec((1, HEADS, residues, residues), by_row_four),
        pl.BlockSpec((1, HEADS, 1, residues), by_row_four),
        pl.BlockSpec((1, width, residues), by_row),
        pl.BlockSpec((1, width, residues), by_row),
    ]
    out_shape = [
        jax.ShapeDtypeStruct((own, residues, width), BF16),
        jax.ShapeDtypeStruct((own,) + flat_live.shape, BF16),
        jax.ShapeDtypeStruct((own, sides, residues), BF16),
        jax.ShapeDtypeStruct((own, 3 * width, residues), BF16),
        jax.ShapeDtypeStruct((own, width, residues), F32),
        jax.ShapeDtypeStruct((own, HEADS, residues, residues), BF16),
        jax.ShapeDtypeStruct((own, HEADS, 1, residues), F32),
        jax.ShapeDtypeStruct((own, width, residues), F32),
        jax.ShapeDtypeStruct((own, width, residues), BF16),
    ]
    scratch = [
        pltpu.VMEM((HEADS, residues, residues), F32),
        pltpu.VMEM((width // 128, residues, 128), F32),
        pltpu.VMEM((2, residues, width), F32),
        pltpu.SemaphoreType.DMA((2,)),
    ]
    params = dict(vmem_limit_bytes=VMEM)
    if share:
        params.update(collective_id=2, has_side_effects=True)
        out_specs += [hbm] * 3
        out_shape += [
            jax.ShapeDtypeStruct((4, 8, early, lines, 128), BF16),
            jax.ShapeDtypeStruct((8, 4, early, sides, cols), BF16),
            jax.ShapeDtypeStruct((own // 2, residues, width), BF16),
        ]
        scratch += [
            pltpu.VMEM((8, early, lines, 128), BF16),
            pltpu.VMEM((4, early, sides, cols), BF16),
            pltpu.VMEM((8, early, lines, 128), BF16),
            pltpu.VMEM((4, early, sides, cols), BF16),
            pltpu.SemaphoreType.DMA((2,)),
            pltpu.SemaphoreType.DMA((ROW_SENDS,)),
            pltpu.SemaphoreType.DMA((ROW_SENDS,)),
            pltpu.SemaphoreType.DMA((2, own // 2)),
        ]
    out = pl.pallas_call(
        functools.partial(forward_kernel, share=share),
        grid=(own,),
        in_specs=[
            hbm,
            once(scales),
            once(weights),
            once(outer_t),
            once(bias),
            once(residue),
            pl.BlockSpec((1, 1, 128), by_row),
            once(flat_live),
        ],
        out_specs=out_specs,
        scratch_shapes=scratch,
        out_shape=out_shape,
        cost_estimate=cost(30),
        compiler_params=pltpu.CompilerParams(**params),
    )(rows, scales, weights, outer_t, bias, residue, row_live, flat_live)
    return out[0], out[1], out[2], tuple(out[3:9]), tuple(out[9:])


def backward_kernel(*refs, earlier, adds):
    (order, rows, update, back, scales, weights, outer_w, left_grad, right_grad, residue, row_live, flat_live,
     qkv, gate, powers, inverse, mixed, attended), refs = refs[:18], refs[18:]
    if earlier:
        so_far, early, table_grad, base = refs[0], refs[1:5], refs[5], refs[6]
        pieces, refs = refs[7 : 7 + adds], refs[7 + adds :]
        added, part, bias_grad, packed, norms = refs[:5]
        bias_low, base_in, piece_in, load_sem, piece_sem, store_sem = refs[-6:]
        heads_in_grad, heads_out_grad, outer_in_grad = refs[-9:-6]
        refs = refs[5:-9]
    else:
        if adds:
            pairs, total, pairs_new = refs[0], refs[1], refs[8]
            pairs_new[...] = pairs[...] + total[...].astype(F32)
            refs = refs[2:8] + refs[9:]
        part, bias_grad, heads_in_grad, heads_out_grad, outer_in_grad, norms = refs[:6]
        refs = refs[6:]
    bias_total, mixed_grad, proj_grad, spread, bias_sem = refs
    row = pl.program_id(0)
    own = pl.num_programs(0)
    width = rows.shape[2]
    residues = rows.shape[1]
    size = width // HEADS
    last_row = row == own - 1
    rows_here = base.shape[0] if earlier else 0
    if earlier:
        per, each = base_in.shape[1:3]
        bounds = [0]
        for piece in pieces:
            bounds.append(bounds[-1] + piece.shape[0] // each)
        steps = bounds[-1]

        def bias_load(head):
            return pltpu.make_async_copy(so_far.at[head], bias_total.at[head], bias_sem.at[head])

        def row_of(step):
            return pl.ds(order[step * each], each)

        def fetch(batch, slot):
            for n in range(per):
                step = batch * per + n
                for piece in range(adds):
                    low, high = bounds[piece], bounds[piece + 1]

                    @pl.when((step >= low) & (step < high))
                    def _():
                        pltpu.make_async_copy(base.at[row_of(step)], base_in.at[slot, n], load_sem.at[slot, n]).start()
                        source = pieces[piece].at[pl.ds((step - low) * each, each)]
                        pltpu.make_async_copy(source, piece_in.at[slot, n], piece_sem.at[slot, n]).start()

        def store(batch, slot, n):
            return pltpu.make_async_copy(base_in.at[slot, n], added.at[row_of(batch * per + n)], store_sem.at[slot, n])

        def add_batch(batch, slot):
            for n in range(per):
                step = batch * per + n

                @pl.when((batch >= 1) & (step - per < steps))
                def _():
                    store(batch - 1, 1 - slot, n).wait()
            fetch(batch + 1, 1 - slot)
            for n in range(per):
                step = batch * per + n

                @pl.when(step < steps)
                def _():
                    pltpu.make_async_copy(base.at[row_of(step)], base_in.at[slot, n], load_sem.at[slot, n]).wait()
                    source = pieces[0].at[pl.ds(0, each)]
                    pltpu.make_async_copy(source, piece_in.at[slot, n], piece_sem.at[slot, n]).wait()
                    base_in[slot, n] = base_in[slot, n] + piece_in[slot, n].astype(F32)
                    store(batch, slot, n).start()

    @pl.when(row == 0)
    def _():
        for n, ref in enumerate((heads_in_grad, heads_out_grad, outer_in_grad, norms)):
            ref[...] = early[n][...] if earlier else jnp.zeros_like(ref)
        if earlier:
            for head in range(HEADS):
                bias_load(head).start()
            fetch(0, 0)

    half = outer_w.shape[0] // 2
    outer_t = outer_w[...].astype(BF16)
    gain_one, shift_one, gain_two, shift_two = norm_rows(scales, width)
    count = residues // QUADS
    hat, rstd = normalize(rows[0] + update[0].astype(F32))
    second = hat * gain_two + shift_two
    put(spread, second)
    grads = (right_grad[0].astype(F32) * (residue[...] * row_live[0][:, :1])).astype(BF16)
    outer_in_grad[half:] += dot(grads, second.astype(BF16), (1, 0))
    flat = (left_grad[0].astype(F32) * flat_live[...] * row_live[0]).astype(BF16).T
    for q in range(QUADS):
        mine = flat[q * half : (q + 1) * half]
        outer_in_grad[:half] += dot(mine, take(spread, q).astype(BF16), (1, 0))
        back_to = dot(mine, outer_t[:half], (0, 0))
        for n in range(spread.shape[0]):
            spread[n, pl.ds(q, count, stride=QUADS), :] = back_to[:, n * 128 : (n + 1) * 128]
    spread_grad = jnp.concatenate([spread[n] for n in range(spread.shape[0])], axis=1)
    second_grad = spread_grad + dot(grads, outer_t[half:], (0, 0))
    norms[2:3] += jnp.sum(second_grad * hat, axis=0, keepdims=True)
    norms[3:4] += jnp.sum(second_grad, axis=0, keepdims=True)
    new_part = norm_backward(hat, rstd, gain_two, second_grad)
    put(spread, new_part)
    out_grad = (back[0] + new_part).astype(BF16)
    heads_out_grad[...] += dot(attended[0], out_grad, (1, 0))
    attended_grad = dot(weights[4], out_grad, (1, 1))
    sig = gate[0]
    gated = attended_grad * sig
    proj_grad[3 * width :] = (gated * mixed[0] * (1.0 - sig)).astype(BF16)
    deltas = []
    for head in range(HEADS):
        span = slice(head * size, (head + 1) * size)
        grad = gated[span] * inverse[0, head]
        mixed_grad[span] = grad.astype(BF16)
        deltas.append(jnp.sum(grad * mixed[0, span], axis=0, keepdims=True))

    if earlier:
        @pl.when(row == 0)
        def _():
            for head in range(HEADS):
                bias_load(head).wait()

    for head in range(HEADS):
        at = head * size
        query = qkv[0, at : at + size]
        keys = qkv[0, width + at : width + at + size]
        values = qkv[0, 2 * width + at : 2 * width + at + size]
        grad = mixed_grad[at : at + size]
        low = powers[0, head]
        prob_grad = dot(values, grad, (0, 0))
        score_grad = low.astype(F32) * (prob_grad - deltas[head])
        if earlier:
            bias_total[head] += score_grad
        else:
            bias_total[head] = jnp.where(row == 0, 0.0, bias_total[head]) + score_grad
        score_low = score_grad.astype(BF16)
        proj_grad[2 * width + at : 2 * width + at + size] = dot(grad, low, (1, 1)).astype(BF16)
        proj_grad[width + at : width + at + size] = (dot(query, score_low, (1, 1)) / LOG2E).astype(BF16)
        proj_grad[at : at + size] = (dot(keys, score_low, (1, 0)) * size**-0.5).astype(BF16)
        if earlier and (head + 1) % per == 0:
            add_batch(row * (HEADS // per) + head // per, head // per % 2)
        if not earlier:
            @pl.when(last_row)
            def _():
                pltpu.make_async_copy(bias_total.at[head], bias_grad.at[head], bias_sem.at[head]).start()

    if earlier:
        @pl.when(last_row)
        def _():
            across, down, _, lines, cols = bias_grad.shape
            group = max(1, 128 // lines)
            for head in range(HEADS):
                for r in range(0, across, group):
                    for c in range(down):
                        tile = bias_total[head, c * cols : (c + 1) * cols, r * lines : (r + group) * lines]
                        tile = tile.T.astype(BF16)
                        for g in range(group):
                            bias_low[head, r + g, c] = tile[g * lines : (g + 1) * lines]
                pltpu.make_async_copy(bias_low.at[head], bias_grad.at[:, :, head], bias_sem.at[head]).start()

    hat, rstd = normalize(rows[0])
    normed = (hat * gain_one + shift_one).astype(BF16)
    grads = proj_grad[...]
    heads_in_grad[...] += dot(grads, normed, (1, 0))
    normed_grad = dot(grads, weights[:4].reshape(4 * width, width), (0, 0))
    norms[0:1] += jnp.sum(normed_grad * hat, axis=0, keepdims=True)
    norms[1:2] += jnp.sum(normed_grad, axis=0, keepdims=True)
    new_part = jnp.concatenate([spread[n] for n in range(spread.shape[0])], axis=1)
    part[0] = (new_part + norm_backward(hat, rstd, gain_one, normed_grad)).astype(BF16)

    @pl.when(last_row)
    def _():
        if earlier:
            first = 0
            for ref in (heads_in_grad, heads_out_grad, outer_in_grad):
                lines = ref.shape[0]
                packed[first : first + lines] = ref[:, :128].astype(BF16)
                packed[first + lines : first + 2 * lines] = ref[:, 128:].astype(BF16)
                first += 2 * lines
            lines = table_grad.shape[0]
            packed[first : first + lines] = table_grad[...].astype(BF16)
            first += lines
            packed[first:] = jnp.zeros((packed.shape[0] - first, 128), BF16)
            batch = rows_here // each // per - 1
            for n in range(per):
                if batch * per + n < steps:
                    store(batch, batch % 2, n).wait()
            for head in range(HEADS):
                pltpu.make_async_copy(bias_low.at[head], bias_grad.at[:, :, head], bias_sem.at[head]).wait()
        else:
            for head in range(HEADS):
                pltpu.make_async_copy(bias_total.at[head], bias_grad.at[head], bias_sem.at[head]).wait()


def attention_backward(
    order, rows, update, back, scales, weights, outer_t, left_grad, right_grad, residue, row_live, flat_live,
    kept, blocks, first, own, earlier=None, early=(), table_grad=None, pieces=(), pairs=(),
):
    _, residues, width = rows.shape
    qkv, gate, powers, inverse, mixed, attended = kept
    here = lambda s, order: (order[0] + first + s, 0, 0)
    by_row = lambda s, order: (first + s, 0, 0)
    by_row_four = lambda s, order: (first + s, 0, 0, 0)
    hbm = pl.BlockSpec(memory_space=pl.ANY)
    once = lambda array: pl.BlockSpec(
        array.shape, lambda s, order: (0,) * array.ndim, pipeline_mode=pl.Buffered(1)
    )
    whole = lambda array: pl.BlockSpec(array.shape, lambda s, order: (0,) * array.ndim)
    one = pl.BlockSpec((1, residues, width), here)
    args = [rows, update, back, scales, weights, outer_t, left_grad, right_grad, residue, row_live, flat_live]
    args += [qkv, gate, powers, inverse, mixed, attended]
    in_specs = [
        one,
        pl.BlockSpec((1, residues, width), by_row),
        one,
        once(scales),
        once(weights),
        once(outer_t),
        pl.BlockSpec((1,) + left_grad.shape[1:], by_row),
        pl.BlockSpec((1,) + right_grad.shape[1:], by_row),
        once(residue),
        pl.BlockSpec((1, 1, 128), by_row),
        once(flat_live),
        pl.BlockSpec((1, 3 * width, residues), by_row),
        pl.BlockSpec((1, width, residues), by_row),
        pl.BlockSpec((1, HEADS, residues, residues), by_row_four),
        pl.BlockSpec((1, HEADS, 1, residues), by_row_four),
        pl.BlockSpec((1, width, residues), by_row),
        pl.BlockSpec((1, width, residues), by_row),
    ]
    part = jax.ShapeDtypeStruct((own, residues, width), BF16)
    part_spec = pl.BlockSpec((1, residues, width), lambda s, order: (s, 0, 0))
    grads = [jax.ShapeDtypeStruct(shape, F32) for shape in ((4 * width, width), (width, width), outer_t.shape)]
    norms = jax.ShapeDtypeStruct((4, width), F32)
    scratch = [
        pltpu.VMEM((HEADS, residues, residues), F32),
        pltpu.VMEM((width, residues), BF16),
        pltpu.VMEM((4 * width, residues), BF16),
        pltpu.VMEM((width // 128, residues, 128), F32),
        pltpu.SemaphoreType.DMA((HEADS,)),
    ]
    if earlier is None:
        out_shape = [part, jax.ShapeDtypeStruct((HEADS, residues, residues), F32)] + grads + [norms]
        out_specs = [part_spec, hbm] + [whole(array) for array in grads + [norms]]
        if pairs:
            slab = pl.BlockSpec((pairs[0].shape[0] // own,) + pairs[0].shape[1:], lambda s, order: (s, 0, 0))
            args += pairs
            in_specs += [slab, slab]
            out_specs.append(slab)
            out_shape.append(jax.ShapeDtypeStruct(pairs[0].shape, F32))
    else:
        each = max(1, rows.shape[0] // (own * HEADS))
        args += [earlier, *early, table_grad, rows] + list(pieces)
        in_specs += [hbm] + [once(array) for array in [*early, table_grad]] + [hbm] * (1 + len(pieces))
        count = 2 * sum(array.shape[0] for array in grads) + table_grad.shape[0]
        count += -count % 512
        packed = jax.ShapeDtypeStruct((count, 128), BF16)
        out_shape = [jax.ShapeDtypeStruct(rows.shape, F32), part, jax.ShapeDtypeStruct(blocks, BF16), packed, norms]
        out_specs = [hbm, part_spec, hbm, whole(packed), whole(norms)]
        scratch += [pltpu.VMEM(array.shape, F32) for array in grads] + [
            pltpu.VMEM((HEADS,) + blocks[:2] + blocks[3:], BF16),
            pltpu.VMEM((2, HEADS // 2, each, residues, width), F32),
            pltpu.VMEM((2, HEADS // 2, each, residues, width), BF16),
            pltpu.SemaphoreType.DMA((2, HEADS // 2)),
            pltpu.SemaphoreType.DMA((2, HEADS // 2)),
            pltpu.SemaphoreType.DMA((2, HEADS // 2)),
        ]
    return pl.pallas_call(
        functools.partial(backward_kernel, earlier=earlier is not None, adds=len(pieces) + len(pairs)),
        grid_spec=pltpu.PrefetchScalarGridSpec(
            num_scalar_prefetch=1, grid=(own,), in_specs=in_specs, out_specs=out_specs, scratch_shapes=scratch
        ),
        out_shape=out_shape,
        compiler_params=pltpu.CompilerParams(vmem_limit_bytes=VMEM),
        cost_estimate=cost(20),
    )(order, *args)


def outer_product_plain(left, right, pairs_back, table, all_rows):
    low = pairs_back.astype(BF16)
    product = mm("sei,sfj->eifj", left, right).astype(BF16)
    total = mm("eifj,efz->ijz", product, table) / all_rows
    table_grad = mm("eifj,ijz->efz", product, low) / all_rows
    back = mm("ijz,efz->eifj", low, table).astype(BF16)
    left_grad = mm("eifj,sfj->sei", back, right) / all_rows
    right_grad = mm("eifj,sei->sfj", back, left) / all_rows
    return total, table_grad, left_grad.astype(BF16), right_grad.astype(BF16)


def mm(spec, a, b):
    return jnp.einsum(spec, a, b, preferred_element_type=F32)


def pair_forward(pairs, gain, shift, bias_low):
    hat, _ = normalize(pairs)
    low = (hat * gain + shift).astype(BF16)
    return (mm("ijc,ch->hij", low, bias_low) * LOG2E).astype(BF16)


def pair_backward(pairs, pairs_back, gain, shift, bias_low, bias_grad):
    hat, rstd = normalize(pairs)
    low = (hat * gain + shift).astype(BF16)
    weight_grad = mm("ijc,hij->ch", low, bias_grad)
    in_grad = mm("hij,ch->ijc", bias_grad, bias_low)
    gain_grad = jnp.sum(in_grad * hat, axis=(0, 1))
    shift_grad = jnp.sum(in_grad, axis=(0, 1))
    return pairs_back + norm_backward(hat, rstd, gain, in_grad), weight_grad, gain_grad, shift_grad


MESH = pl.DeviceIdType.MESH
CORE, ACROSS, DOWN, CORNER = 1, 2, 4, 6


def place():
    return lax.axis_index("row"), lax.axis_index("head")


def flip(row, way):
    out = row
    for bit in (1, 2, 4):
        if way & bit:
            out = out + bit - 2 * bit * ((row // bit) % 2)
    return out


def greet(devices):
    barrier = pltpu.get_barrier_semaphore()
    for device in devices:
        pl.semaphore_signal(barrier, inc=1, device_id=device, device_id_type=MESH)
    pl.semaphore_wait(barrier, len(devices))


class Sends:
    def __init__(self, send_sem, recv_sem):
        self.send_sem, self.recv_sem, self.count, self.open = send_sem, recv_sem, 0, []

    def start(self, source, target, device):
        copy = pltpu.make_async_remote_copy(
            src_ref=source,
            dst_ref=target,
            send_sem=self.send_sem.at[self.count],
            recv_sem=self.recv_sem.at[self.count],
            device_id=device,
            device_id_type=MESH,
        )
        copy.start()
        self.count += 1
        self.open.append(copy)
        return copy

    def finish(self):
        for copy in self.open:
            copy.wait_send()


PARTS = 2
GATHER_SENDS = 6 + PARTS * (3 + 12 + 16)


def pair_bias_kernel(
    pairs, norm, weight, heads_in, heads_out, bias, weights, values_in, shard, block, low,
    load_sem, local_sem, send_sem, recv_sem,
):
    row, head = place()
    rows, cols, channels = pairs.shape
    part = shard.shape[1] // 2
    core = row % 2
    lines = rows // PARTS
    loads = []
    for n in range(PARTS):
        at = pl.ds(n * lines, lines)
        loads.append(pltpu.make_async_copy(pairs.at[at], values_in.at[at], load_sem.at[n]))
        loads[n].start()
    shard[:4] = heads_in[...].astype(BF16)
    shard[4] = heads_out[...].astype(BF16)
    beyond = [(head + k) % 4 for k in range(4)]
    behind = [(head + 4 - k) % 4 for k in range(4)]
    across, down, other = (flip(row, ACROSS), head), (flip(row, DOWN), head), (flip(row, CORE), head)
    greet([across, down, other] + [(row, beyond[k]) for k in (1, 2, 3)])
    sends = Sends(send_sem, recv_sem)

    def own_part(at, side):
        return weights.at[:, pl.ds(pl.multiple_of(at * 2 * part + side * part, part), part), :]

    keep = pltpu.make_async_copy(
        shard, weights.at[:, pl.ds(pl.multiple_of(head * 2 * part, 2 * part), 2 * part), :], local_sem.at[PARTS]
    )
    keep.start()
    step = 8
    first_pair = norm.shape[1] - channels
    gain, shift = norm[0:1, first_pair:], norm[1:2, first_pair:]
    low_weight = weight[...].astype(BF16)

    def norm_block(n, carry):
        first = pl.multiple_of(n * step, step)
        values = values_in[pl.ds(first, step)].reshape(step * cols, channels)
        center = values - jnp.mean(values, axis=-1, keepdims=True)
        rstd = lax.rsqrt(jnp.mean(center * center, axis=-1, keepdims=True) + 1e-05)
        normed = (center * rstd * gain + shift).astype(BF16)
        out = lax.dot_general(low_weight, normed, (((1,), (1,)), ((), ())), preferred_element_type=F32)
        for i in range(step):
            block[:, pl.ds(first + i, 1), :] = (out[:, i * cols : (i + 1) * cols] * LOG2E).reshape(
                HEADS, 1, cols
            )
        return carry

    ends, mine = [], []

    class Part:
        def __init__(self, n):
            self.at = pl.ds(n * lines, lines)
            loads[n].wait()
            lax.fori_loop(n * lines // step, (n + 1) * lines // step, norm_block, 0)
            low[n] = block[:, n * lines : (n + 1) * lines].astype(BF16)
            self.own = low.at[n]
            copy = pltpu.make_async_copy(self.own, self.slot(row, 0), local_sem.at[n])
            copy.start()
            mine.append(copy)
            self.along = [None] + [
                sends.start(self.own, self.slot(row, 0), (row, beyond[k])) for k in (1, 2, 3)
            ]
            self.across, self.down, self.corner = [None] * 4, [None] * 4, [None] * 4
            self.spread(0)

        def slot(self, at, k):
            return bias.at[at, behind[k], :, self.at]

        def spread(self, k):
            if k:
                self.along[k].wait_recv()
            here = self.slot(row, k)
            source = here if k else self.own
            self.across[k] = sends.start(source, here, across)
            self.down[k] = sends.start(source, here, down)
            ends.append(sends.start(source, here, other))

        def relay(self, k):
            self.across[k].wait_recv()
            here = self.slot(flip(row, ACROSS), k)
            if k < 2:
                self.corner[k] = sends.start(here, here, down)
            ends.append(sends.start(here, here, other))
            self.down[k].wait_recv()
            here = self.slot(flip(row, DOWN), k)
            if k >= 2:
                self.corner[k] = sends.start(here, here, across)
            ends.append(sends.start(here, here, other))

        def finish(self, k):
            self.corner[k].wait_recv()
            here = self.slot(flip(row, CORNER), k)
            ends.append(sends.start(here, here, other))

    parts = [Part(n) for n in range(PARTS)]
    half = shard.at[:, pl.ds(pl.multiple_of(core * part, part), part), :]
    shards = [None] + [sends.start(half, own_part(head, core), (row, beyond[k])) for k in (1, 2, 3)]
    for k in range(4):
        for one in parts:
            if k:
                one.spread(k)
                one.relay(k - 1)
    for one in parts:
        one.relay(3)
    for k in range(4):
        for one in parts:
            one.finish(k)
    for k in (1, 2, 3):
        shards[k].wait_recv()
        piece = own_part(behind[k], core)
        ends.append(sends.start(piece, piece, other))
    for copy in ends:
        copy.wait_recv()
    sends.finish()
    keep.wait()
    for copy in mine:
        copy.wait()


def pair_bias(pairs, norm, weight, heads_in, heads_out):
    rows, cols, channels = pairs.shape
    vmem = pl.BlockSpec(memory_space=pltpu.VMEM)
    hbm = pl.BlockSpec(memory_space=pl.ANY)
    shard = (heads_in.shape[0] + 1,) + heads_out.shape
    return pl.pallas_call(
        pair_bias_kernel,
        out_shape=[
            jax.ShapeDtypeStruct((8, 4, HEADS, rows, cols), BF16),
            jax.ShapeDtypeStruct((shard[0], 4 * shard[1], shard[2]), BF16),
        ],
        in_specs=[hbm, vmem, vmem, vmem, vmem],
        out_specs=[hbm, hbm],
        scratch_shapes=[
            pltpu.VMEM(pairs.shape, F32),
            pltpu.VMEM(shard, BF16),
            pltpu.VMEM((HEADS, rows, cols), F32),
            pltpu.VMEM((PARTS, HEADS, rows // PARTS, cols), BF16),
            pltpu.SemaphoreType.DMA((PARTS,)),
            pltpu.SemaphoreType.DMA((PARTS + 1,)),
            pltpu.SemaphoreType.DMA((GATHER_SENDS,)),
            pltpu.SemaphoreType.DMA((GATHER_SENDS,)),
        ],
        compiler_params=pltpu.CompilerParams(
            collective_id=0, has_side_effects=True, vmem_limit_bytes=VMEM
        ),
        cost_estimate=cost(34),
    )(pairs, norm, weight, heads_in, heads_out)


OUTER_SENDS = 2 + 3 + 7 + 1 + 3 + 3


def outer_kernel(
    left, right, left_early, right_early, pairs_back, outer_out, update, hop_early,
    total, left_out, right_out, table_grad, hop_one, hop_two,
    left_stage, right_stage, left_plane, right_line, left_all, right_all, left_last, right_last, left_wide, right_wide, left_rows, right_rows,
    backed, product, back, low, table, table_t, total_low,
    left_part, right_part, left_send, right_send, right_core, chip_sum, right_in, right_sum, left_line, left_sum, left_land, right_land,
    load_sem, local_sem, out_sem, row_local, row_send, row_recv, send_sem, recv_sem,
    *, scale, block, group,
):
    row, head = place()
    beyond = [(head + k) % 4 for k in range(4)]
    plane = [(flip(row, way), head) for way in range(8)]
    core, chip = row % 2, row // 2
    own, wide, _ = right.shape
    rows, cols, channels = back.shape
    size = wide
    lines = left_all.shape[3]
    chunks = rows // block
    half, most = own // 2, own - 1
    greet(plane[1:] + [(row, beyond[k]) for k in (1, 2, 3)])
    sends = Sends(send_sem, recv_sem)
    sides = Exchange(
        left.at[pl.ds(most, own - most)], right.at[pl.ds(most, own - most)], left_stage, right_stage,
        left_plane, right_line, left_last, right_last, row_local, row_send, row_recv,
    )
    sides.begin()
    gather = [
        pltpu.make_async_copy(left_early, left_all, local_sem.at[0]),
        pltpu.make_async_copy(right_early, right_all, local_sem.at[1]),
    ]
    loads = []
    for n in range(chunks):
        copy = pltpu.make_async_copy(
            pairs_back.at[pl.ds(n * block, block)], back.at[pl.ds(n * block, block)], load_sem.at[n]
        )
        copy.start()
        loads.append(copy)
    for copy in gather:
        copy.start()

    for f in range(wide):
        table[f * size : (f + 1) * size] = outer_out[pl.ds(f, size, stride=wide), :].astype(BF16)
    for n in range(wide * size // 128):
        table_t[:, n * 128 : (n + 1) * 128] = table[n * 128 : (n + 1) * 128].T

    def spread_pair(p, carry):
        first = p * group
        both = back[pl.ds(first, group)].astype(BF16)
        low[pl.ds(first, group)] = both
        spread = dot(table[...], both.reshape(group * cols, channels), (1, 1)).astype(BF16)
        for g in range(group):
            at = pl.ds(pl.multiple_of((first + g) * size, size), size)
            for f in range(wide):
                backed[at, f * cols : (f + 1) * cols] = spread[
                    f * size : (f + 1) * size, g * cols : (g + 1) * cols
                ]
        return carry

    pairs_of = rows // group

    def spread_part(k):
        for n in range(k * chunks // 4, (k + 1) * chunks // 4):
            loads[n].wait()
        lax.fori_loop(k * pairs_of // 4, (k + 1) * pairs_of // 4, spread_pair, 0)

    spread_part(0)
    sides.go_on()
    hops = [
        sends.start(update.at[pl.ds(half, own - half)], hop_one, (row, beyond[1])),
        sends.start(hop_early, hop_two, (row, beyond[1])),
    ]
    spread_part(1)
    spread_part(2)
    sides.core()
    spread_part(3)
    sides.end()
    for copy in gather:
        copy.wait()

    count = 32
    for r in range(8):
        for h in range(4):
            left_wide[r * 4 + h, :most] = left_all[h, r].astype(F32)
            left_wide[r * 4 + h, most:] = left_last[h, r].astype(F32)
    right_wide[:, :most] = right_all[...].astype(F32).reshape((count, most) + right_wide.shape[2:])
    right_wide[:, most:] = right_last[...].astype(F32).reshape((count, own - most) + right_wide.shape[2:])
    for s in range(own):
        at = slice(s * count, (s + 1) * count)
        for n in range(lines):
            left_rows[at, n * 128 : (n + 1) * 128] = left_wide[:, s, n, :].astype(BF16)
        for f in range(wide):
            right_rows[at, f * cols : (f + 1) * cols] = right_wide[:, s, f, :].astype(BF16)

    deep = block * size

    def left_step(n, carry):
        at = pl.ds(pl.multiple_of(n * deep, deep), deep)
        left_part[:, at] = dot(right_rows[...], backed[at, :], (1, 1)) * scale
        return carry

    lax.fori_loop(0, chunks, left_step, 0)
    for s in range(own):
        at = slice(s * count, (s + 1) * count)
        for n in range(lines):
            left_wide[:, s, n, :] = left_part[at, n * 128 : (n + 1) * 128]
    for r in range(8):
        for h in range(4):
            left_send[h, r] = left_wide[r * 4 + h].astype(BF16)
    lefts = [
        sends.start(left_send.at[beyond[k]], left_line.at[k - 1], (row, beyond[k])) for k in (2, 1, 3)
    ]
    step = 4 * cols

    def right_step(n, carry):
        at = pl.ds(pl.multiple_of(n * step, step), step)
        right_part[:, at] = dot(left_rows[...], backed[:, at], (1, 0)) * scale
        return carry

    lax.fori_loop(0, wide * cols // step, right_step, 0)
    for s in range(own):
        at = slice(s * count, (s + 1) * count)
        for f in range(wide):
            right_wide[:, s, f, :] = right_part[at, f * cols : (f + 1) * cols]
    right_send[...] = right_wide[...].astype(BF16).reshape(right_send.shape)
    swap = sends.start(right_send.at[:, 1 - core], right_core, plane[CORE])
    table_grad[...] = jnp.zeros_like(table_grad)

    def outer_chunk(n, carry):
        at = pl.ds(pl.multiple_of(n * deep, deep), deep)
        product[...] = dot(left_rows[:, at], right_rows[...], (0, 0)).astype(BF16)
        for first in range(0, block, group):
            both = jnp.concatenate(
                [
                    jnp.concatenate(
                        [
                            product[(first + g) * size : (first + g + 1) * size, f * cols : (f + 1) * cols]
                            for f in range(wide)
                        ],
                        axis=0,
                    )
                    for g in range(group)
                ],
                axis=1,
            )
            out = dot(table_t[...], both, (1, 0)) * scale
            for g in range(group):
                total_low[n * block + first + g] = out[:, g * cols : (g + 1) * cols].T.astype(BF16)
            seen = low[pl.ds(n * block + first, group)].reshape(group * cols, channels)
            table_grad[...] += dot(both, seen, (1, 0)) * scale
        return carry

    stores = []

    def outer_part(n):
        first, last = n * chunks // 4, (n + 1) * chunks // 4
        lax.fori_loop(first, last, outer_chunk, 0)
        at = pl.ds(first * block, (last - first) * block)
        copy = pltpu.make_async_copy(total_low.at[at], total.at[at], out_sem.at[n])
        copy.start()
        stores.append(copy)

    swap.wait_recv()
    rights = []
    for slot, way in enumerate((CORNER, ACROSS, DOWN)):
        n = plane[way][0] // 2
        for h in range(4):
            chip_sum[slot, h] = (
                right_send[n, core, h].astype(F32) + right_core[n, h].astype(F32)
            ).astype(BF16)
        rights.append(sends.start(chip_sum.at[slot], right_in.at[slot], plane[way]))
    outer_part(0)
    for copy in lefts:
        copy.wait_recv()
    for r in range(8):
        summed = left_send[head, r].astype(F32)
        for k in range(3):
            summed = summed + left_line[k, r].astype(F32)
        left_sum[r] = summed.astype(BF16)
    across = [
        sends.start(left_sum.at[plane[way][0]], left_land.at[row], plane[way])
        for way in (2, 4, 6, 3, 5, 7, 1)
    ]
    left_land[row] = left_sum[row]
    outer_part(1)
    for copy in rights:
        copy.wait_recv()
    for h in range(4):
        summed = right_send[chip, core, h].astype(F32) + right_core[chip, h].astype(F32)
        for slot in range(3):
            summed = summed + right_in[slot, h].astype(F32)
        right_sum[h] = summed.astype(BF16)
    line = [
        sends.start(right_sum.at[beyond[k]], right_land.at[head], (row, beyond[k])) for k in (1, 2, 3)
    ]
    right_land[head] = right_sum[head]
    outer_part(2)
    outer_part(3)
    for copy in across + line:
        copy.wait_recv()
    for r in range(8):
        left_out[:, r * lines : (r + 1) * lines, :] = left_land[r]
    for h in range(4):
        right_out[:, :, h * cols : (h + 1) * cols] = right_land[h]
    for copy in hops:
        copy.wait_recv()
    sends.finish()
    for copy in stores:
        copy.wait()


def outer_product(left, right, early, pairs_back, outer_out, update, all_rows, block=8, group=2):
    left_early, right_early, hop_early = early
    rows, cols, channels = pairs_back.shape
    own, wide, residues = right.shape
    size = left.shape[1] * left.shape[2] // residues
    lines = left.shape[1] // 8
    vmem = pl.BlockSpec(memory_space=pltpu.VMEM)
    hbm = pl.BlockSpec(memory_space=pl.ANY)
    low = lambda *shape: pltpu.VMEM(shape, BF16)
    full = lambda *shape: pltpu.VMEM(shape, F32)
    one = (lines, 128)
    other = (wide, cols)
    rest = 1
    dma = pltpu.SemaphoreType.DMA
    return pl.pallas_call(
        functools.partial(outer_kernel, scale=1.0 / all_rows, block=block, group=group),
        out_shape=[
            jax.ShapeDtypeStruct(pairs_back.shape, BF16),
            jax.ShapeDtypeStruct(left.shape, BF16),
            jax.ShapeDtypeStruct(right.shape, BF16),
            jax.ShapeDtypeStruct((wide * size, channels), F32),
            jax.ShapeDtypeStruct((own - own // 2,) + update.shape[1:], BF16),
            jax.ShapeDtypeStruct(hop_early.shape, BF16),
        ],
        in_specs=[vmem, vmem, hbm, hbm, hbm, vmem, hbm, hbm],
        out_specs=[hbm, vmem, vmem, vmem, hbm, hbm],
        scratch_shapes=[
            low(8, rest, *one), low(4, rest, *other), low(8, rest, *one), low(4, rest, *other),
            low(4, 8, own - rest, *one), low(8, 4, own - rest, *other),
            low(4, 8, rest, *one), low(8, 4, rest, *other), full(32, own, *one), full(32, own, *other),
            low(all_rows, rows * size), low(all_rows, wide * cols),
            low(rows * size, wide * cols), low(block * size, wide * cols), full(rows, cols, channels),
            low(rows, cols, channels), low(wide * size, channels), low(channels, wide * size), low(rows, cols, channels),
            full(all_rows, rows * size), full(all_rows, wide * cols), low(4, 8, own, *one), low(4, 2, 4, own, *other),
            low(4, 4, own, *other), low(3, 4, own, *other), low(3, 4, own, *other), low(4, own, *other),
            low(3, 8, own, *one), low(8, own, *one), low(8, own, *one), low(4, own, *other),
            dma((rows // block,)), dma((2,)), dma((4,)), dma((2,)), dma((ROW_SENDS,)), dma((ROW_SENDS,)),
            dma((OUTER_SENDS,)), dma((OUTER_SENDS,)),
        ],
        compiler_params=pltpu.CompilerParams(
            collective_id=1, has_side_effects=True, vmem_limit_bytes=VMEM
        ),
        cost_estimate=cost(50),
    )(left, right, left_early, right_early, pairs_back, outer_out, update, hop_early)


SUM_SENDS = 4 + 4 + 8 + 3 + 1 + 3 + 3 + 3 + 12 + 16


def sum_kernel(
    grads, parts, out, spread,
    swapped, chip_sum, by_across, by_down, from_across, from_down, down_sum, line_in,
    part_swapped, part_sum, part_plane, part_down, part_line, piece,
    local_sem, send_sem, recv_sem,
):
    row, head = place()
    beyond = [(head + k) % 4 for k in range(4)]
    core, chip = row % 2, row // 2
    ways = (CORNER, ACROSS, DOWN)
    plane = [(flip(row, way), head) for way in range(8)]
    other, across, down = plane[CORE], plane[ACROSS], plane[DOWN]
    greet([plane[way] for way in (CORE,) + ways] + [(row, beyond[k]) for k in (1, 2, 3)])
    sends = Sends(send_sem, recv_sem)
    chips = [plane[way][0] // 2 for way in ways] + [chip]
    part_swap = sends.start(parts.at[1 - core], part_swapped, other)
    swaps = [sends.start(grads.at[n, 1 - core], swapped.at[slot], other) for slot, n in enumerate(chips)]
    first, second = (2, 1), (3, 0)

    def add(slot, k):
        z = beyond[k]
        chip_sum[slot, k] = (
            grads[chips[slot], core, z].astype(F32) + swapped[slot, z].astype(F32)
        ).astype(BF16)

    part_swap.wait_recv()
    part_arrive = []
    for slot, n in enumerate(chips):
        for z in range(4):
            part_sum[slot, z] = (parts[core, n, z].astype(F32) + part_swapped[n, z].astype(F32)).astype(BF16)
        if slot < 3:
            part_arrive.append(sends.start(part_sum.at[slot], part_plane.at[slot], plane[ways[slot]]))
    swaps[0].wait_recv()
    relays_across, relays_down = [], []
    for n in range(2):
        add(0, first[n])
        relays_across.append(sends.start(chip_sum.at[0, first[n]], by_across.at[n], across))
        add(0, second[n])
        relays_down.append(sends.start(chip_sum.at[0, second[n]], by_down.at[n], down))
    last_across, last_down = [None] * 4, [None] * 4
    swaps[1].wait_recv()
    for k in first:
        add(1, k)
        last_across[k] = sends.start(chip_sum.at[1, k], from_across.at[k], across)
    swaps[2].wait_recv()
    for k in second:
        add(2, k)
        last_down[k] = sends.start(chip_sum.at[2, k], from_down.at[k], down)
    for n in range(2):
        add(1, second[n])
        add(2, first[n])
        relays_across[n].wait_recv()
        k = first[n]
        chip_sum[2, k] = (chip_sum[2, k].astype(F32) + by_across[n].astype(F32)).astype(BF16)
        last_down[k] = sends.start(chip_sum.at[2, k], from_down.at[k], down)
        relays_down[n].wait_recv()
        k = second[n]
        chip_sum[1, k] = (chip_sum[1, k].astype(F32) + by_down[n].astype(F32)).astype(BF16)
        last_across[k] = sends.start(chip_sum.at[1, k], from_across.at[k], across)
    for copy in part_arrive:
        copy.wait_recv()
    for z in range(4):
        total = part_sum[3, z].astype(F32)
        for slot in range(3):
            total = total + part_plane[slot, z].astype(F32)
        part_down[z] = total.astype(BF16)
    part_arrive = [
        sends.start(part_down.at[beyond[k]], part_line.at[k - 1], (row, beyond[k])) for k in (1, 2, 3)
    ]
    swaps[3].wait_recv()
    for k in first + second:
        add(3, k)
    total = part_down[head].astype(F32)
    for slot, copy in enumerate(part_arrive):
        copy.wait_recv()
        total = total + part_line[slot].astype(F32)
    piece[...] = total.astype(BF16)
    behind = [(head + 4 - k) % 4 for k in range(4)]
    part_line_all = [None] + [sends.start(piece, spread.at[core, chip, head], (row, beyond[k])) for k in (1, 2, 3)]
    mine = pltpu.make_async_copy(piece, spread.at[core, chip, head], local_sem)
    mine.start()
    wide, end = [], []

    def forward(k):
        here = spread.at[core, chip, behind[k]]
        source = here if k else piece
        for way in ways:
            wide.append((plane[way][0] // 2, k, sends.start(source, here, plane[way])))
        end.append(sends.start(source, here, other))

    forward(0)
    line = []
    for k in first + second:
        last_across[k].wait_recv()
        last_down[k].wait_recv()
        total = chip_sum[3, k].astype(F32) + from_across[k].astype(F32) + from_down[k].astype(F32)
        if k:
            down_sum[k - 1] = total.astype(BF16)
            line.append(sends.start(down_sum.at[k - 1], line_in.at[k - 1], (row, beyond[k])))
        else:
            out[...] = total
        if k == first[0]:
            for n in (1, 2, 3):
                part_line_all[n].wait_recv()
                forward(n)
    for n, k, copy in wide:
        copy.wait_recv()
        block = spread.at[core, n, behind[k]]
        end.append(sends.start(block, block, other))
    for slot, copy in zip((1, 0, 2), line):
        copy.wait_recv()
        out[...] += line_in[slot].astype(F32)
    for copy in end:
        copy.wait_recv()
    mine.wait()
    sends.finish()


def sum_gradients(grads, parts):
    block = grads.shape[2:]
    lines = block[0] * block[1]
    rows, cols = parts.shape
    share = rows // 32
    vmem = pl.BlockSpec(memory_space=pltpu.VMEM)
    wide = lambda *first: pltpu.VMEM(first + (lines, block[2]), BF16)
    thin = lambda *first: pltpu.VMEM(first + (share, cols), BF16)
    out, spread = pl.pallas_call(
        sum_kernel,
        out_shape=[
            jax.ShapeDtypeStruct((lines, block[2]), F32),
            jax.ShapeDtypeStruct((2, 4, 4, share, cols), BF16),
        ],
        in_specs=[vmem, vmem],
        out_specs=[vmem, vmem],
        scratch_shapes=[
            wide(4, 4), wide(4, 4), wide(2), wide(2), wide(4), wide(4), wide(3), wide(3),
            thin(4, 4), thin(4, 4), thin(3, 4), thin(4), thin(3), thin(),
            pltpu.SemaphoreType.DMA,
            pltpu.SemaphoreType.DMA((SUM_SENDS,)),
            pltpu.SemaphoreType.DMA((SUM_SENDS,)),
        ],
        compiler_params=pltpu.CompilerParams(
            collective_id=3, has_side_effects=True, vmem_limit_bytes=VMEM
        ),
        cost_estimate=cost(40),
    )(grads.reshape(4, 2, 4, lines, block[2]), parts.reshape(2, 4, 4, share, cols))
    return out.reshape(block), spread.reshape(rows, cols)


SMALL_SENDS = 3 + 7


def small_kernel(small, total, line_in, line_sum, plane_in, send_sem, recv_sem):
    row, head = place()
    line = [(row, (head + k) % 4) for k in (1, 2, 3)]
    plane = [(flip(row, way), head) for way in range(1, 8)]
    greet(plane + line)
    sends = Sends(send_sem, recv_sem)
    arrive = [sends.start(small, line_in.at[head], device) for device in line]
    line_in[head] = small[...]
    for copy in arrive:
        copy.wait_recv()
    line_sum[...] = (line_in[0] + line_in[1]) + (line_in[2] + line_in[3])
    arrive = [sends.start(line_sum, plane_in.at[row], device) for device in plane]
    plane_in[row] = line_sum[...]
    for copy in arrive:
        copy.wait_recv()
    summed = plane_in[0]
    for n in range(1, 8):
        summed = summed + plane_in[n]
    total[...] = summed
    sends.finish()


def small_sum(small):
    vmem = pl.BlockSpec(memory_space=pltpu.VMEM)
    return pl.pallas_call(
        small_kernel,
        out_shape=jax.ShapeDtypeStruct(small.shape, F32),
        in_specs=[vmem],
        out_specs=vmem,
        scratch_shapes=[
            pltpu.VMEM((4,) + small.shape, F32),
            pltpu.VMEM(small.shape, F32),
            pltpu.VMEM((8,) + small.shape, F32),
            pltpu.SemaphoreType.DMA((SMALL_SENDS,)),
            pltpu.SemaphoreType.DMA((SMALL_SENDS,)),
        ],
        compiler_params=pltpu.CompilerParams(
            collective_id=4, has_side_effects=True, vmem_limit_bytes=VMEM
        ),
        cost_estimate=cost(9),
    )(small)


def add_pieces(step, base, pieces, out):
    for n, piece in enumerate(pieces):
        @pl.when(step == n)
        def _():
            out[...] = base[...] + piece[...].astype(F32)


def added_specs(base, pieces):
    block = pieces[0].shape
    by_order = pl.BlockSpec(
        block, lambda n, order: (order[jnp.minimum(n, len(pieces) - 1) * block[0]] // block[0], 0, 0)
    )
    return by_order, [by_order] + [pl.BlockSpec(block, lambda n, order: (0, 0, 0))] * len(pieces)


def pair_backward_kernel(order, pairs, back, grads, norm, weight, norms, base, *refs):
    pieces, (out, small, changed) = refs[:-3], refs[-3:]
    step = pl.program_id(0)
    rows, cols, channels = pairs.shape
    add_pieces(step, base, pieces, changed)

    @pl.when(step == 0)
    def _():
        small[...] = jnp.zeros_like(small)
        small[2 * HEADS :] = jnp.concatenate([norms[:, :128], norms[:, 128:]], axis=0)

    values = pairs[...].reshape(rows * cols, channels)
    hat, rstd = normalize(values)
    gain, shift = norm[0:1, norm.shape[1] - channels :], norm[1:2, norm.shape[1] - channels :]
    low = (hat * gain + shift).astype(BF16)
    bias = jnp.concatenate([grads[:, i, :] for i in range(rows)], axis=1).astype(BF16)
    small[0:HEADS] += dot(bias, low, (1, 0))
    in_grad = dot(bias, weight[...].astype(BF16), (0, 0))
    small[HEADS : HEADS + 1] += jnp.sum(in_grad * hat, axis=0, keepdims=True)
    small[HEADS + 1 : HEADS + 2] += jnp.sum(in_grad, axis=0, keepdims=True)
    change = norm_backward(hat, rstd, gain, in_grad)
    out[...] = back[...] + change.reshape(rows, cols, channels)


def pair_norm_backward(order, pairs, back, grads, norm, weight, norms, base, pieces, steps=8):
    rows, cols, channels = pairs.shape
    block = rows // steps
    by_row = lambda n, order: (n, 0, 0)
    whole = lambda n, order: (0, 0)
    by_order, added = added_specs(base, pieces)
    grads = grads.reshape(HEADS, steps, block, cols)
    return pl.pallas_call(
        pair_backward_kernel,
        grid_spec=pltpu.PrefetchScalarGridSpec(
            num_scalar_prefetch=1,
            grid=(steps,),
            in_specs=[
                pl.BlockSpec((block, cols, channels), by_row),
                pl.BlockSpec((block, cols, channels), by_row),
                pl.BlockSpec((HEADS, None, block, cols), lambda n, order: (0, n, 0, 0)),
                pl.BlockSpec(norm.shape, whole),
                pl.BlockSpec(weight.shape, whole),
                pl.BlockSpec(norms.shape, whole),
            ]
            + added,
            out_specs=[
                pl.BlockSpec((block, cols, channels), by_row),
                pl.BlockSpec((3 * HEADS, channels), whole),
                by_order,
            ],
        ),
        out_shape=[
            jax.ShapeDtypeStruct(pairs.shape, F32),
            jax.ShapeDtypeStruct((3 * HEADS, channels), F32),
            jax.ShapeDtypeStruct(base.shape, F32),
        ],
        compiler_params=pltpu.CompilerParams(vmem_limit_bytes=VMEM),
        cost_estimate=cost(9),
    )(order, pairs, back, grads, norm, weight, norms, base, *pieces)


def add_kernel(place_ref, base, piece, *refs):
    refs[-1][...] = base[...] + piece[...].astype(F32)


def add_rows(at, base, piece, into=None):
    own = piece.shape[0]
    block = (1,) + piece.shape[1:]
    spread = lambda n, at: (at[0] * own + n, 0, 0)
    return pl.pallas_call(
        add_kernel,
        grid_spec=pltpu.PrefetchScalarGridSpec(
            num_scalar_prefetch=1,
            grid=(own,),
            in_specs=[pl.BlockSpec(block, spread), pl.BlockSpec(block, lambda n, at: (n, 0, 0))]
            + ([] if into is None else [pl.BlockSpec(memory_space=pl.ANY)]),
            out_specs=pl.BlockSpec(block, spread),
        ),
        out_shape=jax.ShapeDtypeStruct(base.shape, F32),
        input_output_aliases={} if into is None else {3: 0},
        cost_estimate=cost(2),
    )(*((at, base, piece) if into is None else (at, base, piece, into)))


def hop(piece):
    count = lax.axis_size("head")
    return lax.ppermute(piece, "head", [(i, (i + 1) % count) for i in range(count)])


def together(moved, *values):
    return lax.optimization_barrier((moved,) + values)


def adam_kernel(at, packed, pair_side, *refs, rates, pieces):
    olds, base, adds, news = refs[:18], refs[18], refs[19 : 19 + pieces], refs[20 + pieces : 38 + pieces]
    changed, table = refs[38 + pieces :]
    step = pl.program_id(0)
    add_pieces(step, base, adds, changed)

    @pl.when(step == 0)
    def _():
        adam_step(at, packed, pair_side, olds, news, table, rates)


def adam_step(at, packed, pair_side, olds, news, table, rates):
    norms, heads_in, heads_out, bias_weight, outer_in, outer_out = [olds[3 * n : 3 * n + 3] for n in range(6)]
    count, local, all_heads = heads_in[0].shape
    sides, size = outer_in[0].shape[:2]

    def rows(first, lines):
        return packed[pl.ds(first, lines), :].astype(F32)

    def pair_of(first, offset, lines, span):
        return jnp.concatenate([rows(first + offset, lines), rows(first + span + offset, lines)], axis=1)

    def update(n, index, grad):
        weight, moment_one, moment_two = [ref[index] for ref in olds[3 * n : 3 * n + 3]]
        for ref, new in zip(
            news[3 * n : 3 * n + 3], adam_update(weight, grad, moment_one, moment_two, rates[n])
        ):
            ref[index] = new

    mine = pl.multiple_of(at[4], local)
    span = count * all_heads
    for k in range(count):
        update(1, k, pair_of(0, k * all_heads + mine, local, span))
    first = 2 * span
    update(2, slice(None), pair_of(first, mine, local, all_heads))
    first += 2 * all_heads
    for k in range(sides):
        update(4, k, pair_of(first, k * size, size, sides * size))
    first += 2 * sides * size
    table[...] = rows(first, size * size)
    for e in range(size):
        update(5, slice(e * size, (e + 1) * size), table[pl.ds(e, size, stride=size), :])
    pair = pair_side[...]
    low = pair[2 * HEADS :]
    lines = [
        jnp.concatenate([low[n : n + 1], low[n + 4 : n + 5], low[n + 2 : n + 3], low[n + 6 : n + 7], pair[HEADS + n : HEADS + n + 1]], axis=1)
        for n in range(2)
    ]
    update(0, slice(None), jnp.concatenate(lines, axis=0))
    update(3, slice(None), pair[:HEADS])


def adam_all(at, packed, pair_side, olds, rates, base, pieces, into):
    turned = (1, 3, 4)
    flat = [array.swapaxes(-1, -2) if n in turned else array for n, triple in enumerate(olds) for array in triple]
    size = olds[4][0].shape[2]
    by_order, added = added_specs(base, pieces)
    whole = lambda array: pl.BlockSpec(array.shape, lambda n, at: (0,) * array.ndim)
    *news, changed = pl.pallas_call(
        functools.partial(adam_kernel, rates=rates, pieces=len(pieces)),
        grid_spec=pltpu.PrefetchScalarGridSpec(
            num_scalar_prefetch=1,
            grid=(len(pieces),),
            in_specs=[whole(array) for array in [packed, pair_side] + flat]
            + added
            + [pl.BlockSpec(memory_space=pl.ANY)],
            out_specs=[whole(array) for array in flat] + [by_order],
            scratch_shapes=[pltpu.VMEM((size * size, packed.shape[1]), F32)],
        ),
        out_shape=[jax.ShapeDtypeStruct(array.shape, F32) for array in flat + [base]],
        input_output_aliases={3 + len(flat) + 1 + len(pieces): len(flat)},
        compiler_params=pltpu.CompilerParams(vmem_limit_bytes=VMEM),
        cost_estimate=cost(5),
    )(at, packed, pair_side, *flat, base, *pieces, into)
    news = [array.swapaxes(-1, -2) if n // 3 in turned else array for n, array in enumerate(news)]
    return news + [changed]


def per_device(
    alignment,
    pairs,
    residue_mask,
    row_mask,
    alignment_back,
    pairs_back,
    norm_scales,
    heads_in,
    heads_out,
    bias_weight,
    outer_in,
    outer_out,
    first_norms,
    second_norms,
    first_heads_in,
    second_heads_in,
    first_heads_out,
    second_heads_out,
    first_bias_weight,
    second_bias_weight,
    first_outer_in,
    second_outer_in,
    first_outer_out,
    second_outer_out,
):
    row_count = lax.axis_size("row")
    head_count = lax.axis_size("head")
    head_index = lax.axis_index("head")
    devices = row_count * head_count
    rows_here, residues, width = alignment.shape
    pair_rows, pair_cols, pair_width = pairs.shape
    size = width // HEADS
    outer_width = outer_in.shape[2]
    all_rows = rows_here * row_count
    own = rows_here // head_count
    start = head_index * own
    pair_gain = norm_scales[0:1, 2 * width :]
    pair_shift = norm_scales[1:2, 2 * width :]
    residue_live = residue_mask.astype(F32)
    row_live = lax.dynamic_slice_in_dim(row_mask, start, own, 0).astype(F32)
    flat_live = jnp.repeat(residue_live.reshape(-1, QUADS), outer_in.shape[2], axis=1)
    row_live = jnp.broadcast_to(row_live[:, None, None], (own, 1, 128))
    bias_low = bias_weight.astype(BF16)

    fast = (row_count, head_count, pair_cols, own * outer_width) == (8, 4, 128, 128)

    local = heads_in.shape[2]
    outer_t = outer_in.swapaxes(1, 2).reshape(2 * outer_width, width)
    if fast:
        bias, weights = pair_bias(
            pairs, norm_scales, bias_weight.T, heads_in.swapaxes(1, 2), heads_out
        )
    else:
        shard = jnp.concatenate([heads_in.astype(BF16).swapaxes(1, 2), heads_out.astype(BF16)[None]])
        weights = lax.all_gather(shard, "head", axis=1, tiled=True)
        bias = pair_forward(pairs, pair_gain, pair_shift, bias_low)
        bias = lax.all_gather(bias, "head", axis=2, tiled=True)
        bias = lax.all_gather(bias, "row", axis=1, tiled=True)[None, None]

    update, left, right, kept, early = attention_forward(
        alignment, norm_scales, weights, outer_t, bias, residue_live[None], row_live, flat_live, fast
    )

    if fast:
        total, left_grad, right_grad, table_grad, hop_one, hop_two = outer_product(
            left, right, early, pairs_back, outer_out, update, all_rows
        )
        updates = [update, early[2], hop_one, hop_two]
    else:
        table = outer_out.astype(BF16).reshape(outer_width, outer_width, pair_width)
        updates = [update]
        for _ in range(head_count - 1):
            updates.append(hop(updates[-1]))
        left = left.reshape(own, residues, outer_width).swapaxes(1, 2)
        left = left.reshape(own, outer_width, row_count, pair_rows).transpose(2, 0, 1, 3)
        right = right.reshape(own, outer_width, head_count, pair_cols).transpose(2, 0, 1, 3)
        both = (row_count, head_count, own, outer_width)
        send = jnp.concatenate(
            [
                jnp.broadcast_to(left[:, None], both + (pair_rows,)),
                jnp.broadcast_to(right[None], both + (pair_cols,)),
            ],
            axis=4,
        )
        flat = (devices, own, outer_width, pair_rows + pair_cols)
        got = lax.all_to_all(send.reshape(flat), EVERY, split_axis=0, concat_axis=0, tiled=True)
        got = got.reshape(all_rows, outer_width, pair_rows + pair_cols)
        total, table_grad, left_grad, right_grad = outer_product_plain(
            got[:, :, :pair_rows], got[:, :, pair_rows:], pairs_back, table, all_rows
        )
        pairs_new = pairs + total
        send = jnp.concatenate([left_grad, right_grad], axis=2).reshape(flat)
        got = lax.all_to_all(send, EVERY, split_axis=0, concat_axis=0, tiled=True)
        got = got.reshape(both + (pair_rows + pair_cols,)).astype(F32)
        left_grad = jnp.sum(got[..., :pair_rows], axis=1).transpose(1, 0, 3, 2).astype(BF16)
        left_grad = left_grad.reshape(own, residues // QUADS, QUADS * outer_width)
        right_grad = jnp.sum(got[..., pair_rows:], axis=0).transpose(1, 2, 0, 3).astype(BF16)
        right_grad = right_grad.reshape(own, outer_width, residues)
        table_grad = table_grad.swapaxes(0, 1).reshape(outer_width * outer_width, pair_width)

    turns = (head_index + head_count - jnp.arange(head_count, dtype=jnp.int32)) % head_count
    order = (turns[:, None] * own + jnp.arange(own, dtype=jnp.int32)[None]).reshape(-1)
    half = own // 2

    def mine(first, hops, second, more):
        parts = [(first, step) for step in hops] + [(second, step) for step in more]
        return jnp.concatenate([order[step * own + n * half : step * own + (n + 1) * half] for n, step in parts])

    backward = functools.partial(
        attention_backward,
        order, alignment, update, alignment_back, norm_scales, weights, outer_t, left_grad, right_grad,
        residue_live[None], row_live, flat_live, kept, bias.shape,
    )
    if fast:
        moved = [hop(hop_one), hop(hop_two)]
    part, bias_grad, *early = backward(first=0, own=half, pairs=[pairs, total] if fast else ())
    if fast:
        pairs_new = early.pop()
        moved, bias_grad, part, early = together(moved, bias_grad, part, early)
        updates += moved
        left_over = hop(moved[0])
    changes = [[part, hop(part)]]
    alignment_new, part, bias_grad, packed, norms = backward(
        first=half, own=half, earlier=bias_grad, early=early, table_grad=table_grad, pieces=updates
    )
    if fast:
        left_over, changes[0][1], bias_grad, part, packed, norms = together(
            left_over, changes[0][1], bias_grad, part, packed, norms
        )
        changes[0].append(hop(changes[0][1]))
        changes.append([part, hop(part)])
        bias_grad, packed = sum_gradients(bias_grad, packed)
        changes[0][2], changes[1][1], bias_grad = together(changes[0][2], changes[1][1], bias_grad)
        changes[0].append(hop(changes[0][2]))
        changes[1].append(hop(changes[1][1]))
        pairs_grad, pair_side, alignment_grad = pair_norm_backward(
            mine(0, (0, 1, 2), 1, (0, 1)),
            pairs,
            pairs_back,
            bias_grad,
            norm_scales,
            bias_weight.T,
            norms,
            alignment_back,
            changes[0][:3] + changes[1][:2],
        )
        pair_side = small_sum(pair_side)
        changes[0][3], changes[1][2], pair_side = together(changes[0][3], changes[1][2], pair_side)
        changes[1].append(hop(changes[1][2]))
    else:
        for _ in range(head_count - 2):
            changes[0].append(hop(changes[0][-1]))
        changes.append([part])
        for _ in range(head_count - 1):
            changes[1].append(hop(changes[1][-1]))
        bias_grad = lax.psum_scatter(bias_grad[0, 0], "row", scatter_dimension=1, tiled=True)
        bias_grad = lax.psum_scatter(bias_grad, "head", scatter_dimension=2, tiled=True)
        pairs_grad, bias_weight_grad, pair_gain_grad, pair_shift_grad = pair_backward(
            pairs, pairs_back, pair_gain, pair_shift, bias_low, bias_grad
        )
        packed, norms, bias_weight_total, pair_norms_total = lax.psum(
            (packed.astype(F32), norms, bias_weight_grad, jnp.stack([pair_gain_grad, pair_shift_grad])), EVERY
        )
    olds = (
        (norm_scales, first_norms, second_norms),
        (heads_in, first_heads_in, second_heads_in),
        (heads_out, first_heads_out, second_heads_out),
        (bias_weight, first_bias_weight, second_bias_weight),
        (outer_in, first_outer_in, second_outer_in),
        (outer_out, first_outer_out, second_outer_out),
    )
    rates = (
        0.5,
        width ** (-0.5),
        max(2 * HEADS * size // residues, 1) ** (-0.5),
        pair_width ** (-0.5),
        width ** (-0.5),
        max(outer_width * outer_width // all_rows, 1) ** (-0.5),
    )
    if fast:
        at = (head_index * local).astype(jnp.int32)[None]
        *news, alignment_grad = adam_all(
            jnp.concatenate([mine(0, (3,), 1, (2,)), at]),
            packed, pair_side, olds, rates, alignment_back, [changes[0][3], changes[1][2]], alignment_grad,
        )
        at = (turns[3] * 2 + 1)[None]
        alignment_new = add_rows(at, alignment, left_over, alignment_new)
        alignment_grad = add_rows(at, alignment_back, changes[1][3], alignment_grad)
        return (alignment_new, pairs_new, alignment_grad, pairs_grad, *news)
    alignment_grad = None
    for step in range(head_count):
        for n in range(2):
            at = (turns[step] * 2 + n)[None]
            alignment_grad = add_rows(at, alignment_back, changes[n][step], alignment_grad)
    def unpack(first, lines):
        return jnp.concatenate([packed[first : first + lines], packed[first + lines : first + 2 * lines]], axis=1)

    lines = 4 * width
    heads_in_total = lax.dynamic_slice_in_dim(
        unpack(0, lines).reshape(4, width, width), head_index * local, local, 1
    ).swapaxes(1, 2)
    heads_out_total = lax.dynamic_slice_in_dim(unpack(2 * lines, width), head_index * local, local, 0)
    lines = 2 * (lines + width)
    outer_in_total = unpack(lines, 2 * outer_width).reshape(2, outer_width, width).swapaxes(1, 2)
    lines += 4 * outer_width
    table_total = packed[lines : lines + outer_width * outer_width]
    table_total = table_total.reshape(outer_width, outer_width, pair_width).swapaxes(0, 1)
    table_total = table_total.reshape(outer_width * outer_width, pair_width)
    norms_total = jnp.concatenate(
        [norms.reshape(2, 2, width).swapaxes(0, 1).reshape(2, 2 * width), pair_norms_total], axis=1
    )
    totals = (norms_total, heads_in_total, heads_out_total, bias_weight_total, outer_in_total, table_total)
    news = []
    for (weight, moment_one, moment_two), total, rate in zip(olds, totals, rates):
        news += adam_update(weight, total, moment_one, moment_two, rate)
    return (alignment_new, pairs_new, alignment_grad, pairs_grad, *news)


def solution(mesh):
    row_msa = P("row", None, None)
    pair = P("row", "head", None)
    columns = P(None, None, "head")
    lines = P("head", None)
    in_specs = (
        (row_msa, pair, P(), P("row"), row_msa, pair, P(), columns, lines)
        + (P(),) * 5
        + (columns,) * 2
        + (lines,) * 2
        + (P(),) * 6
    )
    out_specs = (row_msa, pair, row_msa, pair) + (P(),) * 3 + (columns,) * 3 + (lines,) * 3 + (P(),) * 9
    return jax.shard_map(
        per_device, mesh=mesh, in_specs=in_specs, out_specs=out_specs, check_vma=False
    )
```
